32 devices in a mesh: runs: 2 (over y), chain: 4 (over z), basin: 2 (over x), feat: 2 (over core).
Axes of the slice: x: 2, y: 2, z: 4, core: 2. Of those that a mesh axis runs over, the one named last changes fastest.
Arguments:
- features: bfloat16 [12288, 256], P(('runs', 'chain', 'basin')), parts along dimension 0, may hold values from -6 to 6
- cotangent: float32 [12288, 256], P(('runs', 'chain', 'basin')), parts along dimension 0, may hold values from -6 to 6
- w_in: bfloat16 [3, 256, 1024], P(None, None, 'feat'), may hold values from -0.375 to 0.375
- w_out: bfloat16 [3, 1024, 256], P(None, 'feat'), may hold values from -0.1875 to 0.1875
- block_index: int32 [48, 4], P(('chain', 'basin')), may hold values from 0 to 8, as said below
- block_values: bfloat16 [48, 4, 128, 128], P(('chain', 'basin')), may hold values from -0.25 to 0.25
- send_rows: int32 [8, 2, 128], P(('chain', 'basin')), may hold values from 0 to 767
- send_count: int32 [8, 2], P(('chain', 'basin')), may hold values from 42 to 128, as said below
Outputs:
- grad_features: float32 [12288, 256], P(('runs', 'chain', 'basin')), parts along dimension 0
- grad_w_in: float32 [6, 256, 1024], P('runs', None, 'feat'), parts along dimension 0
- grad_w_out: float32 [6, 1024, 256], P('runs', 'feat'), parts along dimension 0
The draws below stay inside these ranges and needn't reach their ends.
There are 2 independent parts, one for each index of `runs`. The reference program is written for one: setup_inputs(seed, part) draws one part's arguments, and reference() takes and returns one part's arrays. A program takes and returns all parts, laid end to end along the dimension named above; an argument that names none is the same for every part. Nothing has to cross between parts.
Inputs may be any that keep to these rules, and one draw needn't show every extreme that they name: `block_index`: in every shard, block row k lists block k first among its 4 entries, and every block from 6 to 8 appears in some block row. `send_count`: at most 128 live slots from one shard to one group; in every draw some group receives 128 live slots from every shard.
All inputs are finite; a program needn't handle non-finite values.
Results may differ from the reference program's by a relative error of at most 0.018.
Values may be sent and summed in bfloat16 or wider, within the bound.
No kernel may reach another device: no remote copies, remote signals or barrier semaphores. Data moves between devices by JAX's collectives and lax.ppermute only.
A program may use at most 64 MiB of HBM per device.

```python
import jax
import jax.numpy as jnp
from jax import lax

LATENT = 256
EDGE_FF = 1024
BLOCK = 128
BLOCKS_ROW = 4
LAYERS = 3
REACH_DEV = 768
ROW_BLOCKS = 6
DIVERT_CAP = 128
REACHES = 6144
N_CHAIN = 4
N_BASIN = 2


def draw_block_index(key, part):
    key = jax.random.fold_in(key, 11)
    shards = N_CHAIN * N_BASIN
    slots = ROW_BLOCKS * (BLOCKS_ROW - 1)
    shard_keys = jax.random.split(jax.random.fold_in(key, 1), shards)
    ranks = jax.vmap(lambda sub_key: jax.random.permutation(sub_key, slots))(shard_keys)
    ranks = ranks.reshape(shards, ROW_BLOCKS, BLOCKS_ROW - 1).astype(jnp.int32)
    spare = jax.random.randint(jax.random.fold_in(key, 2), (shards, ROW_BLOCKS, BLOCKS_ROW - 1), 0, ROW_BLOCKS + 1 + N_BASIN, dtype=jnp.int32)
    others = jnp.where(ranks < N_BASIN + 1, ROW_BLOCKS + ranks, spare)
    own_block = jnp.broadcast_to(jnp.arange(ROW_BLOCKS, dtype=jnp.int32)[None, :, None], (shards, ROW_BLOCKS, 1))
    return jnp.concatenate([own_block, others], axis=2).reshape(shards * ROW_BLOCKS, BLOCKS_ROW)


def draw_send_count(key, part):
    key = jax.random.fold_in(key, 23)
    shards = N_CHAIN * N_BASIN
    counts = jax.random.randint(jax.random.fold_in(key, 1), (shards, N_BASIN), DIVERT_CAP // 3, DIVERT_CAP + 1, dtype=jnp.int32)
    filled = jax.random.randint(jax.random.fold_in(key, 2), (), 0, N_BASIN, dtype=jnp.int32)
    return jnp.where(jnp.arange(N_BASIN, dtype=jnp.int32)[None, :] == filled, DIVERT_CAP, counts)


def touch_ends(values, own_key, low, top_value):
    shape = values.shape
    index_at = [jax.random.randint(jax.random.fold_in(own_key, axis), (), 0, shape[axis]) for axis in range(len(shape))]
    values = values.at[tuple(index_at)].set(low)
    longest = shape.index(max(shape))
    index_at[longest] = (index_at[longest] + 1) % shape[longest]
    return values.at[tuple(index_at)].set(top_value)


def shard_levels(stream_key, shape, pieces, least, top_value):
    loudness, own = 1.0, jax.random.fold_in(stream_key, 6)
    for axis_at, blocks in pieces:
        heights = jnp.exp(jax.random.uniform(jax.random.fold_in(own, axis_at), (blocks,), jnp.float32, least / len(pieces), top_value / len(pieces)))
        loudness = loudness * jnp.repeat(heights, shape[axis_at] // blocks).reshape([-1 if axis == axis_at else 1 for axis in range(len(shape))])
    return loudness


def gaussian(rng, shape, scale, most, cuts=(), held_as=jnp.bfloat16):
    values = jax.random.normal(rng, shape, jnp.float32) * scale
    if len(cuts) > 0:
        values = shard_levels(rng, shape, cuts, -0.22, 0.18) * values
    return jnp.clip(values, min=-most, max=most).astype(held_as)


def setup_inputs(seed: int = 0, part: int = 0) -> dict:
    arg_keys = jax.random.split(jax.random.key(seed), 9)
    part_keys = jax.random.split(jax.random.fold_in(arg_keys[8], part), 9)
    features = gaussian(part_keys[0], (REACHES, LATENT), 1.0, 6.0, ((0, 8),))
    cotangent = gaussian(part_keys[1], (REACHES, LATENT), 1.0, 6.0, ((0, 8),), jnp.float32)
    w_in = gaussian(arg_keys[2], (LAYERS, LATENT, EDGE_FF), LATENT ** -0.5, 0.375, ((2, 2),))
    w_out = gaussian(arg_keys[3], (LAYERS, EDGE_FF, LATENT), EDGE_FF ** -0.5, 0.1875, ((1, 2),))
    block_index = draw_block_index(jax.random.fold_in(arg_keys[8], 71), part)
    block_values = gaussian(arg_keys[5], (N_CHAIN * N_BASIN * ROW_BLOCKS, BLOCKS_ROW, BLOCK, BLOCK), (BLOCKS_ROW * BLOCK) ** -0.5, 0.25, ((0, 8),))
    send_rows = touch_ends(jax.random.randint(arg_keys[6], (N_CHAIN * N_BASIN, N_BASIN, DIVERT_CAP), 0, REACH_DEV), jax.random.fold_in(arg_keys[6], 1), 0, REACH_DEV - 1).astype(jnp.int32)
    send_count = draw_send_count(jax.random.fold_in(arg_keys[8], 71), part)
    return dict(features=features, cotangent=cotangent, w_in=w_in, w_out=w_out, block_index=block_index, block_values=block_values, send_rows=send_rows, send_count=send_count)


eps = 1e-06
highest = lax.Precision.HIGHEST

def silu_grad(pre_act):
    sigm = jax.nn.sigmoid(pre_act)
    return sigm * (1.0 + pre_act * (1.0 - sigm))

def aggregate(source_table, index_rows, value_rows):
    latent = source_table.shape[-1]
    blocks = source_table.reshape(-1, BLOCK, latent)
    picked = blocks[index_rows]
    mixed_rows = jnp.einsum('ktij,ktjh->kih', value_rows.astype(jnp.float32), picked.astype(jnp.float32), precision=highest)
    return mixed_rows.reshape(-1, latent)

def spread(grad_rows, index_rows, value_rows, sources):
    latent = grad_rows.shape[-1]
    grad_blocks = grad_rows.reshape(-1, BLOCK, latent).astype(jnp.float32)
    products = jnp.einsum('ktij,kih->ktjh', value_rows.astype(jnp.float32), grad_blocks, precision=highest)
    onehot = (index_rows[:, :, None] == jnp.arange(sources, dtype=jnp.int32)[None, None, :]).astype(jnp.float32)
    return jnp.einsum('kts,ktjh->sjh', onehot, products, precision=highest).reshape(-1, latent)

def reference(features, cotangent, w_in, w_out, block_index, block_values, send_rows, send_count):
    chains = N_CHAIN
    groups = N_BASIN
    latent = LATENT
    sources = ROW_BLOCKS + 1 + N_BASIN
    index_dev = block_index.reshape(chains * groups, ROW_BLOCKS, BLOCKS_ROW)
    values_dev = block_values.reshape(chains * groups, ROW_BLOCKS, BLOCKS_ROW, BLOCK, BLOCK)
    rows_dev = send_rows.reshape(chains, groups, groups, DIVERT_CAP)
    live_slots = jnp.arange(DIVERT_CAP, dtype=jnp.int32)[None, None, None, :] < send_count.reshape(chains, groups, groups)[..., None]
    state_now = features.astype(jnp.float32)
    saved = []
    for layer_id in range(LAYERS):
        inputs = state_now.astype(jnp.bfloat16)
        pre_act = jnp.dot(inputs, w_in[layer_id], preferred_element_type=jnp.float32)
        active = jax.nn.silu(pre_act).astype(jnp.bfloat16)
        message = jnp.dot(active, w_out[layer_id], preferred_element_type=jnp.float32).astype(jnp.bfloat16)
        msg_grid = message.reshape(chains, groups, REACH_DEV, latent)
        upstream = jnp.concatenate([jnp.zeros((1, groups, BLOCK, latent), jnp.bfloat16), msg_grid[:-1, :, REACH_DEV - BLOCK:]], axis=0)
        outgoing = jax.vmap(jax.vmap(lambda shard_rows, row_picks: shard_rows[row_picks]))(msg_grid, rows_dev)
        outgoing = jnp.where(live_slots[..., None], outgoing, jnp.zeros((), jnp.bfloat16))
        incoming = jnp.swapaxes(outgoing, 1, 2).reshape(chains, groups, groups * DIVERT_CAP, latent)
        source_table = jnp.concatenate([msg_grid, upstream, incoming], axis=2).reshape(chains * groups, sources * BLOCK, latent)
        mixed_rows = lax.map(lambda bundle: aggregate(bundle[0], bundle[1], bundle[2]), (source_table, index_dev, values_dev))
        residual = state_now + mixed_rows.reshape(-1, latent)
        row_scale = lax.rsqrt(lax.optimization_barrier(jnp.mean(residual * residual, axis=-1, keepdims=True)) + eps)
        saved.append((inputs, pre_act, active, residual, row_scale))
        state_now = residual * row_scale
    grad_state = cotangent
    grad_scale = float(REACHES) ** (-0.5)
    grads_in = []
    grads_out = []
    for layer_id in reversed(range(LAYERS)):
        inputs, pre_act, active, residual, row_scale = saved[layer_id]
        normed = residual * row_scale
        dtotal = row_scale * (grad_state - normed * lax.optimization_barrier(jnp.mean(grad_state * normed, axis=-1, keepdims=True)))
        dround = dtotal.astype(jnp.bfloat16).reshape(chains * groups, REACH_DEV, latent)
        dtable = lax.map(lambda bundle: spread(bundle[0], bundle[1], bundle[2], sources), (dround, index_dev, values_dev))
        dtable = dtable.reshape(chains, groups, sources * BLOCK, latent)
        dlocal = dtable[:, :, :REACH_DEV]
        grad_up = dtable[:, :, REACH_DEV:REACH_DEV + BLOCK]
        grad_inc = dtable[:, :, REACH_DEV + BLOCK:].reshape(chains, groups, groups, DIVERT_CAP, latent)
        downhill = jnp.concatenate([grad_up[1:], jnp.zeros((1, groups, BLOCK, latent), jnp.float32)], axis=0)
        dlocal = dlocal.at[:, :, REACH_DEV - BLOCK:].add(downhill)
        returned = jnp.where(live_slots[..., None], jnp.swapaxes(grad_inc, 1, 2), 0.0)
        dlocal = jax.vmap(jax.vmap(lambda accum, row_picks, values: accum.at[row_picks.reshape(-1)].add(values.reshape(-1, latent))))(dlocal, rows_dev, returned)
        grad_msg = dlocal.reshape(-1, latent).astype(jnp.bfloat16)
        grad_act = jnp.dot(grad_msg, w_out[layer_id].T, preferred_element_type=jnp.float32)
        grad_pre = (grad_act * silu_grad(pre_act)).astype(jnp.bfloat16)
        grad_state = dtotal + jnp.dot(grad_pre, w_in[layer_id].T, preferred_element_type=jnp.float32)
        grads_out.append(jnp.dot(active.T, grad_msg, preferred_element_type=jnp.float32) * grad_scale)
        grads_in.append(jnp.dot(inputs.T, grad_pre, preferred_element_type=jnp.float32) * grad_scale)
    return (grad_state, jnp.stack(grads_in[::-1]), jnp.stack(grads_out[::-1]))
```

```python
import functools

import jax
import jax.numpy as jnp
from jax import lax
from jax.experimental import pallas as pl
from jax.experimental.pallas import tpu as pltpu
from jax.sharding import PartitionSpec as P

BLOCK = 128
EPS = 1e-06
F32 = jnp.float32
BF16 = jnp.bfloat16
VMEM = pl.BlockSpec(memory_space=pltpu.VMEM)
SMEM = pl.BlockSpec(memory_space=pltpu.SMEM)
NN = (((1,), (0,)), ((), ()))
NT = (((1,), (1,)), ((), ()))
TN = (((0,), (0,)), ((), ()))


def mm(a, b, dims=NN):
    return lax.dot_general(a, b, dims, preferred_element_type=F32)


def call(body, outs, ins, flops, scratch=(), name=None):
    return pl.pallas_call(
        body,
        out_shape=[jax.ShapeDtypeStruct(s, d) for s, d in outs],
        in_specs=[SMEM if x.dtype == jnp.int32 and x.size < 100 else VMEM for x in ins],
        out_specs=[VMEM] * len(outs),
        scratch_shapes=list(scratch),
        compiler_params=pltpu.CompilerParams(vmem_limit_bytes=32 * 1024 * 1024),
        cost_estimate=pl.CostEstimate(flops=flops, bytes_accessed=4_000_000, transcendentals=0),
        name=name,
    )(*ins)


def sigmoid(v):
    return 1.0 / (1.0 + jnp.exp(-v))


def message_of(x, halves):
    total = None
    for w_in, w_out in halves:
        pre = mm(x, w_in)
        part = mm((pre * sigmoid(pre)).astype(BF16), w_out)
        total = part if total is None else total + part
    return total.astype(BF16)


def message_grad(x, dmsg, halves):
    total = None
    kept = None
    for w_in, w_out in halves:
        pre = mm(x, w_in)
        sig = sigmoid(pre)
        dact = mm(dmsg, w_out, NT)
        dpre = (dact * (sig * (1.0 + pre * (1.0 - sig)))).astype(BF16)
        if kept is None:
            kept = ((pre * sig).astype(BF16), dpre)
        part = mm(dpre, w_in, NT)
        total = part if total is None else total + part
    return total, kept


def normed_of(total):
    scale = lax.rsqrt(jnp.mean(total * total, axis=-1, keepdims=True) + EPS)
    return scale, scale * total


def norm_grad(grad, total):
    scale, normed = normed_of(total)
    return scale * (grad - normed * jnp.mean(grad * normed, axis=-1, keepdims=True))


def setup_kernel(groups, rows, send_rows, send_count, features, *outs):
    pick, spread, pick_self, up = outs[:4]
    sends = outs[4:]
    b = lax.axis_index("basin")
    lane = lax.broadcasted_iota(jnp.int32, (1, BLOCK), 1)
    for s in range(groups):
        target = lax.rem(b + s, groups)
        chosen = send_rows[0, pl.ds(target, 1), :]
        chosen = jnp.where(lane < send_count[0, target], chosen, -1)
        across = jnp.broadcast_to(chosen, (BLOCK, BLOCK))
        down = across.T
        for r in range(rows // BLOCK):
            at = lax.broadcasted_iota(jnp.int32, (BLOCK, BLOCK), 1) + r * BLOCK
            hot = (down == at).astype(F32).astype(BF16)
            if s == 0:
                pick_self[:, r * BLOCK : (r + 1) * BLOCK] = hot
            else:
                pick[(s - 1) * BLOCK : s * BLOCK, r * BLOCK : (r + 1) * BLOCK] = hot
                at = lax.broadcasted_iota(jnp.int32, (BLOCK, BLOCK), 0) + r * BLOCK
                spread[r * BLOCK : (r + 1) * BLOCK, (s - 1) * BLOCK : s * BLOCK] = (
                    (across == at).astype(F32).astype(BF16)
                )
    up[...] = features[rows - BLOCK :, :]
    for s, send in enumerate(sends):
        send[...] = mm(pick[s * BLOCK : (s + 1) * BLOCK, :], features[...]).astype(BF16)


def adjacency_kernel(groups, rows, index, values, pick_self, local, local_t, remote, remote_t, acc):
    own = rows // BLOCK
    b = lax.axis_index("basin")
    acc[...] = jnp.zeros_like(acc)
    for k in range(own):
        for t in range(index.shape[1]):
            v = index[k, t]
            sender = lax.rem(b + groups - (v - own - 1), groups)
            far = jnp.where(v == own, own + 1, jnp.where(sender == 0, own, own + 1 + sender))
            at = jnp.where(v < own, v, far)
            here = (pl.ds(k * BLOCK, BLOCK), pl.ds(pl.multiple_of(at * BLOCK, BLOCK), BLOCK))
            acc[here] += values[k, t].astype(F32)
    mine = acc[:, rows : rows + BLOCK].astype(BF16)
    full = acc[:, :rows] + mm(mine, pick_self[...])
    local[...] = full.astype(BF16)
    local_t[...] = full.T.astype(BF16)
    far = acc[:, rows + BLOCK :]
    remote[...] = far.astype(BF16)
    remote_t[...] = far.T.astype(BF16)


def shadow_fwd_kernel(layer, inputs, local, wi0, wi1, wo0, wo1, mixed, msg):
    halves = [(wi0[layer], wo0[layer]), (wi1[layer], wo1[layer])]
    rows = inputs.shape[0]
    for r in range(0, rows, 256):
        msg[r : r + 256, :] = message_of(inputs[r : r + 256, :], halves)
    mixed[...] = mm(local[...], msg[...])


def mixed_total(layer, state, mixed, received, remote, weights):
    wi0, wi1, wo0, wo1 = weights
    halves = [(wi0[layer], wo0[layer]), (wi1[layer], wo1[layer])]
    far = jnp.concatenate([x[...] for x in received], axis=0)
    return state + mixed[...] + mm(remote[...], message_of(far, halves))


def post_fwd_kernel(layer, groups, *refs):
    prev, mixed, remote, pick = refs[:4]
    weights = refs[4:8]
    received = refs[8 : 8 + groups]
    total, inputs, up = refs[8 + groups : 11 + groups]
    sends = refs[11 + groups :]
    state = prev[...].astype(F32) if layer == 0 else normed_of(prev[...])[1]
    total[...] = mixed_total(layer, state, mixed, received, remote, weights)
    new = normed_of(total[...])[1].astype(BF16)
    inputs[...] = new
    up[...] = new[new.shape[0] - BLOCK :, :]
    for s, send in enumerate(sends):
        send[...] = mm(pick[s * BLOCK : (s + 1) * BLOCK, :], new).astype(BF16)


def start_bwd(layer, dtotal_now, weights, received, remote_t, outs):
    dtotal, dround, far_x, far_dmsg, far_act, far_dpre = outs[:6]
    backs = outs[6:]
    wi0, wi1, wo0, wo1 = weights
    halves = [(wi0[layer], wo0[layer]), (wi1[layer], wo1[layer])]
    dtotal[...] = dtotal_now
    dround[...] = dtotal_now.astype(BF16)
    far = jnp.concatenate([x[...] for x in received], axis=0)
    dmsg = mm(remote_t[...], dround[...]).astype(BF16)
    back, (act, dpre) = message_grad(far, dmsg, halves)
    far_x[...] = far
    far_dmsg[...] = dmsg
    far_act[...] = act
    far_dpre[...] = dpre
    for s, out in enumerate(backs):
        out[...] = back[s * BLOCK : (s + 1) * BLOCK, :].astype(BF16)


def turn_kernel(layer, groups, *refs):
    prev, mixed, remote, remote_t, cot = refs[:5]
    weights = refs[5:9]
    received = refs[9 : 9 + groups]
    outs = refs[9 + groups :]
    state = normed_of(prev[...])[1]
    total = mixed_total(layer, state, mixed, received, remote, weights)
    start_bwd(layer, norm_grad(cot[...], total), weights, received, remote_t, outs)


def shadow_bwd_kernel(layer, grad_scale, *refs):
    dround, inputs, local_t = refs[:3]
    wi0, wi1, wo0, wo1 = refs[3:7]
    far_x, far_dmsg, far_act, far_dpre = refs[7:11]
    back, g_in, g_out, dmsg, act, dpre = refs[11:]
    halves = [(wi0[layer], wo0[layer]), (wi1[layer], wo1[layer])]
    dmsg[...] = mm(local_t[...], dround[...]).astype(BF16)
    rows = inputs.shape[0]
    for r in range(0, rows, 256):
        here = slice(r, r + 256)
        grad, (a, d) = message_grad(inputs[here, :], dmsg[here, :], halves)
        back[here, :] = grad
        act[here, :] = a
        dpre[here, :] = d
    g_in[...] = (
        (mm(inputs[...], dpre[...], TN) + mm(far_x[...], far_dpre[...], TN)) * grad_scale
    ).astype(BF16)
    g_out[...] = (
        (mm(act[...], dmsg[...], TN) + mm(far_act[...], far_dmsg[...], TN)) * grad_scale
    ).astype(BF16)


def gathered_grad(dtotal, back, returned, spread):
    grad = dtotal[...] + back[...]
    if len(returned) > 1:
        far = jnp.concatenate([x[...] for x in returned[1:]], axis=0)
        grad = grad + mm(spread[...], far)
    rows = grad.shape[0]
    low = grad[rows - BLOCK :, :] + returned[0][...].astype(F32)
    return jnp.concatenate([grad[: rows - BLOCK, :], low], axis=0)


def post_bwd_kernel(layer, groups, *refs):
    dtotal, back, spread, remote_t, total = refs[:5]
    weights = refs[5:9]
    returned = refs[9 : 9 + groups]
    received = refs[9 + groups : 9 + 2 * groups]
    outs = refs[9 + 2 * groups :]
    grad = gathered_grad(dtotal, back, returned, spread)
    start_bwd(layer, norm_grad(grad, total[...]), weights, received, remote_t, outs)


def last_kernel(groups, *refs):
    dtotal, back, spread = refs[:3]
    refs[3 + groups][...] = gathered_grad(dtotal, back, refs[3 : 3 + groups], spread)


def along(x, axis, distance):
    n = lax.axis_size(axis)
    return lax.ppermute(x, axis, [(i, i + distance) for i in range(n) if 0 <= i + distance < n])


def around(x, axis, distance):
    n = lax.axis_size(axis)
    return lax.ppermute(x, axis, [(i, (i + distance) % n) for i in range(n)])


def exchange(up, sends, sign):
    return [along(up, "chain", sign)] + [
        around(x, "basin", sign * (s + 1)) for s, x in enumerate(sends)
    ]


def shards(features, cotangent, w_in, w_out, block_index, block_values, send_rows, send_count):
    rows, latent = features.shape
    groups = lax.axis_size("basin")
    layers, _, half = w_in.shape
    far_rows = groups * BLOCK
    sent_rows = max(groups - 1, 1) * BLOCK
    own = rows // BLOCK
    grad_scale = float(rows * lax.axis_size("chain") * groups) ** (-0.5)

    def act16(n, m=latent):
        return ((n, m), BF16)

    wi1 = around(w_in, "feat", 1)
    wo1 = around(w_out, "feat", 1)
    weights = (w_in, wi1, w_out, wo1)
    ffn = 4 * latent * 2 * half

    pick, spread, pick_self, up, *sends = call(
        functools.partial(setup_kernel, groups, rows),
        [act16(sent_rows, rows), act16(rows, sent_rows), act16(BLOCK, rows), act16(BLOCK)]
        + [act16(BLOCK)] * (groups - 1),
        [send_rows, send_count, features],
        2 * rows * sent_rows * latent,
        name="setup",
    )
    received = [exchange(up, sends, 1)]
    local, local_t, remote, remote_t = call(
        functools.partial(adjacency_kernel, groups, rows),
        [act16(rows, rows), act16(rows, rows), act16(rows, far_rows), act16(far_rows, rows)],
        [block_index, block_values, pick_self],
        2 * rows * rows * BLOCK,
        scratch=[pltpu.VMEM((rows, (own + groups + 1) * BLOCK), F32)],
        name="adjacency",
    )
    inputs = [features]
    totals = []
    for layer in range(layers):
        mixed, _ = call(
            functools.partial(shadow_fwd_kernel, layer),
            [((rows, latent), F32), act16(rows)],
            [inputs[layer], local, *weights],
            rows * ffn + 2 * rows * rows * latent,
            name=f"local{layer}",
        )
        prev = features if layer == 0 else totals[-1]
        if layer + 1 < layers:
            total, new, up, *sends = call(
                functools.partial(post_fwd_kernel, layer, groups),
                [((rows, latent), F32), act16(rows)] + [act16(BLOCK)] * groups,
                [prev, mixed, remote, pick, *weights, *received[layer]],
                far_rows * ffn + 2 * rows * far_rows * latent,
                name=f"mix{layer}",
            )
            totals.append(total)
            inputs.append(new)
            received.append(exchange(up, sends, 1))
    bwd_outs = (
        [((rows, latent), F32), act16(rows), act16(far_rows), act16(far_rows)]
        + [act16(far_rows, half)] * 2
        + [act16(BLOCK)] * groups
    )
    last = layers - 1
    outs = call(
        functools.partial(turn_kernel, last, groups),
        bwd_outs,
        [totals[-1], mixed, remote, remote_t, cotangent, *weights, *received[last]],
        2 * far_rows * ffn,
        name="turn",
    )
    summed = []
    for layer in reversed(range(layers)):
        dtotal, dround = outs[:2]
        far_saved = outs[2:6]
        returned = exchange(outs[6], outs[7:], -1)
        back, g_in, g_out, *_ = call(
            functools.partial(shadow_bwd_kernel, layer, grad_scale),
            [((rows, latent), F32), act16(latent, half), act16(half), act16(rows)]
            + [act16(rows, half)] * 2,
            [dround, inputs[layer], local_t, *weights, *far_saved],
            3 * rows * ffn + 2 * rows * rows * latent,
            name=f"back{layer}",
        )
        summed.append(lax.psum((g_in, g_out), ("chain", "basin")))
        if layer:
            outs = call(
                functools.partial(post_bwd_kernel, layer - 1, groups),
                bwd_outs,
                [dtotal, back, spread, remote_t, totals[layer - 1]]
                + [*weights, *returned, *received[layer - 1]],
                2 * far_rows * ffn,
                name=f"join{layer}",
            )
    (grad,) = call(
        functools.partial(last_kernel, groups),
        [((rows, latent), F32)],
        [dtotal, back, spread, *returned],
        2 * rows * sent_rows * latent,
        name="join0",
    )
    summed_in = jnp.stack([x for x, _ in summed[::-1]]).astype(F32)
    summed_out = jnp.stack([x for _, x in summed[::-1]]).astype(F32)
    return (grad, summed_in, summed_out)


def solution(mesh):
    placed = (
        P(("runs", "chain", "basin"), None),
        P(("runs", "chain", "basin"), None),
        P(None, None, "feat"),
        P(None, "feat", None),
        P(("chain", "basin"), None),
        P(("chain", "basin"), None, None, None),
        P(("chain", "basin"), None, None),
        P(("chain", "basin"), None),
    )
    return jax.shard_map(
        shards,
        mesh=mesh,
        in_specs=placed,
        out_specs=(
            P(("runs", "chain", "basin"), None),
            P("runs", None, "feat"),
            P("runs", "feat", None),
        ),
        check_vma=False,
    )
```

```python
import functools

import jax
import jax.numpy as jnp
from jax import lax
from jax.experimental import pallas as pl
from jax.experimental.pallas import tpu as pltpu
from jax.sharding import PartitionSpec as P

BLOCK = 128
LANES = 128
EPS = 1e-06
F32 = jnp.float32
BF16 = jnp.bfloat16
VMEM = pl.BlockSpec(memory_space=pltpu.VMEM)
ANY = pl.BlockSpec(memory_space=pl.ANY)
SMEM = pl.BlockSpec(memory_space=pltpu.SMEM)
NN = (((1,), (0,)), ((), ()))
NT = (((1,), (1,)), ((), ()))
TN = (((0,), (0,)), ((), ()))


def mm(a, b, dims=NN):
    return lax.dot_general(a, b, dims, preferred_element_type=F32)


def call(body, outs, ins, flops, scratch=(), name=None):
    return pl.pallas_call(
        body,
        out_shape=[jax.ShapeDtypeStruct(s, d) for s, d in outs],
        in_specs=[SMEM if x.dtype == jnp.int32 and x.size < 100 else VMEM for x in ins],
        out_specs=[VMEM] * len(outs),
        scratch_shapes=list(scratch),
        compiler_params=pltpu.CompilerParams(vmem_limit_bytes=32 * 1024 * 1024),
        cost_estimate=pl.CostEstimate(flops=flops, bytes_accessed=4_000_000, transcendentals=0),
        name=name,
    )(*ins)


def sigmoid(v):
    return 1.0 / (1.0 + jnp.exp(-v))


def message_of(x, halves):
    total = None
    for w_in, w_out in halves:
        pre = mm(x, w_in)
        part = mm((pre * sigmoid(pre)).astype(BF16), w_out)
        total = part if total is None else total + part
    return total.astype(BF16)


def message_grad(x, dmsg, halves):
    total = None
    kept = None
    for w_in, w_out in halves:
        pre = mm(x, w_in)
        sig = sigmoid(pre)
        dact = mm(dmsg, w_out, NT)
        dpre = (dact * (sig * (1.0 + pre * (1.0 - sig)))).astype(BF16)
        if kept is None:
            kept = ((pre * sig).astype(BF16), dpre)
        part = mm(dpre, w_in, NT)
        total = part if total is None else total + part
    return total, kept


def normed_of(total):
    scale = lax.rsqrt(jnp.mean(total * total, axis=-1, keepdims=True) + EPS)
    return scale, scale * total


def norm_grad(grad, total):
    scale, normed = normed_of(total)
    return scale * (grad - normed * jnp.mean(grad * normed, axis=-1, keepdims=True))


def setup_kernel(groups, rows, send_rows, send_count, features, *outs):
    pick, spread, pick_self, up = outs[:4]
    sends = outs[4:]
    b = lax.axis_index("basin")
    lane = lax.broadcasted_iota(jnp.int32, (1, BLOCK), 1)
    for s in range(groups):
        target = lax.rem(b + s, groups)
        chosen = send_rows[0, pl.ds(target, 1), :]
        chosen = jnp.where(lane < send_count[0, target], chosen, -1)
        across = jnp.broadcast_to(chosen, (BLOCK, BLOCK))
        down = across.T
        for r in range(rows // BLOCK):
            at = lax.broadcasted_iota(jnp.int32, (BLOCK, BLOCK), 1) + r * BLOCK
            hot = (down == at).astype(F32).astype(BF16)
            if s == 0:
                pick_self[:, r * BLOCK : (r + 1) * BLOCK] = hot
            else:
                pick[(s - 1) * BLOCK : s * BLOCK, r * BLOCK : (r + 1) * BLOCK] = hot
                at = lax.broadcasted_iota(jnp.int32, (BLOCK, BLOCK), 0) + r * BLOCK
                spread[r * BLOCK : (r + 1) * BLOCK, (s - 1) * BLOCK : s * BLOCK] = (
                    (across == at).astype(F32).astype(BF16)
                )
    up[...] = features[rows - BLOCK :, :]
    for s, send in enumerate(sends):
        send[...] = mm(pick[s * BLOCK : (s + 1) * BLOCK, :], features[...]).astype(BF16)


def adjacency_kernel(groups, rows, index, values, pick_self, local, local_t, remote, remote_t, acc):
    own = rows // BLOCK
    b = lax.axis_index("basin")
    acc[...] = jnp.zeros_like(acc)
    for k in range(own):
        for t in range(index.shape[1]):
            v = index[k, t]
            sender = lax.rem(b + groups - (v - own - 1), groups)
            far = jnp.where(v == own, own + 1, jnp.where(sender == 0, own, own + 1 + sender))
            at = jnp.where(v < own, v, far)
            here = (pl.ds(k * BLOCK, BLOCK), pl.ds(pl.multiple_of(at * BLOCK, BLOCK), BLOCK))
            acc[here] += values[k, t].astype(F32)
    mine = acc[:, rows : rows + BLOCK].astype(BF16)
    full = acc[:, :rows] + mm(mine, pick_self[...])
    local[...] = full.astype(BF16)
    local_t[...] = full.T.astype(BF16)
    far = acc[:, rows + BLOCK :]
    remote[...] = far.astype(BF16)
    remote_t[...] = far.T.astype(BF16)


def shadow_fwd_kernel(layer, inputs, local, wi0, wi1, wo0, wo1, mixed, msg):
    halves = [(wi0[layer], wo0[layer]), (wi1[layer], wo1[layer])]
    rows = inputs.shape[0]
    for r in range(0, rows, 256):
        msg[r : r + 256, :] = message_of(inputs[r : r + 256, :], halves)
    mixed[...] = mm(local[...], msg[...])


def mixed_total(layer, state, mixed, received, remote, weights):
    wi0, wi1, wo0, wo1 = weights
    halves = [(wi0[layer], wo0[layer]), (wi1[layer], wo1[layer])]
    far = jnp.concatenate([x[...] for x in received], axis=0)
    return state + mixed[...] + mm(remote[...], message_of(far, halves))


def post_fwd_kernel(layer, groups, *refs):
    prev, mixed, remote, pick = refs[:4]
    weights = refs[4:8]
    received = refs[8 : 8 + groups]
    total, inputs, up = refs[8 + groups : 11 + groups]
    sends = refs[11 + groups :]
    state = prev[...].astype(F32) if layer == 0 else normed_of(prev[...])[1]
    total[...] = mixed_total(layer, state, mixed, received, remote, weights)
    new = normed_of(total[...])[1].astype(BF16)
    inputs[...] = new
    up[...] = new[new.shape[0] - BLOCK :, :]
    for s, send in enumerate(sends):
        send[...] = mm(pick[s * BLOCK : (s + 1) * BLOCK, :], new).astype(BF16)


def start_bwd(layer, dtotal_now, weights, received, remote_t, outs):
    dtotal, dround, far_x, far_dmsg, far_act, far_dpre = outs[:6]
    backs = outs[6:]
    wi0, wi1, wo0, wo1 = weights
    halves = [(wi0[layer], wo0[layer]), (wi1[layer], wo1[layer])]
    dtotal[...] = dtotal_now
    dround[...] = dtotal_now.astype(BF16)
    far = jnp.concatenate([x[...] for x in received], axis=0)
    dmsg = mm(remote_t[...], dround[...]).astype(BF16)
    back, (act, dpre) = message_grad(far, dmsg, halves)
    far_x[...] = far
    far_dmsg[...] = dmsg
    far_act[...] = act
    far_dpre[...] = dpre
    for s, out in enumerate(backs):
        out[...] = back[s * BLOCK : (s + 1) * BLOCK, :].astype(BF16)


def turn_kernel(layer, groups, *refs):
    prev, mixed, remote, remote_t, cot = refs[:5]
    weights = refs[5:9]
    received = refs[9 : 9 + groups]
    outs = refs[9 + groups :]
    state = normed_of(prev[...])[1]
    total = mixed_total(layer, state, mixed, received, remote, weights)
    start_bwd(layer, norm_grad(cot[...], total), weights, received, remote_t, outs)


def shadow_bwd_kernel(layer, grad_scale, pieces, *refs):
    dround, inputs, local_t = refs[:3]
    wi0, wi1, wo0, wo1 = refs[3:7]
    far_x, far_dmsg, far_act, far_dpre = refs[7:11]
    back = refs[11]
    grads, dmsg, act, dpre = refs[-4:]
    halves = [(wi0[layer], wo0[layer]), (wi1[layer], wo1[layer])]
    dmsg[...] = mm(local_t[...], dround[...]).astype(BF16)
    rows, latent = inputs.shape
    hidden = act.shape[1]
    for r in range(0, rows, 256):
        here = slice(r, r + 256)
        grad, (a, d) = message_grad(inputs[here, :], dmsg[here, :], halves)
        back[here, :] = grad
        act[here, :] = a
        dpre[here, :] = d
    g_in = (mm(inputs[...], dpre[...], TN) + mm(far_x[...], far_dpre[...], TN)) * grad_scale
    for j in range(hidden // LANES):
        grads[j * latent : (j + 1) * latent, :] = g_in[:, j * LANES : (j + 1) * LANES]
    g_out = (mm(act[...], dmsg[...], TN) + mm(far_act[...], far_dmsg[...], TN)) * grad_scale
    for j in range(latent // LANES):
        at = hidden // LANES * latent + j * hidden
        grads[at : at + hidden, :] = g_out[:, j * LANES : (j + 1) * LANES]
    outs = refs[12:-4]
    for lo, hi, axes in pieces:
        n = lax.axis_size(axes[0])
        scatter_parts(grads.at[lo:hi], axes[0], outs[:n])
        outs = outs[n:]


def scatter_parts(block, axis, outs):
    n = lax.axis_size(axis)
    m = block.shape[0] // n
    me = lax.axis_index(axis)
    for s, out in enumerate(outs):
        part = block[pl.ds(pl.multiple_of(lax.rem(me + s, n) * m, m), m), :]
        out[...] = part.astype(out.dtype)


def add_scatter_kernel(axis, parts, *refs):
    acc = refs[-1]
    acc[...] = refs[0][...]
    for part in refs[1:parts]:
        acc[...] += part[...].astype(F32)
    scatter_parts(acc, axis, refs[parts:-1])


def add_kernel(*refs):
    total = refs[0][...]
    for part in refs[1:-1]:
        total = total + part[...].astype(F32)
    refs[-1][...] = total.astype(BF16)


def place(axis, parts, out):
    n = lax.axis_size(axis)
    m = parts[0].shape[0]
    me = lax.axis_index(axis)
    for s, part in enumerate(parts):
        at = pl.ds(pl.multiple_of(lax.rem(me + n - s, n) * m, m), m)
        out[at, :] = part[...].astype(out.dtype)


def place_kernel(axis, *refs):
    place(axis, refs[:-1], refs[-1])


def write_kernel(layer, pieces, kept, *refs):
    out_in, out_out, grads, slab_in, slab_out, sem = refs[-6:]
    parts = refs[kept : kept + sum(lax.axis_size(axes[0]) for _, _, axes in pieces)]
    for lo, hi, axes in pieces:
        n = lax.axis_size(axes[0])
        place(axes[0], parts[:n], grads.at[lo:hi])
        parts = parts[n:]
    latent, hidden = slab_in.shape
    for j in range(hidden // LANES):
        slab_in[:, j * LANES : (j + 1) * LANES] = grads[j * latent : (j + 1) * latent, :]
    first = pltpu.make_async_copy(slab_in, out_in.at[layer], sem.at[0])
    first.start()
    for j in range(latent // LANES):
        at = hidden // LANES * latent + j * hidden
        slab_out[:, j * LANES : (j + 1) * LANES] = grads[at : at + hidden, :]
    second = pltpu.make_async_copy(slab_out, out_out.at[layer], sem.at[1])
    second.start()
    first.wait()
    second.wait()


def shifted(parts, axis):
    return [around(x, axis, s + 1) for s, x in enumerate(parts)]


def summed_piece(parts, axes, name):
    n0, n1 = lax.axis_size(axes[0]), lax.axis_size(axes[1])
    m = parts[0].shape[0]
    got = shifted(parts[1:], axes[0])
    parts = call(
        functools.partial(add_scatter_kernel, axes[1], n0),
        [((m // n1, LANES), F32)] + [((m // n1, LANES), BF16)] * (n1 - 1),
        [parts[0], *got],
        1_000_000,
        scratch=[pltpu.VMEM((m, LANES), F32)],
        name=f"add_{name}",
    )
    got = shifted(parts[1:], axes[1])
    (own,) = call(add_kernel, [((m // n1, LANES), BF16)], [parts[0], *got], 1_000_000, name=f"end_{name}")
    got = shifted([own] * (n1 - 1), axes[1])
    (own,) = call(
        functools.partial(place_kernel, axes[1]),
        [((m, LANES), BF16)],
        [own, *got],
        1_000_000,
        name=f"place_{name}",
    )
    return [own, *shifted([own] * (n0 - 1), axes[0])]


def gathered_grad(dtotal, back, returned, spread):
    grad = dtotal[...] + back[...]
    if len(returned) > 1:
        far = jnp.concatenate([x[...] for x in returned[1:]], axis=0)
        grad = grad + mm(spread[...], far)
    rows = grad.shape[0]
    low = grad[rows - BLOCK :, :] + returned[0][...].astype(F32)
    return jnp.concatenate([grad[: rows - BLOCK, :], low], axis=0)


def post_bwd_kernel(layer, groups, *refs):
    dtotal, back, spread, remote_t, total = refs[:5]
    weights = refs[5:9]
    returned = refs[9 : 9 + groups]
    received = refs[9 + groups : 9 + 2 * groups]
    outs = refs[9 + 2 * groups :]
    grad = gathered_grad(dtotal, back, returned, spread)
    start_bwd(layer, norm_grad(grad, total[...]), weights, received, remote_t, outs)


def last_kernel(groups, *refs):
    dtotal, back, spread = refs[:3]
    refs[3 + groups][...] = gathered_grad(dtotal, back, refs[3 : 3 + groups], spread)


def along(x, axis, distance):
    n = lax.axis_size(axis)
    return lax.ppermute(x, axis, [(i, i + distance) for i in range(n) if 0 <= i + distance < n])


def around(x, axis, distance):
    n = lax.axis_size(axis)
    return lax.ppermute(x, axis, [(i, (i + distance) % n) for i in range(n)])


def exchange(up, sends, sign):
    return [along(up, "chain", sign)] + [
        around(x, "basin", sign * (s + 1)) for s, x in enumerate(sends)
    ]


def shards(features, cotangent, w_in, w_out, block_index, block_values, send_rows, send_count):
    rows, latent = features.shape
    groups = lax.axis_size("basin")
    layers, _, half = w_in.shape
    far_rows = groups * BLOCK
    sent_rows = max(groups - 1, 1) * BLOCK
    own = rows // BLOCK
    grad_scale = float(rows * lax.axis_size("chain") * groups) ** (-0.5)

    def act16(n, m=latent):
        return ((n, m), BF16)

    wi1 = around(w_in, "feat", 1)
    wo1 = around(w_out, "feat", 1)
    weights = (w_in, wi1, w_out, wo1)
    ffn = 4 * latent * 2 * half

    pick, spread, pick_self, up, *sends = call(
        functools.partial(setup_kernel, groups, rows),
        [act16(sent_rows, rows), act16(rows, sent_rows), act16(BLOCK, rows), act16(BLOCK)]
        + [act16(BLOCK)] * (groups - 1),
        [send_rows, send_count, features],
        2 * rows * sent_rows * latent,
        name="setup",
    )
    received = [exchange(up, sends, 1)]
    local, local_t, remote, remote_t = call(
        functools.partial(adjacency_kernel, groups, rows),
        [act16(rows, rows), act16(rows, rows), act16(rows, far_rows), act16(far_rows, rows)],
        [block_index, block_values, pick_self],
        2 * rows * rows * BLOCK,
        scratch=[pltpu.VMEM((rows, (own + groups + 1) * BLOCK), F32)],
        name="adjacency",
    )
    inputs = [features]
    totals = []
    for layer in range(layers):
        mixed, _ = call(
            functools.partial(shadow_fwd_kernel, layer),
            [((rows, latent), F32), act16(rows)],
            [inputs[layer], local, *weights],
            rows * ffn + 2 * rows * rows * latent,
            name=f"local{layer}",
        )
        prev = features if layer == 0 else totals[-1]
        if layer + 1 < layers:
            total, new, up, *sends = call(
                functools.partial(post_fwd_kernel, layer, groups),
                [((rows, latent), F32), act16(rows)] + [act16(BLOCK)] * groups,
                [prev, mixed, remote, pick, *weights, *received[layer]],
                far_rows * ffn + 2 * rows * far_rows * latent,
                name=f"mix{layer}",
            )
            totals.append(total)
            inputs.append(new)
            received.append(exchange(up, sends, 1))
    bwd_outs = (
        [((rows, latent), F32), act16(rows), act16(far_rows), act16(far_rows)]
        + [act16(far_rows, half)] * 2
        + [act16(BLOCK)] * groups
    )
    last = layers - 1
    outs = call(
        functools.partial(turn_kernel, last, groups),
        bwd_outs,
        [totals[-1], mixed, remote, remote_t, cotangent, *weights, *received[last]],
        2 * far_rows * ffn,
        name="turn",
    )
    grad_rows = 2 * latent * half // LANES
    pieces = [(0, grad_rows, ("basin", "chain"))]
    part_shapes = []
    for lo, hi, axes in pieces:
        n = lax.axis_size(axes[0])
        m = (hi - lo) // n
        part_shapes += [((m, LANES), F32)] + [((m, LANES), BF16)] * (n - 1)
    written = []
    for layer in reversed(range(layers)):
        dtotal, dround = outs[:2]
        far_saved = outs[2:6]
        returned = exchange(outs[6], outs[7:], -1)
        back, *parts = call(
            functools.partial(shadow_bwd_kernel, layer, grad_scale, pieces),
            [((rows, latent), F32)] + part_shapes,
            [dround, inputs[layer], local_t, *weights, *far_saved],
            3 * rows * ffn + 2 * rows * rows * latent,
            scratch=[
                pltpu.VMEM((grad_rows, LANES), F32),
                pltpu.VMEM((rows, latent), BF16),
                pltpu.VMEM((rows, half), BF16),
                pltpu.VMEM((rows, half), BF16),
            ],
            name=f"back{layer}",
        )
        ready = []
        for i, (_, _, axes) in enumerate(pieces):
            n = lax.axis_size(axes[0])
            ready += summed_piece(parts[:n], axes, f"{layer}_{i}")
            parts = parts[n:]
        written = pl.pallas_call(
            functools.partial(write_kernel, layer, pieces, len(written)),
            out_shape=[
                jax.ShapeDtypeStruct((layers, latent, half), F32),
                jax.ShapeDtypeStruct((layers, half, latent), F32),
            ],
            in_specs=[ANY] * len(written) + [VMEM] * len(ready),
            out_specs=[ANY] * 2,
            scratch_shapes=[
                pltpu.VMEM((grad_rows, LANES), F32),
                pltpu.VMEM((latent, half), F32),
                pltpu.VMEM((half, latent), F32),
                pltpu.SemaphoreType.DMA((2,)),
            ],
            input_output_aliases={i: i for i in range(len(written))},
            compiler_params=pltpu.CompilerParams(vmem_limit_bytes=32 * 1024 * 1024),
            cost_estimate=pl.CostEstimate(flops=0, bytes_accessed=4_000_000, transcendentals=0),
            name=f"write{layer}",
        )(*written, *ready)
        if layer:
            outs = call(
                functools.partial(post_bwd_kernel, layer - 1, groups),
                bwd_outs,
                [dtotal, back, spread, remote_t, totals[layer - 1]]
                + [*weights, *returned, *received[layer - 1]],
                2 * far_rows * ffn,
                name=f"join{layer}",
            )
    (grad,) = call(
        functools.partial(last_kernel, groups),
        [((rows, latent), F32)],
        [dtotal, back, spread, *returned],
        2 * rows * sent_rows * latent,
        name="join0",
    )
    return (grad, *written)


def solution(mesh):
    placed = (
        P(("runs", "chain", "basin"), None),
        P(("runs", "chain", "basin"), None),
        P(None, None, "feat"),
        P(None, "feat", None),
        P(("chain", "basin"), None),
        P(("chain", "basin"), None, None, None),
        P(("chain", "basin"), None, None),
        P(("chain", "basin"), None),
    )
    return jax.shard_map(
        shards,
        mesh=mesh,
        in_specs=placed,
        out_specs=(
            P(("runs", "chain", "basin"), None),
            P("runs", None, "feat"),
            P("runs", "feat", None),
        ),
        check_vma=False,
    )
```

```python
import functools

import jax
import jax.numpy as jnp
from jax import lax
from jax.experimental import pallas as pl
from jax.experimental.pallas import tpu as pltpu
from jax.sharding import PartitionSpec as P

BLOCK = 128
LANES = 128
EPS = 1e-06
F32 = jnp.float32
BF16 = jnp.bfloat16
VMEM = pl.BlockSpec(memory_space=pltpu.VMEM)
ANY = pl.BlockSpec(memory_space=pl.ANY)
SMEM = pl.BlockSpec(memory_space=pltpu.SMEM)
NN = (((1,), (0,)), ((), ()))
NT = (((1,), (1,)), ((), ()))
TN = (((0,), (0,)), ((), ()))


def mm(a, b, dims=NN):
    return lax.dot_general(a, b, dims, preferred_element_type=F32)


def call(body, outs, ins, flops, scratch=(), name=None, after=()):
    skipped = len(after)
    return pl.pallas_call(
        lambda *refs: body(*refs[skipped:]),
        out_shape=[jax.ShapeDtypeStruct(s, d) for s, d in outs],
        in_specs=[ANY] * skipped
        + [SMEM if x.dtype == jnp.int32 and x.size < 100 else VMEM for x in ins],
        out_specs=[VMEM] * len(outs),
        scratch_shapes=list(scratch),
        compiler_params=pltpu.CompilerParams(vmem_limit_bytes=32 * 1024 * 1024),
        cost_estimate=pl.CostEstimate(flops=flops, bytes_accessed=4_000_000, transcendentals=0),
        name=name,
    )(*after, *ins)


def sigmoid(v):
    return 1.0 / (1.0 + jnp.exp(-v))


def message_of(x, halves):
    total = None
    for w_in, w_out in halves:
        pre = mm(x, w_in)
        part = mm((pre * sigmoid(pre)).astype(BF16), w_out)
        total = part if total is None else total + part
    return total.astype(BF16)


def message_grad(x, dmsg, halves):
    total = None
    kept = None
    for w_in, w_out in halves:
        pre = mm(x, w_in)
        sig = sigmoid(pre)
        dact = mm(dmsg, w_out, NT)
        dpre = (dact * (sig * (1.0 + pre * (1.0 - sig)))).astype(BF16)
        if kept is None:
            kept = ((pre * sig).astype(BF16), dpre)
        part = mm(dpre, w_in, NT)
        total = part if total is None else total + part
    return total, kept


def normed_of(total):
    scale = lax.rsqrt(jnp.mean(total * total, axis=-1, keepdims=True) + EPS)
    return scale, scale * total


def norm_grad(grad, total):
    scale, normed = normed_of(total)
    return scale * (grad - normed * jnp.mean(grad * normed, axis=-1, keepdims=True))


def setup_kernel(groups, rows, send_rows, send_count, features, *outs):
    pick, spread, pick_self, up = outs[:4]
    sends = outs[4:]
    b = lax.axis_index("basin")
    lane = lax.broadcasted_iota(jnp.int32, (1, BLOCK), 1)
    for s in range(groups):
        target = lax.rem(b + s, groups)
        chosen = send_rows[0, pl.ds(target, 1), :]
        chosen = jnp.where(lane < send_count[0, target], chosen, -1)
        across = jnp.broadcast_to(chosen, (BLOCK, BLOCK))
        down = across.T
        for r in range(rows // BLOCK):
            at = lax.broadcasted_iota(jnp.int32, (BLOCK, BLOCK), 1) + r * BLOCK
            hot = (down == at).astype(F32).astype(BF16)
            if s == 0:
                pick_self[:, r * BLOCK : (r + 1) * BLOCK] = hot
            else:
                pick[(s - 1) * BLOCK : s * BLOCK, r * BLOCK : (r + 1) * BLOCK] = hot
                at = lax.broadcasted_iota(jnp.int32, (BLOCK, BLOCK), 0) + r * BLOCK
                spread[r * BLOCK : (r + 1) * BLOCK, (s - 1) * BLOCK : s * BLOCK] = (
                    (across == at).astype(F32).astype(BF16)
                )
    up[...] = features[rows - BLOCK :, :]
    for s, send in enumerate(sends):
        send[...] = mm(pick[s * BLOCK : (s + 1) * BLOCK, :], features[...]).astype(BF16)


def adjacency_kernel(groups, rows, index, values, pick_self, local, local_t, remote, remote_t, acc):
    own = rows // BLOCK
    b = lax.axis_index("basin")
    acc[...] = jnp.zeros_like(acc)
    for k in range(own):
        for t in range(index.shape[1]):
            v = index[k, t]
            sender = lax.rem(b + groups - (v - own - 1), groups)
            far = jnp.where(v == own, own + 1, jnp.where(sender == 0, own, own + 1 + sender))
            at = jnp.where(v < own, v, far)
            here = (pl.ds(k * BLOCK, BLOCK), pl.ds(pl.multiple_of(at * BLOCK, BLOCK), BLOCK))
            acc[here] += values[k, t].astype(F32)
    mine = acc[:, rows : rows + BLOCK].astype(BF16)
    full = acc[:, :rows] + mm(mine, pick_self[...])
    local[...] = full.astype(BF16)
    local_t[...] = full.T.astype(BF16)
    far = acc[:, rows + BLOCK :]
    remote[...] = far.astype(BF16)
    remote_t[...] = far.T.astype(BF16)


def shadow_fwd_kernel(layer, inputs, local, wi0, wi1, wo0, wo1, mixed, msg):
    halves = [(wi0[layer], wo0[layer]), (wi1[layer], wo1[layer])]
    rows = inputs.shape[0]
    for r in range(0, rows, 256):
        msg[r : r + 256, :] = message_of(inputs[r : r + 256, :], halves)
    mixed[...] = mm(local[...], msg[...])


def mixed_total(layer, state, mixed, received, remote, weights):
    wi0, wi1, wo0, wo1 = weights
    halves = [(wi0[layer], wo0[layer]), (wi1[layer], wo1[layer])]
    far = jnp.concatenate([x[...] for x in received], axis=0)
    return state + mixed[...] + mm(remote[...], message_of(far, halves))


def post_fwd_kernel(layer, groups, *refs):
    prev, mixed, remote, pick = refs[:4]
    weights = refs[4:8]
    received = refs[8 : 8 + groups]
    total, inputs, up = refs[8 + groups : 11 + groups]
    sends = refs[11 + groups :]
    state = prev[...].astype(F32) if layer == 0 else normed_of(prev[...])[1]
    total[...] = mixed_total(layer, state, mixed, received, remote, weights)
    new = normed_of(total[...])[1].astype(BF16)
    inputs[...] = new
    up[...] = new[new.shape[0] - BLOCK :, :]
    for s, send in enumerate(sends):
        send[...] = mm(pick[s * BLOCK : (s + 1) * BLOCK, :], new).astype(BF16)


def start_bwd(layer, dtotal_now, weights, received, remote_t, outs):
    dtotal, dround, far_x, far_dmsg, far_act, far_dpre = outs[:6]
    backs = outs[6:]
    wi0, wi1, wo0, wo1 = weights
    halves = [(wi0[layer], wo0[layer]), (wi1[layer], wo1[layer])]
    dtotal[...] = dtotal_now
    dround[...] = dtotal_now.astype(BF16)
    far = jnp.concatenate([x[...] for x in received], axis=0)
    dmsg = mm(remote_t[...], dround[...]).astype(BF16)
    back, (act, dpre) = message_grad(far, dmsg, halves)
    far_x[...] = far
    far_dmsg[...] = dmsg
    far_act[...] = act
    far_dpre[...] = dpre
    for s, out in enumerate(backs):
        out[...] = back[s * BLOCK : (s + 1) * BLOCK, :].astype(BF16)


def turn_kernel(layer, groups, *refs):
    prev, mixed, remote, remote_t, cot = refs[:5]
    weights = refs[5:9]
    received = refs[9 : 9 + groups]
    outs = refs[9 + groups :]
    state = normed_of(prev[...])[1]
    total = mixed_total(layer, state, mixed, received, remote, weights)
    start_bwd(layer, norm_grad(cot[...], total), weights, received, remote_t, outs)


def shadow_bwd_kernel(layer, grad_scale, pieces, *refs):
    dround, inputs, local_t = refs[:3]
    wi0, wi1, wo0, wo1 = refs[3:7]
    far_x, far_dmsg, far_act, far_dpre = refs[7:11]
    back = refs[11]
    grads, dmsg, act, dpre = refs[-4:]
    halves = [(wi0[layer], wo0[layer]), (wi1[layer], wo1[layer])]
    dmsg[...] = mm(local_t[...], dround[...]).astype(BF16)
    rows, latent = inputs.shape
    hidden = act.shape[1]
    for r in range(0, rows, 256):
        here = slice(r, r + 256)
        grad, (a, d) = message_grad(inputs[here, :], dmsg[here, :], halves)
        back[here, :] = grad
        act[here, :] = a
        dpre[here, :] = d
    g_in = (mm(inputs[...], dpre[...], TN) + mm(far_x[...], far_dpre[...], TN)) * grad_scale
    for j in range(hidden // LANES):
        grads[j * latent : (j + 1) * latent, :] = g_in[:, j * LANES : (j + 1) * LANES]
    g_out = (mm(act[...], dmsg[...], TN) + mm(far_act[...], far_dmsg[...], TN)) * grad_scale
    for j in range(latent // LANES):
        at = hidden // LANES * latent + j * hidden
        grads[at : at + hidden, :] = g_out[:, j * LANES : (j + 1) * LANES]
    outs = refs[12:-4]
    for lo, hi, axes in pieces:
        n = lax.axis_size(axes[0])
        scatter_parts(grads.at[lo:hi], axes[0], outs[:n])
        outs = outs[n:]


def scatter_parts(block, axis, outs):
    n = lax.axis_size(axis)
    m = block.shape[0] // n
    me = lax.axis_index(axis)
    for s, out in enumerate(outs):
        part = block[pl.ds(pl.multiple_of(lax.rem(me + s, n) * m, m), m), :]
        out[...] = part.astype(out.dtype)


def add_scatter_kernel(axis, parts, *refs):
    acc = refs[-1]
    acc[...] = refs[0][...]
    for part in refs[1:parts]:
        acc[...] += part[...].astype(F32)
    scatter_parts(acc, axis, refs[parts:-1])


def add_kernel(*refs):
    total = refs[0][...]
    for part in refs[1:-1]:
        total = total + part[...].astype(F32)
    refs[-1][...] = total.astype(BF16)


def place(axis, parts, out):
    n = lax.axis_size(axis)
    m = parts[0].shape[0]
    me = lax.axis_index(axis)
    for s, part in enumerate(parts):
        at = pl.ds(pl.multiple_of(lax.rem(me + n - s, n) * m, m), m)
        out[at, :] = part[...].astype(out.dtype)


def place_kernel(axis, *refs):
    place(axis, refs[:-1], refs[-1])


def write_kernel(layer, pieces, kept, *refs):
    out_in, out_out, grads, slab_in, slab_out, sem = refs[-6:]
    parts = refs[kept : kept + sum(lax.axis_size(axes[0]) for _, _, axes in pieces)]
    for lo, hi, axes in pieces:
        n = lax.axis_size(axes[0])
        place(axes[0], parts[:n], grads.at[lo:hi])
        parts = parts[n:]
    latent, hidden = slab_in.shape
    for j in range(hidden // LANES):
        slab_in[:, j * LANES : (j + 1) * LANES] = grads[j * latent : (j + 1) * latent, :]
    first = pltpu.make_async_copy(slab_in, out_in.at[layer], sem.at[0])
    first.start()
    for j in range(latent // LANES):
        at = hidden // LANES * latent + j * hidden
        slab_out[:, j * LANES : (j + 1) * LANES] = grads[at : at + hidden, :]
    second = pltpu.make_async_copy(slab_out, out_out.at[layer], sem.at[1])
    second.start()
    first.wait()
    second.wait()


def shifted(parts, axis):
    return [around(x, axis, s + 1) for s, x in enumerate(parts)]


class Sum:
    def __init__(self, parts, axes, name):
        self.axes, self.name = axes, name
        self.parts = [parts[0], *shifted(parts[1:], axes[0])]

    def add(self, after):
        n = lax.axis_size(self.axes[1])
        m = self.parts[0].shape[0]
        own, *sent = call(
            functools.partial(add_scatter_kernel, self.axes[1], len(self.parts)),
            [((m // n, LANES), F32)] + [((m // n, LANES), BF16)] * (n - 1),
            self.parts,
            1_000_000,
            scratch=[pltpu.VMEM((m, LANES), F32)],
            name=f"add_{self.name}",
            after=after,
        )
        self.parts = [own, *shifted(sent, self.axes[1])]
        return [own]

    def end(self, after):
        n = lax.axis_size(self.axes[1])
        (own,) = call(
            add_kernel,
            [(self.parts[0].shape, BF16)],
            self.parts,
            1_000_000,
            name=f"end_{self.name}",
            after=after,
        )
        self.parts = [own, *shifted([own] * (n - 1), self.axes[1])]
        return [own]

    def place(self, after):
        n = lax.axis_size(self.axes[0])
        m = self.parts[0].shape[0]
        (own,) = call(
            functools.partial(place_kernel, self.axes[1]),
            [((m * len(self.parts), LANES), BF16)],
            self.parts,
            1_000_000,
            name=f"place_{self.name}",
            after=after,
        )
        self.parts = [own, *shifted([own] * (n - 1), self.axes[0])]
        return [own]


def gathered_grad(dtotal, back, returned, spread):
    grad = dtotal[...] + back[...]
    if len(returned) > 1:
        far = jnp.concatenate([x[...] for x in returned[1:]], axis=0)
        grad = grad + mm(spread[...], far)
    rows = grad.shape[0]
    low = grad[rows - BLOCK :, :] + returned[0][...].astype(F32)
    return jnp.concatenate([grad[: rows - BLOCK, :], low], axis=0)


def post_bwd_kernel(layer, groups, *refs):
    dtotal, back, spread, remote_t, total = refs[:5]
    weights = refs[5:9]
    returned = refs[9 : 9 + groups]
    received = refs[9 + groups : 9 + 2 * groups]
    outs = refs[9 + 2 * groups :]
    grad = gathered_grad(dtotal, back, returned, spread)
    start_bwd(layer, norm_grad(grad, total[...]), weights, received, remote_t, outs)


def last_kernel(groups, *refs):
    dtotal, back, spread = refs[:3]
    refs[3 + groups][...] = gathered_grad(dtotal, back, refs[3 : 3 + groups], spread)


def along(x, axis, distance):
    n = lax.axis_size(axis)
    return lax.ppermute(x, axis, [(i, i + distance) for i in range(n) if 0 <= i + distance < n])


def around(x, axis, distance):
    n = lax.axis_size(axis)
    return lax.ppermute(x, axis, [(i, (i + distance) % n) for i in range(n)])


def exchange(up, sends, sign):
    return [along(up, "chain", sign)] + [
        around(x, "basin", sign * (s + 1)) for s, x in enumerate(sends)
    ]


def shards(features, cotangent, w_in, w_out, block_index, block_values, send_rows, send_count):
    rows, latent = features.shape
    groups = lax.axis_size("basin")
    layers, _, half = w_in.shape
    far_rows = groups * BLOCK
    sent_rows = max(groups - 1, 1) * BLOCK
    own = rows // BLOCK
    grad_scale = float(rows * lax.axis_size("chain") * groups) ** (-0.5)

    def act16(n, m=latent):
        return ((n, m), BF16)

    wi1 = around(w_in, "feat", 1)
    wo1 = around(w_out, "feat", 1)
    weights = (w_in, wi1, w_out, wo1)
    ffn = 4 * latent * 2 * half

    pick, spread, pick_self, up, *sends = call(
        functools.partial(setup_kernel, groups, rows),
        [act16(sent_rows, rows), act16(rows, sent_rows), act16(BLOCK, rows), act16(BLOCK)]
        + [act16(BLOCK)] * (groups - 1),
        [send_rows, send_count, features],
        2 * rows * sent_rows * latent,
        name="setup",
    )
    received = [exchange(up, sends, 1)]
    local, local_t, remote, remote_t = call(
        functools.partial(adjacency_kernel, groups, rows),
        [act16(rows, rows), act16(rows, rows), act16(rows, far_rows), act16(far_rows, rows)],
        [block_index, block_values, pick_self],
        2 * rows * rows * BLOCK,
        scratch=[pltpu.VMEM((rows, (own + groups + 1) * BLOCK), F32)],
        name="adjacency",
    )
    inputs = [features]
    totals = []
    for layer in range(layers):
        mixed, _ = call(
            functools.partial(shadow_fwd_kernel, layer),
            [((rows, latent), F32), act16(rows)],
            [inputs[layer], local, *weights],
            rows * ffn + 2 * rows * rows * latent,
            name=f"local{layer}",
        )
        prev = features if layer == 0 else totals[-1]
        if layer + 1 < layers:
            total, new, up, *sends = call(
                functools.partial(post_fwd_kernel, layer, groups),
                [((rows, latent), F32), act16(rows)] + [act16(BLOCK)] * groups,
                [prev, mixed, remote, pick, *weights, *received[layer]],
                far_rows * ffn + 2 * rows * far_rows * latent,
                name=f"mix{layer}",
            )
            totals.append(total)
            inputs.append(new)
            received.append(exchange(up, sends, 1))
    bwd_outs = (
        [((rows, latent), F32), act16(rows), act16(far_rows), act16(far_rows)]
        + [act16(far_rows, half)] * 2
        + [act16(BLOCK)] * groups
    )
    last = layers - 1
    outs = call(
        functools.partial(turn_kernel, last, groups),
        bwd_outs,
        [totals[-1], mixed, remote, remote_t, cotangent, *weights, *received[last]],
        2 * far_rows * ffn,
        name="turn",
    )
    grad_rows = 2 * latent * half // LANES
    pieces = [(0, grad_rows, ("basin", "chain"))]
    part_shapes = []
    for lo, hi, axes in pieces:
        n = lax.axis_size(axes[0])
        m = (hi - lo) // n
        part_shapes += [((m, LANES), F32)] + [((m, LANES), BF16)] * (n - 1)
    returned = {}
    sums = {}

    def back(layer, outs, after=()):
        returned[layer] = exchange(outs[6], outs[7:], -1)
        grad, *parts = call(
            functools.partial(shadow_bwd_kernel, layer, grad_scale, pieces),
            [((rows, latent), F32)] + part_shapes,
            [outs[1], inputs[layer], local_t, *weights, *outs[2:6]],
            3 * rows * ffn + 2 * rows * rows * latent,
            scratch=[
                pltpu.VMEM((grad_rows, LANES), F32),
                pltpu.VMEM((rows, latent), BF16),
                pltpu.VMEM((rows, half), BF16),
                pltpu.VMEM((rows, half), BF16),
            ],
            name=f"back{layer}",
            after=after,
        )
        sums[layer] = []
        for i, (_, _, axes) in enumerate(pieces):
            n = lax.axis_size(axes[0])
            sums[layer].append(Sum(parts[:n], axes, f"{layer}_{i}"))
            parts = parts[n:]
        return [outs[0], grad]

    def join(layer, state, after=()):
        if layer:
            return call(
                functools.partial(post_bwd_kernel, layer - 1, groups),
                bwd_outs,
                [*state, spread, remote_t, totals[layer - 1]]
                + [*weights, *returned[layer], *received[layer - 1]],
                2 * far_rows * ffn,
                name=f"join{layer}",
                after=after,
            )
        return call(
            functools.partial(last_kernel, groups),
            [((rows, latent), F32)],
            [*state, spread, *returned[layer]],
            2 * rows * sent_rows * latent,
            name="join0",
            after=after,
        )

    def write(layer, written, after):
        ready = [x for piece in sums[layer] for x in piece.parts]
        kept = [*written, *after]
        return pl.pallas_call(
            functools.partial(write_kernel, layer, pieces, len(kept)),
            out_shape=[
                jax.ShapeDtypeStruct((layers, latent, half), F32),
                jax.ShapeDtypeStruct((layers, half, latent), F32),
            ],
            in_specs=[ANY] * len(kept) + [VMEM] * len(ready),
            out_specs=[ANY] * 2,
            scratch_shapes=[
                pltpu.VMEM((grad_rows, LANES), F32),
                pltpu.VMEM((latent, half), F32),
                pltpu.VMEM((half, latent), F32),
                pltpu.SemaphoreType.DMA((2,)),
            ],
            input_output_aliases={i: i for i in range(len(written))},
            compiler_params=pltpu.CompilerParams(vmem_limit_bytes=32 * 1024 * 1024),
            cost_estimate=pl.CostEstimate(flops=0, bytes_accessed=4_000_000, transcendentals=0),
            name=f"write{layer}",
        )(*written, *after, *ready)

    def stage(which, layer, after):
        for piece in sums[layer]:
            after = getattr(piece, which)(after)
        return after

    at = []
    for layer in reversed(range(layers)):
        state = back(layer, outs, at)
        at = state[1:]
        if layer + 2 < layers:
            at = stage("end", layer + 2, at)
        if layer + 1 < layers:
            at = stage("add", layer + 1, at)
        if layer:
            outs = join(layer, state, at)
            at = outs[1:2]
    (grad,) = join(0, state, at)
    at = [grad]
    for layer in reversed(range(2, layers)):
        at = stage("place", layer, at)
    at = stage("add", 0, at)
    at = stage("end", 1, at)
    written = []
    for layer in reversed(range(2, layers)):
        written = write(layer, written, at)
    at = stage("end", 0, written[:1] or at)
    at = stage("place", 1, at)
    at = stage("place", 0, at)
    written = write(1, written, at)
    written = write(0, written, [])
    return (grad, *written)


def solution(mesh):
    placed = (
        P(("runs", "chain", "basin"), None),
        P(("runs", "chain", "basin"), None),
        P(None, None, "feat"),
        P(None, "feat", None),
        P(("chain", "basin"), None),
        P(("chain", "basin"), None, None, None),
        P(("chain", "basin"), None, None),
        P(("chain", "basin"), None),
    )
    return jax.shard_map(
        shards,
        mesh=mesh,
        in_specs=placed,
        out_specs=(
            P(("runs", "chain", "basin"), None),
            P("runs", None, "feat"),
            P("runs", "feat", None),
        ),
        check_vma=False,
    )
```

```python
import functools

import jax
import jax.numpy as jnp
from jax import lax
from jax.experimental import pallas as pl
from jax.experimental.pallas import tpu as pltpu
from jax.sharding import PartitionSpec as P

BLOCK = 128
LANES = 128
EPS = 1e-06
F32 = jnp.float32
BF16 = jnp.bfloat16
VMEM = pl.BlockSpec(memory_space=pltpu.VMEM)
SMEM = pl.BlockSpec(memory_space=pltpu.SMEM)
ANY = pl.BlockSpec(memory_space=pl.ANY)
NN = (((1,), (0,)), ((), ()))
NT = (((1,), (1,)), ((), ()))
TN = (((0,), (0,)), ((), ()))


def mm(a, b, dims=NN):
    return lax.dot_general(a, b, dims, preferred_element_type=F32)


LIMIT = 24 * 1024 * 1024


def call(body, outs, ins, flops, scratch=(), name=None, after=()):
    skipped = len(after)
    return pl.pallas_call(
        lambda *refs: body(*refs[skipped:]),
        out_shape=[jax.ShapeDtypeStruct(s, d) for s, d in outs],
        in_specs=[ANY] * skipped + [SMEM if x.ndim == 2 and x.shape[1] == 4 else VMEM for x in ins],
        out_specs=[VMEM] * len(outs),
        scratch_shapes=list(scratch),
        compiler_params=pltpu.CompilerParams(vmem_limit_bytes=LIMIT),
        cost_estimate=pl.CostEstimate(flops=flops, bytes_accessed=4_000_000, transcendentals=0),
        name=name,
    )(*after, *ins)


def sigmoid(v):
    return 1.0 / (1.0 + jnp.exp(-v))


def message_of(x, halves):
    total = None
    for w_in, w_out in halves:
        pre = mm(x, w_in)
        part = mm((pre * sigmoid(pre)).astype(BF16), w_out)
        total = part if total is None else total + part
    return total.astype(BF16)


def message_grad(x, dmsg, halves):
    total = None
    kept = None
    for w_in, w_out in halves:
        pre = mm(x, w_in)
        sig = sigmoid(pre)
        dact = mm(dmsg, w_out, NT)
        dpre = (dact * (sig * (1.0 + pre * (1.0 - sig)))).astype(BF16)
        if kept is None:
            kept = ((pre * sig).astype(BF16), dpre)
        part = mm(dpre, w_in, NT)
        total = part if total is None else total + part
    return total, kept


def normed_of(total):
    scale = lax.rsqrt(jnp.mean(total * total, axis=-1, keepdims=True) + EPS)
    return scale, scale * total


def norm_grad(grad, total):
    scale, normed = normed_of(total)
    return scale * (grad - normed * jnp.mean(grad * normed, axis=-1, keepdims=True))


def route_place(route, feat, pairs):
    return route // 2 + jnp.where(route % 2 == feat, 0, pairs)


def setup_kernel(groups, pairs, features, sent, *refs):
    pick, spread, pick_self = refs[:3]
    sends = refs[3:]
    rows = features.shape[0]
    b, feat = lax.axis_index("basin"), lax.axis_index("feat")
    for route in range(-1, 2 * pairs):
        if route == 0:
            chosen = lax.broadcasted_iota(jnp.int32, (1, BLOCK), 1) + (rows - BLOCK)
        elif route >= groups:
            chosen = jnp.full((1, BLOCK), -1, jnp.int32)
        else:
            chosen = sent[pl.ds(lax.rem(b + max(route, 0), groups), 1), :]
        across = jnp.broadcast_to(chosen, (BLOCK, BLOCK))
        down = across.T
        for r in range(0, rows, BLOCK):
            at = lax.broadcasted_iota(jnp.int32, (BLOCK, BLOCK), 1) + r
            hot = (down == at).astype(F32).astype(BF16)
            if route < 0:
                pick_self[:, r : r + BLOCK] = hot
                continue

            @pl.when(route % 2 == feat)
            def _():
                pick[route // 2 * BLOCK : (route // 2 + 1) * BLOCK, r : r + BLOCK] = hot

            at = lax.broadcasted_iota(jnp.int32, (BLOCK, BLOCK), 0) + r
            place = pl.multiple_of(route_place(route, feat, pairs) * BLOCK, BLOCK)
            spread[r : r + BLOCK, pl.ds(place, BLOCK)] = (across == at).astype(F32).astype(BF16)
    for i, send in enumerate(sends):
        send[...] = mm(pick[i * BLOCK : (i + 1) * BLOCK, :], features[...]).astype(BF16)


def build_adjacency(groups, pairs, rows, index, values, pick_self, outs, acc):
    local, local_t, remote, remote_t = outs
    own = rows // BLOCK
    b, feat = lax.axis_index("basin"), lax.axis_index("feat")
    acc[...] = jnp.zeros_like(acc)
    for k in range(own):
        for t in range(index.shape[1]):
            v = index[k, t]
            route = jnp.where(v == own, 0, lax.rem(b + groups - (v - own - 1), groups))
            far = own + 1 + route_place(route, feat, pairs)
            far = jnp.where((v > own) & (route == 0), own, far)
            at = jnp.where(v < own, v, far)
            here = (pl.ds(k * BLOCK, BLOCK), pl.ds(pl.multiple_of(at * BLOCK, BLOCK), BLOCK))
            acc[here] += values[k, t].astype(F32)
    mine = acc[:, rows : rows + BLOCK].astype(BF16)
    full = acc[:, :rows] + mm(mine, pick_self[...])
    local[...] = full.astype(BF16)
    local_t[...] = full.T.astype(BF16)
    far = acc[:, rows + BLOCK :]
    remote[...] = far.astype(BF16)
    remote_t[...] = far.T.astype(BF16)


def own_messages(layer, inputs, weights, msg):
    wi0, wi1, wo0, wo1 = weights
    halves = [(wi0[layer], wo0[layer]), (wi1[layer], wo1[layer])]
    for r in range(0, inputs.shape[0], 256):
        msg[r : r + 256, :] = message_of(inputs[r : r + 256, :], halves)


def first_kernel(groups, pairs, *refs):
    inputs, pick_self, index, values = refs[:4]
    weights, msg, outs = refs[4:8], refs[8], refs[9:13]
    own_messages(0, inputs, weights, msg)
    build_adjacency(groups, pairs, inputs.shape[0], index, values, pick_self, outs, refs[13])


def local_kernel(layer, *refs):
    own_messages(layer, refs[0], refs[1:5], refs[5])


def remote_mixed(layer, received, remote, weights):
    wi0, wi1, wo0, wo1 = weights
    halves = [(wi0[layer], wo0[layer]), (wi1[layer], wo1[layer])]
    far = jnp.concatenate([x[...] for x in received], axis=0)
    return mm(remote, message_of(far, halves))


def part_kernel(layer, pairs, *refs):
    local, msg, remote = refs[:3]
    weights, received, mixed = refs[3:7], refs[7 : 7 + pairs], refs[-1]
    mixed[...] = mm(local[...], msg[...]) + remote_mixed(
        layer, received, remote[:, : pairs * BLOCK], weights
    )


def mixed_total(layer, state, mixed, received, remote, weights):
    return state + mixed[...] + remote_mixed(
        layer, received, remote[:, len(received) * BLOCK :], weights
    )


def mix_kernel(layer, pairs, *refs):
    prev, mixed, remote, pick = refs[:4]
    weights = refs[4:8]
    received = refs[8 : 8 + pairs]
    total, inputs = refs[8 + pairs : 10 + pairs]
    sends = refs[10 + pairs :]
    state = prev[...].astype(F32) if layer == 0 else normed_of(prev[...])[1]
    total[...] = mixed_total(layer, state, mixed, received, remote, weights)
    new = normed_of(total[...])[1].astype(BF16)
    inputs[...] = new
    for i, send in enumerate(sends):
        send[...] = mm(pick[i * BLOCK : (i + 1) * BLOCK, :], new).astype(BF16)


def start_bwd(layer, dtotal_now, weights, received, remote_t, outs):
    dtotal, dround, far_dmsg, far_act, far_dpre = outs[:5]
    backs = outs[5:]
    wi0, wi1, wo0, wo1 = weights
    halves = [(wi0[layer], wo0[layer]), (wi1[layer], wo1[layer])]
    dtotal[...] = dtotal_now
    dround[...] = dtotal_now.astype(BF16)
    far = jnp.concatenate([x[...] for x in received], axis=0)
    dmsg = mm(remote_t[: far.shape[0], :], dround[...]).astype(BF16)
    back, (act, dpre) = message_grad(far, dmsg, halves)
    far_dmsg[...] = dmsg
    far_act[...] = act
    far_dpre[...] = dpre
    for i, out in enumerate(backs):
        out[...] = back[i * BLOCK : (i + 1) * BLOCK, :].astype(BF16)


def turn_kernel(layer, pairs, *refs):
    prev, mixed, remote, remote_t, cot = refs[:5]
    weights = refs[5:9]
    mine, others = refs[9 : 9 + pairs], refs[9 + pairs : 9 + 2 * pairs]
    outs = refs[9 + 2 * pairs :]
    state = normed_of(prev[...])[1]
    total = mixed_total(layer, state, mixed, others, remote, weights)
    start_bwd(layer, norm_grad(cot[...], total), weights, mine, remote_t, outs)


def back_kernel(layer, *refs):
    dround, inputs, local_t = refs[:3]
    wi0, wi1, wo0, wo1 = refs[3:7]
    back, dmsg, act, dpre = refs[7:]
    halves = [(wi0[layer], wo0[layer]), (wi1[layer], wo1[layer])]
    dmsg[...] = mm(local_t[...], dround[...]).astype(BF16)
    for r in range(0, inputs.shape[0], 256):
        here = slice(r, r + 256)
        back[here, :], (act[here, :], dpre[here, :]) = message_grad(
            inputs[here, :], dmsg[here, :], halves
        )


def weights_kernel(layer, grad_scale, pairs, pieces, *refs):
    dround, remote_t, w_in, w_out, inputs, dmsg, act, dpre = refs[:8]
    far_dmsg, far_act, far_dpre = refs[8:11]
    mine, others = refs[11 : 11 + pairs], refs[11 + pairs : 11 + 2 * pairs]
    outs = refs[11 + 2 * pairs : -1]
    grads = refs[-1]
    near = jnp.concatenate([x[...] for x in mine], axis=0)
    far = jnp.concatenate([x[...] for x in others], axis=0)
    dmsg2 = mm(remote_t[near.shape[0] :, :], dround[...]).astype(BF16)
    pre = mm(far, w_in[layer])
    sig = sigmoid(pre)
    dpre2 = (mm(dmsg2, w_out[layer], NT) * (sig * (1.0 + pre * (1.0 - sig)))).astype(BF16)
    act2 = (pre * sig).astype(BF16)
    latent, hidden = inputs.shape[1], act.shape[1]
    g_in = mm(inputs[...], dpre[...], TN) + mm(near, far_dpre[...], TN) + mm(far, dpre2, TN)
    g_in = g_in * grad_scale
    for j in range(hidden // LANES):
        grads[j * latent : (j + 1) * latent, :] = g_in[:, j * LANES : (j + 1) * LANES]
    g_out = mm(act[...], dmsg[...], TN) + mm(far_act[...], far_dmsg[...], TN) + mm(act2, dmsg2, TN)
    g_out = g_out * grad_scale
    for j in range(latent // LANES):
        at = hidden // LANES * latent + j * hidden
        grads[at : at + hidden, :] = g_out[:, j * LANES : (j + 1) * LANES]
    for lo, hi, stages in pieces:
        if stages:
            split(grads.at[lo:hi], stages[0], outs[:2])
            outs = outs[2:]
        else:
            outs[0][...] = grads[lo:hi, :].astype(BF16)
            outs = outs[1:]


def upper(stage):
    axis, d = stage
    return lax.rem(lax.axis_index(axis) // d, 2)


def split(block, stage, outs):
    m = block.shape[0] // 2
    bit = upper(stage)
    keep, send = outs
    keep[...] = block[pl.ds(pl.multiple_of(bit * m, m), m), :]
    send[...] = block[pl.ds(pl.multiple_of((1 - bit) * m, m), m), :].astype(BF16)


def add_split_kernel(stage, keep, got, *refs):
    acc = refs[-1]
    acc[...] = keep[...] + got[...].astype(F32)
    split(acc, stage, refs[:-1])


def add_kernel(keep, got, out):
    out[...] = (keep[...] + got[...].astype(F32)).astype(BF16)


def place(stage, own, got, out):
    m = own.shape[0]
    bit = upper(stage)
    out[pl.ds(pl.multiple_of(bit * m, m), m), :] = own[...].astype(out.dtype)
    out[pl.ds(pl.multiple_of((1 - bit) * m, m), m), :] = got[...].astype(out.dtype)


def place_kernel(stage, own, got, out):
    place(stage, own, got, out)


def write_kernel(layer, pieces, kept, *refs):
    out_in, out_out, token, grads, slab_in, slab_out, sem = refs[-7:]
    parts = refs[kept:-7]
    token[...] = jnp.zeros_like(token)
    for lo, hi, stages in pieces:
        if stages:
            place(stages[0], parts[0], parts[1], grads.at[lo:hi])
            parts = parts[2:]
        else:
            grads[lo:hi, :] = parts[0][...].astype(F32)
            parts = parts[1:]
    latent, hidden = slab_in.shape
    for j in range(hidden // LANES):
        slab_in[:, j * LANES : (j + 1) * LANES] = grads[j * latent : (j + 1) * latent, :]
    first = pltpu.make_async_copy(slab_in, out_in.at[layer], sem.at[0])
    first.start()
    for j in range(latent // LANES):
        at = hidden // LANES * latent + j * hidden
        slab_out[:, j * LANES : (j + 1) * LANES] = grads[at : at + hidden, :]
    second = pltpu.make_async_copy(slab_out, out_out.at[layer], sem.at[1])
    second.start()
    first.wait()
    second.wait()


class Sum:
    def __init__(self, parts, stages, name):
        self.stages, self.name = stages, name
        self.done = 0
        if stages:
            self.keep, send = parts
            self.got = swapped(send, stages[0])
        else:
            self.parts = [lax.psum(parts[0], ("chain", "basin"))]

    def step(self, after):
        n = len(self.stages)
        i = self.done
        self.done += 1
        name = f"sum_{self.name}_{i}"
        if i < n - 1:
            half = (self.keep.shape[0] // 2, LANES)
            self.keep, send = call(
                functools.partial(add_split_kernel, self.stages[i + 1]),
                [(half, F32), (half, BF16)],
                [self.keep, self.got],
                1_000_000,
                scratch=[pltpu.VMEM(self.keep.shape, F32)],
                name=name,
                after=after,
            )
            self.got = swapped(send, self.stages[i + 1])
        else:
            if i == n - 1:
                body, shape = add_kernel, self.keep.shape
            else:
                body = functools.partial(place_kernel, self.stages[2 * n - 1 - i])
                shape = (self.keep.shape[0] * 2, LANES)
            (self.keep,) = call(
                body, [(shape, BF16)], [self.keep, self.got], 1_000_000, name=name, after=after
            )
            self.got = swapped(self.keep, self.stages[2 * n - 2 - i])
        self.parts = [self.keep, self.got]
        return [self.keep]


def gathered_grad(dtotal, back, returned, spread):
    far = jnp.concatenate([x[...] for x in returned], axis=0)
    return dtotal[...] + back[...] + mm(spread[...], far)


def join_kernel(layer, pairs, *refs):
    dtotal, back, spread, remote_t, total = refs[:5]
    weights = refs[5:9]
    returned = refs[9 : 9 + 2 * pairs]
    mine = refs[9 + 2 * pairs : 9 + 3 * pairs]
    outs = refs[9 + 3 * pairs :]
    grad = gathered_grad(dtotal, back, returned, spread)
    start_bwd(layer, norm_grad(grad, total[...]), weights, mine, remote_t, outs)


def last_kernel(*refs):
    dtotal, back, spread = refs[:3]
    refs[-2][...] = gathered_grad(dtotal, back, refs[3:-2], spread)
    refs[-1][...] = jnp.zeros_like(refs[-1])


def around(x, axis, distance):
    n = lax.axis_size(axis)
    return lax.ppermute(x, axis, [(i, (i + distance) % n) for i in range(n)])


def swapped(x, stage):
    axis, d = stage
    return lax.ppermute(x, axis, [(i, i ^ d) for i in range(lax.axis_size(axis))])


def routed(sends, sign):
    chain, groups = lax.axis_size("chain"), lax.axis_size("basin")
    got = []
    for i, x in enumerate(sends):
        perm = []
        for c in range(chain):
            for b in range(groups):
                for feat in range(2):
                    route = 2 * i + feat
                    to_c = c + sign if route == 0 else c
                    to_b = (b + sign * route) % groups
                    if 0 <= to_c < chain and route < groups:
                        start, end = (c * groups + b) * 2 + feat, (to_c * groups + to_b) * 2 + feat
                        perm.append((start, end))
        got.append(lax.ppermute(x, ("chain", "basin", "feat"), perm))
    return got


def other_core(got):
    return [around(x, "feat", 1) for x in got]


def shards(features, cotangent, w_in, w_out, block_index, block_values, send_rows, send_count):
    rows, latent = features.shape
    groups = lax.axis_size("basin")
    pairs = (groups + 1) // 2
    layers, _, half = w_in.shape
    far_rows = 2 * pairs * BLOCK
    own = rows // BLOCK
    grad_scale = float(rows * lax.axis_size("chain") * groups) ** (-0.5)
    last = layers - 1

    def act16(n, m=latent):
        return ((n, m), BF16)

    wi1 = around(w_in, "feat", 1)
    wo1 = around(w_out, "feat", 1)
    ffn = 4 * latent * 2 * half

    live = jnp.arange(BLOCK, dtype=jnp.int32)[None, :] < send_count[0][:, None]
    pick, spread, pick_self, *sends = call(
        functools.partial(setup_kernel, groups, pairs),
        [act16(pairs * BLOCK, rows), act16(rows, far_rows), act16(BLOCK, rows)]
        + [act16(BLOCK)] * pairs,
        [features, jnp.where(live, send_rows[0], -1)],
        2 * rows * far_rows * latent,
        name="setup",
    )
    weights = (w_in, wi1, w_out, wo1)
    msg, local, local_t, remote, remote_t = [None] * 5
    inputs = [features]
    totals = []
    mine = []
    others = []
    for layer in range(layers):
        mine.append(routed(sends, 1))
        if layer == 0:
            msg, local, local_t, remote, remote_t = call(
                functools.partial(first_kernel, groups, pairs),
                [act16(rows), act16(rows, rows), act16(rows, rows)]
                + [act16(rows, far_rows), act16(far_rows, rows)],
                [features, pick_self, block_index, block_values, *weights],
                rows * ffn + 2 * rows * rows * BLOCK,
                scratch=[pltpu.VMEM((rows, rows + BLOCK + far_rows), F32)],
                name="first",
            )
        else:
            (msg,) = call(
                functools.partial(local_kernel, layer),
                [act16(rows)],
                [inputs[layer], *weights],
                rows * ffn,
                name=f"local{layer}",
            )
        mine[layer], msg = lax.optimization_barrier((mine[layer], msg))
        others.append(other_core(mine[layer]))
        (mixed,) = call(
            functools.partial(part_kernel, layer, pairs),
            [((rows, latent), F32)],
            [local, msg, remote, *weights, *mine[layer]],
            2 * rows * rows * latent,
            name=f"part{layer}",
        )
        prev = totals[-1] if layer else features
        if layer < last:
            total, new, *sends = call(
                functools.partial(mix_kernel, layer, pairs),
                [((rows, latent), F32), act16(rows)] + [act16(BLOCK)] * pairs,
                [prev, mixed, remote, pick, *weights, *others[layer]],
                far_rows * ffn + 2 * rows * far_rows * latent,
                name=f"mix{layer}",
            )
            totals.append(total)
            inputs.append(new)
    near_rows = pairs * BLOCK
    bwd_outs = (
        [((rows, latent), F32), act16(rows), act16(near_rows)]
        + [act16(near_rows, half)] * 2
        + [act16(BLOCK)] * pairs
    )
    outs = call(
        functools.partial(turn_kernel, last, pairs),
        bwd_outs,
        [totals[-1], mixed, remote, remote_t, cotangent, *weights, *mine[last], *others[last]],
        2 * far_rows * ffn,
        name="turn",
    )
    grad_rows = 2 * latent * half // LANES

    def pair_stages(axis):
        return [(axis, 1 << i) for i in range(lax.axis_size(axis).bit_length() - 1)]

    pieces = [[(0, grad_rows, pair_stages("basin") + pair_stages("chain"))]] * layers
    returned = {}
    sums = {}

    def back(layer, outs, after):
        near = routed(outs[5:], -1)
        grad, dmsg, act, dpre = call(
            functools.partial(back_kernel, layer),
            [((rows, latent), F32), act16(rows), act16(rows, half), act16(rows, half)],
            [outs[1], inputs[layer], local_t, *weights],
            2 * rows * ffn + 2 * rows * rows * latent,
            name=f"back{layer}",
            after=after,
        )
        if layer:
            near, grad = lax.optimization_barrier((near, grad))
            returned[layer] = near + other_core(near)
        else:
            returned[layer] = near
        shapes = []
        for lo, hi, stages in pieces[layer]:
            m = (hi - lo) // 2 if stages else hi - lo
            shapes += [((m, LANES), F32)] * bool(stages) + [((m, LANES), BF16)]
        parts = call(
            functools.partial(weights_kernel, layer, grad_scale, pairs, pieces[layer]),
            shapes,
            [outs[1], remote_t, w_in, w_out, inputs[layer], dmsg, act, dpre]
            + [*outs[2:5], *mine[layer], *others[layer]],
            rows * ffn,
            scratch=[pltpu.VMEM((grad_rows, LANES), F32)],
            name=f"weights{layer}",
        )
        parts_made = parts[:1]
        sums[layer] = []
        for i, (_, _, stages) in enumerate(pieces[layer]):
            n = 2 if stages else 1
            sums[layer].append(Sum(parts[:n], stages, f"{layer}_{i}"))
            parts = parts[n:]
        return [outs[0], grad], parts_made

    def join(layer, state, after):
        if layer:
            return call(
                functools.partial(join_kernel, layer - 1, pairs),
                bwd_outs,
                [*state, spread, remote_t, totals[layer - 1]]
                + [*weights, *returned[layer], *mine[layer - 1]],
                2 * far_rows * ffn,
                name=f"join{layer}",
                after=after,
            )
        return call(
            last_kernel,
            [((rows, latent), F32), ((8, LANES), F32)],
            [*state, spread, *returned[layer]],
            2 * rows * far_rows * latent,
            name="join0",
            after=after,
        )

    def write(layer, written, after):
        ready = [x for piece in sums.pop(layer) for x in piece.parts]
        kept = [*written, *after]
        return pl.pallas_call(
            functools.partial(write_kernel, layer, pieces[layer], len(kept)),
            out_shape=[
                jax.ShapeDtypeStruct((layers, latent, half), F32),
                jax.ShapeDtypeStruct((layers, half, latent), F32),
                jax.ShapeDtypeStruct((8, LANES), F32),
            ],
            in_specs=[ANY] * len(kept) + [VMEM] * len(ready),
            out_specs=[ANY] * 2 + [VMEM],
            scratch_shapes=[
                pltpu.VMEM((grad_rows, LANES), F32),
                pltpu.VMEM((latent, half), F32),
                pltpu.VMEM((half, latent), F32),
                pltpu.SemaphoreType.DMA((2,)),
            ],
            input_output_aliases={i: i for i in range(len(written))},
            compiler_params=pltpu.CompilerParams(vmem_limit_bytes=LIMIT),
            cost_estimate=pl.CostEstimate(flops=0, bytes_accessed=4_000_000, transcendentals=0),
            name=f"write{layer}",
        )(*written, *after, *ready)

    def step(layer, after):
        for piece in sums[layer]:
            after = piece.step(after)
        return after

    count = 2 * max(len(stages) for _, _, stages in pieces[0]) - 1
    at = []
    for layer in reversed(range(layers)):
        state, at = back(layer, outs, at)
        for above in reversed(range(layer + 1, layers)):
            at = step(above, at)
            if layer == 0 and above == last:
                near, at = lax.optimization_barrier((returned[0], at))
                returned[0] = near + other_core(near)
        if layer:
            outs = join(layer, state, at)
            at = outs[1:2]
    grad, token = join(0, state, at)
    at = [token]
    written = []
    for turn in range(layers - 1, layers - 1 + count):
        for layer in reversed(range(layers)):
            if layer in sums and sums[layer][0].done <= turn - (last - layer) < count:
                at = step(layer, at)
            elif layer and turn - (last - layer) == count:
                *written, token = write(layer, written, at)
                at = [token]
    for layer in reversed(range(layers)):
        if layer in sums:
            *written, _ = write(layer, written, [])
    return (grad, *written)


def solution(mesh):
    placed = (
        P(("runs", "chain", "basin"), None),
        P(("runs", "chain", "basin"), None),
        P(None, None, "feat"),
        P(None, "feat", None),
        P(("chain", "basin"), None),
        P(("chain", "basin"), None, None, None),
        P(("chain", "basin"), None, None),
        P(("chain", "basin"), None),
    )
    return jax.shard_map(
        shards,
        mesh=mesh,
        in_specs=placed,
        out_specs=(
            P(("runs", "chain", "basin"), None),
            P("runs", None, "feat"),
            P("runs", "feat", None),
        ),
        check_vma=False,
    )
```

```python
import functools

import jax
import jax.numpy as jnp
from jax import lax
from jax.experimental import pallas as pl
from jax.experimental.pallas import tpu as pltpu
from jax.sharding import PartitionSpec as P

BLOCK = 128
LANES = 128
EPS = 1e-06
F32 = jnp.float32
BF16 = jnp.bfloat16
VMEM = pl.BlockSpec(memory_space=pltpu.VMEM)
SMEM = pl.BlockSpec(memory_space=pltpu.SMEM)
ANY = pl.BlockSpec(memory_space=pl.ANY)
NN = (((1,), (0,)), ((), ()))
NT = (((1,), (1,)), ((), ()))
TN = (((0,), (0,)), ((), ()))


def mm(a, b, dims=NN):
    return lax.dot_general(a, b, dims, preferred_element_type=F32)


LIMIT = 24 * 1024 * 1024


def call(body, outs, ins, flops, scratch=(), name=None, after=()):
    skipped = len(after)
    return pl.pallas_call(
        lambda *refs: body(*refs[skipped:]),
        out_shape=[jax.ShapeDtypeStruct(s, d) for s, d in outs],
        in_specs=[ANY] * skipped + [SMEM if x.ndim == 2 and x.shape[1] == 4 else VMEM for x in ins],
        out_specs=[VMEM] * len(outs),
        scratch_shapes=list(scratch),
        compiler_params=pltpu.CompilerParams(vmem_limit_bytes=LIMIT),
        cost_estimate=pl.CostEstimate(flops=flops, bytes_accessed=4_000_000, transcendentals=0),
        name=name,
    )(*after, *ins)


def sigmoid(v):
    return 1.0 / (1.0 + jnp.exp(-v))


def message_of(x, halves):
    total = None
    for w_in, w_out in halves:
        pre = mm(x, w_in)
        part = mm((pre * sigmoid(pre)).astype(BF16), w_out)
        total = part if total is None else total + part
    return total.astype(BF16)


def message_grad(x, dmsg, halves):
    total = None
    kept = None
    for w_in, w_out in halves:
        pre = mm(x, w_in)
        sig = sigmoid(pre)
        dact = mm(dmsg, w_out, NT)
        dpre = (dact * (sig * (1.0 + pre * (1.0 - sig)))).astype(BF16)
        if kept is None:
            kept = ((pre * sig).astype(BF16), dpre)
        part = mm(dpre, w_in, NT)
        total = part if total is None else total + part
    return total, kept


def normed_of(total):
    scale = lax.rsqrt(jnp.mean(total * total, axis=-1, keepdims=True) + EPS)
    return scale, scale * total


def norm_grad(grad, total):
    scale, normed = normed_of(total)
    return scale * (grad - normed * jnp.mean(grad * normed, axis=-1, keepdims=True))


def setup_kernel(groups, pairs, features, sent, *refs):
    pick, spread, pick_self = refs[:3]
    sends = refs[3:]
    rows = features.shape[0]
    b, feat = lax.axis_index("basin"), lax.axis_index("feat")
    for route in range(-1, 2 * pairs):
        if route == 0:
            chosen = lax.broadcasted_iota(jnp.int32, (1, BLOCK), 1) + (rows - BLOCK)
        elif route >= groups:
            chosen = jnp.full((1, BLOCK), -1, jnp.int32)
        else:
            chosen = sent[pl.ds(lax.rem(b + max(route, 0), groups), 1), :]
        across = jnp.broadcast_to(chosen, (BLOCK, BLOCK))
        down = across.T
        for r in range(0, rows, BLOCK):
            at = lax.broadcasted_iota(jnp.int32, (BLOCK, BLOCK), 1) + r
            hot = (down == at).astype(F32).astype(BF16)
            if route < 0:
                pick_self[:, r : r + BLOCK] = hot
                continue

            @pl.when(route % 2 == feat)
            def _():
                pick[route // 2 * BLOCK : (route // 2 + 1) * BLOCK, r : r + BLOCK] = hot

            at = lax.broadcasted_iota(jnp.int32, (BLOCK, BLOCK), 0) + r
            if route < groups:
                spread[r : r + BLOCK, route * BLOCK : (route + 1) * BLOCK] = (
                    (across == at).astype(F32).astype(BF16)
                )
    for i, send in enumerate(sends):
        send[...] = mm(pick[i * BLOCK : (i + 1) * BLOCK, :], features[...]).astype(BF16)


def build_adjacency(groups, rows, index, values, pick_self, outs, acc):
    local, local_t, remote, remote_t = outs
    own = rows // BLOCK
    b = lax.axis_index("basin")
    acc[...] = jnp.zeros_like(acc)
    for k in range(own):
        for t in range(index.shape[1]):
            v = index[k, t]
            route = jnp.where(v == own, 0, lax.rem(b + groups - (v - own - 1), groups))
            far = jnp.where((v > own) & (route == 0), own, own + 1 + route)
            at = jnp.where(v < own, v, far)
            here = (pl.ds(k * BLOCK, BLOCK), pl.ds(pl.multiple_of(at * BLOCK, BLOCK), BLOCK))
            acc[here] += values[k, t].astype(F32)
    mine = acc[:, rows : rows + BLOCK].astype(BF16)
    full = acc[:, :rows] + mm(mine, pick_self[...])
    local[...] = full.astype(BF16)
    local_t[...] = full.T.astype(BF16)
    far = acc[:, rows + BLOCK :]
    remote[...] = far.astype(BF16)
    remote_t[...] = far.T.astype(BF16)


def own_messages(layer, inputs, weights, msg):
    wi0, wi1, wo0, wo1 = weights
    halves = [(wi0[layer], wo0[layer]), (wi1[layer], wo1[layer])]
    for r in range(0, inputs.shape[0], 256):
        msg[r : r + 256, :] = message_of(inputs[r : r + 256, :], halves)


def first_kernel(groups, *refs):
    inputs, pick_self, index, values = refs[:4]
    weights, msg, outs = refs[4:8], refs[8], refs[9:13]
    own_messages(0, inputs, weights, msg)
    build_adjacency(groups, inputs.shape[0], index, values, pick_self, outs, refs[13])


def local_kernel(layer, *refs):
    own_messages(layer, refs[0], refs[1:5], refs[5])


def remote_mixed(layer, received, remote, feat, weights):
    wi0, wi1, wo0, wo1 = weights
    halves = [(wi0[layer], wo0[layer]), (wi1[layer], wo1[layer])]
    total = None
    for i, block in enumerate(received):
        route = jnp.minimum(2 * i + feat, remote.shape[1] // BLOCK - 1)
        columns = remote[:, pl.ds(pl.multiple_of(route * BLOCK, BLOCK), BLOCK)]
        part = mm(columns, message_of(block[...], halves))
        total = part if total is None else total + part
    return total


def part_kernel(layer, pairs, *refs):
    local, msg, remote = refs[:3]
    weights, received, mixed = refs[3:7], refs[7 : 7 + pairs], refs[-1]
    mixed[...] = mm(local[...], msg[...]) + remote_mixed(
        layer, received, remote, lax.axis_index("feat"), weights
    )


def mixed_total(layer, state, mixed, received, remote, weights):
    return state + mixed[...] + remote_mixed(
        layer, received, remote, 1 - lax.axis_index("feat"), weights
    )


def mix_kernel(layer, pairs, *refs):
    prev, mixed, remote, pick = refs[:4]
    weights = refs[4:8]
    received = refs[8 : 8 + pairs]
    total, inputs = refs[8 + pairs : 10 + pairs]
    sends = refs[10 + pairs :]
    state = prev[...].astype(F32) if layer == 0 else normed_of(prev[...])[1]
    total[...] = mixed_total(layer, state, mixed, received, remote, weights)
    new = normed_of(total[...])[1].astype(BF16)
    inputs[...] = new
    for i, send in enumerate(sends):
        send[...] = mm(pick[i * BLOCK : (i + 1) * BLOCK, :], new).astype(BF16)


def start_bwd(layer, groups, dtotal_now, weights, mine, others, remote_t, outs):
    dtotal, dround, far_x, far_dmsg, far_act, far_dpre = outs[:6]
    backs = outs[6:]
    wi0, wi1, wo0, wo1 = weights
    halves = [(wi0[layer], wo0[layer]), (wi1[layer], wo1[layer])]
    dtotal[...] = dtotal_now
    dround[...] = dtotal_now.astype(BF16)
    for first in range(2):

        @pl.when(lax.axis_index("feat") == first)
        def _():
            for route in range(groups):
                block = (mine, others)[(route + first) % 2][route // 2]
                far_x[route * BLOCK : (route + 1) * BLOCK, :] = block[...]

    dmsg = mm(remote_t[...], dround[...]).astype(BF16)
    back, (act, dpre) = message_grad(far_x[...], dmsg, halves)
    far_dmsg[...] = dmsg
    far_act[...] = act
    far_dpre[...] = dpre
    for i, out in enumerate(backs):
        out[...] = back[i * BLOCK : (i + 1) * BLOCK, :].astype(BF16)


def turn_kernel(layer, groups, pairs, *refs):
    prev, mixed, remote, remote_t, cot = refs[:5]
    weights = refs[5:9]
    mine, others = refs[9 : 9 + pairs], refs[9 + pairs : 9 + 2 * pairs]
    outs = refs[9 + 2 * pairs :]
    state = normed_of(prev[...])[1]
    total = mixed_total(layer, state, mixed, others, remote, weights)
    dtotal = norm_grad(cot[...], total)
    start_bwd(layer, groups, dtotal, weights, mine, others, remote_t, outs)


def back_kernel(layer, grad_scale, stage, *refs):
    dround, inputs, local_t = refs[:3]
    wi0, wi1, wo0, wo1 = refs[3:7]
    far_x, far_dmsg, far_act, far_dpre = refs[7:11]
    back, keep, send = refs[11:14]
    grads, dmsg, act, dpre = refs[14:]
    halves = [(wi0[layer], wo0[layer]), (wi1[layer], wo1[layer])]
    dmsg[...] = mm(local_t[...], dround[...]).astype(BF16)
    for r in range(0, inputs.shape[0], 256):
        here = slice(r, r + 256)
        back[here, :], (act[here, :], dpre[here, :]) = message_grad(
            inputs[here, :], dmsg[here, :], halves
        )
    latent, hidden = inputs.shape[1], act.shape[1]
    g_in = (mm(inputs[...], dpre[...], TN) + mm(far_x[...], far_dpre[...], TN)) * grad_scale
    for j in range(hidden // LANES):
        grads[j * latent : (j + 1) * latent, :] = g_in[:, j * LANES : (j + 1) * LANES]
    g_out = (mm(act[...], dmsg[...], TN) + mm(far_act[...], far_dmsg[...], TN)) * grad_scale
    for j in range(latent // LANES):
        at = hidden // LANES * latent + j * hidden
        grads[at : at + hidden, :] = g_out[:, j * LANES : (j + 1) * LANES]
    split(grads, stage, (keep, send))


def upper(stage):
    (axis0, d0), (axis1, d1) = stage
    bit0 = lax.rem(lax.axis_index(axis0) // d0, 2)
    bit1 = lax.rem(lax.axis_index(axis1) // d1, 2)
    return jnp.where(lax.axis_index("feat") == 0, bit0, bit1)


def split(block, stage, outs):
    m = block.shape[0] // 2
    bit = upper(stage)
    keep, send = outs
    keep[...] = block[pl.ds(pl.multiple_of(bit * m, m), m), :]
    send[...] = block[pl.ds(pl.multiple_of((1 - bit) * m, m), m), :].astype(BF16)


def add_split_kernel(stage, keep, got, *refs):
    acc = refs[-1]
    acc[...] = keep[...] + got[...].astype(F32)
    split(acc, stage, refs[:-1])


def add_kernel(keep, got, out):
    out[...] = (keep[...] + got[...].astype(F32)).astype(BF16)


def place(stage, own, got, out):
    m = own.shape[0]
    bit = upper(stage)
    out[pl.ds(pl.multiple_of(bit * m, m), m), :] = own[...].astype(out.dtype)
    out[pl.ds(pl.multiple_of((1 - bit) * m, m), m), :] = got[...].astype(out.dtype)


def place_kernel(stage, own, got, out):
    place(stage, own, got, out)


def write_kernel(layer, stage, kept, *refs):
    own, got = refs[kept : kept + 2]
    out_in, out_out, token, grads, slab_in, slab_out, sem = refs[kept + 2 :]
    token[...] = jnp.zeros_like(token)
    place(stage, own, got, grads)
    latent, hidden = slab_in.shape
    for j in range(hidden // LANES):
        slab_in[:, j * LANES : (j + 1) * LANES] = grads[j * latent : (j + 1) * latent, :]
    first = pltpu.make_async_copy(slab_in, out_in.at[layer], sem.at[0])
    first.start()
    for j in range(latent // LANES):
        at = hidden // LANES * latent + j * hidden
        slab_out[:, j * LANES : (j + 1) * LANES] = grads[at : at + hidden, :]
    second = pltpu.make_async_copy(slab_out, out_out.at[layer], sem.at[1])
    second.start()
    first.wait()
    second.wait()


class Sum:
    def __init__(self, parts, stages, name):
        self.stages, self.name = stages, name
        self.done = 0
        self.keep, send = parts
        self.got = swapped(send, stages[0])

    def step(self, after):
        n = len(self.stages)
        i = self.done
        self.done += 1
        name = f"sum_{self.name}_{i}"
        if i < n - 1:
            half = (self.keep.shape[0] // 2, LANES)
            self.keep, send = call(
                functools.partial(add_split_kernel, self.stages[i + 1]),
                [(half, F32), (half, BF16)],
                [self.keep, self.got],
                1_000_000,
                scratch=[pltpu.VMEM(self.keep.shape, F32)],
                name=name,
                after=after,
            )
            self.got = swapped(send, self.stages[i + 1])
        else:
            if i == n - 1:
                body, shape = add_kernel, self.keep.shape
            else:
                body = functools.partial(place_kernel, self.stages[2 * n - 1 - i])
                shape = (self.keep.shape[0] * 2, LANES)
            (self.keep,) = call(
                body, [(shape, BF16)], [self.keep, self.got], 1_000_000, name=name, after=after
            )
            self.got = swapped(self.keep, self.stages[2 * n - 2 - i])
        return [self.keep]


def gathered_grad(dtotal, back, returned, spread):
    far = jnp.concatenate([x[...] for x in returned], axis=0)
    return dtotal[...] + back[...] + mm(spread[...], far)


def join_kernel(layer, groups, pairs, *refs):
    dtotal, back, spread, remote_t, total = refs[:5]
    weights, refs = refs[5:9], refs[9:]
    returned, refs = refs[:groups], refs[groups:]
    mine, others, outs = refs[:pairs], refs[pairs : 2 * pairs], refs[2 * pairs :]
    grad = gathered_grad(dtotal, back, returned, spread)
    dtotal = norm_grad(grad, total[...])
    start_bwd(layer, groups, dtotal, weights, mine, others, remote_t, outs)


def last_kernel(*refs):
    dtotal, back, spread = refs[:3]
    refs[-2][...] = gathered_grad(dtotal, back, refs[3:-2], spread)
    refs[-1][...] = jnp.zeros_like(refs[-1])


def around(x, axis, distance):
    n = lax.axis_size(axis)
    return lax.ppermute(x, axis, [(i, (i + distance) % n) for i in range(n)])


def over_mesh(x, target):
    chain, groups, cores = (lax.axis_size(axis) for axis in ("chain", "basin", "feat"))
    perm = []
    for c in range(chain):
        for b in range(groups):
            for feat in range(cores):
                to = target(c, b, feat)
                if to is not None:
                    start, end = (c * groups + b) * cores + feat, (to[0] * groups + to[1]) * cores
                    perm.append((start, end + feat))
    return lax.ppermute(x, ("chain", "basin", "feat"), perm)


def swapped(x, stage):
    def partner(c, b, feat):
        axis, d = stage[feat]
        return (c ^ d, b) if axis == "chain" else (c, b ^ d)

    return over_mesh(x, partner)


def forward(sends):
    def target(i, c, b, feat):
        route = 2 * i + feat
        if route == 0:
            return (c + 1, b) if c + 1 < lax.axis_size("chain") else None
        groups = lax.axis_size("basin")
        return (c, (b + route) % groups) if route < groups else None

    return [over_mesh(x, functools.partial(target, i)) for i, x in enumerate(sends)]


def backward(grads):
    chain = lax.axis_size("chain")
    up = lax.ppermute(grads[0], "chain", [(c, c - 1) for c in range(1, chain)])
    return [up] + [around(x, "basin", -s) for s, x in enumerate(grads) if s]


def other_core(got):
    return [around(x, "feat", 1) for x in got]


def shards(features, cotangent, w_in, w_out, block_index, block_values, send_rows, send_count):
    rows, latent = features.shape
    groups = lax.axis_size("basin")
    pairs = (groups + 1) // 2
    layers, _, half = w_in.shape
    far_rows = groups * BLOCK
    own = rows // BLOCK
    grad_scale = float(rows * lax.axis_size("chain") * groups) ** (-0.5)
    last = layers - 1

    def act16(n, m=latent):
        return ((n, m), BF16)

    wi1 = around(w_in, "feat", 1)
    wo1 = around(w_out, "feat", 1)
    ffn = 4 * latent * 2 * half

    live = jnp.arange(BLOCK, dtype=jnp.int32)[None, :] < send_count[0][:, None]
    pick, spread, pick_self, *sends = call(
        functools.partial(setup_kernel, groups, pairs),
        [act16(pairs * BLOCK, rows), act16(rows, far_rows), act16(BLOCK, rows)]
        + [act16(BLOCK)] * pairs,
        [features, jnp.where(live, send_rows[0], -1)],
        2 * rows * far_rows * latent,
        name="setup",
    )
    weights = (w_in, wi1, w_out, wo1)
    msg, local, local_t, remote, remote_t = [None] * 5
    inputs = [features]
    totals = []
    mine = []
    others = []
    for layer in range(layers):
        mine.append(forward(sends))
        if layer == 0:
            msg, local, local_t, remote, remote_t = call(
                functools.partial(first_kernel, groups),
                [act16(rows), act16(rows, rows), act16(rows, rows)]
                + [act16(rows, far_rows), act16(far_rows, rows)],
                [features, pick_self, block_index, block_values, *weights],
                rows * ffn + 2 * rows * rows * BLOCK,
                scratch=[pltpu.VMEM((rows, rows + BLOCK + far_rows), F32)],
                name="first",
            )
        else:
            (msg,) = call(
                functools.partial(local_kernel, layer),
                [act16(rows)],
                [inputs[layer], *weights],
                rows * ffn,
                name=f"local{layer}",
            )
        mine[layer], msg = lax.optimization_barrier((mine[layer], msg))
        others.append(other_core(mine[layer]))
        (mixed,) = call(
            functools.partial(part_kernel, layer, pairs),
            [((rows, latent), F32)],
            [local, msg, remote, *weights, *mine[layer]],
            2 * rows * rows * latent,
            name=f"part{layer}",
        )
        prev = totals[-1] if layer else features
        if layer < last:
            total, new, *sends = call(
                functools.partial(mix_kernel, layer, pairs),
                [((rows, latent), F32), act16(rows)] + [act16(BLOCK)] * pairs,
                [prev, mixed, remote, pick, *weights, *others[layer]],
                far_rows * ffn + 2 * rows * far_rows * latent,
                name=f"mix{layer}",
            )
            totals.append(total)
            inputs.append(new)
    bwd_outs = (
        [((rows, latent), F32), act16(rows), act16(far_rows), act16(far_rows)]
        + [act16(far_rows, half)] * 2
        + [act16(BLOCK)] * groups
    )
    outs = call(
        functools.partial(turn_kernel, last, groups, pairs),
        bwd_outs,
        [totals[-1], mixed, remote, remote_t, cotangent, *weights, *mine[last], *others[last]],
        2 * far_rows * ffn,
        name="turn",
    )
    grad_rows = 2 * latent * half // LANES

    def distances(axis):
        return [(axis, 1 << i) for i in range(lax.axis_size(axis).bit_length() - 1)]

    over_basin, over_chain = distances("basin"), distances("chain")
    n = len(over_basin)
    stages = list(
        zip(over_basin + over_chain, over_chain[:n] + over_basin + over_chain[n:], strict=True)
    )
    returned = {}
    sums = {}

    def back(layer, outs, after):
        returned[layer] = backward(outs[6:])
        grad, *parts = call(
            functools.partial(back_kernel, layer, grad_scale, stages[0]),
            [((rows, latent), F32), ((grad_rows // 2, LANES), F32)]
            + [((grad_rows // 2, LANES), BF16)],
            [outs[1], inputs[layer], local_t, *weights, *outs[2:6]],
            3 * rows * ffn + 2 * rows * rows * latent,
            scratch=[
                pltpu.VMEM((grad_rows, LANES), F32),
                pltpu.VMEM((rows, latent), BF16),
                pltpu.VMEM((rows, half), BF16),
                pltpu.VMEM((rows, half), BF16),
            ],
            name=f"back{layer}",
            after=after,
        )
        sums[layer] = Sum(parts, stages, f"{layer}")
        return [outs[0], grad], [parts[0]]

    def join(layer, state, after):
        if layer:
            return call(
                functools.partial(join_kernel, layer - 1, groups, pairs),
                bwd_outs,
                [*state, spread, remote_t, totals[layer - 1]]
                + [*weights, *returned[layer], *mine[layer - 1], *others[layer - 1]],
                2 * far_rows * ffn,
                name=f"join{layer}",
                after=after,
            )
        return call(
            last_kernel,
            [((rows, latent), F32), ((8, LANES), F32)],
            [*state, spread, *returned[layer]],
            2 * rows * far_rows * latent,
            name="join0",
            after=after,
        )

    def write(layer, written, after):
        ready = [sums[layer].keep, sums[layer].got]
        kept = [*written, *after]
        return pl.pallas_call(
            functools.partial(write_kernel, layer, stages[0], len(kept)),
            out_shape=[
                jax.ShapeDtypeStruct((layers, latent, half), F32),
                jax.ShapeDtypeStruct((layers, half, latent), F32),
                jax.ShapeDtypeStruct((8, LANES), F32),
            ],
            in_specs=[ANY] * len(kept) + [VMEM] * len(ready),
            out_specs=[ANY] * 2 + [VMEM],
            scratch_shapes=[
                pltpu.VMEM((grad_rows, LANES), F32),
                pltpu.VMEM((latent, half), F32),
                pltpu.VMEM((half, latent), F32),
                pltpu.SemaphoreType.DMA((2,)),
            ],
            input_output_aliases={i: i for i in range(len(written))},
            compiler_params=pltpu.CompilerParams(vmem_limit_bytes=LIMIT),
            cost_estimate=pl.CostEstimate(flops=0, bytes_accessed=4_000_000, transcendentals=0),
            name=f"write{layer}",
        )(*written, *after, *ready)

    count = 2 * len(stages) - 1
    at = []
    for layer in reversed(range(layers)):
        state, at = back(layer, outs, at)
        if layer:
            for above in reversed(range(layer + 1, layers)):
                at = sums[above].step(at)
            outs = join(layer, state, at)
            at = outs[1:2]
    written = []
    waiting = list(reversed(range(layers)))
    while waiting:
        for layer in list(waiting):
            if sums[layer].done < count:
                at = sums[layer].step(at)
            else:
                *written, token = write(layer, written, at)
                at = [token]
                waiting.remove(layer)
            if layer == 1 and sums[layer].done == 1:
                grad, token = join(0, state, at)
                at = [token]
    return (grad, *written)


def solution(mesh):
    placed = (
        P(("runs", "chain", "basin"), None),
        P(("runs", "chain", "basin"), None),
        P(None, None, "feat"),
        P(None, "feat", None),
        P(("chain", "basin"), None),
        P(("chain", "basin"), None, None, None),
        P(("chain", "basin"), None, None),
        P(("chain", "basin"), None),
    )
    return jax.shard_map(
        shards,
        mesh=mesh,
        in_specs=placed,
        out_specs=(
            P(("runs", "chain", "basin"), None),
            P("runs", None, "feat"),
            P("runs", "feat", None),
        ),
        check_vma=False,
    )
```

```python
import functools

import jax
import jax.numpy as jnp
from jax import lax
from jax.experimental import pallas as pl
from jax.experimental.pallas import tpu as pltpu
from jax.sharding import PartitionSpec as P

BLOCK = 128
LANES = 128
EPS = 1e-06
F32 = jnp.float32
BF16 = jnp.bfloat16
VMEM = pl.BlockSpec(memory_space=pltpu.VMEM)
SMEM = pl.BlockSpec(memory_space=pltpu.SMEM)
ANY = pl.BlockSpec(memory_space=pl.ANY)
NN = (((1,), (0,)), ((), ()))
NT = (((1,), (1,)), ((), ()))
TN = (((0,), (0,)), ((), ()))


def mm(a, b, dims=NN):
    return lax.dot_general(a, b, dims, preferred_element_type=F32)


LIMIT = 24 * 1024 * 1024


def call(body, outs, ins, flops, scratch=(), name=None, after=(), bytes_accessed=4_000_000):
    skipped = len(after)
    return pl.pallas_call(
        lambda *refs: body(*refs[skipped:]),
        out_shape=[jax.ShapeDtypeStruct(s, d) for s, d in outs],
        in_specs=[ANY] * skipped + [SMEM if x.ndim == 2 and x.shape[1] == 4 else VMEM for x in ins],
        out_specs=[VMEM] * len(outs),
        scratch_shapes=list(scratch),
        compiler_params=pltpu.CompilerParams(vmem_limit_bytes=LIMIT),
        cost_estimate=pl.CostEstimate(
            flops=flops, bytes_accessed=bytes_accessed, transcendentals=0
        ),
        name=name,
    )(*after, *ins)


def sigmoid(v):
    return 1.0 / (1.0 + jnp.exp(-v))


def message_of(x, halves):
    total = None
    for w_in, w_out in halves:
        pre = mm(x, w_in)
        part = mm((pre * sigmoid(pre)).astype(BF16), w_out)
        total = part if total is None else total + part
    return total.astype(BF16)


def message_grad(x, dmsg, halves):
    total = None
    kept = None
    for w_in, w_out in halves:
        pre = mm(x, w_in)
        sig = sigmoid(pre)
        dact = mm(dmsg, w_out, NT)
        dpre = (dact * (sig * (1.0 + pre * (1.0 - sig)))).astype(BF16)
        if kept is None:
            kept = ((pre * sig).astype(BF16), dpre)
        part = mm(dpre, w_in, NT)
        total = part if total is None else total + part
    return total, kept


def normed_of(total):
    scale = lax.rsqrt(jnp.mean(total * total, axis=-1, keepdims=True) + EPS)
    return scale, scale * total


def norm_grad(grad, total):
    scale, normed = normed_of(total)
    return scale * (grad - normed * jnp.mean(grad * normed, axis=-1, keepdims=True))


def setup_kernel(groups, pairs, features, sent, *refs):
    pick, spread, pick_self = refs[:3]
    sends = refs[3:]
    rows = features.shape[0]
    b, feat = lax.axis_index("basin"), lax.axis_index("feat")
    for route in range(-1, 2 * pairs):
        if route == 0:
            chosen = lax.broadcasted_iota(jnp.int32, (1, BLOCK), 1) + (rows - BLOCK)
        elif route >= groups:
            chosen = jnp.full((1, BLOCK), -1, jnp.int32)
        else:
            chosen = sent[pl.ds(lax.rem(b + max(route, 0), groups), 1), :]
        across = jnp.broadcast_to(chosen, (BLOCK, BLOCK))
        down = across.T
        for r in range(0, rows, BLOCK):
            at = lax.broadcasted_iota(jnp.int32, (BLOCK, BLOCK), 1) + r
            hot = (down == at).astype(F32).astype(BF16)
            if route < 0:
                pick_self[:, r : r + BLOCK] = hot
                continue

            @pl.when(route % 2 == feat)
            def _():
                pick[route // 2 * BLOCK : (route // 2 + 1) * BLOCK, r : r + BLOCK] = hot

            at = lax.broadcasted_iota(jnp.int32, (BLOCK, BLOCK), 0) + r
            if route < groups:
                spread[r : r + BLOCK, route * BLOCK : (route + 1) * BLOCK] = (
                    (across == at).astype(F32).astype(BF16)
                )
    for i, send in enumerate(sends):
        send[...] = mm(pick[i * BLOCK : (i + 1) * BLOCK, :], features[...]).astype(BF16)


def build_adjacency(groups, rows, index, values, pick_self, outs, acc):
    local, local_t, remote, remote_t = outs
    own = rows // BLOCK
    b = lax.axis_index("basin")
    acc[...] = jnp.zeros_like(acc)
    for k in range(own):
        for t in range(index.shape[1]):
            v = index[k, t]
            route = jnp.where(v == own, 0, lax.rem(b + groups - (v - own - 1), groups))
            far = jnp.where((v > own) & (route == 0), own, own + 1 + route)
            at = jnp.where(v < own, v, far)
            here = (pl.ds(k * BLOCK, BLOCK), pl.ds(pl.multiple_of(at * BLOCK, BLOCK), BLOCK))
            acc[here] += values[k, t].astype(F32)
    mine = acc[:, rows : rows + BLOCK].astype(BF16)
    full = acc[:, :rows] + mm(mine, pick_self[...])
    local[...] = full.astype(BF16)
    local_t[...] = full.T.astype(BF16)
    far = acc[:, rows + BLOCK :]
    remote[...] = far.astype(BF16)
    remote_t[...] = far.T.astype(BF16)


def own_messages(layer, inputs, weights, msg):
    wi0, wi1, wo0, wo1 = weights
    halves = [(wi0[layer], wo0[layer]), (wi1[layer], wo1[layer])]
    for r in range(0, inputs.shape[0], 256):
        msg[r : r + 256, :] = message_of(inputs[r : r + 256, :], halves)


def first_kernel(groups, *refs):
    inputs, pick_self, index, values = refs[:4]
    weights, msg, outs = refs[4:8], refs[8], refs[9:13]
    own_messages(0, inputs, weights, msg)
    build_adjacency(groups, inputs.shape[0], index, values, pick_self, outs, refs[13])


def local_kernel(layer, *refs):
    own_messages(layer, refs[0], refs[1:5], refs[5])


def remote_mixed(layer, received, remote, feat, weights):
    wi0, wi1, wo0, wo1 = weights
    halves = [(wi0[layer], wo0[layer]), (wi1[layer], wo1[layer])]
    total = None
    for i, block in enumerate(received):
        route = jnp.minimum(2 * i + feat, remote.shape[1] // BLOCK - 1)
        columns = remote[:, pl.ds(pl.multiple_of(route * BLOCK, BLOCK), BLOCK)]
        part = mm(columns, message_of(block[...], halves))
        total = part if total is None else total + part
    return total


def part_kernel(layer, pairs, *refs):
    local, msg, remote = refs[:3]
    weights, received, mixed = refs[3:7], refs[7 : 7 + pairs], refs[-1]
    mixed[...] = mm(local[...], msg[...]) + remote_mixed(
        layer, received, remote, lax.axis_index("feat"), weights
    )


def mixed_total(layer, state, mixed, received, remote, weights):
    return state + mixed[...] + remote_mixed(
        layer, received, remote, 1 - lax.axis_index("feat"), weights
    )


def mix_kernel(layer, pairs, *refs):
    prev, mixed, remote, pick = refs[:4]
    weights = refs[4:8]
    received = refs[8 : 8 + pairs]
    total, inputs = refs[8 + pairs : 10 + pairs]
    sends = refs[10 + pairs :]
    state = prev[...].astype(F32) if layer == 0 else normed_of(prev[...])[1]
    total[...] = mixed_total(layer, state, mixed, received, remote, weights)
    new = normed_of(total[...])[1].astype(BF16)
    inputs[...] = new
    for i, send in enumerate(sends):
        send[...] = mm(pick[i * BLOCK : (i + 1) * BLOCK, :], new).astype(BF16)


def start_bwd(layer, groups, dtotal_now, weights, mine, others, remote_t, outs):
    dtotal, dround, far_x, far_dmsg, far_act, far_dpre = outs[:6]
    backs = outs[6:]
    wi0, wi1, wo0, wo1 = weights
    halves = [(wi0[layer], wo0[layer]), (wi1[layer], wo1[layer])]
    dtotal[...] = dtotal_now
    dround[...] = dtotal_now.astype(BF16)
    for first in range(2):

        @pl.when(lax.axis_index("feat") == first)
        def _():
            for route in range(groups):
                block = (mine, others)[(route + first) % 2][route // 2]
                far_x[route * BLOCK : (route + 1) * BLOCK, :] = block[...]

    dmsg = mm(remote_t[...], dround[...]).astype(BF16)
    back, (act, dpre) = message_grad(far_x[...], dmsg, halves)
    far_dmsg[...] = dmsg
    far_act[...] = act
    far_dpre[...] = dpre
    for i, out in enumerate(backs):
        out[...] = back[i * BLOCK : (i + 1) * BLOCK, :].astype(BF16)


def turn_kernel(layer, groups, pairs, *refs):
    prev, mixed, remote, remote_t, cot = refs[:5]
    weights = refs[5:9]
    mine, others = refs[9 : 9 + pairs], refs[9 + pairs : 9 + 2 * pairs]
    outs = refs[9 + 2 * pairs :]
    state = normed_of(prev[...])[1]
    total = mixed_total(layer, state, mixed, others, remote, weights)
    dtotal = norm_grad(cot[...], total)
    start_bwd(layer, groups, dtotal, weights, mine, others, remote_t, outs)


def back_kernel(layer, grad_scale, stage, *refs):
    dround, inputs, local_t = refs[:3]
    wi0, wi1, wo0, wo1 = refs[3:7]
    far_x, far_dmsg, far_act, far_dpre = refs[7:11]
    back = refs[11]
    grads, dmsg, act, dpre = refs[-4:]
    halves = [(wi0[layer], wo0[layer]), (wi1[layer], wo1[layer])]
    dmsg[...] = mm(local_t[...], dround[...]).astype(BF16)
    for r in range(0, inputs.shape[0], 256):
        here = slice(r, r + 256)
        back[here, :], (act[here, :], dpre[here, :]) = message_grad(
            inputs[here, :], dmsg[here, :], halves
        )
    latent, hidden = inputs.shape[1], act.shape[1]
    g_in = (mm(inputs[...], dpre[...], TN) + mm(far_x[...], far_dpre[...], TN)) * grad_scale
    for j in range(hidden // LANES):
        grads[j * latent : (j + 1) * latent, :] = g_in[:, j * LANES : (j + 1) * LANES]
    g_out = (mm(act[...], dmsg[...], TN) + mm(far_act[...], far_dmsg[...], TN)) * grad_scale
    for j in range(latent // LANES):
        at = hidden // LANES * latent + j * hidden
        grads[at : at + hidden, :] = g_out[:, j * LANES : (j + 1) * LANES]
    split(grads, stage, refs[12:14])


def upper(stage):
    (axis0, d0), (axis1, d1) = stage
    bit0 = lax.rem(lax.axis_index(axis0) // d0, 2)
    bit1 = lax.rem(lax.axis_index(axis1) // d1, 2)
    return jnp.where(lax.axis_index("feat") == 0, bit0, bit1)


def split(block, stage, outs):
    m = block.shape[0] // 2
    bit = upper(stage)
    keep, send = outs
    keep[...] = block[pl.ds(pl.multiple_of(bit * m, m), m), :]
    send[...] = block[pl.ds(pl.multiple_of((1 - bit) * m, m), m), :].astype(BF16)


def add_split_kernel(stage, keep, got, *refs):
    acc = refs[-1]
    acc[...] = keep[...] + got[...].astype(F32)
    split(acc, stage, refs[:-1])


def add_all_kernel(keep, got, own, send):
    own[...] = keep[...] + got[...].astype(F32)
    send[...] = own[...].astype(BF16)


def add_kernel(keep, got, out):
    out[...] = (keep[...] + got[...].astype(F32)).astype(BF16)


def place(stage, own, got, out):
    m = own.shape[0]
    bit = upper(stage)
    out[pl.ds(pl.multiple_of(bit * m, m), m), :] = own[...].astype(out.dtype)
    out[pl.ds(pl.multiple_of((1 - bit) * m, m), m), :] = got[...].astype(out.dtype)


def place_kernel(stage, own, got, out):
    place(stage, own, got, out)


def write_kernel(layer, stage, kept, *refs):
    out_in, out_out, token, grads, slab_in, slab_out, sem = refs[-7:]
    token[...] = jnp.zeros_like(token)
    place(stage, refs[kept], refs[kept + 1], grads)
    latent, hidden = slab_in.shape
    for j in range(hidden // LANES):
        slab_in[:, j * LANES : (j + 1) * LANES] = grads[j * latent : (j + 1) * latent, :]
    first = pltpu.make_async_copy(slab_in, out_in.at[layer], sem.at[0])
    first.start()
    for j in range(latent // LANES):
        at = hidden // LANES * latent + j * hidden
        slab_out[:, j * LANES : (j + 1) * LANES] = grads[at : at + hidden, :]
    second = pltpu.make_async_copy(slab_out, out_out.at[layer], sem.at[1])
    second.start()
    first.wait()
    second.wait()


class Sum:
    def __init__(self, parts, stages, name):
        self.stages, self.name = stages, name
        self.done = 0
        self.keep, send = parts
        self.got = swapped(send, stages[0])

    def step(self, after):
        n = len(self.stages)
        i = self.done
        self.done += 1
        rows = self.keep.shape[0]
        scratch = []
        if i < n - 2:
            body = functools.partial(add_split_kernel, self.stages[i + 1])
            outs = [((rows // 2, LANES), F32), ((rows // 2, LANES), BF16)]
            scratch = [pltpu.VMEM(self.keep.shape, F32)]
        elif i == n - 2:
            body, outs = add_all_kernel, [((rows, LANES), F32), ((rows, LANES), BF16)]
        elif i == n - 1:
            body, outs = add_kernel, [((rows, LANES), BF16)]
        else:
            body = functools.partial(place_kernel, self.stages[2 * n - 2 - i])
            outs = [((rows * 2, LANES), BF16)]
        self.keep, *send = call(
            body,
            outs,
            [self.keep, self.got],
            1,
            scratch=scratch,
            bytes_accessed=1,
            name=f"sum_{self.name}_{i}",
            after=after,
        )
        to = i + 1 if i < n - 1 else 2 * n - 3 - i
        self.got = swapped(send[0] if send else self.keep, self.stages[to])
        return [self.keep]


def gathered_grad(dtotal, back, returned, spread):
    far = jnp.concatenate([x[...] for x in returned], axis=0)
    return dtotal[...] + back[...] + mm(spread[...], far)


def join_kernel(layer, groups, pairs, *refs):
    dtotal, back, spread, remote_t, total = refs[:5]
    weights, refs = refs[5:9], refs[9:]
    returned, refs = refs[:groups], refs[groups:]
    mine, others, outs = refs[:pairs], refs[pairs : 2 * pairs], refs[2 * pairs :]
    grad = gathered_grad(dtotal, back, returned, spread)
    dtotal = norm_grad(grad, total[...])
    start_bwd(layer, groups, dtotal, weights, mine, others, remote_t, outs)


def last_kernel(*refs):
    dtotal, back, spread = refs[:3]
    refs[-2][...] = gathered_grad(dtotal, back, refs[3:-2], spread)
    refs[-1][...] = jnp.zeros_like(refs[-1])


def around(x, axis, distance):
    n = lax.axis_size(axis)
    return lax.ppermute(x, axis, [(i, (i + distance) % n) for i in range(n)])


def over_mesh(x, target):
    chain, groups, cores = (lax.axis_size(axis) for axis in ("chain", "basin", "feat"))
    perm = []
    for c in range(chain):
        for b in range(groups):
            for feat in range(cores):
                to = target(c, b, feat)
                if to is not None:
                    start, end = (c * groups + b) * cores + feat, (to[0] * groups + to[1]) * cores
                    perm.append((start, end + feat))
    return lax.ppermute(x, ("chain", "basin", "feat"), perm)


def swapped(x, stage):
    def partner(c, b, feat):
        axis, d = stage[feat]
        return (c ^ d, b) if axis == "chain" else (c, b ^ d)

    return over_mesh(x, partner)


def forward(sends):
    def target(i, c, b, feat):
        route = 2 * i + feat
        if route == 0:
            return (c + 1, b) if c + 1 < lax.axis_size("chain") else None
        groups = lax.axis_size("basin")
        return (c, (b + route) % groups) if route < groups else None

    return [over_mesh(x, functools.partial(target, i)) for i, x in enumerate(sends)]


def backward(grads):
    chain = lax.axis_size("chain")
    up = lax.ppermute(grads[0], "chain", [(c, c - 1) for c in range(1, chain)])
    return [up] + [around(x, "basin", -s) for s, x in enumerate(grads) if s]


def other_core(got):
    return [around(x, "feat", 1) for x in got]


def shards(features, cotangent, w_in, w_out, block_index, block_values, send_rows, send_count):
    rows, latent = features.shape
    groups = lax.axis_size("basin")
    pairs = (groups + 1) // 2
    layers, _, half = w_in.shape
    far_rows = groups * BLOCK
    own = rows // BLOCK
    grad_scale = float(rows * lax.axis_size("chain") * groups) ** (-0.5)
    last = layers - 1

    def act16(n, m=latent):
        return ((n, m), BF16)

    wi1 = around(w_in, "feat", 1)
    wo1 = around(w_out, "feat", 1)
    ffn = 4 * latent * 2 * half

    live = jnp.arange(BLOCK, dtype=jnp.int32)[None, :] < send_count[0][:, None]
    pick, spread, pick_self, *sends = call(
        functools.partial(setup_kernel, groups, pairs),
        [act16(pairs * BLOCK, rows), act16(rows, far_rows), act16(BLOCK, rows)]
        + [act16(BLOCK)] * pairs,
        [features, jnp.where(live, send_rows[0], -1)],
        2 * rows * far_rows * latent,
        name="setup",
    )
    weights = (w_in, wi1, w_out, wo1)
    msg, local, local_t, remote, remote_t = [None] * 5
    inputs = [features]
    totals = []
    mine = []
    others = []
    for layer in range(layers):
        mine.append(forward(sends))
        if layer == 0:
            msg, local, local_t, remote, remote_t = call(
                functools.partial(first_kernel, groups),
                [act16(rows), act16(rows, rows), act16(rows, rows)]
                + [act16(rows, far_rows), act16(far_rows, rows)],
                [features, pick_self, block_index, block_values, *weights],
                rows * ffn + 2 * rows * rows * BLOCK,
                scratch=[pltpu.VMEM((rows, rows + BLOCK + far_rows), F32)],
                name="first",
            )
        else:
            (msg,) = call(
                functools.partial(local_kernel, layer),
                [act16(rows)],
                [inputs[layer], *weights],
                rows * ffn,
                name=f"local{layer}",
            )
        mine[layer], msg = lax.optimization_barrier((mine[layer], msg))
        others.append(other_core(mine[layer]))
        (mixed,) = call(
            functools.partial(part_kernel, layer, pairs),
            [((rows, latent), F32)],
            [local, msg, remote, *weights, *mine[layer]],
            2 * rows * rows * latent,
            name=f"part{layer}",
        )
        prev = totals[-1] if layer else features
        if layer < last:
            total, new, *sends = call(
                functools.partial(mix_kernel, layer, pairs),
                [((rows, latent), F32), act16(rows)] + [act16(BLOCK)] * pairs,
                [prev, mixed, remote, pick, *weights, *others[layer]],
                far_rows * ffn + 2 * rows * far_rows * latent,
                name=f"mix{layer}",
            )
            totals.append(total)
            inputs.append(new)
    bwd_outs = (
        [((rows, latent), F32), act16(rows), act16(far_rows), act16(far_rows)]
        + [act16(far_rows, half)] * 2
        + [act16(BLOCK)] * groups
    )
    outs = call(
        functools.partial(turn_kernel, last, groups, pairs),
        bwd_outs,
        [totals[-1], mixed, remote, remote_t, cotangent, *weights, *mine[last], *others[last]],
        2 * far_rows * ffn,
        name="turn",
    )
    grad_rows = 2 * latent * half // LANES

    def distances(axis):
        return [(axis, 1 << i) for i in range(lax.axis_size(axis).bit_length() - 1)]

    over_basin, over_chain = distances("basin"), distances("chain")
    n = len(over_basin)
    stages = list(
        zip(over_basin + over_chain, over_chain[:n] + over_basin + over_chain[n:], strict=True)
    )
    returned = {}
    sums = {}

    def back(layer, outs, after):
        returned[layer] = backward(outs[6:])
        parts = [((grad_rows // 2, LANES), F32), ((grad_rows // 2, LANES), BF16)]
        grad, *parts = call(
            functools.partial(back_kernel, layer, grad_scale, stages[0]),
            [((rows, latent), F32), *parts],
            [outs[1], inputs[layer], local_t, *weights, *outs[2:6]],
            3 * rows * ffn + 2 * rows * rows * latent,
            scratch=[
                pltpu.VMEM((grad_rows, LANES), F32),
                pltpu.VMEM((rows, latent), BF16),
                pltpu.VMEM((rows, half), BF16),
                pltpu.VMEM((rows, half), BF16),
            ],
            name=f"back{layer}",
            after=after,
        )
        sums[layer] = Sum(parts, stages, f"{layer}")
        return [outs[0], grad], [parts[0]]

    def join(layer, state, after):
        if layer:
            return call(
                functools.partial(join_kernel, layer - 1, groups, pairs),
                bwd_outs,
                [*state, spread, remote_t, totals[layer - 1]]
                + [*weights, *returned[layer], *mine[layer - 1], *others[layer - 1]],
                2 * far_rows * ffn,
                name=f"join{layer}",
                after=after,
            )
        return call(
            last_kernel,
            [((rows, latent), F32), ((8, LANES), F32)],
            [*state, spread, *returned[layer]],
            2 * rows * far_rows * latent,
            name="join0",
            after=after,
        )

    def write(layer, written, after):
        ready = [sums[layer].keep, sums[layer].got]
        kept = [*written, *after]
        return pl.pallas_call(
            functools.partial(write_kernel, layer, stages[0], len(kept)),
            out_shape=[
                jax.ShapeDtypeStruct((layers, latent, half), F32),
                jax.ShapeDtypeStruct((layers, half, latent), F32),
                jax.ShapeDtypeStruct((8, LANES), F32),
            ],
            in_specs=[ANY] * len(kept) + [VMEM] * len(ready),
            out_specs=[ANY] * 2 + [VMEM],
            scratch_shapes=[
                pltpu.VMEM((grad_rows, LANES), F32),
                pltpu.VMEM((latent, half), F32),
                pltpu.VMEM((half, latent), F32),
                pltpu.SemaphoreType.DMA((2,)),
            ],
            input_output_aliases={i: i for i in range(len(written))},
            compiler_params=pltpu.CompilerParams(vmem_limit_bytes=LIMIT),
            cost_estimate=pl.CostEstimate(flops=1, bytes_accessed=1, transcendentals=0),
            name=f"write{layer}",
        )(*written, *after, *ready)

    count = 2 * len(stages) - 2
    at = []
    for layer in reversed(range(layers)):
        state, at = back(layer, outs, at)
        if layer:
            for above in reversed(range(layer + 1, layers)):
                at = sums[above].step(at)
            outs = join(layer, state, at)
            at = outs[1:2]
    for layer in reversed(range(1, last)):
        at = sums[layer].step(at)
    grad, token = join(0, state, at)
    at = sums[0].step([token])
    written = []
    waiting = list(reversed(range(layers)))
    while waiting:
        for layer in list(waiting):
            if sums[layer].done < count:
                at = sums[layer].step(at)
            else:
                *written, token = write(layer, written, at)
                at = [token]
                waiting.remove(layer)
    return (grad, *written)


def solution(mesh):
    placed = (
        P(("runs", "chain", "basin"), None),
        P(("runs", "chain", "basin"), None),
        P(None, None, "feat"),
        P(None, "feat", None),
        P(("chain", "basin"), None),
        P(("chain", "basin"), None, None, None),
        P(("chain", "basin"), None, None),
        P(("chain", "basin"), None),
    )
    return jax.shard_map(
        shards,
        mesh=mesh,
        in_specs=placed,
        out_specs=(
            P(("runs", "chain", "basin"), None),
            P("runs", None, "feat"),
            P("runs", "feat", None),
        ),
        check_vma=False,
    )
```

```python
import functools

import jax
import jax.numpy as jnp
from jax import lax
from jax.experimental import pallas as pl
from jax.experimental.pallas import tpu as pltpu
from jax.sharding import PartitionSpec as P

BLOCK = 128
LANES = 128
EPS = 1e-06
F32 = jnp.float32
BF16 = jnp.bfloat16
VMEM = pl.BlockSpec(memory_space=pltpu.VMEM)
SMEM = pl.BlockSpec(memory_space=pltpu.SMEM)
ANY = pl.BlockSpec(memory_space=pl.ANY)
NN = (((1,), (0,)), ((), ()))
NT = (((1,), (1,)), ((), ()))
TN = (((0,), (0,)), ((), ()))


def mm(a, b, dims=NN):
    return lax.dot_general(a, b, dims, preferred_element_type=F32)


LIMIT = 24 * 1024 * 1024


def call(body, outs, ins, flops, scratch=(), name=None, after=(), bytes_accessed=4_000_000):
    skipped = len(after)
    return pl.pallas_call(
        lambda *refs: body(*refs[skipped:]),
        out_shape=[jax.ShapeDtypeStruct(s, d) for s, d in outs],
        in_specs=[ANY] * skipped + [SMEM if x.ndim == 2 and x.shape[1] == 4 else VMEM for x in ins],
        out_specs=[VMEM] * len(outs),
        scratch_shapes=list(scratch),
        compiler_params=pltpu.CompilerParams(vmem_limit_bytes=LIMIT),
        cost_estimate=pl.CostEstimate(
            flops=flops, bytes_accessed=bytes_accessed, transcendentals=0
        ),
        name=name,
    )(*after, *ins)


def sigmoid(v):
    return 1.0 / (1.0 + jnp.exp(-v))


def message_of(x, halves):
    total = None
    for w_in, w_out in halves:
        pre = mm(x, w_in)
        part = mm((pre * sigmoid(pre)).astype(BF16), w_out)
        total = part if total is None else total + part
    return total.astype(BF16)


def message_grad(x, dmsg, halves):
    total = None
    kept = None
    for w_in, w_out in halves:
        pre = mm(x, w_in)
        sig = sigmoid(pre)
        dact = mm(dmsg, w_out, NT)
        dpre = (dact * (sig * (1.0 + pre * (1.0 - sig)))).astype(BF16)
        if kept is None:
            kept = ((pre * sig).astype(BF16), dpre)
        part = mm(dpre, w_in, NT)
        total = part if total is None else total + part
    return total, kept


def normed_of(total):
    scale = lax.rsqrt(jnp.mean(total * total, axis=-1, keepdims=True) + EPS)
    return scale, scale * total


def norm_grad(grad, total):
    scale, normed = normed_of(total)
    return scale * (grad - normed * jnp.mean(grad * normed, axis=-1, keepdims=True))


def setup_kernel(groups, pairs, features, sent, *refs):
    pick, spread, pick_self = refs[:3]
    sends = refs[3:]
    rows = features.shape[0]
    b, feat = lax.axis_index("basin"), lax.axis_index("feat")
    for route in range(-1, 2 * pairs):
        if route == 0:
            chosen = lax.broadcasted_iota(jnp.int32, (1, BLOCK), 1) + (rows - BLOCK)
        elif route >= groups:
            chosen = jnp.full((1, BLOCK), -1, jnp.int32)
        else:
            chosen = sent[pl.ds(lax.rem(b + max(route, 0), groups), 1), :]
        across = jnp.broadcast_to(chosen, (BLOCK, BLOCK))
        down = across.T
        for r in range(0, rows, BLOCK):
            at = lax.broadcasted_iota(jnp.int32, (BLOCK, BLOCK), 1) + r
            hot = (down == at).astype(F32).astype(BF16)
            if route < 0:
                pick_self[:, r : r + BLOCK] = hot
                continue

            @pl.when(route % 2 == feat)
            def _():
                pick[route // 2 * BLOCK : (route // 2 + 1) * BLOCK, r : r + BLOCK] = hot

            at = lax.broadcasted_iota(jnp.int32, (BLOCK, BLOCK), 0) + r
            if route < groups:
                spread[r : r + BLOCK, route * BLOCK : (route + 1) * BLOCK] = (
                    (across == at).astype(F32).astype(BF16)
                )
    for i, send in enumerate(sends):
        send[...] = mm(pick[i * BLOCK : (i + 1) * BLOCK, :], features[...]).astype(BF16)


def build_adjacency(groups, rows, index, values, pick_self, outs, acc):
    local, local_t, remote, remote_t = outs
    own = rows // BLOCK
    b = lax.axis_index("basin")
    acc[...] = jnp.zeros_like(acc)
    for k in range(own):
        for t in range(index.shape[1]):
            v = index[k, t]
            route = jnp.where(v == own, 0, lax.rem(b + groups - (v - own - 1), groups))
            far = jnp.where((v > own) & (route == 0), own, own + 1 + route)
            at = jnp.where(v < own, v, far)
            here = (pl.ds(k * BLOCK, BLOCK), pl.ds(pl.multiple_of(at * BLOCK, BLOCK), BLOCK))
            acc[here] += values[k, t].astype(F32)
    mine = acc[:, rows : rows + BLOCK].astype(BF16)
    full = acc[:, :rows] + mm(mine, pick_self[...])
    local[...] = full.astype(BF16)
    local_t[...] = full.T.astype(BF16)
    far = acc[:, rows + BLOCK :]
    remote[...] = far.astype(BF16)
    remote_t[...] = far.T.astype(BF16)


def own_messages(layer, inputs, weights, msg):
    wi0, wi1, wo0, wo1 = weights
    halves = [(wi0[layer], wo0[layer]), (wi1[layer], wo1[layer])]
    for r in range(0, inputs.shape[0], 256):
        msg[r : r + 256, :] = message_of(inputs[r : r + 256, :], halves)


def first_kernel(groups, *refs):
    inputs, pick_self, index, values = refs[:4]
    weights, msg, outs = refs[4:8], refs[8], refs[9:13]
    own_messages(0, inputs, weights, msg)
    build_adjacency(groups, inputs.shape[0], index, values, pick_self, outs, refs[13])


def local_kernel(layer, *refs):
    own_messages(layer, refs[0], refs[1:5], refs[5])


def remote_mixed(layer, received, remote, feat, weights):
    wi0, wi1, wo0, wo1 = weights
    halves = [(wi0[layer], wo0[layer]), (wi1[layer], wo1[layer])]
    total = None
    for i, block in enumerate(received):
        route = jnp.minimum(2 * i + feat, remote.shape[1] // BLOCK - 1)
        columns = remote[:, pl.ds(pl.multiple_of(route * BLOCK, BLOCK), BLOCK)]
        part = mm(columns, message_of(block[...], halves))
        total = part if total is None else total + part
    return total


def part_kernel(layer, pairs, *refs):
    local, msg, remote = refs[:3]
    weights, received, mixed = refs[3:7], refs[7 : 7 + pairs], refs[-1]
    mixed[...] = mm(local[...], msg[...]) + remote_mixed(
        layer, received, remote, lax.axis_index("feat"), weights
    )


def mixed_total(layer, state, mixed, received, remote, weights):
    return state + mixed[...] + remote_mixed(
        layer, received, remote, 1 - lax.axis_index("feat"), weights
    )


def mix_kernel(layer, pairs, *refs):
    prev, mixed, remote, pick = refs[:4]
    weights = refs[4:8]
    received = refs[8 : 8 + pairs]
    total, inputs = refs[8 + pairs : 10 + pairs]
    sends = refs[10 + pairs :]
    state = prev[...].astype(F32) if layer == 0 else normed_of(prev[...])[1]
    total[...] = mixed_total(layer, state, mixed, received, remote, weights)
    new = normed_of(total[...])[1].astype(BF16)
    inputs[...] = new
    for i, send in enumerate(sends):
        send[...] = mm(pick[i * BLOCK : (i + 1) * BLOCK, :], new).astype(BF16)


def start_bwd(layer, groups, dtotal_now, weights, mine, others, remote_t, outs):
    dtotal, dround, far_x, far_dmsg, far_act, far_dpre = outs[:6]
    backs = outs[6:]
    wi0, wi1, wo0, wo1 = weights
    halves = [(wi0[layer], wo0[layer]), (wi1[layer], wo1[layer])]
    dtotal[...] = dtotal_now
    dround[...] = dtotal_now.astype(BF16)
    for first in range(2):

        @pl.when(lax.axis_index("feat") == first)
        def _():
            for route in range(groups):
                block = (mine, others)[(route + first) % 2][route // 2]
                far_x[route * BLOCK : (route + 1) * BLOCK, :] = block[...]

    dmsg = mm(remote_t[...], dround[...]).astype(BF16)
    back, (act, dpre) = message_grad(far_x[...], dmsg, halves)
    far_dmsg[...] = dmsg
    far_act[...] = act
    far_dpre[...] = dpre
    for i, out in enumerate(backs):
        out[...] = back[i * BLOCK : (i + 1) * BLOCK, :].astype(BF16)


def turn_kernel(layer, groups, pairs, *refs):
    prev, mixed, remote, remote_t, cot = refs[:5]
    weights = refs[5:9]
    mine, others = refs[9 : 9 + pairs], refs[9 + pairs : 9 + 2 * pairs]
    outs = refs[9 + 2 * pairs :]
    state = normed_of(prev[...])[1]
    total = mixed_total(layer, state, mixed, others, remote, weights)
    dtotal = norm_grad(cot[...], total)
    start_bwd(layer, groups, dtotal, weights, mine, others, remote_t, outs)


def back_kernel(layer, grad_scale, *refs):
    dround, inputs, local_t = refs[:3]
    wi0, wi1, wo0, wo1 = refs[3:7]
    far_x, far_dmsg, far_act, far_dpre = refs[7:11]
    back, grads, dmsg, act, dpre = refs[11:]
    halves = [(wi0[layer], wo0[layer]), (wi1[layer], wo1[layer])]
    dmsg[...] = mm(local_t[...], dround[...]).astype(BF16)
    for r in range(0, inputs.shape[0], 256):
        here = slice(r, r + 256)
        back[here, :], (act[here, :], dpre[here, :]) = message_grad(
            inputs[here, :], dmsg[here, :], halves
        )
    latent, hidden = inputs.shape[1], act.shape[1]
    g_in = (mm(inputs[...], dpre[...], TN) + mm(far_x[...], far_dpre[...], TN)) * grad_scale
    for j in range(hidden // LANES):
        grads[j * latent : (j + 1) * latent, :] = g_in[:, j * LANES : (j + 1) * LANES]
    g_out = (mm(act[...], dmsg[...], TN) + mm(far_act[...], far_dmsg[...], TN)) * grad_scale
    for j in range(latent // LANES):
        at = hidden // LANES * latent + j * hidden
        grads[at : at + hidden, :] = g_out[:, j * LANES : (j + 1) * LANES]


def upper(stage):
    (axis0, d0), (axis1, d1) = stage
    bit0 = lax.rem(lax.axis_index(axis0) // d0, 2)
    bit1 = lax.rem(lax.axis_index(axis1) // d1, 2)
    return jnp.where(lax.axis_index("feat") == 0, bit0, bit1)


def place(stage, own, got, out):
    m = own.shape[0]
    bit = upper(stage)
    out[pl.ds(pl.multiple_of(bit * m, m), m), :] = own[...].astype(out.dtype)
    out[pl.ds(pl.multiple_of((1 - bit) * m, m), m), :] = got[...].astype(out.dtype)


def sum_kernel(steps, *refs):
    n_in = sum(1 + (kind != "split") for kind, *_ in steps)
    n_out = len(steps) + 1 + max(group for *_, group, _ in steps)
    ins, outs, accs = refs[:n_in], refs[n_in : n_in + n_out], refs[n_in + n_out :]
    sends = outs[len(steps) :]
    for (kind, stage, back, at, group, to), out in zip(steps, outs):
        own, ins = ins[0], ins[1:]
        m = own.shape[0]
        send = sends[group].at[to : to + out.shape[0]]
        if kind != "split":
            got, ins = ins[0].at[at : at + m], ins[1:]
        if kind in ("split", "add_split"):
            if kind == "add_split":
                acc, accs = accs[0], accs[1:]
                acc[...] = own[...] + got[...].astype(F32)
                own = acc
            m = m // 2
            bit = upper(stage)
            out[...] = own[pl.ds(pl.multiple_of(bit * m, m), m), :]
            send[...] = own[pl.ds(pl.multiple_of((1 - bit) * m, m), m), :].astype(BF16)
        else:
            if kind == "place":
                place(back, own, got, out)
            else:
                out[...] = (own[...] + got[...].astype(F32)).astype(out.dtype)
            send[...] = out[...].astype(BF16)


def write_kernel(layer, stage, kept, at, *refs):
    out_in, out_out, token, grads, slab_in, slab_out, sem = refs[-7:]
    token[...] = jnp.zeros_like(token)
    own = refs[kept]
    place(stage, own, refs[kept + 1].at[at : at + own.shape[0]], grads)
    latent, hidden = slab_in.shape
    for j in range(hidden // LANES):
        slab_in[:, j * LANES : (j + 1) * LANES] = grads[j * latent : (j + 1) * latent, :]
    first = pltpu.make_async_copy(slab_in, out_in.at[layer], sem.at[0])
    first.start()
    for j in range(latent // LANES):
        at = hidden // LANES * latent + j * hidden
        slab_out[:, j * LANES : (j + 1) * LANES] = grads[at : at + hidden, :]
    second = pltpu.make_async_copy(slab_out, out_out.at[layer], sem.at[1])
    second.start()
    first.wait()
    second.wait()


class Sum:
    def __init__(self, whole, stages):
        self.own, self.got, self.stages, self.done = whole, None, stages, 0

    def next(self):
        n, i, rows = len(self.stages), self.done, self.own.shape[0]
        if i < n - 1:
            return "add_split" if i else "split", self.stages[i], None, rows // 2, F32
        if i == n - 1:
            return "add", self.stages[i], None, rows, F32
        stage = self.stages[2 * n - 2 - i]
        if i == n:
            return "add", stage, None, rows, BF16
        return "place", stage, self.stages[2 * n - 1 - i], rows * 2, BF16


def sum_step(sums, after):
    steps, ins, outs, scratch, groups = [], [], [], [], {}
    for one in sums:
        kind, stage, back, rows, dtype = one.next()
        group = groups.setdefault(stage, [len(groups), 0])
        steps.append((kind, stage, back, one.got and one.got[1], *group))
        group[1] += rows
        ins += [one.own, one.got[0]] if one.got else [one.own]
        outs.append(((rows, LANES), dtype))
        if kind == "add_split":
            scratch.append(pltpu.VMEM(one.own.shape, F32))
    made = call(
        functools.partial(sum_kernel, steps),
        outs + [((rows, LANES), BF16) for _, rows in groups.values()],
        ins,
        1,
        bytes_accessed=1,
        scratch=scratch,
        name="sum",
        after=after,
    )
    arrived = [swapped(x, stage) for x, stage in zip(made[len(sums) :], groups)]
    for one, own, (*_, group, at) in zip(sums, made, steps):
        one.own, one.got = own, (arrived[group], at)
        one.done += 1
    return [made[0]]


def gathered_grad(dtotal, back, returned, spread):
    far = jnp.concatenate([x[...] for x in returned], axis=0)
    return dtotal[...] + back[...] + mm(spread[...], far)


def join_kernel(layer, groups, pairs, *refs):
    dtotal, back, spread, remote_t, total = refs[:5]
    weights, refs = refs[5:9], refs[9:]
    returned, refs = refs[:groups], refs[groups:]
    mine, others, outs = refs[:pairs], refs[pairs : 2 * pairs], refs[2 * pairs :]
    grad = gathered_grad(dtotal, back, returned, spread)
    dtotal = norm_grad(grad, total[...])
    start_bwd(layer, groups, dtotal, weights, mine, others, remote_t, outs)


def last_kernel(*refs):
    dtotal, back, spread = refs[:3]
    refs[-2][...] = gathered_grad(dtotal, back, refs[3:-2], spread)
    refs[-1][...] = jnp.zeros_like(refs[-1])


def around(x, axis, distance):
    n = lax.axis_size(axis)
    return lax.ppermute(x, axis, [(i, (i + distance) % n) for i in range(n)])


def over_mesh(x, target):
    chain, groups, cores = (lax.axis_size(axis) for axis in ("chain", "basin", "feat"))
    perm = []
    for c in range(chain):
        for b in range(groups):
            for feat in range(cores):
                to = target(c, b, feat)
                if to is not None:
                    start, end = (c * groups + b) * cores + feat, (to[0] * groups + to[1]) * cores
                    perm.append((start, end + feat))
    return lax.ppermute(x, ("chain", "basin", "feat"), perm)


def swapped(x, stage):
    def partner(c, b, feat):
        axis, d = stage[feat]
        return (c ^ d, b) if axis == "chain" else (c, b ^ d)

    return over_mesh(x, partner)


def forward(sends):
    def target(i, c, b, feat):
        route = 2 * i + feat
        if route == 0:
            return (c + 1, b) if c + 1 < lax.axis_size("chain") else None
        groups = lax.axis_size("basin")
        return (c, (b + route) % groups) if route < groups else None

    return [over_mesh(x, functools.partial(target, i)) for i, x in enumerate(sends)]


def backward(grads):
    chain = lax.axis_size("chain")
    up = lax.ppermute(grads[0], "chain", [(c, c - 1) for c in range(1, chain)])
    return [up] + [around(x, "basin", -s) for s, x in enumerate(grads) if s]


def other_core(got):
    return [around(x, "feat", 1) for x in got]


def shards(features, cotangent, w_in, w_out, block_index, block_values, send_rows, send_count):
    rows, latent = features.shape
    groups = lax.axis_size("basin")
    pairs = (groups + 1) // 2
    layers, _, half = w_in.shape
    far_rows = groups * BLOCK
    own = rows // BLOCK
    grad_scale = float(rows * lax.axis_size("chain") * groups) ** (-0.5)
    last = layers - 1

    def act16(n, m=latent):
        return ((n, m), BF16)

    wi1 = around(w_in, "feat", 1)
    wo1 = around(w_out, "feat", 1)
    ffn = 4 * latent * 2 * half

    live = jnp.arange(BLOCK, dtype=jnp.int32)[None, :] < send_count[0][:, None]
    pick, spread, pick_self, *sends = call(
        functools.partial(setup_kernel, groups, pairs),
        [act16(pairs * BLOCK, rows), act16(rows, far_rows), act16(BLOCK, rows)]
        + [act16(BLOCK)] * pairs,
        [features, jnp.where(live, send_rows[0], -1)],
        2 * rows * far_rows * latent,
        name="setup",
    )
    weights = (w_in, wi1, w_out, wo1)
    msg, local, local_t, remote, remote_t = [None] * 5
    inputs = [features]
    totals = []
    mine = []
    others = []
    for layer in range(layers):
        mine.append(forward(sends))
        if layer == 0:
            msg, local, local_t, remote, remote_t = call(
                functools.partial(first_kernel, groups),
                [act16(rows), act16(rows, rows), act16(rows, rows)]
                + [act16(rows, far_rows), act16(far_rows, rows)],
                [features, pick_self, block_index, block_values, *weights],
                rows * ffn + 2 * rows * rows * BLOCK,
                scratch=[pltpu.VMEM((rows, rows + BLOCK + far_rows), F32)],
                name="first",
            )
        else:
            (msg,) = call(
                functools.partial(local_kernel, layer),
                [act16(rows)],
                [inputs[layer], *weights],
                rows * ffn,
                name=f"local{layer}",
            )
        mine[layer], msg = lax.optimization_barrier((mine[layer], msg))
        others.append(other_core(mine[layer]))
        (mixed,) = call(
            functools.partial(part_kernel, layer, pairs),
            [((rows, latent), F32)],
            [local, msg, remote, *weights, *mine[layer]],
            2 * rows * rows * latent,
            name=f"part{layer}",
        )
        prev = totals[-1] if layer else features
        if layer < last:
            total, new, *sends = call(
                functools.partial(mix_kernel, layer, pairs),
                [((rows, latent), F32), act16(rows)] + [act16(BLOCK)] * pairs,
                [prev, mixed, remote, pick, *weights, *others[layer]],
                far_rows * ffn + 2 * rows * far_rows * latent,
                name=f"mix{layer}",
            )
            totals.append(total)
            inputs.append(new)
    bwd_outs = (
        [((rows, latent), F32), act16(rows), act16(far_rows), act16(far_rows)]
        + [act16(far_rows, half)] * 2
        + [act16(BLOCK)] * groups
    )
    outs = call(
        functools.partial(turn_kernel, last, groups, pairs),
        bwd_outs,
        [totals[-1], mixed, remote, remote_t, cotangent, *weights, *mine[last], *others[last]],
        2 * far_rows * ffn,
        name="turn",
    )
    grad_rows = 2 * latent * half // LANES

    def distances(axis):
        return [(axis, 1 << i) for i in range(lax.axis_size(axis).bit_length() - 1)]

    over_basin, over_chain = distances("basin"), distances("chain")
    n = len(over_basin)
    orders = over_basin + over_chain, over_chain[:n] + over_basin + over_chain[n:]
    stages = list(zip(*orders, strict=True)), list(zip(*orders[::-1], strict=True))
    returned = {}
    sums = {}

    def back(layer, outs, after):
        returned[layer] = backward(outs[6:])
        grad, whole = call(
            functools.partial(back_kernel, layer, grad_scale),
            [((rows, latent), F32), ((grad_rows, LANES), F32)],
            [outs[1], inputs[layer], local_t, *weights, *outs[2:6]],
            3 * rows * ffn + 2 * rows * rows * latent,
            scratch=[
                pltpu.VMEM((rows, latent), BF16),
                pltpu.VMEM((rows, half), BF16),
                pltpu.VMEM((rows, half), BF16),
            ],
            name=f"back{layer}",
            after=after,
        )
        sums[layer] = Sum(whole, stages[layer % 2])
        return [outs[0], grad], [grad]

    def join(layer, state, after):
        if layer:
            return call(
                functools.partial(join_kernel, layer - 1, groups, pairs),
                bwd_outs,
                [*state, spread, remote_t, totals[layer - 1]]
                + [*weights, *returned[layer], *mine[layer - 1], *others[layer - 1]],
                2 * far_rows * ffn,
                name=f"join{layer}",
                after=after,
            )
        return call(
            last_kernel,
            [((rows, latent), F32), ((8, LANES), F32)],
            [*state, spread, *returned[layer]],
            2 * rows * far_rows * latent,
            name="join0",
            after=after,
        )

    def write(layer, written, after):
        ready = [sums[layer].own, sums[layer].got[0]]
        kept = [*written, *after]
        return pl.pallas_call(
            functools.partial(
                write_kernel, layer, stages[layer % 2][0], len(kept), sums[layer].got[1]
            ),
            out_shape=[
                jax.ShapeDtypeStruct((layers, latent, half), F32),
                jax.ShapeDtypeStruct((layers, half, latent), F32),
                jax.ShapeDtypeStruct((8, LANES), F32),
            ],
            in_specs=[ANY] * len(kept) + [VMEM] * len(ready),
            out_specs=[ANY] * 2 + [VMEM],
            scratch_shapes=[
                pltpu.VMEM((grad_rows, LANES), F32),
                pltpu.VMEM((latent, half), F32),
                pltpu.VMEM((half, latent), F32),
                pltpu.SemaphoreType.DMA((2,)),
            ],
            input_output_aliases={i: i for i in range(len(written))},
            compiler_params=pltpu.CompilerParams(vmem_limit_bytes=LIMIT),
            cost_estimate=pl.CostEstimate(flops=1, bytes_accessed=1, transcendentals=0),
            name=f"write{layer}",
        )(*written, *after, *ready)

    count = 2 * len(stages[0]) - 1
    at = []
    for layer in reversed(range(layers)):
        state, at = back(layer, outs, at)
        if layer:
            at = [*at, *returned[layer]]
            at = sum_step([sums[above] for above in range(layer, layers)], at)
            outs = join(layer, state, at)
            at = outs[1:2]
    grad = None
    while sums[0].done < count:
        ready = [sums[0]]
        if layers > 1 and sums[1].done < count and sums[1].next()[1] == sums[0].next()[1]:
            ready.append(sums[1])
        at = sum_step(ready, at)
        if grad is None and sums[0].done == 3:
            grad, token = join(0, state, at)
            at = [token]
        for layer in range(1, layers):
            if sums[layer] not in ready and sums[layer].done < count:
                if layer > 1 and sums[0].done == len(stages[0]):
                    at = [*at, sums[0].got[0]]
                at = sum_step([sums[layer]], at)
    written = []
    for layer in reversed(range(layers)):
        *written, token = write(layer, written, at)
        at = [token]
    return (grad, *written)


def solution(mesh):
    placed = (
        P(("runs", "chain", "basin"), None),
        P(("runs", "chain", "basin"), None),
        P(None, None, "feat"),
        P(None, "feat", None),
        P(("chain", "basin"), None),
        P(("chain", "basin"), None, None, None),
        P(("chain", "basin"), None, None),
        P(("chain", "basin"), None),
    )
    return jax.shard_map(
        shards,
        mesh=mesh,
        in_specs=placed,
        out_specs=(
            P(("runs", "chain", "basin"), None),
            P("runs", None, "feat"),
            P("runs", "feat", None),
        ),
        check_vma=False,
    )
```

```python
import functools

import jax
import jax.numpy as jnp
from jax import lax
from jax.experimental import pallas as pl
from jax.experimental.pallas import tpu as pltpu
from jax.sharding import PartitionSpec as P

BLOCK = 128
LANES = 128
EPS = 1e-06
F32 = jnp.float32
BF16 = jnp.bfloat16
VMEM = pl.BlockSpec(memory_space=pltpu.VMEM)
SMEM = pl.BlockSpec(memory_space=pltpu.SMEM)
ANY = pl.BlockSpec(memory_space=pl.ANY)
NN = (((1,), (0,)), ((), ()))
NT = (((1,), (1,)), ((), ()))
TN = (((0,), (0,)), ((), ()))


def mm(a, b, dims=NN):
    return lax.dot_general(a, b, dims, preferred_element_type=F32)


LIMIT = 24 * 1024 * 1024


def call(body, outs, ins, flops, scratch=(), name=None, after=(), bytes_accessed=4_000_000, scalars=None):
    skipped = len(after)
    return pl.pallas_call(
        lambda *refs: body(*refs[skipped:]),
        out_shape=[jax.ShapeDtypeStruct(s, d) for s, d in outs],
        in_specs=[ANY] * skipped + [SMEM if x is scalars else VMEM for x in ins],
        out_specs=[VMEM] * len(outs),
        scratch_shapes=list(scratch),
        compiler_params=pltpu.CompilerParams(vmem_limit_bytes=LIMIT),
        cost_estimate=pl.CostEstimate(
            flops=flops, bytes_accessed=bytes_accessed, transcendentals=0
        ),
        name=name,
    )(*after, *ins)


def sigmoid(v):
    return 1.0 / (1.0 + jnp.exp(-v))


def message_of(x, halves):
    total = None
    for w_in, w_out in halves:
        pre = mm(x, w_in)
        part = mm((pre * sigmoid(pre)).astype(BF16), w_out)
        total = part if total is None else total + part
    return total.astype(BF16)


def message_grad(x, dmsg, halves):
    total = None
    kept = None
    for w_in, w_out in halves:
        pre = mm(x, w_in)
        sig = sigmoid(pre)
        dact = mm(dmsg, w_out, NT)
        dpre = (dact * (sig * (1.0 + pre * (1.0 - sig)))).astype(BF16)
        if kept is None:
            kept = ((pre * sig).astype(BF16), dpre)
        part = mm(dpre, w_in, NT)
        total = part if total is None else total + part
    return total, kept


def normed_of(total):
    scale = lax.rsqrt(jnp.mean(total * total, axis=-1, keepdims=True) + EPS)
    return scale, scale * total


def norm_grad(grad, total):
    scale, normed = normed_of(total)
    return scale * (grad - normed * jnp.mean(grad * normed, axis=-1, keepdims=True))


def setup_kernel(groups, pairs, features, sent, *refs):
    pick, spread, pick_self, held = refs[:4]
    sends = refs[4:]
    rows = features.shape[0]
    held[...] = features[...]
    b, feat = lax.axis_index("basin"), lax.axis_index("feat")
    for route in range(-1, 2 * pairs):
        if route == 0:
            chosen = lax.broadcasted_iota(jnp.int32, (1, BLOCK), 1) + (rows - BLOCK)
        elif route >= groups:
            chosen = jnp.full((1, BLOCK), -1, jnp.int32)
        else:
            chosen = sent[pl.ds(lax.rem(b + max(route, 0), groups), 1), :]
        across = jnp.broadcast_to(chosen, (BLOCK, BLOCK))
        down = across.T
        for r in range(0, rows, BLOCK):
            at = lax.broadcasted_iota(jnp.int32, (BLOCK, BLOCK), 1) + r
            hot = (down == at).astype(F32).astype(BF16)
            if route < 0:
                pick_self[:, r : r + BLOCK] = hot
                continue

            @pl.when(route % 2 == feat)
            def _():
                pick[route // 2 * BLOCK : (route // 2 + 1) * BLOCK, r : r + BLOCK] = hot

            at = lax.broadcasted_iota(jnp.int32, (BLOCK, BLOCK), 0) + r
            if route < groups:
                spread[r : r + BLOCK, route * BLOCK : (route + 1) * BLOCK] = (
                    (across == at).astype(F32).astype(BF16)
                )
    for i, send in enumerate(sends):
        send[...] = mm(pick[i * BLOCK : (i + 1) * BLOCK, :], features[...]).astype(BF16)


def adjacency_kernel(groups, sources, values, pick_self, _, *refs):
    local, local_t, remote, remote_t, acc = refs
    rows = local.shape[0]
    own = rows // BLOCK
    b = lax.axis_index("basin")
    acc[...] = jnp.zeros_like(acc)
    for k in range(own):
        for t in range(values.shape[1]):
            v = sources[t, k]
            route = jnp.where(v == own, 0, lax.rem(b + groups - (v - own - 1), groups))
            far = jnp.where((v > own) & (route == 0), own, own + 1 + route)
            at = jnp.where(v < own, v, far)
            here = (pl.ds(k * BLOCK, BLOCK), pl.ds(pl.multiple_of(at * BLOCK, BLOCK), BLOCK))
            acc[here] += values[k, t].astype(F32)
    mine = acc[:, rows : rows + BLOCK].astype(BF16)
    full = acc[:, :rows] + mm(mine, pick_self[...])
    local[...] = full.astype(BF16)
    local_t[...] = full.T.astype(BF16)
    far = acc[:, rows + BLOCK :]
    remote[...] = far.astype(BF16)
    remote_t[...] = far.T.astype(BF16)


def own_messages(layer, inputs, weights, msg):
    wi0, wi1, wo0, wo1 = weights
    halves = [(wi0[layer], wo0[layer]), (wi1[layer], wo1[layer])]
    for r in range(0, inputs.shape[0], 256):
        msg[r : r + 256, :] = message_of(inputs[r : r + 256, :], halves)


def local_kernel(layer, *refs):
    own_messages(layer, refs[0], refs[1:5], refs[5])


def remote_mixed(layer, received, remote, feat, weights):
    wi0, wi1, wo0, wo1 = weights
    halves = [(wi0[layer], wo0[layer]), (wi1[layer], wo1[layer])]
    total = None
    for i, block in enumerate(received):
        route = jnp.minimum(2 * i + feat, remote.shape[1] // BLOCK - 1)
        columns = remote[:, pl.ds(pl.multiple_of(route * BLOCK, BLOCK), BLOCK)]
        part = mm(columns, message_of(block[...], halves))
        total = part if total is None else total + part
    return total


def part_kernel(layer, pairs, *refs):
    local, msg, remote = refs[:3]
    weights, received, mixed = refs[3:7], refs[7 : 7 + pairs], refs[-1]
    mixed[...] = mm(local[...], msg[...]) + remote_mixed(
        layer, received, remote, lax.axis_index("feat"), weights
    )


def mixed_total(layer, state, mixed, received, remote, weights):
    return state + mixed[...] + remote_mixed(
        layer, received, remote, 1 - lax.axis_index("feat"), weights
    )


def mix_kernel(layer, pairs, *refs):
    prev, mixed, remote, pick = refs[:4]
    weights = refs[4:8]
    received = refs[8 : 8 + pairs]
    total, inputs = refs[8 + pairs : 10 + pairs]
    sends = refs[10 + pairs :]
    state = prev[...].astype(F32) if layer == 0 else normed_of(prev[...])[1]
    total[...] = mixed_total(layer, state, mixed, received, remote, weights)
    new = normed_of(total[...])[1].astype(BF16)
    inputs[...] = new
    for i, send in enumerate(sends):
        send[...] = mm(pick[i * BLOCK : (i + 1) * BLOCK, :], new).astype(BF16)


def start_bwd(layer, groups, dtotal_now, weights, mine, others, remote_t, outs):
    dtotal, dround, far_x, far_dmsg, far_act, far_dpre = outs[:6]
    backs = outs[6:]
    wi0, wi1, wo0, wo1 = weights
    halves = [(wi0[layer], wo0[layer]), (wi1[layer], wo1[layer])]
    dtotal[...] = dtotal_now
    dround[...] = dtotal_now.astype(BF16)
    for first in range(2):

        @pl.when(lax.axis_index("feat") == first)
        def _():
            for route in range(groups):
                block = (mine, others)[(route + first) % 2][route // 2]
                far_x[route * BLOCK : (route + 1) * BLOCK, :] = block[...]

    dmsg = mm(remote_t[...], dround[...]).astype(BF16)
    back, (act, dpre) = message_grad(far_x[...], dmsg, halves)
    far_dmsg[...] = dmsg
    far_act[...] = act
    far_dpre[...] = dpre
    for i, out in enumerate(backs):
        out[...] = back[i * BLOCK : (i + 1) * BLOCK, :].astype(BF16)


def turn_kernel(layer, groups, pairs, *refs):
    prev, mixed, remote, remote_t, cot = refs[:5]
    weights = refs[5:9]
    mine, others = refs[9 : 9 + pairs], refs[9 + pairs : 9 + 2 * pairs]
    outs = refs[9 + 2 * pairs :]
    state = normed_of(prev[...])[1]
    total = mixed_total(layer, state, mixed, others, remote, weights)
    dtotal = norm_grad(cot[...], total)
    start_bwd(layer, groups, dtotal, weights, mine, others, remote_t, outs)


def back_kernel(layer, grad_scale, *refs):
    dround, inputs, local_t = refs[:3]
    wi0, wi1, wo0, wo1 = refs[3:7]
    far_x, far_dmsg, far_act, far_dpre = refs[7:11]
    back, grads, dmsg, act, dpre = refs[11:]
    halves = [(wi0[layer], wo0[layer]), (wi1[layer], wo1[layer])]
    dmsg[...] = mm(local_t[...], dround[...]).astype(BF16)
    for r in range(0, inputs.shape[0], 256):
        here = slice(r, r + 256)
        back[here, :], (act[here, :], dpre[here, :]) = message_grad(
            inputs[here, :], dmsg[here, :], halves
        )
    latent, hidden = inputs.shape[1], act.shape[1]
    g_in = (mm(inputs[...], dpre[...], TN) + mm(far_x[...], far_dpre[...], TN)) * grad_scale
    for j in range(hidden // LANES):
        grads[j * latent : (j + 1) * latent, :] = g_in[:, j * LANES : (j + 1) * LANES]
    g_out = (mm(act[...], dmsg[...], TN) + mm(far_act[...], far_dmsg[...], TN)) * grad_scale
    for j in range(latent // LANES):
        at = hidden // LANES * latent + j * hidden
        grads[at : at + hidden, :] = g_out[:, j * LANES : (j + 1) * LANES]


def upper(stage):
    (axis0, d0), (axis1, d1) = stage
    bit0 = lax.rem(lax.axis_index(axis0) // d0, 2)
    bit1 = lax.rem(lax.axis_index(axis1) // d1, 2)
    return jnp.where(lax.axis_index("feat") == 0, bit0, bit1)


def place(stage, own, got, out):
    m = own.shape[0]
    bit = upper(stage)
    out[pl.ds(pl.multiple_of(bit * m, m), m), :] = own[...].astype(out.dtype)
    out[pl.ds(pl.multiple_of((1 - bit) * m, m), m), :] = got[...].astype(out.dtype)


def sum_kernel(steps, *refs):
    n_in = sum(1 + (kind != "split") for kind, *_ in steps)
    n_out = len(steps) + 1 + max(group for *_, group, _ in steps)
    ins, outs, accs = refs[:n_in], refs[n_in : n_in + n_out], refs[n_in + n_out :]
    sends = outs[len(steps) :]
    for (kind, stage, back, at, group, to), out in zip(steps, outs):
        own, ins = ins[0], ins[1:]
        m = own.shape[0]
        send = sends[group].at[to : to + out.shape[0]]
        if kind != "split":
            got, ins = ins[0].at[at : at + m], ins[1:]
        if kind in ("split", "add_split"):
            if kind == "add_split":
                acc, accs = accs[0], accs[1:]
                acc[...] = own[...] + got[...].astype(F32)
                own = acc
            m = m // 2
            bit = upper(stage)
            out[...] = own[pl.ds(pl.multiple_of(bit * m, m), m), :]
            send[...] = own[pl.ds(pl.multiple_of((1 - bit) * m, m), m), :].astype(BF16)
        else:
            if kind == "place":
                place(back, own, got, out)
            else:
                out[...] = (own[...] + got[...].astype(F32)).astype(out.dtype)
            send[...] = out[...].astype(BF16)


def write_kernel(layer, stage, kept, at, *refs):
    out_in, out_out, token, grads, slab_in, slab_out, sem = refs[-7:]
    token[...] = jnp.zeros_like(token)
    own = refs[kept]
    place(stage, own, refs[kept + 1].at[at : at + own.shape[0]], grads)
    latent, hidden = slab_in.shape
    for j in range(hidden // LANES):
        slab_in[:, j * LANES : (j + 1) * LANES] = grads[j * latent : (j + 1) * latent, :]
    first = pltpu.make_async_copy(slab_in, out_in.at[layer], sem.at[0])
    first.start()
    for j in range(latent // LANES):
        at = hidden // LANES * latent + j * hidden
        slab_out[:, j * LANES : (j + 1) * LANES] = grads[at : at + hidden, :]
    second = pltpu.make_async_copy(slab_out, out_out.at[layer], sem.at[1])
    second.start()
    first.wait()
    second.wait()


class Sum:
    def __init__(self, whole, stages):
        self.own, self.got, self.stages, self.done = whole, None, stages, 0

    def next(self):
        n, i, rows = len(self.stages), self.done, self.own.shape[0]
        if i < n - 1:
            return "add_split" if i else "split", self.stages[i], None, rows // 2, F32
        if i == n - 1:
            return "add", self.stages[i], None, rows, F32
        stage = self.stages[2 * n - 2 - i]
        if i == n:
            return "add", stage, None, rows, BF16
        return "place", stage, self.stages[2 * n - 1 - i], rows * 2, BF16


def sum_step(sums, after):
    steps, ins, outs, scratch, groups = [], [], [], [], {}
    for one in sums:
        kind, stage, back, rows, dtype = one.next()
        group = groups.setdefault(stage, [len(groups), 0])
        steps.append((kind, stage, back, one.got and one.got[1], *group))
        group[1] += rows
        ins += [one.own, one.got[0]] if one.got else [one.own]
        outs.append(((rows, LANES), dtype))
        if kind == "add_split":
            scratch.append(pltpu.VMEM(one.own.shape, F32))
    made = call(
        functools.partial(sum_kernel, steps),
        outs + [((rows, LANES), BF16) for _, rows in groups.values()],
        ins,
        1,
        bytes_accessed=1,
        scratch=scratch,
        name="sum",
        after=after,
    )
    arrived = [swapped(x, stage) for x, stage in zip(made[len(sums) :], groups)]
    for one, own, (*_, group, at) in zip(sums, made, steps):
        one.own, one.got = own, (arrived[group], at)
        one.done += 1
    return [made[0]]


def gathered_grad(dtotal, back, returned, spread):
    far = jnp.concatenate([x[...] for x in returned], axis=0)
    return dtotal[...] + back[...] + mm(spread[...], far)


def join_kernel(layer, groups, pairs, *refs):
    dtotal, back, spread, remote_t, total = refs[:5]
    weights, refs = refs[5:9], refs[9:]
    returned, refs = refs[:groups], refs[groups:]
    mine, others, outs = refs[:pairs], refs[pairs : 2 * pairs], refs[2 * pairs :]
    grad = gathered_grad(dtotal, back, returned, spread)
    dtotal = norm_grad(grad, total[...])
    start_bwd(layer, groups, dtotal, weights, mine, others, remote_t, outs)


def last_kernel(*refs):
    dtotal, back, spread = refs[:3]
    refs[-2][...] = gathered_grad(dtotal, back, refs[3:-2], spread)
    refs[-1][...] = jnp.zeros_like(refs[-1])


def around(x, axis, distance):
    n = lax.axis_size(axis)
    return lax.ppermute(x, axis, [(i, (i + distance) % n) for i in range(n)])


def over_mesh(x, target):
    chain, groups, cores = (lax.axis_size(axis) for axis in ("chain", "basin", "feat"))
    perm = []
    for c in range(chain):
        for b in range(groups):
            for feat in range(cores):
                to = target(c, b, feat)
                if to is not None:
                    start, end = (c * groups + b) * cores + feat, (to[0] * groups + to[1]) * cores
                    perm.append((start, end + feat))
    return lax.ppermute(x, ("chain", "basin", "feat"), perm)


def swapped(x, stage):
    def partner(c, b, feat):
        axis, d = stage[feat]
        return (c ^ d, b) if axis == "chain" else (c, b ^ d)

    return over_mesh(x, partner)


def forward(sends):
    def target(i, c, b, feat):
        route = 2 * i + feat
        if route == 0:
            return (c + 1, b) if c + 1 < lax.axis_size("chain") else None
        groups = lax.axis_size("basin")
        return (c, (b + route) % groups) if route < groups else None

    return [over_mesh(x, functools.partial(target, i)) for i, x in enumerate(sends)]


def backward(grads):
    chain = lax.axis_size("chain")
    up = lax.ppermute(grads[0], "chain", [(c, c - 1) for c in range(1, chain)])
    return [up] + [around(x, "basin", -s) for s, x in enumerate(grads) if s]


def other_core(got):
    return [around(x, "feat", 1) for x in got]


def shards(features, cotangent, w_in, w_out, block_index, block_values, send_rows, send_count):
    rows, latent = features.shape
    groups = lax.axis_size("basin")
    pairs = (groups + 1) // 2
    layers, _, half = w_in.shape
    far_rows = groups * BLOCK
    own = rows // BLOCK
    grad_scale = float(rows * lax.axis_size("chain") * groups) ** (-0.5)
    last = layers - 1

    def act16(n, m=latent):
        return ((n, m), BF16)

    wi1 = around(w_in, "feat", 1)
    wo1 = around(w_out, "feat", 1)
    ffn = 4 * latent * 2 * half

    live = jnp.arange(BLOCK, dtype=jnp.int32)[None, :] < send_count[0][:, None]
    sent = jnp.where(live, send_rows[0], -1)
    sources = block_index.T
    pick, spread, pick_self, features, *sends = call(
        functools.partial(setup_kernel, groups, pairs),
        [act16(pairs * BLOCK, rows), act16(rows, far_rows), act16(BLOCK, rows), act16(rows)]
        + [act16(BLOCK)] * pairs,
        [features, sent],
        2 * rows * far_rows * latent,
        name="setup",
    )
    weights = (w_in, wi1, w_out, wo1)
    inputs = [features]
    totals = []
    mine = []
    others = []
    for layer in range(layers):
        mine.append(forward(sends))
        (msg,) = call(
            functools.partial(local_kernel, layer),
            [act16(rows)],
            [inputs[layer], *weights],
            rows * ffn,
            name=f"local{layer}",
        )
        if layer == 0:
            local, local_t, remote, remote_t = call(
                functools.partial(adjacency_kernel, groups),
                [act16(rows, rows), act16(rows, rows), act16(rows, far_rows), act16(far_rows, rows)],
                [sources, block_values, pick_self, msg],
                2 * rows * rows * BLOCK,
                scratch=[pltpu.VMEM((rows, rows + BLOCK + far_rows), F32)],
                name="adjacency",
                scalars=sources,
            )
            mine[0], local = lax.optimization_barrier((mine[0], local))
        mine[layer], msg = lax.optimization_barrier((mine[layer], msg))
        others.append(other_core(mine[layer]))
        (mixed,) = call(
            functools.partial(part_kernel, layer, pairs),
            [((rows, latent), F32)],
            [local, msg, remote, *weights, *mine[layer]],
            2 * rows * rows * latent,
            name=f"part{layer}",
        )
        prev = totals[-1] if layer else features
        if layer < last:
            total, new, *sends = call(
                functools.partial(mix_kernel, layer, pairs),
                [((rows, latent), F32), act16(rows)] + [act16(BLOCK)] * pairs,
                [prev, mixed, remote, pick, *weights, *others[layer]],
                far_rows * ffn + 2 * rows * far_rows * latent,
                name=f"mix{layer}",
            )
            totals.append(total)
            inputs.append(new)
    bwd_outs = (
        [((rows, latent), F32), act16(rows), act16(far_rows), act16(far_rows)]
        + [act16(far_rows, half)] * 2
        + [act16(BLOCK)] * groups
    )
    outs = call(
        functools.partial(turn_kernel, last, groups, pairs),
        bwd_outs,
        [totals[-1], mixed, remote, remote_t, cotangent, *weights, *mine[last], *others[last]],
        2 * far_rows * ffn,
        name="turn",
    )
    grad_rows = 2 * latent * half // LANES

    def distances(axis):
        return [(axis, 1 << i) for i in range(lax.axis_size(axis).bit_length() - 1)]

    over_basin, over_chain = distances("basin"), distances("chain")
    n = len(over_basin)
    orders = over_basin + over_chain, over_chain[:n] + over_basin + over_chain[n:]
    stages = list(zip(*orders, strict=True)), list(zip(*orders[::-1], strict=True))
    returned = {}
    sums = {}

    def back(layer, outs, after):
        returned[layer] = backward(outs[6:])
        grad, whole = call(
            functools.partial(back_kernel, layer, grad_scale),
            [((rows, latent), F32), ((grad_rows, LANES), F32)],
            [outs[1], inputs[layer], local_t, *weights, *outs[2:6]],
            3 * rows * ffn + 2 * rows * rows * latent,
            scratch=[
                pltpu.VMEM((rows, latent), BF16),
                pltpu.VMEM((rows, half), BF16),
                pltpu.VMEM((rows, half), BF16),
            ],
            name=f"back{layer}",
            after=after,
        )
        sums[layer] = Sum(whole, stages[layer % 2])
        return [outs[0], grad], [grad]

    def join(layer, state, after):
        if layer:
            return call(
                functools.partial(join_kernel, layer - 1, groups, pairs),
                bwd_outs,
                [*state, spread, remote_t, totals[layer - 1]]
                + [*weights, *returned[layer], *mine[layer - 1], *others[layer - 1]],
                2 * far_rows * ffn,
                name=f"join{layer}",
                after=after,
            )
        return call(
            last_kernel,
            [((rows, latent), F32), ((8, LANES), F32)],
            [*state, spread, *returned[layer]],
            2 * rows * far_rows * latent,
            name="join0",
            after=after,
        )

    def write(layer, written, after):
        ready = [sums[layer].own, sums[layer].got[0]]
        kept = [*written, *after]
        return pl.pallas_call(
            functools.partial(
                write_kernel, layer, stages[layer % 2][0], len(kept), sums[layer].got[1]
            ),
            out_shape=[
                jax.ShapeDtypeStruct((layers, latent, half), F32),
                jax.ShapeDtypeStruct((layers, half, latent), F32),
                jax.ShapeDtypeStruct((8, LANES), F32),
            ],
            in_specs=[ANY] * len(kept) + [VMEM] * len(ready),
            out_specs=[ANY] * 2 + [VMEM],
            scratch_shapes=[
                pltpu.VMEM((grad_rows, LANES), F32),
                pltpu.VMEM((latent, half), F32),
                pltpu.VMEM((half, latent), F32),
                pltpu.SemaphoreType.DMA((2,)),
            ],
            input_output_aliases={i: i for i in range(len(written))},
            compiler_params=pltpu.CompilerParams(vmem_limit_bytes=LIMIT),
            cost_estimate=pl.CostEstimate(flops=1, bytes_accessed=1, transcendentals=0),
            name=f"write{layer}",
        )(*written, *after, *ready)

    count = 2 * len(stages[0]) - 1
    at = []
    for layer in reversed(range(layers)):
        state, at = back(layer, outs, at)
        if layer:
            at = [*at, *returned[layer]]
            at = sum_step([sums[above] for above in range(layer, layers)], at)
            outs = join(layer, state, at)
            at = outs[1:2]
    grad = None
    while sums[0].done < count:
        ready = [sums[0]]
        if layers > 1 and sums[1].done < count and sums[1].next()[1] == sums[0].next()[1]:
            ready.append(sums[1])
        if sums[0].done == len(stages[0]):
            at = at + [sums[above].got[0] for above in range(2, layers)]
        at = sum_step(ready, at)
        if grad is None and sums[0].done == len(stages[0]) + 1:
            grad, token = join(0, state, at)
            at = [token]
        for layer in range(1, layers)[:: 1 if sums[0].done < len(stages[0]) else -1]:
            if sums[layer] not in ready and sums[layer].done < count:
                at = sum_step([sums[layer]], at)
    written = []
    for layer in reversed(range(layers)):
        *written, token = write(layer, written, at)
        at = [token]
    return (grad, *written)


def solution(mesh):
    placed = (
        P(("runs", "chain", "basin"), None),
        P(("runs", "chain", "basin"), None),
        P(None, None, "feat"),
        P(None, "feat", None),
        P(("chain", "basin"), None),
        P(("chain", "basin"), None, None, None),
        P(("chain", "basin"), None, None),
        P(("chain", "basin"), None),
    )
    return jax.shard_map(
        shards,
        mesh=mesh,
        in_specs=placed,
        out_specs=(
            P(("runs", "chain", "basin"), None),
            P("runs", None, "feat"),
            P("runs", "feat", None),
        ),
        check_vma=False,
    )
```

```python
import functools

import jax
import jax.numpy as jnp
from jax import lax
from jax.experimental import pallas as pl
from jax.experimental.pallas import tpu as pltpu
from jax.sharding import PartitionSpec as P

BLOCK = 128
LANES = 128
EPS = 1e-06
F32 = jnp.float32
BF16 = jnp.bfloat16
VMEM = pl.BlockSpec(memory_space=pltpu.VMEM)
SMEM = pl.BlockSpec(memory_space=pltpu.SMEM)
ANY = pl.BlockSpec(memory_space=pl.ANY)
NN = (((1,), (0,)), ((), ()))
NT = (((1,), (1,)), ((), ()))
TN = (((0,), (0,)), ((), ()))


def mm(a, b, dims=NN):
    return lax.dot_general(a, b, dims, preferred_element_type=F32)


LIMIT = 24 * 1024 * 1024


def call(body, outs, ins, flops, scratch=(), name=None, after=(), bytes_accessed=4_000_000, scalars=None):
    skipped = len(after)
    return pl.pallas_call(
        lambda *refs: body(*refs[skipped:]),
        out_shape=[jax.ShapeDtypeStruct(s, d) for s, d in outs],
        in_specs=[ANY] * skipped + [SMEM if x is scalars else VMEM for x in ins],
        out_specs=[VMEM] * len(outs),
        scratch_shapes=list(scratch),
        compiler_params=pltpu.CompilerParams(vmem_limit_bytes=LIMIT),
        cost_estimate=pl.CostEstimate(
            flops=flops, bytes_accessed=bytes_accessed, transcendentals=0
        ),
        name=name,
    )(*after, *ins)


def sigmoid(v):
    return 1.0 / (1.0 + jnp.exp(-v))


def message_of(x, halves):
    total = None
    for w_in, w_out in halves:
        pre = mm(x, w_in)
        part = mm((pre * sigmoid(pre)).astype(BF16), w_out)
        total = part if total is None else total + part
    return total.astype(BF16)


def message_grad(x, dmsg, halves):
    total = None
    kept = None
    for w_in, w_out in halves:
        pre = mm(x, w_in)
        sig = sigmoid(pre)
        dact = mm(dmsg, w_out, NT)
        dpre = (dact * (sig * (1.0 + pre * (1.0 - sig)))).astype(BF16)
        if kept is None:
            kept = ((pre * sig).astype(BF16), dpre)
        part = mm(dpre, w_in, NT)
        total = part if total is None else total + part
    return total, kept


def normed_of(total):
    scale = lax.rsqrt(jnp.mean(total * total, axis=-1, keepdims=True) + EPS)
    return scale, scale * total


def norm_grad(grad, total):
    scale, normed = normed_of(total)
    return scale * (grad - normed * jnp.mean(grad * normed, axis=-1, keepdims=True))


def setup_kernel(groups, pairs, features, sent, *refs):
    pick, spread, pick_self, held = refs[:4]
    sends = refs[4:]
    rows = features.shape[0]
    held[...] = features[...]
    b, feat = lax.axis_index("basin"), lax.axis_index("feat")
    for route in range(-1, 2 * pairs):
        if route == 0:
            chosen = lax.broadcasted_iota(jnp.int32, (1, BLOCK), 1) + (rows - BLOCK)
        elif route >= groups:
            chosen = jnp.full((1, BLOCK), -1, jnp.int32)
        else:
            chosen = sent[pl.ds(lax.rem(b + max(route, 0), groups), 1), :]
        across = jnp.broadcast_to(chosen, (BLOCK, BLOCK))
        down = across.T
        for r in range(0, rows, BLOCK):
            at = lax.broadcasted_iota(jnp.int32, (BLOCK, BLOCK), 1) + r
            hot = (down == at).astype(F32).astype(BF16)
            if route < 0:
                pick_self[:, r : r + BLOCK] = hot
                continue

            @pl.when(route % 2 == feat)
            def _():
                pick[route // 2 * BLOCK : (route // 2 + 1) * BLOCK, r : r + BLOCK] = hot

            at = lax.broadcasted_iota(jnp.int32, (BLOCK, BLOCK), 0) + r
            if route < groups:
                spread[r : r + BLOCK, route * BLOCK : (route + 1) * BLOCK] = (
                    (across == at).astype(F32).astype(BF16)
                )
    for i, send in enumerate(sends):
        send[...] = mm(pick[i * BLOCK : (i + 1) * BLOCK, :], features[...]).astype(BF16)


def adjacency_kernel(groups, sources, values, pick_self, _, *refs):
    local, local_t, remote, remote_t, acc = refs
    rows = local.shape[0]
    own = rows // BLOCK
    b = lax.axis_index("basin")
    acc[...] = jnp.zeros_like(acc)
    for k in range(own):
        for t in range(values.shape[1]):
            v = sources[t, k]
            route = jnp.where(v == own, 0, lax.rem(b + groups - (v - own - 1), groups))
            far = jnp.where((v > own) & (route == 0), own, own + 1 + route)
            at = jnp.where(v < own, v, far)
            here = (pl.ds(k * BLOCK, BLOCK), pl.ds(pl.multiple_of(at * BLOCK, BLOCK), BLOCK))
            acc[here] += values[k, t].astype(F32)
    mine = acc[:, rows : rows + BLOCK].astype(BF16)
    full = acc[:, :rows] + mm(mine, pick_self[...])
    local[...] = full.astype(BF16)
    local_t[...] = full.T.astype(BF16)
    far = acc[:, rows + BLOCK :]
    remote[...] = far.astype(BF16)
    remote_t[...] = far.T.astype(BF16)


def own_messages(layer, inputs, weights, msg):
    wi0, wi1, wo0, wo1 = weights
    halves = [(wi0[layer], wo0[layer]), (wi1[layer], wo1[layer])]
    for r in range(0, inputs.shape[0], 256):
        msg[r : r + 256, :] = message_of(inputs[r : r + 256, :], halves)


def local_kernel(layer, *refs):
    own_messages(layer, refs[0], refs[1:5], refs[5])


def remote_mixed(layer, received, remote, feat, weights):
    wi0, wi1, wo0, wo1 = weights
    halves = [(wi0[layer], wo0[layer]), (wi1[layer], wo1[layer])]
    total = None
    for i, block in enumerate(received):
        route = jnp.minimum(2 * i + feat, remote.shape[1] // BLOCK - 1)
        columns = remote[:, pl.ds(pl.multiple_of(route * BLOCK, BLOCK), BLOCK)]
        part = mm(columns, message_of(block[...], halves))
        total = part if total is None else total + part
    return total


def part_kernel(layer, pairs, *refs):
    local, msg, remote = refs[:3]
    weights, received, mixed = refs[3:7], refs[7 : 7 + pairs], refs[-1]
    mixed[...] = mm(local[...], msg[...]) + remote_mixed(
        layer, received, remote, lax.axis_index("feat"), weights
    )


def mixed_total(layer, state, mixed, received, remote, weights):
    return state + mixed[...] + remote_mixed(
        layer, received, remote, 1 - lax.axis_index("feat"), weights
    )


def mix_kernel(layer, pairs, *refs):
    prev, mixed, remote, pick = refs[:4]
    weights = refs[4:8]
    received = refs[8 : 8 + pairs]
    total, inputs = refs[8 + pairs : 10 + pairs]
    sends = refs[10 + pairs :]
    state = prev[...].astype(F32) if layer == 0 else normed_of(prev[...])[1]
    total[...] = mixed_total(layer, state, mixed, received, remote, weights)
    new = normed_of(total[...])[1].astype(BF16)
    inputs[...] = new
    for i, send in enumerate(sends):
        send[...] = mm(pick[i * BLOCK : (i + 1) * BLOCK, :], new).astype(BF16)


def start_bwd(layer, groups, dtotal_now, weights, mine, others, remote_t, outs):
    dtotal, dround, far_x, far_dmsg, far_act, far_dpre = outs[:6]
    backs = outs[6:]
    wi0, wi1, wo0, wo1 = weights
    halves = [(wi0[layer], wo0[layer]), (wi1[layer], wo1[layer])]
    dtotal[...] = dtotal_now
    dround[...] = dtotal_now.astype(BF16)
    for first in range(2):

        @pl.when(lax.axis_index("feat") == first)
        def _():
            for route in range(groups):
                block = (mine, others)[(route + first) % 2][route // 2]
                far_x[route * BLOCK : (route + 1) * BLOCK, :] = block[...]

    dmsg = mm(remote_t[...], dround[...]).astype(BF16)
    back, (act, dpre) = message_grad(far_x[...], dmsg, halves)
    far_dmsg[...] = dmsg
    far_act[...] = act
    far_dpre[...] = dpre
    for i, out in enumerate(backs):
        out[...] = back[i * BLOCK : (i + 1) * BLOCK, :].astype(BF16)


def turn_kernel(layer, groups, pairs, *refs):
    prev, mixed, remote, remote_t, cot = refs[:5]
    weights = refs[5:9]
    mine, others = refs[9 : 9 + pairs], refs[9 + pairs : 9 + 2 * pairs]
    outs = refs[9 + 2 * pairs :]
    state = normed_of(prev[...])[1]
    total = mixed_total(layer, state, mixed, others, remote, weights)
    dtotal = norm_grad(cot[...], total)
    start_bwd(layer, groups, dtotal, weights, mine, others, remote_t, outs)


def back_kernel(layer, grad_scale, *refs):
    dround, inputs, local_t = refs[:3]
    wi0, wi1, wo0, wo1 = refs[3:7]
    far_x, far_dmsg, far_act, far_dpre = refs[7:11]
    back, grads, dmsg, act, dpre = refs[11:]
    halves = [(wi0[layer], wo0[layer]), (wi1[layer], wo1[layer])]
    dmsg[...] = mm(local_t[...], dround[...]).astype(BF16)
    for r in range(0, inputs.shape[0], 256):
        here = slice(r, r + 256)
        back[here, :], (act[here, :], dpre[here, :]) = message_grad(
            inputs[here, :], dmsg[here, :], halves
        )
    latent, hidden = inputs.shape[1], act.shape[1]
    g_in = (mm(inputs[...], dpre[...], TN) + mm(far_x[...], far_dpre[...], TN)) * grad_scale
    for j in range(hidden // LANES):
        grads[j * latent : (j + 1) * latent, :] = g_in[:, j * LANES : (j + 1) * LANES]
    g_out = (mm(act[...], dmsg[...], TN) + mm(far_act[...], far_dmsg[...], TN)) * grad_scale
    for j in range(latent // LANES):
        at = hidden // LANES * latent + j * hidden
        grads[at : at + hidden, :] = g_out[:, j * LANES : (j + 1) * LANES]


def upper(stage):
    (axis0, d0), (axis1, d1) = stage
    bit0 = lax.rem(lax.axis_index(axis0) // d0, 2)
    bit1 = lax.rem(lax.axis_index(axis1) // d1, 2)
    return jnp.where(lax.axis_index("feat") == 0, bit0, bit1)


def place(stage, own, got, out):
    m = own.shape[0]
    bit = upper(stage)
    out[pl.ds(pl.multiple_of(bit * m, m), m), :] = own[...].astype(out.dtype)
    out[pl.ds(pl.multiple_of((1 - bit) * m, m), m), :] = got[...].astype(out.dtype)


def sum_kernel(steps, *refs):
    n_in = sum(1 + (kind != "split") for kind, *_ in steps)
    n_out = len(steps) + 1 + max(group for *_, group, _ in steps)
    ins, outs, accs = refs[:n_in], refs[n_in : n_in + n_out], refs[n_in + n_out :]
    sends = outs[len(steps) :]
    for (kind, stage, back, at, group, to), out in zip(steps, outs):
        own, ins = ins[0], ins[1:]
        m = own.shape[0]
        send = sends[group].at[to : to + out.shape[0]]
        if kind != "split":
            got, ins = ins[0].at[at : at + m], ins[1:]
        if kind in ("split", "add_split"):
            if kind == "add_split":
                acc, accs = accs[0], accs[1:]
                acc[...] = own[...] + got[...].astype(F32)
                own = acc
            m = m // 2
            bit = upper(stage)
            out[...] = own[pl.ds(pl.multiple_of(bit * m, m), m), :]
            send[...] = own[pl.ds(pl.multiple_of((1 - bit) * m, m), m), :].astype(BF16)
        else:
            if kind == "place":
                place(back, own, got, out)
            else:
                out[...] = (own[...] + got[...].astype(F32)).astype(out.dtype)
            send[...] = out[...].astype(BF16)


def write_kernel(layer, stage, kept, at, *refs):
    out_in, out_out, token, grads, slab_in, slab_out, sem = refs[-7:]
    token[...] = jnp.zeros_like(token)
    own = refs[kept]
    place(stage, own, refs[kept + 1].at[at : at + own.shape[0]], grads)
    latent, hidden = slab_in.shape
    for j in range(hidden // LANES):
        slab_in[:, j * LANES : (j + 1) * LANES] = grads[j * latent : (j + 1) * latent, :]
    first = pltpu.make_async_copy(slab_in, out_in.at[layer], sem.at[0])
    first.start()
    for j in range(latent // LANES):
        at = hidden // LANES * latent + j * hidden
        slab_out[:, j * LANES : (j + 1) * LANES] = grads[at : at + hidden, :]
    second = pltpu.make_async_copy(slab_out, out_out.at[layer], sem.at[1])
    second.start()
    first.wait()
    second.wait()


class Sum:
    def __init__(self, whole, stages):
        self.own, self.got, self.stages, self.done = whole, None, stages, 0

    def next(self):
        n, i, rows = len(self.stages), self.done, self.own.shape[0]
        if i < n - 1:
            return "add_split" if i else "split", self.stages[i], None, rows // 2, F32
        if i == n - 1:
            return "add", self.stages[i], None, rows, F32
        stage = self.stages[2 * n - 2 - i]
        if i == n:
            return "add", stage, None, rows, BF16
        return "place", stage, self.stages[2 * n - 1 - i], rows * 2, BF16


def sum_step(sums, after):
    steps, ins, outs, scratch, groups = [], [], [], [], {}
    for one in sums:
        kind, stage, back, rows, dtype = one.next()
        group = groups.setdefault(stage, [len(groups), 0])
        steps.append((kind, stage, back, one.got and one.got[1], *group))
        group[1] += rows
        ins += [one.own, one.got[0]] if one.got else [one.own]
        outs.append(((rows, LANES), dtype))
        if kind == "add_split":
            scratch.append(pltpu.VMEM(one.own.shape, F32))
    made = call(
        functools.partial(sum_kernel, steps),
        outs + [((rows, LANES), BF16) for _, rows in groups.values()],
        ins,
        1,
        bytes_accessed=1,
        scratch=scratch,
        name="sum",
        after=after,
    )
    arrived = [swapped(x, stage) for x, stage in zip(made[len(sums) :], groups)]
    for one, own, (*_, group, at) in zip(sums, made, steps):
        one.own, one.got = own, (arrived[group], at)
        one.done += 1
    return [made[0]]


def gathered_grad(dtotal, back, returned, spread):
    far = jnp.concatenate([x[...] for x in returned], axis=0)
    return dtotal[...] + back[...] + mm(spread[...], far)


def join_kernel(layer, groups, pairs, *refs):
    dtotal, back, spread, remote_t, total = refs[:5]
    weights, refs = refs[5:9], refs[9:]
    returned, refs = refs[:groups], refs[groups:]
    mine, others, outs = refs[:pairs], refs[pairs : 2 * pairs], refs[2 * pairs :]
    grad = gathered_grad(dtotal, back, returned, spread)
    dtotal = norm_grad(grad, total[...])
    start_bwd(layer, groups, dtotal, weights, mine, others, remote_t, outs)


def last_kernel(*refs):
    dtotal, back, spread = refs[:3]
    refs[-2][...] = gathered_grad(dtotal, back, refs[3:-2], spread)
    refs[-1][...] = jnp.zeros_like(refs[-1])


def around(x, axis, distance):
    n = lax.axis_size(axis)
    return lax.ppermute(x, axis, [(i, (i + distance) % n) for i in range(n)])


def over_mesh(x, target):
    chain, groups, cores = (lax.axis_size(axis) for axis in ("chain", "basin", "feat"))
    perm = []
    for c in range(chain):
        for b in range(groups):
            for feat in range(cores):
                to = target(c, b, feat)
                if to is not None:
                    start, end = (c * groups + b) * cores + feat, (to[0] * groups + to[1]) * cores
                    perm.append((start, end + feat))
    return lax.ppermute(x, ("chain", "basin", "feat"), perm)


def swapped(x, stage):
    def partner(c, b, feat):
        axis, d = stage[feat]
        return (c ^ d, b) if axis == "chain" else (c, b ^ d)

    return over_mesh(x, partner)


def forward(sends):
    def target(i, c, b, feat):
        route = 2 * i + feat
        if route == 0:
            return (c + 1, b) if c + 1 < lax.axis_size("chain") else None
        groups = lax.axis_size("basin")
        return (c, (b + route) % groups) if route < groups else None

    return [over_mesh(x, functools.partial(target, i)) for i, x in enumerate(sends)]


def backward(grads):
    chain = lax.axis_size("chain")
    up = lax.ppermute(grads[0], "chain", [(c, c - 1) for c in range(1, chain)])
    return [up] + [around(x, "basin", -s) for s, x in enumerate(grads) if s]


def other_core(got):
    return [around(x, "feat", 1) for x in got]


def shards(features, cotangent, w_in, w_out, block_index, block_values, send_rows, send_count):
    rows, latent = features.shape
    groups = lax.axis_size("basin")
    pairs = (groups + 1) // 2
    layers, _, half = w_in.shape
    far_rows = groups * BLOCK
    own = rows // BLOCK
    grad_scale = float(rows * lax.axis_size("chain") * groups) ** (-0.5)
    last = layers - 1

    def act16(n, m=latent):
        return ((n, m), BF16)

    wi1 = around(w_in, "feat", 1)
    wo1 = around(w_out, "feat", 1)
    ffn = 4 * latent * 2 * half

    live = jnp.arange(BLOCK, dtype=jnp.int32)[None, :] < send_count[0][:, None]
    sent = jnp.where(live, send_rows[0], -1)
    sources = block_index.T
    pick, spread, pick_self, features, *sends = call(
        functools.partial(setup_kernel, groups, pairs),
        [act16(pairs * BLOCK, rows), act16(rows, far_rows), act16(BLOCK, rows), act16(rows)]
        + [act16(BLOCK)] * pairs,
        [features, sent],
        2 * rows * far_rows * latent,
        name="setup",
    )
    weights = (w_in, wi1, w_out, wo1)
    inputs = [features]
    totals = []
    mine = []
    others = []
    for layer in range(layers):
        mine.append(forward(sends))
        (msg,) = call(
            functools.partial(local_kernel, layer),
            [act16(rows)],
            [inputs[layer], *weights],
            rows * ffn,
            name=f"local{layer}",
        )
        if layer == 0:
            local, local_t, remote, remote_t = call(
                functools.partial(adjacency_kernel, groups),
                [act16(rows, rows), act16(rows, rows), act16(rows, far_rows), act16(far_rows, rows)],
                [sources, block_values, pick_self, msg],
                2 * rows * rows * BLOCK,
                scratch=[pltpu.VMEM((rows, rows + BLOCK + far_rows), F32)],
                name="adjacency",
                scalars=sources,
            )
            mine[0], local = lax.optimization_barrier((mine[0], local))
        mine[layer], msg = lax.optimization_barrier((mine[layer], msg))
        others.append(other_core(mine[layer]))
        (mixed,) = call(
            functools.partial(part_kernel, layer, pairs),
            [((rows, latent), F32)],
            [local, msg, remote, *weights, *mine[layer]],
            2 * rows * rows * latent,
            name=f"part{layer}",
        )
        prev = totals[-1] if layer else features
        if layer < last:
            total, new, *sends = call(
                functools.partial(mix_kernel, layer, pairs),
                [((rows, latent), F32), act16(rows)] + [act16(BLOCK)] * pairs,
                [prev, mixed, remote, pick, *weights, *others[layer]],
                far_rows * ffn + 2 * rows * far_rows * latent,
                name=f"mix{layer}",
            )
            totals.append(total)
            inputs.append(new)
    bwd_outs = (
        [((rows, latent), F32), act16(rows), act16(far_rows), act16(far_rows)]
        + [act16(far_rows, half)] * 2
        + [act16(BLOCK)] * groups
    )
    outs = call(
        functools.partial(turn_kernel, last, groups, pairs),
        bwd_outs,
        [totals[-1], mixed, remote, remote_t, cotangent, *weights, *mine[last], *others[last]],
        2 * far_rows * ffn,
        name="turn",
    )
    grad_rows = 2 * latent * half // LANES

    def distances(axis):
        return [(axis, 1 << i) for i in range(lax.axis_size(axis).bit_length() - 1)]

    over_basin, over_chain = distances("basin"), distances("chain")
    n = len(over_basin)
    orders = over_basin + over_chain, over_chain[:n] + over_basin + over_chain[n:]
    stages = list(zip(*orders, strict=True))
    returned = {}
    sums = {}

    def back(layer, outs, after):
        returned[layer] = backward(outs[6:])
        grad, whole = call(
            functools.partial(back_kernel, layer, grad_scale),
            [((rows, latent), F32), ((grad_rows, LANES), F32)],
            [outs[1], inputs[layer], local_t, *weights, *outs[2:6]],
            3 * rows * ffn + 2 * rows * rows * latent,
            scratch=[
                pltpu.VMEM((rows, latent), BF16),
                pltpu.VMEM((rows, half), BF16),
                pltpu.VMEM((rows, half), BF16),
            ],
            name=f"back{layer}",
            after=after,
        )
        sums[layer] = Sum(whole, stages)
        return [outs[0], grad], [grad]

    def join(layer, state, after):
        if layer:
            return call(
                functools.partial(join_kernel, layer - 1, groups, pairs),
                bwd_outs,
                [*state, spread, remote_t, totals[layer - 1]]
                + [*weights, *returned[layer], *mine[layer - 1], *others[layer - 1]],
                2 * far_rows * ffn,
                name=f"join{layer}",
                after=after,
            )
        return call(
            last_kernel,
            [((rows, latent), F32), ((8, LANES), F32)],
            [*state, spread, *returned[layer]],
            2 * rows * far_rows * latent,
            name="join0",
            after=after,
        )

    def write(layer, written, after):
        ready = [sums[layer].own, sums[layer].got[0]]
        kept = [*written, *after]
        return pl.pallas_call(
            functools.partial(
                write_kernel, layer, stages[0], len(kept), sums[layer].got[1]
            ),
            out_shape=[
                jax.ShapeDtypeStruct((layers, latent, half), F32),
                jax.ShapeDtypeStruct((layers, half, latent), F32),
                jax.ShapeDtypeStruct((8, LANES), F32),
            ],
            in_specs=[ANY] * len(kept) + [VMEM] * len(ready),
            out_specs=[ANY] * 2 + [VMEM],
            scratch_shapes=[
                pltpu.VMEM((grad_rows, LANES), F32),
                pltpu.VMEM((latent, half), F32),
                pltpu.VMEM((half, latent), F32),
                pltpu.SemaphoreType.DMA((2,)),
            ],
            input_output_aliases={i: i for i in range(len(written))},
            compiler_params=pltpu.CompilerParams(vmem_limit_bytes=LIMIT),
            cost_estimate=pl.CostEstimate(flops=1, bytes_accessed=1, transcendentals=0),
            name=f"write{layer}",
        )(*written, *after, *ready)

    count = 2 * len(stages) - 1
    at = []
    for layer in reversed(range(layers)):
        state, at = back(layer, outs, at)
        arrived = [sums[above].got[0] for above in range(layer + 2, layers)]
        at = sum_step([sums[layer]], at + returned[layer] + arrived)
        if layer:
            for above in range(layer + 1, layers):
                at = sum_step([sums[above]], at)
            outs = join(layer, state, at)
            at = outs[1:2]
    for layer in reversed(range(1, layers)):
        at = sum_step([sums[layer]], at)
    grad, token = join(0, state, at)
    at = sum_step([sums[0]], [token])
    while sums[0].done < count:
        for layer in reversed(range(layers)):
            if sums[layer].done < count:
                if layer == 0 and sums[0].done == count - 1:
                    at = at + [sums[above].got[0] for above in range(2, layers)]
                at = sum_step([sums[layer]], at)
    written = []
    for layer in reversed(range(layers)):
        *written, token = write(layer, written, at)
        at = [token]
    return (grad, *written)


def solution(mesh):
    placed = (
        P(("runs", "chain", "basin"), None),
        P(("runs", "chain", "basin"), None),
        P(None, None, "feat"),
        P(None, "feat", None),
        P(("chain", "basin"), None),
        P(("chain", "basin"), None, None, None),
        P(("chain", "basin"), None, None),
        P(("chain", "basin"), None),
    )
    return jax.shard_map(
        shards,
        mesh=mesh,
        in_specs=placed,
        out_specs=(
            P(("runs", "chain", "basin"), None),
            P("runs", None, "feat"),
            P("runs", "feat", None),
        ),
        check_vma=False,
    )
```

```python
import functools

import jax
import jax.numpy as jnp
from jax import lax
from jax.experimental import pallas as pl
from jax.experimental.pallas import tpu as pltpu
from jax.sharding import PartitionSpec as P

BLOCK = 128
LANES = 128
EPS = 1e-06
F32 = jnp.float32
BF16 = jnp.bfloat16
VMEM = pl.BlockSpec(memory_space=pltpu.VMEM)
SMEM = pl.BlockSpec(memory_space=pltpu.SMEM)
ANY = pl.BlockSpec(memory_space=pl.ANY)
NN = (((1,), (0,)), ((), ()))
NT = (((1,), (1,)), ((), ()))
TN = (((0,), (0,)), ((), ()))


def mm(a, b, dims=NN):
    return lax.dot_general(a, b, dims, preferred_element_type=F32)


LIMIT = 24 * 1024 * 1024


def call(body, outs, ins, flops, scratch=(), name=None, after=(), bytes_accessed=4_000_000, scalars=None):
    skipped = len(after)
    return pl.pallas_call(
        lambda *refs: body(*refs[skipped:]),
        out_shape=[jax.ShapeDtypeStruct(s, d) for s, d in outs],
        in_specs=[ANY] * skipped + [SMEM if x is scalars else VMEM for x in ins],
        out_specs=[VMEM] * len(outs),
        scratch_shapes=list(scratch),
        compiler_params=pltpu.CompilerParams(vmem_limit_bytes=LIMIT),
        cost_estimate=pl.CostEstimate(
            flops=flops, bytes_accessed=bytes_accessed, transcendentals=0
        ),
        name=name,
    )(*after, *ins)


def sigmoid(v):
    return 1.0 / (1.0 + jnp.exp(-v))


def half_message(x, w_in, w_out):
    pre = mm(x, w_in)
    return mm((pre * sigmoid(pre)).astype(BF16), w_out)


def message_of(x, halves):
    total = None
    for w_in, w_out in halves:
        part = half_message(x, w_in, w_out)
        total = part if total is None else total + part
    return total.astype(BF16)


def message_grad(x, dmsg, halves):
    total = None
    kept = None
    for w_in, w_out in halves:
        pre = mm(x, w_in)
        sig = sigmoid(pre)
        dact = mm(dmsg, w_out, NT)
        dpre = (dact * (sig * (1.0 + pre * (1.0 - sig)))).astype(BF16)
        if kept is None:
            kept = ((pre * sig).astype(BF16), dpre)
        part = mm(dpre, w_in, NT)
        total = part if total is None else total + part
    return total, kept


def normed_of(total):
    scale = lax.rsqrt(jnp.mean(total * total, axis=-1, keepdims=True) + EPS)
    return scale, scale * total


def norm_grad(grad, total):
    scale, normed = normed_of(total)
    return scale * (grad - normed * jnp.mean(grad * normed, axis=-1, keepdims=True))


def setup_kernel(groups, features, sent, *refs):
    pick, spread, pick_self, held = refs[:4]
    sends = refs[4:]
    rows = features.shape[0]
    held[...] = features[...]
    b = lax.axis_index("basin")
    for route in range(-1, groups):
        if route == 0:
            chosen = lax.broadcasted_iota(jnp.int32, (1, BLOCK), 1) + (rows - BLOCK)
        else:
            chosen = sent[pl.ds(lax.rem(b + max(route, 0), groups), 1), :]
        across = jnp.broadcast_to(chosen, (BLOCK, BLOCK))
        down = across.T
        for r in range(0, rows, BLOCK):
            at = lax.broadcasted_iota(jnp.int32, (BLOCK, BLOCK), 1) + r
            hot = (down == at).astype(F32).astype(BF16)
            if route < 0:
                pick_self[:, r : r + BLOCK] = hot
                continue
            if route > 0:
                pick[(route - 1) * BLOCK : route * BLOCK, r : r + BLOCK] = hot
            at = lax.broadcasted_iota(jnp.int32, (BLOCK, BLOCK), 0) + r
            spread[r : r + BLOCK, route * BLOCK : (route + 1) * BLOCK] = (
                (across == at).astype(F32).astype(BF16)
            )
    pick_sends(features[...], pick, sends)


def pick_sends(rows, pick, sends):
    sends[0][...] = rows[rows.shape[0] - BLOCK :, :]
    for s, send in enumerate(sends[1:]):
        send[...] = mm(pick[s * BLOCK : (s + 1) * BLOCK, :], rows).astype(BF16)


def adjacency_kernel(groups, sources, values, pick_self, _, *refs):
    local, local_t, remote, remote_t, acc = refs
    rows = local.shape[0]
    own = rows // BLOCK
    b = lax.axis_index("basin")
    acc[...] = jnp.zeros_like(acc)
    for k in range(own):
        for t in range(values.shape[1]):
            v = sources[t, k]
            route = jnp.where(v == own, 0, lax.rem(b + groups - (v - own - 1), groups))
            far = jnp.where((v > own) & (route == 0), own, own + 1 + route)
            at = jnp.where(v < own, v, far)
            here = (pl.ds(k * BLOCK, BLOCK), pl.ds(pl.multiple_of(at * BLOCK, BLOCK), BLOCK))
            acc[here] += values[k, t].astype(F32)
    mine = acc[:, rows : rows + BLOCK].astype(BF16)
    full = acc[:, :rows] + mm(mine, pick_self[...])
    local[...] = full.astype(BF16)
    local_t[...] = full.T.astype(BF16)
    far = acc[:, rows + BLOCK :]
    remote[...] = far.astype(BF16)
    remote_t[...] = far.T.astype(BF16)


def own_messages(layer, inputs, weights, msg):
    wi0, wi1, wo0, wo1 = weights
    halves = [(wi0[layer], wo0[layer]), (wi1[layer], wo1[layer])]
    for r in range(0, inputs.shape[0], 256):
        msg[r : r + 256, :] = message_of(inputs[r : r + 256, :], halves)


def local_kernel(layer, *refs):
    own_messages(layer, refs[0], refs[1:5], refs[5])


def half_kernel(x, w_in, w_out, part):
    for r in range(0, x.shape[0], 256):
        here = slice(r, r + 256)
        part[here, :] = half_message(x[here, :], w_in[0], w_out[0])


def other_half_kernel(x, w_in, w_out, part, msg):
    for r in range(0, x.shape[0], 256):
        here = slice(r, r + 256)
        msg[here, :] = (part[here, :] + half_message(x[here, :], w_in[0], w_out[0])).astype(BF16)


def remote_mixed(layer, received, columns, weights):
    wi0, wi1, wo0, wo1 = weights
    halves = [(wi0[layer], wo0[layer]), (wi1[layer], wo1[layer])]
    far = jnp.concatenate([x[...] for x in received], axis=0)
    return mm(columns, message_of(far, halves))


def part_kernel(layer, *refs):
    local, msg, remote = refs[:3]
    weights, received, mixed = refs[3:7], refs[7:-1], refs[-1]
    total = mm(local[...], msg[...])
    if received:
        total = total + remote_mixed(layer, received, remote[:, BLOCK:], weights)
    mixed[...] = total


def upstream_rows(got, swapped_got):
    return got[...] + swapped_got[...]


def mixed_total(layer, state, mixed, up, remote, weights):
    return state + mixed[...] + remote_mixed(layer, [up], remote[:, :BLOCK], weights)


def mix_kernel(layer, *refs):
    prev, mixed, remote, pick = refs[:4]
    weights, up = refs[4:8], upstream_rows(*refs[8:10])
    total, inputs = refs[10:12]
    state = prev[...].astype(F32) if layer == 0 else normed_of(prev[...])[1]
    total[...] = mixed_total(layer, state, mixed, up, remote, weights)
    new = normed_of(total[...])[1].astype(BF16)
    inputs[...] = new
    pick_sends(new, pick, refs[12:])


def start_bwd(layer, dtotal_now, weights, received, remote_t, outs):
    dtotal, dround, far_x, far_dmsg, far_act, far_dpre = outs[:6]
    backs = outs[6:]
    wi0, wi1, wo0, wo1 = weights
    halves = [(wi0[layer], wo0[layer]), (wi1[layer], wo1[layer])]
    dtotal[...] = dtotal_now
    dround[...] = dtotal_now.astype(BF16)
    far_x[:BLOCK, :] = upstream_rows(*received[:2])
    for i, block in enumerate(received[2:]):
        far_x[(i + 1) * BLOCK : (i + 2) * BLOCK, :] = block[...]
    dmsg = mm(remote_t[...], dround[...]).astype(BF16)
    back, (act, dpre) = message_grad(far_x[...], dmsg, halves)
    far_dmsg[...] = dmsg
    far_act[...] = act
    far_dpre[...] = dpre
    for i, out in enumerate(backs):
        out[...] = back[i * BLOCK : (i + 1) * BLOCK, :].astype(BF16)


def turn_kernel(layer, groups, *refs):
    prev, mixed, remote, remote_t, cot = refs[:5]
    weights, received, outs = refs[5:9], refs[9 : 10 + groups], refs[10 + groups :]
    state = normed_of(prev[...])[1]
    total = mixed_total(layer, state, mixed, upstream_rows(*received[:2]), remote, weights)
    start_bwd(layer, norm_grad(cot[...], total), weights, received, remote_t, outs)


def back_kernel(layer, grad_scale, *refs):
    dround, inputs, local_t = refs[:3]
    wi0, wi1, wo0, wo1 = refs[3:7]
    far_x, far_dmsg, far_act, far_dpre = refs[7:11]
    back, grads, dmsg, act, dpre = refs[11:]
    halves = [(wi0[layer], wo0[layer]), (wi1[layer], wo1[layer])]
    dmsg[...] = mm(local_t[...], dround[...]).astype(BF16)
    for r in range(0, inputs.shape[0], 256):
        here = slice(r, r + 256)
        back[here, :], (act[here, :], dpre[here, :]) = message_grad(
            inputs[here, :], dmsg[here, :], halves
        )
    latent, hidden = inputs.shape[1], act.shape[1]
    g_in = (mm(inputs[...], dpre[...], TN) + mm(far_x[...], far_dpre[...], TN)) * grad_scale
    for j in range(hidden // LANES):
        grads[j * latent : (j + 1) * latent, :] = g_in[:, j * LANES : (j + 1) * LANES]
    g_out = (mm(act[...], dmsg[...], TN) + mm(far_act[...], far_dmsg[...], TN)) * grad_scale
    for j in range(latent // LANES):
        at = hidden // LANES * latent + j * hidden
        grads[at : at + hidden, :] = g_out[:, j * LANES : (j + 1) * LANES]


def upper(stage):
    (axis0, d0), (axis1, d1) = stage
    bit0 = lax.rem(lax.axis_index(axis0) // d0, 2)
    bit1 = lax.rem(lax.axis_index(axis1) // d1, 2)
    return jnp.where(lax.axis_index("feat") == 0, bit0, bit1)


def place(stage, own, got, out):
    m = own.shape[0]
    bit = upper(stage)
    out[pl.ds(pl.multiple_of(bit * m, m), m), :] = own[...].astype(out.dtype)
    out[pl.ds(pl.multiple_of((1 - bit) * m, m), m), :] = got[...].astype(out.dtype)


def sum_kernel(steps, *refs):
    n_in = sum(1 + (kind != "split") for kind, *_ in steps)
    n_out = len(steps) + 1 + max(group for *_, group, _ in steps)
    ins, outs, accs = refs[:n_in], refs[n_in : n_in + n_out], refs[n_in + n_out :]
    sends = outs[len(steps) :]
    for (kind, stage, back, at, group, to), out in zip(steps, outs):
        own, ins = ins[0], ins[1:]
        m = own.shape[0]
        send = sends[group].at[to : to + out.shape[0]]
        if kind != "split":
            got, ins = ins[0].at[at : at + m], ins[1:]
        if kind in ("split", "add_split"):
            if kind == "add_split":
                acc, accs = accs[0], accs[1:]
                acc[...] = own[...] + got[...].astype(F32)
                own = acc
            m = m // 2
            bit = upper(stage)
            out[...] = own[pl.ds(pl.multiple_of(bit * m, m), m), :]
            send[...] = own[pl.ds(pl.multiple_of((1 - bit) * m, m), m), :].astype(BF16)
        else:
            if kind == "place":
                place(back, own, got, out)
            else:
                out[...] = (own[...] + got[...].astype(F32)).astype(out.dtype)
            send[...] = out[...].astype(BF16)


def write_kernel(layer, stage, kept, at, *refs):
    out_in, out_out, token, grads, slab_in, slab_out, sem = refs[-7:]
    token[...] = jnp.zeros_like(token)
    own = refs[kept]
    place(stage, own, refs[kept + 1].at[at : at + own.shape[0]], grads)
    latent, hidden = slab_in.shape
    for j in range(hidden // LANES):
        slab_in[:, j * LANES : (j + 1) * LANES] = grads[j * latent : (j + 1) * latent, :]
    first = pltpu.make_async_copy(slab_in, out_in.at[layer], sem.at[0])
    first.start()
    for j in range(latent // LANES):
        at = hidden // LANES * latent + j * hidden
        slab_out[:, j * LANES : (j + 1) * LANES] = grads[at : at + hidden, :]
    second = pltpu.make_async_copy(slab_out, out_out.at[layer], sem.at[1])
    second.start()
    first.wait()
    second.wait()


class Sum:
    def __init__(self, whole, stages):
        self.own, self.got, self.stages, self.done = whole, None, stages, 0

    def next(self):
        n, i, rows = len(self.stages), self.done, self.own.shape[0]
        if i < n - 1:
            return "add_split" if i else "split", self.stages[i], None, rows // 2, F32
        if i == n - 1:
            return "add", self.stages[i], None, rows, F32
        stage = self.stages[2 * n - 2 - i]
        if i == n:
            return "add", stage, None, rows, BF16
        return "place", stage, self.stages[2 * n - 1 - i], rows * 2, BF16


def sum_step(sums, after):
    steps, ins, outs, scratch, groups = [], [], [], [], {}
    for one in sums:
        kind, stage, back, rows, dtype = one.next()
        group = groups.setdefault(stage, [len(groups), 0])
        steps.append((kind, stage, back, one.got and one.got[1], *group))
        group[1] += rows
        ins += [one.own, one.got[0]] if one.got else [one.own]
        outs.append(((rows, LANES), dtype))
        if kind == "add_split":
            scratch.append(pltpu.VMEM(one.own.shape, F32))
    made = call(
        functools.partial(sum_kernel, steps),
        outs + [((rows, LANES), BF16) for _, rows in groups.values()],
        ins,
        1,
        bytes_accessed=1,
        scratch=scratch,
        name="sum",
        after=after,
    )
    arrived = [swapped(x, stage) for x, stage in zip(made[len(sums) :], groups)]
    for one, own, (*_, group, at) in zip(sums, made, steps):
        one.own, one.got = own, (arrived[group], at)
        one.done += 1
    return [made[0]]


def gathered_grad(dtotal, back, returned, spread):
    far = jnp.concatenate([x[...] for x in returned], axis=0)
    return dtotal[...] + back[...] + mm(spread[...], far)


def join_kernel(layer, groups, *refs):
    dtotal, back, spread, remote_t, total = refs[:5]
    weights, refs = refs[5:9], refs[9:]
    returned, refs = refs[:groups], refs[groups:]
    received, outs = refs[: groups + 1], refs[groups + 1 :]
    grad = gathered_grad(dtotal, back, returned, spread)
    start_bwd(layer, norm_grad(grad, total[...]), weights, received, remote_t, outs)


def last_kernel(*refs):
    dtotal, back, spread = refs[:3]
    refs[-2][...] = gathered_grad(dtotal, back, refs[3:-2], spread)
    refs[-1][...] = jnp.zeros_like(refs[-1])


def around(x, axis, distance):
    n = lax.axis_size(axis)
    return lax.ppermute(x, axis, [(i, (i + distance) % n) for i in range(n)])


def over_mesh(x, target):
    chain, groups, cores = (lax.axis_size(axis) for axis in ("chain", "basin", "feat"))
    perm = []
    for c in range(chain):
        for b in range(groups):
            for feat in range(cores):
                to = target(c, b, feat)
                if to is not None:
                    start, end = (c * groups + b) * cores + feat, (to[0] * groups + to[1]) * cores
                    perm.append((start, end + feat))
    return lax.ppermute(x, ("chain", "basin", "feat"), perm)


def swapped(x, stage):
    def partner(c, b, feat):
        axis, d = stage[feat]
        return (c ^ d, b) if axis == "chain" else (c, b ^ d)

    return over_mesh(x, partner)


def forward(sends):
    chain = lax.axis_size("chain")

    def downstream(c, b, feat):
        return (c + 1, b) if c % 2 == feat and c + 1 < chain else None

    up = over_mesh(sends[0], downstream)
    return [up] + [around(x, "basin", s + 1) for s, x in enumerate(sends[1:])]


def backward(grads):
    chain = lax.axis_size("chain")
    up = lax.ppermute(grads[0], "chain", [(c, c - 1) for c in range(1, chain)])
    return [up] + [around(x, "basin", -s) for s, x in enumerate(grads) if s]


def shards(features, cotangent, w_in, w_out, block_index, block_values, send_rows, send_count):
    rows, latent = features.shape
    groups = lax.axis_size("basin")
    layers, _, half = w_in.shape
    far_rows = groups * BLOCK
    own = rows // BLOCK
    grad_scale = float(rows * lax.axis_size("chain") * groups) ** (-0.5)
    last = layers - 1

    def act16(n, m=latent):
        return ((n, m), BF16)

    wi1 = around(w_in, "feat", 1)
    wo1 = around(w_out, "feat", 1)
    ffn = 4 * latent * 2 * half

    live = jnp.arange(BLOCK, dtype=jnp.int32)[None, :] < send_count[0][:, None]
    sent = jnp.where(live, send_rows[0], -1)
    sources = block_index.T
    pick, spread, pick_self, features, *sends = call(
        functools.partial(setup_kernel, groups),
        [act16(max(groups - 1, 1) * BLOCK, rows), act16(rows, far_rows), act16(BLOCK, rows)]
        + [act16(rows)]
        + [act16(BLOCK)] * groups,
        [features, sent],
        2 * rows * far_rows * latent,
        name="setup",
    )
    weights = (w_in, wi1, w_out, wo1)
    inputs = [features]
    totals = []
    received = []
    for layer in range(layers):
        up, *others = forward(sends)
        if layer == 0:
            (part,) = call(
                half_kernel, [((rows, latent), F32)], [features, wi1, wo1], rows * ffn // 2, name="half"
            )
            (msg,) = call(
                other_half_kernel,
                [act16(rows)],
                [features, w_in, w_out, part],
                rows * ffn // 2,
                name="local0",
            )
            local, local_t, remote, remote_t = call(
                functools.partial(adjacency_kernel, groups),
                [act16(rows, rows), act16(rows, rows), act16(rows, far_rows), act16(far_rows, rows)],
                [sources, block_values, pick_self, msg],
                2 * rows * rows * BLOCK,
                scratch=[pltpu.VMEM((rows, rows + BLOCK + far_rows), F32)],
                name="adjacency",
                scalars=sources,
            )
            up, local = lax.optimization_barrier((up, local))
        else:
            (msg,) = call(
                functools.partial(local_kernel, layer),
                [act16(rows)],
                [inputs[layer], *weights],
                rows * ffn,
                name=f"local{layer}",
            )
            up, msg = lax.optimization_barrier((up, msg))
        received.append([up, around(up, "feat", 1), *others])
        (mixed,) = call(
            functools.partial(part_kernel, layer),
            [((rows, latent), F32)],
            [local, msg, remote, *weights, *others],
            2 * rows * rows * latent,
            name=f"part{layer}",
        )
        prev = totals[-1] if layer else features
        if layer < last:
            total, new, *sends = call(
                functools.partial(mix_kernel, layer),
                [((rows, latent), F32), act16(rows)] + [act16(BLOCK)] * groups,
                [prev, mixed, remote, pick, *weights, *received[layer][:2]],
                far_rows * ffn + 2 * rows * far_rows * latent,
                name=f"mix{layer}",
            )
            totals.append(total)
            inputs.append(new)
    bwd_outs = (
        [((rows, latent), F32), act16(rows), act16(far_rows), act16(far_rows)]
        + [act16(far_rows, half)] * 2
        + [act16(BLOCK)] * groups
    )
    outs = call(
        functools.partial(turn_kernel, last, groups),
        bwd_outs,
        [totals[-1], mixed, remote, remote_t, cotangent, *weights, *received[last]],
        2 * far_rows * ffn,
        name="turn",
    )
    grad_rows = 2 * latent * half // LANES

    def distances(axis):
        return [(axis, 1 << i) for i in range(lax.axis_size(axis).bit_length() - 1)]

    over_basin, over_chain = distances("basin"), distances("chain")
    n = len(over_basin)
    orders = over_basin + over_chain, over_chain[:n] + over_basin + over_chain[n:]
    stages = list(zip(*orders, strict=True))
    returned = {}
    sums = {}

    def back(layer, outs, after):
        returned[layer] = backward(outs[6:])
        grad, whole = call(
            functools.partial(back_kernel, layer, grad_scale),
            [((rows, latent), F32), ((grad_rows, LANES), F32)],
            [outs[1], inputs[layer], local_t, *weights, *outs[2:6]],
            3 * rows * ffn + 2 * rows * rows * latent,
            scratch=[
                pltpu.VMEM((rows, latent), BF16),
                pltpu.VMEM((rows, half), BF16),
                pltpu.VMEM((rows, half), BF16),
            ],
            name=f"back{layer}",
            after=after,
        )
        sums[layer] = Sum(whole, stages)
        return [outs[0], grad], [grad]

    def join(layer, state, after):
        if layer:
            return call(
                functools.partial(join_kernel, layer - 1, groups),
                bwd_outs,
                [*state, spread, remote_t, totals[layer - 1]]
                + [*weights, *returned[layer], *received[layer - 1]],
                2 * far_rows * ffn,
                name=f"join{layer}",
                after=after,
            )
        return call(
            last_kernel,
            [((rows, latent), F32), ((8, LANES), F32)],
            [*state, spread, *returned[layer]],
            2 * rows * far_rows * latent,
            name="join0",
            after=after,
        )

    def write(layer, written, after):
        ready = [sums[layer].own, sums[layer].got[0]]
        kept = [*written, *after]
        return pl.pallas_call(
            functools.partial(
                write_kernel, layer, stages[0], len(kept), sums[layer].got[1]
            ),
            out_shape=[
                jax.ShapeDtypeStruct((layers, latent, half), F32),
                jax.ShapeDtypeStruct((layers, half, latent), F32),
                jax.ShapeDtypeStruct((8, LANES), F32),
            ],
            in_specs=[ANY] * len(kept) + [VMEM] * len(ready),
            out_specs=[ANY] * 2 + [VMEM],
            scratch_shapes=[
                pltpu.VMEM((grad_rows, LANES), F32),
                pltpu.VMEM((latent, half), F32),
                pltpu.VMEM((half, latent), F32),
                pltpu.SemaphoreType.DMA((2,)),
            ],
            input_output_aliases={i: i for i in range(len(written))},
            compiler_params=pltpu.CompilerParams(vmem_limit_bytes=LIMIT),
            cost_estimate=pl.CostEstimate(flops=1, bytes_accessed=1, transcendentals=0),
            name=f"write{layer}",
        )(*written, *after, *ready)

    count = 2 * len(stages) - 1
    at = []
    for layer in reversed(range(layers)):
        state, at = back(layer, outs, at)
        arrived = [sums[above].got[0] for above in range(layer + 2, layers)]
        if layer:
            arrived += returned[layer]
        at = sum_step([sums[layer]], at + arrived)
        if layer:
            for above in range(layer + 1, layers):
                at = sum_step([sums[above]], at)
            outs = join(layer, state, at)
            at = outs[1:2]
    while sums[0].done < count:
        for layer in reversed(range(layers)):
            if sums[layer].done < count:
                if layer == 0 and sums[0].done == count - 1:
                    at = at + [sums[above].got[0] for above in range(2, layers)]
                at = sum_step([sums[layer]], at)
    written = []
    for layer in reversed(range(layers)):
        if layer == 0:
            grad, token = join(0, state, at)
            at = [token]
        *written, token = write(layer, written, at)
        at = [token]
    return (grad, *written)


def solution(mesh):
    placed = (
        P(("runs", "chain", "basin"), None),
        P(("runs", "chain", "basin"), None),
        P(None, None, "feat"),
        P(None, "feat", None),
        P(("chain", "basin"), None),
        P(("chain", "basin"), None, None, None),
        P(("chain", "basin"), None, None),
        P(("chain", "basin"), None),
    )
    return jax.shard_map(
        shards,
        mesh=mesh,
        in_specs=placed,
        out_specs=(
            P(("runs", "chain", "basin"), None),
            P("runs", None, "feat"),
            P("runs", "feat", None),
        ),
        check_vma=False,
    )
```

```python
import functools

import jax
import jax.numpy as jnp
from jax import lax
from jax.experimental import pallas as pl
from jax.experimental.pallas import tpu as pltpu
from jax.sharding import PartitionSpec as P

BLOCK = 128
LANES = 128
EPS = 1e-06
F32 = jnp.float32
BF16 = jnp.bfloat16
VMEM = pl.BlockSpec(memory_space=pltpu.VMEM)
SMEM = pl.BlockSpec(memory_space=pltpu.SMEM)
ANY = pl.BlockSpec(memory_space=pl.ANY)
NN = (((1,), (0,)), ((), ()))
NT = (((1,), (1,)), ((), ()))
TN = (((0,), (0,)), ((), ()))


def mm(a, b, dims=NN):
    return lax.dot_general(a, b, dims, preferred_element_type=F32)


LIMIT = 24 * 1024 * 1024


def call(body, outs, ins, flops, scratch=(), name=None, after=(), bytes_accessed=4_000_000, scalars=None):
    skipped = len(after)
    return pl.pallas_call(
        lambda *refs: body(*refs[skipped:]),
        out_shape=[jax.ShapeDtypeStruct(s, d) for s, d in outs],
        in_specs=[ANY] * skipped + [SMEM if x is scalars else VMEM for x in ins],
        out_specs=[VMEM] * len(outs),
        scratch_shapes=list(scratch),
        compiler_params=pltpu.CompilerParams(vmem_limit_bytes=LIMIT),
        cost_estimate=pl.CostEstimate(
            flops=flops, bytes_accessed=bytes_accessed, transcendentals=0
        ),
        name=name,
    )(*after, *ins)


def sigmoid(v):
    return 1.0 / (1.0 + jnp.exp(-v))


def half_message(x, w_in, w_out):
    pre = mm(x, w_in)
    return mm((pre * sigmoid(pre)).astype(BF16), w_out)


def message_of(x, halves):
    total = None
    for w_in, w_out in halves:
        part = half_message(x, w_in, w_out)
        total = part if total is None else total + part
    return total.astype(BF16)


def message_grad(x, dmsg, halves):
    total = None
    kept = None
    for w_in, w_out in halves:
        pre = mm(x, w_in)
        sig = sigmoid(pre)
        dact = mm(dmsg, w_out, NT)
        dpre = (dact * (sig * (1.0 + pre * (1.0 - sig)))).astype(BF16)
        if kept is None:
            kept = ((pre * sig).astype(BF16), dpre)
        part = mm(dpre, w_in, NT)
        total = part if total is None else total + part
    return total, kept


def normed_of(total):
    scale = lax.rsqrt(jnp.mean(total * total, axis=-1, keepdims=True) + EPS)
    return scale, scale * total


def norm_grad(grad, total):
    scale, normed = normed_of(total)
    return scale * (grad - normed * jnp.mean(grad * normed, axis=-1, keepdims=True))


def setup_kernel(groups, features, sent, *refs):
    pick, spread, pick_self, held = refs[:4]
    sends = refs[4:]
    rows = features.shape[0]
    held[...] = features[...]
    b = lax.axis_index("basin")
    for route in range(-1, groups):
        if route == 0:
            chosen = lax.broadcasted_iota(jnp.int32, (1, BLOCK), 1) + (rows - BLOCK)
        else:
            chosen = sent[pl.ds(lax.rem(b + max(route, 0), groups), 1), :]
        across = jnp.broadcast_to(chosen, (BLOCK, BLOCK))
        down = across.T
        for r in range(0, rows, BLOCK):
            at = lax.broadcasted_iota(jnp.int32, (BLOCK, BLOCK), 1) + r
            hot = (down == at).astype(F32).astype(BF16)
            if route < 0:
                pick_self[:, r : r + BLOCK] = hot
                continue
            if route > 0:
                pick[(route - 1) * BLOCK : route * BLOCK, r : r + BLOCK] = hot
            at = lax.broadcasted_iota(jnp.int32, (BLOCK, BLOCK), 0) + r
            spread[r : r + BLOCK, route * BLOCK : (route + 1) * BLOCK] = (
                (across == at).astype(F32).astype(BF16)
            )
    pick_sends(features[...], pick, sends)


def pick_sends(rows, pick, sends):
    sends[0][...] = rows[rows.shape[0] - BLOCK :, :]
    for s, send in enumerate(sends[1:]):
        send[...] = mm(pick[s * BLOCK : (s + 1) * BLOCK, :], rows).astype(BF16)


def adjacency_kernel(groups, sources, values, pick_self, _, *refs):
    local, local_t, remote, remote_t, acc = refs
    rows = local.shape[0]
    own = rows // BLOCK
    b = lax.axis_index("basin")
    acc[...] = jnp.zeros_like(acc)
    for k in range(own):
        for t in range(values.shape[1]):
            v = sources[t, k]
            route = jnp.where(v == own, 0, lax.rem(b + groups - (v - own - 1), groups))
            far = jnp.where((v > own) & (route == 0), own, own + 1 + route)
            at = jnp.where(v < own, v, far)
            here = (pl.ds(k * BLOCK, BLOCK), pl.ds(pl.multiple_of(at * BLOCK, BLOCK), BLOCK))
            acc[here] += values[k, t].astype(F32)
    mine = acc[:, rows : rows + BLOCK].astype(BF16)
    full = acc[:, :rows] + mm(mine, pick_self[...])
    local[...] = full.astype(BF16)
    local_t[...] = full.T.astype(BF16)
    far = acc[:, rows + BLOCK :]
    remote[...] = far.astype(BF16)
    remote_t[...] = far.T.astype(BF16)


def message_half(x, w_in, w_out, slope, act_t=None):
    pre = mm(x, w_in)
    sig = sigmoid(pre)
    act = (pre * sig).astype(BF16)
    slope[...] = (sig * (1.0 + pre * (1.0 - sig))).astype(BF16)
    if act_t is not None:
        act_t[...] = act.T
    return mm(act, w_out)


def local_kernel(layer, x, wi0, wi1, wo0, wo1, msg, slope0, slope1, act_t, x_t):
    for r in range(0, x.shape[0], 256):
        here = slice(r, r + 256)
        rows = x[here, :]
        x_t[:, here] = rows.T
        part = message_half(rows, wi0[layer], wo0[layer], slope0.at[here, :], act_t.at[:, here])
        part = part + message_half(rows, wi1[layer], wo1[layer], slope1.at[here, :])
        msg[here, :] = part.astype(BF16)


def half_kernel(x, w_in, w_out, part, slope1):
    for r in range(0, x.shape[0], 256):
        here = slice(r, r + 256)
        part[here, :] = message_half(x[here, :], w_in[0], w_out[0], slope1.at[here, :])


def other_half_kernel(x, w_in, w_out, part, msg, slope0, act_t, x_t):
    for r in range(0, x.shape[0], 256):
        here = slice(r, r + 256)
        rows = x[here, :]
        x_t[:, here] = rows.T
        own = message_half(rows, w_in[0], w_out[0], slope0.at[here, :], act_t.at[:, here])
        msg[here, :] = (part[here, :] + own).astype(BF16)


def remote_mixed(layer, received, columns, weights):
    wi0, wi1, wo0, wo1 = weights
    halves = [(wi0[layer], wo0[layer]), (wi1[layer], wo1[layer])]
    far = jnp.concatenate([x[...] for x in received], axis=0)
    return mm(columns, message_of(far, halves))


def part_kernel(layer, *refs):
    local, msg, remote = refs[:3]
    weights, received, mixed = refs[3:7], refs[7:-1], refs[-1]
    total = mm(local[...], msg[...])
    if received:
        total = total + remote_mixed(layer, received, remote[:, BLOCK:], weights)
    mixed[...] = total


def upstream_rows(got, swapped_got):
    return got[...] + swapped_got[...]


def mixed_total(layer, state, mixed, up, remote, weights):
    return state + mixed[...] + remote_mixed(layer, [up], remote[:, :BLOCK], weights)


def mix_kernel(layer, *refs):
    prev, mixed, remote, pick = refs[:4]
    weights, up = refs[4:8], upstream_rows(*refs[8:10])
    total, inputs = refs[10:12]
    state = prev[...].astype(F32) if layer == 0 else normed_of(prev[...])[1]
    total[...] = mixed_total(layer, state, mixed, up, remote, weights)
    new = normed_of(total[...])[1].astype(BF16)
    inputs[...] = new
    pick_sends(new, pick, refs[12:])


def start_bwd(layer, dtotal_now, weights, received, remote_t, outs):
    dtotal, dround, far_x, far_dmsg, far_act, far_dpre = outs[:6]
    backs = outs[6:]
    wi0, wi1, wo0, wo1 = weights
    halves = [(wi0[layer], wo0[layer]), (wi1[layer], wo1[layer])]
    dtotal[...] = dtotal_now
    dround[...] = dtotal_now.astype(BF16)
    far_x[:BLOCK, :] = upstream_rows(*received[:2])
    for i, block in enumerate(received[2:]):
        far_x[(i + 1) * BLOCK : (i + 2) * BLOCK, :] = block[...]
    dmsg = mm(remote_t[...], dround[...]).astype(BF16)
    back, (act, dpre) = message_grad(far_x[...], dmsg, halves)
    far_dmsg[...] = dmsg
    far_act[...] = act
    far_dpre[...] = dpre
    for i, out in enumerate(backs):
        out[...] = back[i * BLOCK : (i + 1) * BLOCK, :].astype(BF16)


def turn_kernel(layer, groups, *refs):
    prev, mixed, remote, remote_t, cot = refs[:5]
    weights, received, outs = refs[5:9], refs[9 : 10 + groups], refs[10 + groups :]
    state = normed_of(prev[...])[1]
    total = mixed_total(layer, state, mixed, upstream_rows(*received[:2]), remote, weights)
    start_bwd(layer, norm_grad(cot[...], total), weights, received, remote_t, outs)


def back_kernel(layer, grad_scale, *refs):
    dround, local_t, slope0, slope1, act_t, x_t = refs[:6]
    wi0, wi1, wo0, wo1 = refs[6:10]
    far_x, far_dmsg, far_act, far_dpre = refs[10:14]
    back, grads, dmsg, dpre = refs[14:]
    dmsg[...] = mm(local_t[...], dround[...]).astype(BF16)
    for r in range(0, dmsg.shape[0], 256):
        here = slice(r, r + 256)
        rows = dmsg[here, :]
        dpre0 = (mm(rows, wo0[layer], NT) * slope0[here, :].astype(F32)).astype(BF16)
        dpre1 = (mm(rows, wo1[layer], NT) * slope1[here, :].astype(F32)).astype(BF16)
        dpre[here, :] = dpre0
        back[here, :] = mm(dpre0, wi0[layer], NT) + mm(dpre1, wi1[layer], NT)
    latent, hidden = x_t.shape[0], act_t.shape[0]
    g_in = (mm(x_t[...], dpre[...]) + mm(far_x[...], far_dpre[...], TN)) * grad_scale
    for j in range(hidden // LANES):
        grads[j * latent : (j + 1) * latent, :] = g_in[:, j * LANES : (j + 1) * LANES]
    g_out = (mm(act_t[...], dmsg[...]) + mm(far_act[...], far_dmsg[...], TN)) * grad_scale
    for j in range(latent // LANES):
        at = hidden // LANES * latent + j * hidden
        grads[at : at + hidden, :] = g_out[:, j * LANES : (j + 1) * LANES]


def upper(stage):
    (axis0, d0), (axis1, d1) = stage
    bit0 = lax.rem(lax.axis_index(axis0) // d0, 2)
    bit1 = lax.rem(lax.axis_index(axis1) // d1, 2)
    return jnp.where(lax.axis_index("feat") == 0, bit0, bit1)


def place(stage, own, got, out):
    m = own.shape[0]
    bit = upper(stage)
    out[pl.ds(pl.multiple_of(bit * m, m), m), :] = own[...].astype(out.dtype)
    out[pl.ds(pl.multiple_of((1 - bit) * m, m), m), :] = got[...].astype(out.dtype)


def sum_kernel(steps, *refs):
    n_in = sum(1 + (kind != "split") for kind, *_ in steps)
    n_out = len(steps) + 1 + max(group for *_, group, _ in steps)
    ins, outs, accs = refs[:n_in], refs[n_in : n_in + n_out], refs[n_in + n_out :]
    sends = outs[len(steps) :]
    for (kind, stage, back, at, group, to), out in zip(steps, outs):
        own, ins = ins[0], ins[1:]
        m = own.shape[0]
        send = sends[group].at[to : to + out.shape[0]]
        if kind != "split":
            got, ins = ins[0].at[at : at + m], ins[1:]
        if kind in ("split", "add_split"):
            if kind == "add_split":
                acc, accs = accs[0], accs[1:]
                acc[...] = own[...] + got[...].astype(F32)
                own = acc
            m = m // 2
            bit = upper(stage)
            out[...] = own[pl.ds(pl.multiple_of(bit * m, m), m), :]
            send[...] = own[pl.ds(pl.multiple_of((1 - bit) * m, m), m), :].astype(BF16)
        else:
            if kind == "place":
                place(back, own, got, out)
            else:
                out[...] = (own[...] + got[...].astype(F32)).astype(out.dtype)
            send[...] = out[...].astype(BF16)


def write_kernel(layer, stage, kept, halves, *refs):
    parts, (out_in, out_out, token, slab_in, slab_out, sem) = refs[kept:-6], refs[-6:]
    token[...] = jnp.zeros_like(token)
    bit = upper(stage)
    copies = []
    for part, (at, other) in zip(parts, halves):
        m = slab_in.size // LANES
        rows = part.at[at : at + m]
        upper_half = (1 - bit) if other else bit

        @pl.when(upper_half == 0)
        def _():
            write_slab(rows, slab_in, out_in.at[layer], sem.at[0])

        @pl.when(upper_half == 1)
        def _():
            write_slab(rows, slab_out, out_out.at[layer], sem.at[1])

        copies.append(upper_half)
    for upper_half in copies:

        @pl.when(upper_half == 0)
        def _():
            pltpu.make_async_copy(slab_in, out_in.at[layer], sem.at[0]).wait()

        @pl.when(upper_half == 1)
        def _():
            pltpu.make_async_copy(slab_out, out_out.at[layer], sem.at[1]).wait()


def write_slab(rows, slab, out, sem):
    n = slab.shape[0]
    for j in range(slab.shape[1] // LANES):
        slab[:, j * LANES : (j + 1) * LANES] = rows[j * n : (j + 1) * n, :].astype(F32)
    pltpu.make_async_copy(slab, out, sem).start()


class Sum:
    def __init__(self, whole, stages):
        self.own, self.got, self.stages, self.done = whole, None, stages, 0

    def next(self):
        n, i, rows = len(self.stages), self.done, self.own.shape[0]
        if i < n - 1:
            return "add_split" if i else "split", self.stages[i], None, rows // 2, F32
        if i == n - 1:
            return "add", self.stages[i], None, rows, F32
        stage = self.stages[2 * n - 2 - i]
        if i == n:
            return "add", stage, None, rows, BF16
        return "place", stage, self.stages[2 * n - 1 - i], rows * 2, BF16


def sum_step(sums, after):
    steps, ins, outs, scratch, groups = [], [], [], [], {}
    for one in sums:
        kind, stage, back, rows, dtype = one.next()
        group = groups.setdefault(stage, [len(groups), 0])
        steps.append((kind, stage, back, one.got and one.got[1], *group))
        group[1] += rows
        ins += [one.own, one.got[0]] if one.got else [one.own]
        outs.append(((rows, LANES), dtype))
        if kind == "add_split":
            scratch.append(pltpu.VMEM(one.own.shape, F32))
    made = call(
        functools.partial(sum_kernel, steps),
        outs + [((rows, LANES), BF16) for _, rows in groups.values()],
        ins,
        1,
        bytes_accessed=1,
        scratch=scratch,
        name="sum",
        after=after,
    )
    arrived = [swapped(x, stage) for x, stage in zip(made[len(sums) :], groups)]
    for one, own, (*_, group, at) in zip(sums, made, steps):
        one.own, one.got = own, (arrived[group], at)
        one.done += 1
    return [made[0]]


def gathered_grad(dtotal, back, returned, spread):
    far = jnp.concatenate([x[...] for x in returned], axis=0)
    return dtotal[...] + back[...] + mm(spread[...], far)


def join_kernel(layer, groups, *refs):
    dtotal, back, spread, remote_t, total = refs[:5]
    weights, refs = refs[5:9], refs[9:]
    returned, refs = refs[:groups], refs[groups:]
    received, outs = refs[: groups + 1], refs[groups + 1 :]
    grad = gathered_grad(dtotal, back, returned, spread)
    start_bwd(layer, norm_grad(grad, total[...]), weights, received, remote_t, outs)


def last_kernel(*refs):
    dtotal, back, spread = refs[:3]
    refs[-2][...] = gathered_grad(dtotal, back, refs[3:-2], spread)
    refs[-1][...] = jnp.zeros_like(refs[-1])


def around(x, axis, distance):
    n = lax.axis_size(axis)
    return lax.ppermute(x, axis, [(i, (i + distance) % n) for i in range(n)])


def over_mesh(x, target):
    chain, groups, cores = (lax.axis_size(axis) for axis in ("chain", "basin", "feat"))
    perm = []
    for c in range(chain):
        for b in range(groups):
            for feat in range(cores):
                to = target(c, b, feat)
                if to is not None:
                    start, end = (c * groups + b) * cores + feat, (to[0] * groups + to[1]) * cores
                    perm.append((start, end + feat))
    return lax.ppermute(x, ("chain", "basin", "feat"), perm)


def swapped(x, stage):
    def partner(c, b, feat):
        axis, d = stage[feat]
        return (c ^ d, b) if axis == "chain" else (c, b ^ d)

    return over_mesh(x, partner)


def forward(sends):
    chain = lax.axis_size("chain")

    def downstream(c, b, feat):
        return (c + 1, b) if c % 2 == feat and c + 1 < chain else None

    up = over_mesh(sends[0], downstream)
    return [up] + [around(x, "basin", s + 1) for s, x in enumerate(sends[1:])]


def backward(grads):
    chain = lax.axis_size("chain")
    up = lax.ppermute(grads[0], "chain", [(c, c - 1) for c in range(1, chain)])
    return [up] + [around(x, "basin", -s) for s, x in enumerate(grads) if s]


def shards(features, cotangent, w_in, w_out, block_index, block_values, send_rows, send_count):
    rows, latent = features.shape
    groups = lax.axis_size("basin")
    layers, _, half = w_in.shape
    far_rows = groups * BLOCK
    own = rows // BLOCK
    grad_scale = float(rows * lax.axis_size("chain") * groups) ** (-0.5)
    last = layers - 1

    def act16(n, m=latent):
        return ((n, m), BF16)

    wi1 = around(w_in, "feat", 1)
    wo1 = around(w_out, "feat", 1)
    ffn = 4 * latent * 2 * half

    live = jnp.arange(BLOCK, dtype=jnp.int32)[None, :] < send_count[0][:, None]
    sent = jnp.where(live, send_rows[0], -1)
    sources = block_index.T
    pick, spread, pick_self, features, *sends = call(
        functools.partial(setup_kernel, groups),
        [act16(max(groups - 1, 1) * BLOCK, rows), act16(rows, far_rows), act16(BLOCK, rows)]
        + [act16(rows)]
        + [act16(BLOCK)] * groups,
        [features, sent],
        2 * rows * far_rows * latent,
        name="setup",
    )
    weights = (w_in, wi1, w_out, wo1)
    inputs = [features]
    saved = []
    totals = []
    received = []
    for layer in range(layers):
        up, *others = forward(sends)
        if layer == 0:
            part, slope1 = call(
                half_kernel,
                [((rows, latent), F32), act16(rows, half)],
                [features, wi1, wo1],
                rows * ffn // 2,
                name="half",
            )
            msg, slope0, act_t, x_t = call(
                other_half_kernel,
                [act16(rows), act16(rows, half), act16(half, rows), act16(latent, rows)],
                [features, w_in, w_out, part],
                rows * ffn // 2,
                name="local0",
            )
            local, local_t, remote, remote_t = call(
                functools.partial(adjacency_kernel, groups),
                [act16(rows, rows), act16(rows, rows), act16(rows, far_rows), act16(far_rows, rows)],
                [sources, block_values, pick_self, msg],
                2 * rows * rows * BLOCK,
                scratch=[pltpu.VMEM((rows, rows + BLOCK + far_rows), F32)],
                name="adjacency",
                scalars=sources,
            )
            up, local = lax.optimization_barrier((up, local))
        else:
            msg, slope0, slope1, act_t, x_t = call(
                functools.partial(local_kernel, layer),
                [act16(rows), act16(rows, half), act16(rows, half)]
                + [act16(half, rows), act16(latent, rows)],
                [inputs[layer], *weights],
                rows * ffn,
                name=f"local{layer}",
            )
            up, msg = lax.optimization_barrier((up, msg))
        saved.append([slope0, slope1, act_t, x_t])
        received.append([up, around(up, "feat", 1), *others])
        (mixed,) = call(
            functools.partial(part_kernel, layer),
            [((rows, latent), F32)],
            [local, msg, remote, *weights, *others],
            2 * rows * rows * latent,
            name=f"part{layer}",
        )
        prev = totals[-1] if layer else features
        if layer < last:
            total, new, *sends = call(
                functools.partial(mix_kernel, layer),
                [((rows, latent), F32), act16(rows)] + [act16(BLOCK)] * groups,
                [prev, mixed, remote, pick, *weights, *received[layer][:2]],
                far_rows * ffn + 2 * rows * far_rows * latent,
                name=f"mix{layer}",
            )
            totals.append(total)
            inputs.append(new)
    bwd_outs = (
        [((rows, latent), F32), act16(rows), act16(far_rows), act16(far_rows)]
        + [act16(far_rows, half)] * 2
        + [act16(BLOCK)] * groups
    )
    outs = call(
        functools.partial(turn_kernel, last, groups),
        bwd_outs,
        [totals[-1], mixed, remote, remote_t, cotangent, *weights, *received[last]],
        2 * far_rows * ffn,
        name="turn",
    )
    grad_rows = 2 * latent * half // LANES

    def distances(axis):
        return [(axis, 1 << i) for i in range(lax.axis_size(axis).bit_length() - 1)]

    over_basin, over_chain = distances("basin"), distances("chain")
    n = len(over_basin)
    orders = over_basin + over_chain, over_chain[:n] + over_basin + over_chain[n:]
    stages = list(zip(*orders, strict=True))
    returned = {}
    sums = {}

    def back(layer, outs, after):
        returned[layer] = backward(outs[6:])
        grad, whole = call(
            functools.partial(back_kernel, layer, grad_scale),
            [((rows, latent), F32), ((grad_rows, LANES), F32)],
            [outs[1], local_t, *saved[layer], *weights, *outs[2:6]],
            3 * rows * ffn + 2 * rows * rows * latent,
            scratch=[
                pltpu.VMEM((rows, latent), BF16),
                pltpu.VMEM((rows, half), BF16),
            ],
            name=f"back{layer}",
            after=after,
        )
        sums[layer] = Sum(whole, stages)
        return [outs[0], grad], [grad]

    def join(layer, state, after):
        if layer:
            return call(
                functools.partial(join_kernel, layer - 1, groups),
                bwd_outs,
                [*state, spread, remote_t, totals[layer - 1]]
                + [*weights, *returned[layer], *received[layer - 1]],
                2 * far_rows * ffn,
                name=f"join{layer}",
                after=after,
            )
        return call(
            last_kernel,
            [((rows, latent), F32), ((8, LANES), F32)],
            [*state, spread, *returned[layer]],
            2 * rows * far_rows * latent,
            name="join0",
            after=after,
        )

    def write(layer, written, after, which=(0, 1)):
        ready = [(sums[layer].own, 0), sums[layer].got]
        ready = [ready[i] for i in which]
        kept = [*written, *after]
        return pl.pallas_call(
            functools.partial(
                write_kernel,
                layer,
                stages[0],
                len(kept),
                [(at, i) for (_, at), i in zip(ready, which)],
            ),
            out_shape=[
                jax.ShapeDtypeStruct((layers, latent, half), F32),
                jax.ShapeDtypeStruct((layers, half, latent), F32),
                jax.ShapeDtypeStruct((8, LANES), F32),
            ],
            in_specs=[ANY] * len(kept) + [VMEM] * len(ready),
            out_specs=[ANY] * 2 + [VMEM],
            scratch_shapes=[
                pltpu.VMEM((latent, half), F32),
                pltpu.VMEM((half, latent), F32),
                pltpu.SemaphoreType.DMA((2,)),
            ],
            input_output_aliases={i: i for i in range(len(written))},
            compiler_params=pltpu.CompilerParams(vmem_limit_bytes=LIMIT),
            cost_estimate=pl.CostEstimate(flops=1, bytes_accessed=1, transcendentals=0),
            name=f"write{layer}",
        )(*written, *after, *[x for x, _ in ready])

    count = 2 * len(stages) - 1
    at = []
    for layer in reversed(range(layers)):
        state, at = back(layer, outs, at)
        arrived = [sums[above].got[0] for above in range(layer + 2, layers)]
        if layer:
            arrived += returned[layer]
        at = sum_step([sums[layer]], at + arrived)
        if layer:
            for above in range(layer + 1, layers):
                at = sum_step([sums[above]], at)
            outs = join(layer, state, at)
            at = outs[1:2]
    while sums[0].done < count:
        for layer in reversed(range(layers)):
            if sums[layer].done < count:
                if layer == 0 and sums[0].done == count - 1:
                    at = at + [sums[above].got[0] for above in range(2, layers)]
                at = sum_step([sums[layer]], at)
    written = []
    for layer in reversed(range(1, layers)):
        *written, token = write(layer, written, at)
        at = [token]
    *written, token = write(0, written, at, (0,))
    grad, token = join(0, state, [token])
    *written, token = write(0, written, [token], (1,))
    return (grad, *written)


def solution(mesh):
    placed = (
        P(("runs", "chain", "basin"), None),
        P(("runs", "chain", "basin"), None),
        P(None, None, "feat"),
        P(None, "feat", None),
        P(("chain", "basin"), None),
        P(("chain", "basin"), None, None, None),
        P(("chain", "basin"), None, None),
        P(("chain", "basin"), None),
    )
    return jax.shard_map(
        shards,
        mesh=mesh,
        in_specs=placed,
        out_specs=(
            P(("runs", "chain", "basin"), None),
            P("runs", None, "feat"),
            P("runs", "feat", None),
        ),
        check_vma=False,
    )
```

```python
import functools

import jax
import jax.numpy as jnp
from jax import lax
from jax.experimental import pallas as pl
from jax.experimental.pallas import tpu as pltpu
from jax.sharding import PartitionSpec as P

BLOCK = 128
LANES = 128
EPS = 1e-06
F32 = jnp.float32
BF16 = jnp.bfloat16
VMEM = pl.BlockSpec(memory_space=pltpu.VMEM)
SMEM = pl.BlockSpec(memory_space=pltpu.SMEM)
ANY = pl.BlockSpec(memory_space=pl.ANY)
NN = (((1,), (0,)), ((), ()))
NT = (((1,), (1,)), ((), ()))
TN = (((0,), (0,)), ((), ()))


def mm(a, b, dims=NN):
    return lax.dot_general(a, b, dims, preferred_element_type=F32)


LIMIT = 24 * 1024 * 1024


def call(body, outs, ins, flops, scratch=(), name=None, after=(), bytes_accessed=4_000_000, scalars=None):
    skipped = len(after)
    return pl.pallas_call(
        lambda *refs: body(*refs[skipped:]),
        out_shape=[jax.ShapeDtypeStruct(s, d) for s, d in outs],
        in_specs=[ANY] * skipped + [SMEM if x is scalars else VMEM for x in ins],
        out_specs=[VMEM] * len(outs),
        scratch_shapes=list(scratch),
        compiler_params=pltpu.CompilerParams(vmem_limit_bytes=LIMIT),
        cost_estimate=pl.CostEstimate(
            flops=flops, bytes_accessed=bytes_accessed, transcendentals=0
        ),
        name=name,
    )(*after, *ins)


def sigmoid(v):
    return 1.0 / (1.0 + jnp.exp(-v))


def half_message(x, w_in, w_out):
    pre = mm(x, w_in)
    return mm((pre * sigmoid(pre)).astype(BF16), w_out)


def message_of(x, halves):
    total = None
    for w_in, w_out in halves:
        part = half_message(x, w_in, w_out)
        total = part if total is None else total + part
    return total.astype(BF16)


def message_grad(x, dmsg, halves):
    total = None
    kept = None
    for w_in, w_out in halves:
        pre = mm(x, w_in)
        sig = sigmoid(pre)
        dact = mm(dmsg, w_out, NT)
        dpre = (dact * (sig * (1.0 + pre * (1.0 - sig)))).astype(BF16)
        if kept is None:
            kept = ((pre * sig).astype(BF16), dpre)
        part = mm(dpre, w_in, NT)
        total = part if total is None else total + part
    return total, kept


def normed_of(total):
    scale = lax.rsqrt(jnp.mean(total * total, axis=-1, keepdims=True) + EPS)
    return scale, scale * total


def norm_grad(grad, total):
    scale, normed = normed_of(total)
    return scale * (grad - normed * jnp.mean(grad * normed, axis=-1, keepdims=True))


def setup_kernel(groups, features, sent, *refs):
    pick, spread, pick_self, held = refs[:4]
    sends = refs[4:]
    rows = features.shape[0]
    held[...] = features[...]
    b = lax.axis_index("basin")
    for route in range(-1, groups):
        if route == 0:
            chosen = lax.broadcasted_iota(jnp.int32, (1, BLOCK), 1) + (rows - BLOCK)
        else:
            chosen = sent[pl.ds(lax.rem(b + max(route, 0), groups), 1), :]
        across = jnp.broadcast_to(chosen, (BLOCK, BLOCK))
        down = across.T
        for r in range(0, rows, BLOCK):
            at = lax.broadcasted_iota(jnp.int32, (BLOCK, BLOCK), 1) + r
            hot = (down == at).astype(F32).astype(BF16)
            if route < 0:
                pick_self[:, r : r + BLOCK] = hot
                continue
            if route > 0:
                pick[(route - 1) * BLOCK : route * BLOCK, r : r + BLOCK] = hot
            at = lax.broadcasted_iota(jnp.int32, (BLOCK, BLOCK), 0) + r
            spread[r : r + BLOCK, route * BLOCK : (route + 1) * BLOCK] = (
                (across == at).astype(F32).astype(BF16)
            )
    pick_sends(features[...], pick, sends)


def pick_sends(rows, pick, sends):
    sends[0][...] = rows[rows.shape[0] - BLOCK :, :]
    for s, send in enumerate(sends[1:]):
        send[...] = mm(pick[s * BLOCK : (s + 1) * BLOCK, :], rows).astype(BF16)


def adjacency_kernel(groups, sources, values, pick_self, _, *refs):
    local, local_t, remote, remote_t, acc = refs
    rows = local.shape[0]
    own = rows // BLOCK
    b = lax.axis_index("basin")
    acc[...] = jnp.zeros_like(acc)
    for k in range(own):
        for t in range(values.shape[1]):
            v = sources[t, k]
            route = jnp.where(v == own, 0, lax.rem(b + groups - (v - own - 1), groups))
            far = jnp.where((v > own) & (route == 0), own, own + 1 + route)
            at = jnp.where(v < own, v, far)
            here = (pl.ds(k * BLOCK, BLOCK), pl.ds(pl.multiple_of(at * BLOCK, BLOCK), BLOCK))
            acc[here] += values[k, t].astype(F32)
    mine = acc[:, rows : rows + BLOCK].astype(BF16)
    full = acc[:, :rows] + mm(mine, pick_self[...])
    local[...] = full.astype(BF16)
    local_t[...] = full.T.astype(BF16)
    far = acc[:, rows + BLOCK :]
    remote[...] = far.astype(BF16)
    remote_t[...] = far.T.astype(BF16)


def message_half(x, w_in, w_out, slope, act_t=None):
    pre = mm(x, w_in)
    sig = sigmoid(pre)
    act = (pre * sig).astype(BF16)
    slope[...] = (sig * (1.0 + pre * (1.0 - sig))).astype(BF16)
    if act_t is not None:
        act_t[...] = act.T
    return mm(act, w_out)


def local_kernel(layer, x, wi0, wi1, wo0, wo1, msg, slope0, slope1, act_t, x_t):
    for r in range(0, x.shape[0], 256):
        here = slice(r, r + 256)
        rows = x[here, :]
        x_t[:, here] = rows.T
        part = message_half(rows, wi0[layer], wo0[layer], slope0.at[here, :], act_t.at[:, here])
        part = part + message_half(rows, wi1[layer], wo1[layer], slope1.at[here, :])
        msg[here, :] = part.astype(BF16)


def half_kernel(x, w_in, w_out, part, slope1):
    for r in range(0, x.shape[0], 256):
        here = slice(r, r + 256)
        part[here, :] = message_half(x[here, :], w_in[0], w_out[0], slope1.at[here, :])


def other_half_kernel(x, w_in, w_out, part, msg, slope0, act_t, x_t):
    for r in range(0, x.shape[0], 256):
        here = slice(r, r + 256)
        rows = x[here, :]
        x_t[:, here] = rows.T
        own = message_half(rows, w_in[0], w_out[0], slope0.at[here, :], act_t.at[:, here])
        msg[here, :] = (part[here, :] + own).astype(BF16)


def remote_mixed(layer, received, columns, weights):
    wi0, wi1, wo0, wo1 = weights
    halves = [(wi0[layer], wo0[layer]), (wi1[layer], wo1[layer])]
    far = jnp.concatenate([x[...] for x in received], axis=0)
    return mm(columns, message_of(far, halves))


def part_kernel(layer, *refs):
    local, msg, remote = refs[:3]
    weights, received, mixed = refs[3:7], refs[7:-1], refs[-1]
    total = mm(local[...], msg[...])
    if received:
        total = total + remote_mixed(layer, received, remote[:, BLOCK:], weights)
    mixed[...] = total


def upstream_rows(got, swapped_got):
    return got[...] + swapped_got[...]


def mixed_total(layer, state, mixed, up, remote, weights):
    return state + mixed[...] + remote_mixed(layer, [up], remote[:, :BLOCK], weights)


def mix_kernel(layer, *refs):
    prev, mixed, remote, pick = refs[:4]
    weights, up = refs[4:8], upstream_rows(*refs[8:10])
    total, inputs = refs[10:12]
    state = prev[...].astype(F32) if layer == 0 else normed_of(prev[...])[1]
    total[...] = mixed_total(layer, state, mixed, up, remote, weights)
    new = normed_of(total[...])[1].astype(BF16)
    inputs[...] = new
    pick_sends(new, pick, refs[12:])


def start_bwd(layer, dtotal_now, weights, received, remote_t, outs):
    dtotal, dround, far_x, far_dmsg, far_act, far_dpre = outs[:6]
    backs = outs[6:]
    wi0, wi1, wo0, wo1 = weights
    halves = [(wi0[layer], wo0[layer]), (wi1[layer], wo1[layer])]
    dtotal[...] = dtotal_now
    dround[...] = dtotal_now.astype(BF16)
    far_x[:BLOCK, :] = upstream_rows(*received[:2])
    for i, block in enumerate(received[2:]):
        far_x[(i + 1) * BLOCK : (i + 2) * BLOCK, :] = block[...]
    dmsg = mm(remote_t[...], dround[...]).astype(BF16)
    back, (act, dpre) = message_grad(far_x[...], dmsg, halves)
    far_dmsg[...] = dmsg
    far_act[...] = act
    far_dpre[...] = dpre
    for i, out in enumerate(backs):
        out[...] = back[i * BLOCK : (i + 1) * BLOCK, :].astype(BF16)


def turn_kernel(layer, groups, *refs):
    prev, mixed, remote, remote_t, cot = refs[:5]
    weights, received, outs = refs[5:9], refs[9 : 10 + groups], refs[10 + groups :]
    state = normed_of(prev[...])[1]
    total = mixed_total(layer, state, mixed, upstream_rows(*received[:2]), remote, weights)
    start_bwd(layer, norm_grad(cot[...], total), weights, received, remote_t, outs)


def back_kernel(layer, grad_scale, *refs):
    dround, local_t, slope0, slope1, act_t, x_t = refs[:6]
    wi0, wi1, wo0, wo1 = refs[6:10]
    far_x, far_dmsg, far_act, far_dpre = refs[10:14]
    back, grads, dmsg, dpre = refs[14:]
    dmsg[...] = mm(local_t[...], dround[...]).astype(BF16)
    for r in range(0, dmsg.shape[0], 256):
        here = slice(r, r + 256)
        rows = dmsg[here, :]
        dpre0 = (mm(rows, wo0[layer], NT) * slope0[here, :].astype(F32)).astype(BF16)
        dpre1 = (mm(rows, wo1[layer], NT) * slope1[here, :].astype(F32)).astype(BF16)
        dpre[here, :] = dpre0
        back[here, :] = mm(dpre0, wi0[layer], NT) + mm(dpre1, wi1[layer], NT)
    latent, hidden = x_t.shape[0], act_t.shape[0]
    g_in = (mm(x_t[...], dpre[...]) + mm(far_x[...], far_dpre[...], TN)) * grad_scale
    for j in range(hidden // LANES):
        grads[j * latent : (j + 1) * latent, :] = g_in[:, j * LANES : (j + 1) * LANES]
    g_out = (mm(act_t[...], dmsg[...]) + mm(far_act[...], far_dmsg[...], TN)) * grad_scale
    for j in range(latent // LANES):
        at = hidden // LANES * latent + j * hidden
        grads[at : at + hidden, :] = g_out[:, j * LANES : (j + 1) * LANES]


def upper(stage):
    (axis0, d0), (axis1, d1) = stage
    bit0 = lax.rem(lax.axis_index(axis0) // d0, 2)
    bit1 = lax.rem(lax.axis_index(axis1) // d1, 2)
    return jnp.where(lax.axis_index("feat") == 0, bit0, bit1)


def place(stage, own, got, out):
    m = own.shape[0]
    bit = upper(stage)
    out[pl.ds(pl.multiple_of(bit * m, m), m), :] = own[...].astype(out.dtype)
    out[pl.ds(pl.multiple_of((1 - bit) * m, m), m), :] = got[...].astype(out.dtype)


def sum_kernel(steps, *refs):
    n_in = sum(1 + (kind != "split") for kind, *_ in steps)
    n_out = len(steps) + 1 + max(group for *_, group, _ in steps)
    ins, outs, accs = refs[:n_in], refs[n_in : n_in + n_out], refs[n_in + n_out :]
    sends = outs[len(steps) :]
    for (kind, stage, back, at, group, to), out in zip(steps, outs):
        own, ins = ins[0], ins[1:]
        m = own.shape[0]
        send = sends[group].at[to : to + out.shape[0]]
        if kind != "split":
            got, ins = ins[0].at[at : at + m], ins[1:]
        if kind in ("split", "add_split"):
            if kind == "add_split":
                acc, accs = accs[0], accs[1:]
                acc[...] = own[...] + got[...].astype(F32)
                own = acc
            m = m // 2
            bit = upper(stage)
            out[...] = own[pl.ds(pl.multiple_of(bit * m, m), m), :]
            send[...] = own[pl.ds(pl.multiple_of((1 - bit) * m, m), m), :].astype(BF16)
        else:
            if kind == "place":
                place(back, own, got, out)
            else:
                out[...] = (own[...] + got[...].astype(F32)).astype(out.dtype)
            send[...] = out[...].astype(BF16)


def write_kernel(layer, stage, kept, halves, *refs):
    parts, (out_in, out_out, token, slab_in, slab_out, sem) = refs[kept:-6], refs[-6:]
    token[...] = jnp.zeros_like(token)
    bit = upper(stage)
    copies = []
    for part, (at, other) in zip(parts, halves):
        m = slab_in.size // LANES
        rows = part.at[at : at + m]
        upper_half = (1 - bit) if other else bit

        @pl.when(upper_half == 0)
        def _():
            write_slab(rows, slab_in, out_in.at[layer], sem.at[0])

        @pl.when(upper_half == 1)
        def _():
            write_slab(rows, slab_out, out_out.at[layer], sem.at[1])

        copies.append(upper_half)
    for upper_half in copies:

        @pl.when(upper_half == 0)
        def _():
            pltpu.make_async_copy(slab_in, out_in.at[layer], sem.at[0]).wait()

        @pl.when(upper_half == 1)
        def _():
            pltpu.make_async_copy(slab_out, out_out.at[layer], sem.at[1]).wait()


def write_slab(rows, slab, out, sem):
    n = slab.shape[0]
    for j in range(slab.shape[1] // LANES):
        slab[:, j * LANES : (j + 1) * LANES] = rows[j * n : (j + 1) * n, :].astype(F32)
    pltpu.make_async_copy(slab, out, sem).start()


class Sum:
    def __init__(self, whole, stages):
        self.own, self.got, self.stages, self.done = whole, None, stages, 0

    def next(self):
        n, i, rows = len(self.stages), self.done, self.own.shape[0]
        if i < n - 1:
            return "add_split" if i else "split", self.stages[i], None, rows // 2, F32
        if i == n - 1:
            return "add", self.stages[i], None, rows, F32
        stage = self.stages[2 * n - 2 - i]
        if i == n:
            return "add", stage, None, rows, BF16
        return "place", stage, self.stages[2 * n - 1 - i], rows * 2, BF16


def sum_step(sums, after):
    steps, ins, outs, scratch, groups = [], [], [], [], {}
    for one in sums:
        kind, stage, back, rows, dtype = one.next()
        group = groups.setdefault(stage, [len(groups), 0])
        steps.append((kind, stage, back, one.got and one.got[1], *group))
        group[1] += rows
        ins += [one.own, one.got[0]] if one.got else [one.own]
        outs.append(((rows, LANES), dtype))
        if kind == "add_split":
            scratch.append(pltpu.VMEM(one.own.shape, F32))
    made = call(
        functools.partial(sum_kernel, steps),
        outs + [((rows, LANES), BF16) for _, rows in groups.values()],
        ins,
        1,
        bytes_accessed=1,
        scratch=scratch,
        name="sum",
        after=after,
    )
    arrived = [swapped(x, stage) for x, stage in zip(made[len(sums) :], groups)]
    for one, own, (*_, group, at) in zip(sums, made, steps):
        one.own, one.got = own, (arrived[group], at)
        one.done += 1
    return [made[0]]


def gathered_grad(dtotal, back, returned, spread):
    far = jnp.concatenate([x[...] for x in returned], axis=0)
    return dtotal[...] + back[...] + mm(spread[...], far)


def join_kernel(layer, groups, *refs):
    dtotal, back, spread, remote_t, total = refs[:5]
    weights, refs = refs[5:9], refs[9:]
    returned, refs = refs[:groups], refs[groups:]
    received, outs = refs[: groups + 1], refs[groups + 1 :]
    grad = gathered_grad(dtotal, back, returned, spread)
    start_bwd(layer, norm_grad(grad, total[...]), weights, received, remote_t, outs)


def last_kernel(*refs):
    dtotal, back, spread = refs[:3]
    refs[-2][...] = gathered_grad(dtotal, back, refs[3:-2], spread)
    refs[-1][...] = jnp.zeros_like(refs[-1])


def around(x, axis, distance):
    n = lax.axis_size(axis)
    return lax.ppermute(x, axis, [(i, (i + distance) % n) for i in range(n)])


def over_mesh(x, target):
    chain, groups, cores = (lax.axis_size(axis) for axis in ("chain", "basin", "feat"))
    perm = []
    for c in range(chain):
        for b in range(groups):
            for feat in range(cores):
                to = target(c, b, feat)
                if to is not None:
                    start, end = (c * groups + b) * cores + feat, (to[0] * groups + to[1]) * cores
                    perm.append((start, end + feat))
    return lax.ppermute(x, ("chain", "basin", "feat"), perm)


def swapped(x, stage):
    def partner(c, b, feat):
        axis, d = stage[feat]
        return (c ^ d, b) if axis == "chain" else (c, b ^ d)

    return over_mesh(x, partner)


def forward(sends):
    chain = lax.axis_size("chain")

    def downstream(c, b, feat):
        return (c + 1, b) if c % 2 == feat and c + 1 < chain else None

    up = over_mesh(sends[0], downstream)
    return [up] + [around(x, "basin", s + 1) for s, x in enumerate(sends[1:])]


def backward(grads):
    chain = lax.axis_size("chain")
    up = lax.ppermute(grads[0], "chain", [(c, c - 1) for c in range(1, chain)])
    return [up] + [around(x, "basin", -s) for s, x in enumerate(grads) if s]


def shards(features, cotangent, w_in, w_out, block_index, block_values, send_rows, send_count):
    rows, latent = features.shape
    groups = lax.axis_size("basin")
    layers, _, half = w_in.shape
    far_rows = groups * BLOCK
    own = rows // BLOCK
    grad_scale = float(rows * lax.axis_size("chain") * groups) ** (-0.5)
    last = layers - 1

    def act16(n, m=latent):
        return ((n, m), BF16)

    wi1 = around(w_in, "feat", 1)
    wo1 = around(w_out, "feat", 1)
    ffn = 4 * latent * 2 * half

    live = jnp.arange(BLOCK, dtype=jnp.int32)[None, :] < send_count[0][:, None]
    sent = jnp.where(live, send_rows[0], -1)
    sources = block_index.T
    pick, spread, pick_self, features, *sends = call(
        functools.partial(setup_kernel, groups),
        [act16(max(groups - 1, 1) * BLOCK, rows), act16(rows, far_rows), act16(BLOCK, rows)]
        + [act16(rows)]
        + [act16(BLOCK)] * groups,
        [features, sent],
        2 * rows * far_rows * latent,
        name="setup",
    )
    weights = (w_in, wi1, w_out, wo1)
    inputs = [features]
    saved = []
    totals = []
    received = []
    for layer in range(layers):
        up, *others = forward(sends)
        if layer == 0:
            part, slope1 = call(
                half_kernel,
                [((rows, latent), F32), act16(rows, half)],
                [features, wi1, wo1],
                rows * ffn // 2,
                name="half",
            )
            msg, slope0, act_t, x_t = call(
                other_half_kernel,
                [act16(rows), act16(rows, half), act16(half, rows), act16(latent, rows)],
                [features, w_in, w_out, part],
                rows * ffn // 2,
                name="local0",
            )
            local, local_t, remote, remote_t = call(
                functools.partial(adjacency_kernel, groups),
                [act16(rows, rows), act16(rows, rows), act16(rows, far_rows), act16(far_rows, rows)],
                [sources, block_values, pick_self, msg],
                2 * rows * rows * BLOCK,
                scratch=[pltpu.VMEM((rows, rows + BLOCK + far_rows), F32)],
                name="adjacency",
                scalars=sources,
            )
            up, local = lax.optimization_barrier((up, local))
        else:
            msg, slope0, slope1, act_t, x_t = call(
                functools.partial(local_kernel, layer),
                [act16(rows), act16(rows, half), act16(rows, half)]
                + [act16(half, rows), act16(latent, rows)],
                [inputs[layer], *weights],
                rows * ffn,
                name=f"local{layer}",
            )
            up, msg = lax.optimization_barrier((up, msg))
        saved.append([slope0, slope1, act_t, x_t])
        received.append([up, around(up, "feat", 1), *others])
        (mixed,) = call(
            functools.partial(part_kernel, layer),
            [((rows, latent), F32)],
            [local, msg, remote, *weights, *others],
            2 * rows * rows * latent,
            name=f"part{layer}",
        )
        prev = totals[-1] if layer else features
        if layer < last:
            total, new, *sends = call(
                functools.partial(mix_kernel, layer),
                [((rows, latent), F32), act16(rows)] + [act16(BLOCK)] * groups,
                [prev, mixed, remote, pick, *weights, *received[layer][:2]],
                far_rows * ffn + 2 * rows * far_rows * latent,
                name=f"mix{layer}",
            )
            totals.append(total)
            inputs.append(new)
    bwd_outs = (
        [((rows, latent), F32), act16(rows), act16(far_rows), act16(far_rows)]
        + [act16(far_rows, half)] * 2
        + [act16(BLOCK)] * groups
    )
    outs = call(
        functools.partial(turn_kernel, last, groups),
        bwd_outs,
        [totals[-1], mixed, remote, remote_t, cotangent, *weights, *received[last]],
        2 * far_rows * ffn,
        name="turn",
    )
    grad_rows = 2 * latent * half // LANES

    def distances(axis):
        return [(axis, 1 << i) for i in range(lax.axis_size(axis).bit_length() - 1)]

    over_basin, over_chain = distances("basin"), distances("chain")
    n = len(over_basin)
    orders = over_basin + over_chain, over_chain[:n] + over_basin + over_chain[n:]
    stages = list(zip(*orders[::-1], strict=True))
    returned = {}
    sums = {}

    def back(layer, outs, after):
        returned[layer] = backward(outs[6:])
        grad, whole = call(
            functools.partial(back_kernel, layer, grad_scale),
            [((rows, latent), F32), ((grad_rows, LANES), F32)],
            [outs[1], local_t, *saved[layer], *weights, *outs[2:6]],
            3 * rows * ffn + 2 * rows * rows * latent,
            scratch=[
                pltpu.VMEM((rows, latent), BF16),
                pltpu.VMEM((rows, half), BF16),
            ],
            name=f"back{layer}",
            after=after,
        )
        sums[layer] = Sum(whole, stages)
        return [outs[0], grad], [grad]

    def join(layer, state, after):
        if layer:
            return call(
                functools.partial(join_kernel, layer - 1, groups),
                bwd_outs,
                [*state, spread, remote_t, totals[layer - 1]]
                + [*weights, *returned[layer], *received[layer - 1]],
                2 * far_rows * ffn,
                name=f"join{layer}",
                after=after,
            )
        return call(
            last_kernel,
            [((rows, latent), F32), ((8, LANES), F32)],
            [*state, spread, *returned[layer]],
            2 * rows * far_rows * latent,
            name="join0",
            after=after,
        )

    def write(layer, written, after, which=(0, 1)):
        ready = [(sums[layer].own, 0), sums[layer].got]
        ready = [ready[i] for i in which]
        kept = [*written, *after]
        return pl.pallas_call(
            functools.partial(
                write_kernel,
                layer,
                stages[0],
                len(kept),
                [(at, i) for (_, at), i in zip(ready, which)],
            ),
            out_shape=[
                jax.ShapeDtypeStruct((layers, latent, half), F32),
                jax.ShapeDtypeStruct((layers, half, latent), F32),
                jax.ShapeDtypeStruct((8, LANES), F32),
            ],
            in_specs=[ANY] * len(kept) + [VMEM] * len(ready),
            out_specs=[ANY] * 2 + [VMEM],
            scratch_shapes=[
                pltpu.VMEM((latent, half), F32),
                pltpu.VMEM((half, latent), F32),
                pltpu.SemaphoreType.DMA((2,)),
            ],
            input_output_aliases={i: i for i in range(len(written))},
            compiler_params=pltpu.CompilerParams(vmem_limit_bytes=LIMIT),
            cost_estimate=pl.CostEstimate(flops=1, bytes_accessed=1, transcendentals=0),
            name=f"write{layer}",
        )(*written, *after, *[x for x, _ in ready])

    count = 2 * len(stages) - 1
    at = []
    for layer in reversed(range(layers)):
        state, at = back(layer, outs, at)
        arrived = [sums[above].got[0] for above in range(layer + 2, layers)]
        if layer:
            arrived += returned[layer]
        at = sum_step([sums[layer]], at + arrived)
        if layer:
            for above in range(layer + 1, layers):
                at = sum_step([sums[above]], at)
            outs = join(layer, state, at)
            at = outs[1:2]
    while sums[0].done < count:
        for layer in reversed(range(layers)):
            if sums[layer].done < count:
                if layer == 0 and sums[0].done == count - 1:
                    at = at + [sums[above].got[0] for above in range(2, layers)]
                at = sum_step([sums[layer]], at)
    written = []
    for layer in reversed(range(1, layers)):
        *written, token = write(layer, written, at)
        at = [token]
    *written, token = write(0, written, at, (0,))
    grad, token = join(0, state, [token])
    *written, token = write(0, written, [token], (1,))
    return (grad, *written)


def solution(mesh):
    placed = (
        P(("runs", "chain", "basin"), None),
        P(("runs", "chain", "basin"), None),
        P(None, None, "feat"),
        P(None, "feat", None),
        P(("chain", "basin"), None),
        P(("chain", "basin"), None, None, None),
        P(("chain", "basin"), None, None),
        P(("chain", "basin"), None),
    )
    return jax.shard_map(
        shards,
        mesh=mesh,
        in_specs=placed,
        out_specs=(
            P(("runs", "chain", "basin"), None),
            P("runs", None, "feat"),
            P("runs", "feat", None),
        ),
        check_vma=False,
    )
```

```python
import functools

import jax
import jax.numpy as jnp
from jax import lax
from jax.experimental import pallas as pl
from jax.experimental.pallas import tpu as pltpu
from jax.sharding import PartitionSpec as P

BLOCK = 128
LANES = 128
EPS = 1e-06
F32 = jnp.float32
BF16 = jnp.bfloat16
VMEM = pl.BlockSpec(memory_space=pltpu.VMEM)
SMEM = pl.BlockSpec(memory_space=pltpu.SMEM)
ANY = pl.BlockSpec(memory_space=pl.ANY)
NN = (((1,), (0,)), ((), ()))
NT = (((1,), (1,)), ((), ()))
TN = (((0,), (0,)), ((), ()))


def mm(a, b, dims=NN):
    return lax.dot_general(a, b, dims, preferred_element_type=F32)


LIMIT = 24 * 1024 * 1024


def call(body, outs, ins, flops, scratch=(), name=None, after=(), bytes_accessed=4_000_000, scalars=None):
    skipped = len(after)
    return pl.pallas_call(
        lambda *refs: body(*refs[skipped:]),
        out_shape=[jax.ShapeDtypeStruct(s, d) for s, d in outs],
        in_specs=[ANY] * skipped + [SMEM if x is scalars else VMEM for x in ins],
        out_specs=[VMEM] * len(outs),
        scratch_shapes=list(scratch),
        compiler_params=pltpu.CompilerParams(vmem_limit_bytes=LIMIT),
        cost_estimate=pl.CostEstimate(
            flops=flops, bytes_accessed=bytes_accessed, transcendentals=0
        ),
        name=name,
    )(*after, *ins)


def sigmoid(v):
    return 1.0 / (1.0 + jnp.exp(-v))


def half_message(x, w_in, w_out):
    pre = mm(x, w_in)
    return mm((pre * sigmoid(pre)).astype(BF16), w_out)


def message_of(x, halves):
    total = None
    for w_in, w_out in halves:
        part = half_message(x, w_in, w_out)
        total = part if total is None else total + part
    return total.astype(BF16)


def message_grad(x, dmsg, halves):
    total = None
    kept = None
    for w_in, w_out in halves:
        pre = mm(x, w_in)
        sig = sigmoid(pre)
        dact = mm(dmsg, w_out, NT)
        dpre = (dact * (sig * (1.0 + pre * (1.0 - sig)))).astype(BF16)
        if kept is None:
            kept = ((pre * sig).astype(BF16), dpre)
        part = mm(dpre, w_in, NT)
        total = part if total is None else total + part
    return total, kept


def normed_of(total):
    scale = lax.rsqrt(jnp.mean(total * total, axis=-1, keepdims=True) + EPS)
    return scale, scale * total


def norm_grad(grad, total):
    scale, normed = normed_of(total)
    return scale * (grad - normed * jnp.mean(grad * normed, axis=-1, keepdims=True))


def setup_kernel(groups, features, sent, *refs):
    pick, spread, pick_self, held = refs[:4]
    sends = refs[4:]
    rows = features.shape[0]
    held[...] = features[...]
    b = lax.axis_index("basin")
    for route in range(-1, groups):
        if route == 0:
            chosen = lax.broadcasted_iota(jnp.int32, (1, BLOCK), 1) + (rows - BLOCK)
        else:
            chosen = sent[pl.ds(lax.rem(b + max(route, 0), groups), 1), :]
        across = jnp.broadcast_to(chosen, (BLOCK, BLOCK))
        down = across.T
        for r in range(0, rows, BLOCK):
            at = lax.broadcasted_iota(jnp.int32, (BLOCK, BLOCK), 1) + r
            hot = (down == at).astype(F32).astype(BF16)
            if route < 0:
                pick_self[:, r : r + BLOCK] = hot
                continue
            if route > 0:
                pick[(route - 1) * BLOCK : route * BLOCK, r : r + BLOCK] = hot
            at = lax.broadcasted_iota(jnp.int32, (BLOCK, BLOCK), 0) + r
            spread[r : r + BLOCK, route * BLOCK : (route + 1) * BLOCK] = (
                (across == at).astype(F32).astype(BF16)
            )
    pick_sends(features[...], pick, sends)


def pick_sends(rows, pick, sends):
    sends[0][...] = rows[rows.shape[0] - BLOCK :, :]
    for s, send in enumerate(sends[1:]):
        send[...] = mm(pick[s * BLOCK : (s + 1) * BLOCK, :], rows).astype(BF16)


def adjacency_kernel(groups, sources, values, pick_self, _, *refs):
    local, local_t, remote, remote_t, acc = refs
    rows = local.shape[0]
    own = rows // BLOCK
    b = lax.axis_index("basin")
    acc[...] = jnp.zeros_like(acc)
    for k in range(own):
        for t in range(values.shape[1]):
            v = sources[t, k]
            route = jnp.where(v == own, 0, lax.rem(b + groups - (v - own - 1), groups))
            far = jnp.where((v > own) & (route == 0), own, own + 1 + route)
            at = jnp.where(v < own, v, far)
            here = (pl.ds(k * BLOCK, BLOCK), pl.ds(pl.multiple_of(at * BLOCK, BLOCK), BLOCK))
            acc[here] += values[k, t].astype(F32)
    mine = acc[:, rows : rows + BLOCK].astype(BF16)
    full = acc[:, :rows] + mm(mine, pick_self[...])
    local[...] = full.astype(BF16)
    local_t[...] = full.T.astype(BF16)
    far = acc[:, rows + BLOCK :]
    remote[...] = far.astype(BF16)
    remote_t[...] = far.T.astype(BF16)


def message_half(x, w_in, w_out, slope, act_t=None):
    pre = mm(x, w_in)
    sig = sigmoid(pre)
    act = (pre * sig).astype(BF16)
    slope[...] = (sig * (1.0 + pre * (1.0 - sig))).astype(BF16)
    if act_t is not None:
        act_t[...] = act.T
    return mm(act, w_out)


def local_kernel(layer, x, wi0, wi1, wo0, wo1, msg, slope0, slope1, act_t, x_t):
    for r in range(0, x.shape[0], 256):
        here = slice(r, r + 256)
        rows = x[here, :]
        x_t[:, here] = rows.T
        part = message_half(rows, wi0[layer], wo0[layer], slope0.at[here, :], act_t.at[:, here])
        part = part + message_half(rows, wi1[layer], wo1[layer], slope1.at[here, :])
        msg[here, :] = part.astype(BF16)


def half_kernel(x, w_in, w_out, part, slope1):
    for r in range(0, x.shape[0], 256):
        here = slice(r, r + 256)
        part[here, :] = message_half(x[here, :], w_in[0], w_out[0], slope1.at[here, :])


def other_half_kernel(x, w_in, w_out, part, msg, slope0, act_t, x_t):
    for r in range(0, x.shape[0], 256):
        here = slice(r, r + 256)
        rows = x[here, :]
        x_t[:, here] = rows.T
        own = message_half(rows, w_in[0], w_out[0], slope0.at[here, :], act_t.at[:, here])
        msg[here, :] = (part[here, :] + own).astype(BF16)


def remote_mixed(layer, received, columns, weights):
    wi0, wi1, wo0, wo1 = weights
    halves = [(wi0[layer], wo0[layer]), (wi1[layer], wo1[layer])]
    far = jnp.concatenate([x[...] for x in received], axis=0)
    return mm(columns, message_of(far, halves))


def part_kernel(layer, *refs):
    local, msg, remote = refs[:3]
    weights, received, mixed = refs[3:7], refs[7:-1], refs[-1]
    total = mm(local[...], msg[...])
    if received:
        total = total + remote_mixed(layer, received, remote[:, BLOCK:], weights)
    mixed[...] = total


def upstream_rows(got, swapped_got):
    return got[...] + swapped_got[...]


def mixed_total(layer, state, mixed, up, remote, weights):
    return state + mixed[...] + remote_mixed(layer, [up], remote[:, :BLOCK], weights)


def mix_kernel(layer, *refs):
    prev, mixed, remote, pick = refs[:4]
    weights, up = refs[4:8], upstream_rows(*refs[8:10])
    total, inputs = refs[10:12]
    state = prev[...].astype(F32) if layer == 0 else normed_of(prev[...])[1]
    total[...] = mixed_total(layer, state, mixed, up, remote, weights)
    new = normed_of(total[...])[1].astype(BF16)
    inputs[...] = new
    pick_sends(new, pick, refs[12:])


def start_bwd(layer, dtotal_now, weights, received, remote_t, outs):
    dtotal, dround, far_x, far_dmsg, far_act, far_dpre = outs[:6]
    backs = outs[6:]
    wi0, wi1, wo0, wo1 = weights
    halves = [(wi0[layer], wo0[layer]), (wi1[layer], wo1[layer])]
    dtotal[...] = dtotal_now
    dround[...] = dtotal_now.astype(BF16)
    far_x[:BLOCK, :] = upstream_rows(*received[:2])
    for i, block in enumerate(received[2:]):
        far_x[(i + 1) * BLOCK : (i + 2) * BLOCK, :] = block[...]
    dmsg = mm(remote_t[...], dround[...]).astype(BF16)
    back, (act, dpre) = message_grad(far_x[...], dmsg, halves)
    far_dmsg[...] = dmsg
    far_act[...] = act
    far_dpre[...] = dpre
    for i, out in enumerate(backs):
        out[...] = back[i * BLOCK : (i + 1) * BLOCK, :].astype(BF16)


def turn_kernel(layer, groups, *refs):
    prev, mixed, remote, remote_t, cot = refs[:5]
    weights, received, outs = refs[5:9], refs[9 : 10 + groups], refs[10 + groups :]
    state = normed_of(prev[...])[1]
    total = mixed_total(layer, state, mixed, upstream_rows(*received[:2]), remote, weights)
    start_bwd(layer, norm_grad(cot[...], total), weights, received, remote_t, outs)


def back_kernel(layer, grad_scale, *refs):
    dround, local_t, slope0, slope1, act_t, x_t = refs[:6]
    wi0, wi1, wo0, wo1 = refs[6:10]
    far_x, far_dmsg, far_act, far_dpre = refs[10:14]
    back, grads, dmsg, dpre = refs[14:]
    dmsg[...] = mm(local_t[...], dround[...]).astype(BF16)
    for r in range(0, dmsg.shape[0], 256):
        here = slice(r, r + 256)
        rows = dmsg[here, :]
        dpre0 = (mm(rows, wo0[layer], NT) * slope0[here, :].astype(F32)).astype(BF16)
        dpre1 = (mm(rows, wo1[layer], NT) * slope1[here, :].astype(F32)).astype(BF16)
        dpre[here, :] = dpre0
        back[here, :] = mm(dpre0, wi0[layer], NT) + mm(dpre1, wi1[layer], NT)
    latent, hidden = x_t.shape[0], act_t.shape[0]
    g_in = (mm(x_t[...], dpre[...]) + mm(far_x[...], far_dpre[...], TN)) * grad_scale
    for j in range(hidden // LANES):
        grads[j * latent : (j + 1) * latent, :] = g_in[:, j * LANES : (j + 1) * LANES]
    g_out = (mm(act_t[...], dmsg[...]) + mm(far_act[...], far_dmsg[...], TN)) * grad_scale
    for j in range(latent // LANES):
        at = hidden // LANES * latent + j * hidden
        grads[at : at + hidden, :] = g_out[:, j * LANES : (j + 1) * LANES]


def upper(stage):
    (axis0, d0), (axis1, d1) = stage
    bit0 = lax.rem(lax.axis_index(axis0) // d0, 2)
    bit1 = lax.rem(lax.axis_index(axis1) // d1, 2)
    return jnp.where(lax.axis_index("feat") == 0, bit0, bit1)


def place(stage, own, got, out):
    m = own.shape[0]
    bit = upper(stage)
    out[pl.ds(pl.multiple_of(bit * m, m), m), :] = own[...].astype(out.dtype)
    out[pl.ds(pl.multiple_of((1 - bit) * m, m), m), :] = got[...].astype(out.dtype)


def sum_kernel(steps, *refs):
    n_in = sum(1 + (kind != "split") for kind, *_ in steps)
    n_out = len(steps) + 1 + max(group for *_, group, _ in steps)
    ins, outs, accs = refs[:n_in], refs[n_in : n_in + n_out], refs[n_in + n_out :]
    sends = outs[len(steps) :]
    for (kind, stage, back, at, group, to), out in zip(steps, outs):
        own, ins = ins[0], ins[1:]
        m = own.shape[0]
        send = sends[group].at[to : to + out.shape[0]]
        if kind != "split":
            got, ins = ins[0].at[at : at + m], ins[1:]
        if kind in ("split", "add_split"):
            if kind == "add_split":
                acc, accs = accs[0], accs[1:]
                acc[...] = own[...] + got[...].astype(F32)
                own = acc
            m = m // 2
            bit = upper(stage)
            out[...] = own[pl.ds(pl.multiple_of(bit * m, m), m), :]
            send[...] = own[pl.ds(pl.multiple_of((1 - bit) * m, m), m), :].astype(BF16)
        else:
            if kind == "place":
                place(back, own, got, out)
            else:
                out[...] = (own[...] + got[...].astype(F32)).astype(out.dtype)
            send[...] = out[...].astype(BF16)


def write_kernel(layer, stage, kept, halves, *refs):
    parts, (out_in, out_out, token, slab_in, slab_out, sem) = refs[kept:-6], refs[-6:]
    token[...] = jnp.zeros_like(token)
    bit = upper(stage)
    copies = []
    for part, (at, other) in zip(parts, halves):
        m = slab_in.size // LANES
        rows = part.at[at : at + m]
        upper_half = (1 - bit) if other else bit

        @pl.when(upper_half == 0)
        def _():
            write_slab(rows, slab_in, out_in.at[layer], sem.at[0])

        @pl.when(upper_half == 1)
        def _():
            write_slab(rows, slab_out, out_out.at[layer], sem.at[1])

        copies.append(upper_half)
    for upper_half in copies:

        @pl.when(upper_half == 0)
        def _():
            pltpu.make_async_copy(slab_in, out_in.at[layer], sem.at[0]).wait()

        @pl.when(upper_half == 1)
        def _():
            pltpu.make_async_copy(slab_out, out_out.at[layer], sem.at[1]).wait()


def write_slab(rows, slab, out, sem):
    n = slab.shape[0]
    for j in range(slab.shape[1] // LANES):
        slab[:, j * LANES : (j + 1) * LANES] = rows[j * n : (j + 1) * n, :].astype(F32)
    pltpu.make_async_copy(slab, out, sem).start()


class Sum:
    def __init__(self, whole, stages):
        self.own, self.got, self.stages, self.done = whole, None, stages, 0

    def next(self):
        n, i, rows = len(self.stages), self.done, self.own.shape[0]
        if i < n - 1:
            return "add_split" if i else "split", self.stages[i], None, rows // 2, F32
        if i == n - 1:
            return "add", self.stages[i], None, rows, F32
        stage = self.stages[2 * n - 2 - i]
        if i == n:
            return "add", stage, None, rows, BF16
        return "place", stage, self.stages[2 * n - 1 - i], rows * 2, BF16


def sum_step(sums, after):
    steps, ins, outs, scratch, groups = [], [], [], [], {}
    for one in sums:
        kind, stage, back, rows, dtype = one.next()
        group = groups.setdefault(stage, [len(groups), 0])
        steps.append((kind, stage, back, one.got and one.got[1], *group))
        group[1] += rows
        ins += [one.own, one.got[0]] if one.got else [one.own]
        outs.append(((rows, LANES), dtype))
        if kind == "add_split":
            scratch.append(pltpu.VMEM(one.own.shape, F32))
    made = call(
        functools.partial(sum_kernel, steps),
        outs + [((rows, LANES), BF16) for _, rows in groups.values()],
        ins,
        1,
        bytes_accessed=1,
        scratch=scratch,
        name="sum",
        after=after,
    )
    arrived = [swapped(x, stage) for x, stage in zip(made[len(sums) :], groups)]
    for one, own, (*_, group, at) in zip(sums, made, steps):
        one.own, one.got = own, (arrived[group], at)
        one.done += 1
    return [made[0]]


def gathered_grad(dtotal, back, returned, spread):
    up = upstream_rows(*returned[:2])
    far = jnp.concatenate([up, *(x[...] for x in returned[2:])], axis=0)
    return dtotal[...] + back[...] + mm(spread[...], far)


def join_kernel(layer, groups, *refs):
    dtotal, back, spread, remote_t, total = refs[:5]
    weights, refs = refs[5:9], refs[9:]
    returned, refs = refs[: groups + 1], refs[groups + 1 :]
    received, outs = refs[: groups + 1], refs[groups + 1 :]
    grad = gathered_grad(dtotal, back, returned, spread)
    start_bwd(layer, norm_grad(grad, total[...]), weights, received, remote_t, outs)


def last_kernel(*refs):
    dtotal, back, spread = refs[:3]
    refs[-2][...] = gathered_grad(dtotal, back, refs[3:-2], spread)
    refs[-1][...] = jnp.zeros_like(refs[-1])


def around(x, axis, distance):
    n = lax.axis_size(axis)
    return lax.ppermute(x, axis, [(i, (i + distance) % n) for i in range(n)])


def over_mesh(x, target):
    chain, groups, cores = (lax.axis_size(axis) for axis in ("chain", "basin", "feat"))
    perm = []
    for c in range(chain):
        for b in range(groups):
            for feat in range(cores):
                to = target(c, b, feat)
                if to is not None:
                    start, end = (c * groups + b) * cores + feat, (to[0] * groups + to[1]) * cores
                    perm.append((start, end + feat))
    return lax.ppermute(x, ("chain", "basin", "feat"), perm)


def swapped(x, stage):
    def partner(c, b, feat):
        axis, d = stage[feat]
        return (c ^ d, b) if axis == "chain" else (c, b ^ d)

    return over_mesh(x, partner)


def forward(sends):
    chain = lax.axis_size("chain")

    def downstream(c, b, feat):
        return (c + 1, b) if c % 2 == feat and c + 1 < chain else None

    others = [around(x, "basin", s + 1) for s, x in enumerate(sends[1:])]
    return [over_mesh(sends[0], downstream), *others]


def backward(grads):
    def upstream(c, b, feat):
        return (c - 1, b) if c % 2 != feat and c > 0 else None

    others = [around(x, "basin", -s) for s, x in enumerate(grads) if s]
    return [over_mesh(grads[0], upstream), *others]


def shards(features, cotangent, w_in, w_out, block_index, block_values, send_rows, send_count):
    rows, latent = features.shape
    groups = lax.axis_size("basin")
    layers, _, half = w_in.shape
    far_rows = groups * BLOCK
    own = rows // BLOCK
    grad_scale = float(rows * lax.axis_size("chain") * groups) ** (-0.5)
    last = layers - 1

    def act16(n, m=latent):
        return ((n, m), BF16)

    wi1 = around(w_in, "feat", 1)
    wo1 = around(w_out, "feat", 1)
    ffn = 4 * latent * 2 * half

    live = jnp.arange(BLOCK, dtype=jnp.int32)[None, :] < send_count[0][:, None]
    sent = jnp.where(live, send_rows[0], -1)
    sources = block_index.T
    pick, spread, pick_self, features, *sends = call(
        functools.partial(setup_kernel, groups),
        [act16(max(groups - 1, 1) * BLOCK, rows), act16(rows, far_rows), act16(BLOCK, rows)]
        + [act16(rows)]
        + [act16(BLOCK)] * groups,
        [features, sent],
        2 * rows * far_rows * latent,
        name="setup",
    )
    weights = (w_in, wi1, w_out, wo1)
    inputs = [features]
    saved = []
    totals = []
    received = []
    for layer in range(layers):
        up, *others = forward(sends)
        if layer == 0:
            part, slope1 = call(
                half_kernel,
                [((rows, latent), F32), act16(rows, half)],
                [features, wi1, wo1],
                rows * ffn // 2,
                name="half",
            )
            msg, slope0, act_t, x_t = call(
                other_half_kernel,
                [act16(rows), act16(rows, half), act16(half, rows), act16(latent, rows)],
                [features, w_in, w_out, part],
                rows * ffn // 2,
                name="local0",
            )
            local, local_t, remote, remote_t = call(
                functools.partial(adjacency_kernel, groups),
                [act16(rows, rows), act16(rows, rows), act16(rows, far_rows), act16(far_rows, rows)],
                [sources, block_values, pick_self, msg],
                2 * rows * rows * BLOCK,
                scratch=[pltpu.VMEM((rows, rows + BLOCK + far_rows), F32)],
                name="adjacency",
                scalars=sources,
            )
            up, local = lax.optimization_barrier((up, local))
        else:
            msg, slope0, slope1, act_t, x_t = call(
                functools.partial(local_kernel, layer),
                [act16(rows), act16(rows, half), act16(rows, half)]
                + [act16(half, rows), act16(latent, rows)],
                [inputs[layer], *weights],
                rows * ffn,
                name=f"local{layer}",
            )
            up, msg = lax.optimization_barrier((up, msg))
        saved.append([slope0, slope1, act_t, x_t])
        received.append([up, around(up, "feat", 1), *others])
        (mixed,) = call(
            functools.partial(part_kernel, layer),
            [((rows, latent), F32)],
            [local, msg, remote, *weights, *others],
            2 * rows * rows * latent,
            name=f"part{layer}",
        )
        prev = totals[-1] if layer else features
        if layer < last:
            total, new, *sends = call(
                functools.partial(mix_kernel, layer),
                [((rows, latent), F32), act16(rows)] + [act16(BLOCK)] * groups,
                [prev, mixed, remote, pick, *weights, *received[layer][:2]],
                far_rows * ffn + 2 * rows * far_rows * latent,
                name=f"mix{layer}",
            )
            totals.append(total)
            inputs.append(new)
    bwd_outs = (
        [((rows, latent), F32), act16(rows), act16(far_rows), act16(far_rows)]
        + [act16(far_rows, half)] * 2
        + [act16(BLOCK)] * groups
    )
    outs = call(
        functools.partial(turn_kernel, last, groups),
        bwd_outs,
        [totals[-1], mixed, remote, remote_t, cotangent, *weights, *received[last]],
        2 * far_rows * ffn,
        name="turn",
    )
    grad_rows = 2 * latent * half // LANES

    def distances(axis):
        return [(axis, 1 << i) for i in range(lax.axis_size(axis).bit_length() - 1)]

    over_basin, over_chain = distances("basin"), distances("chain")
    n = len(over_basin)
    orders = over_basin + over_chain, over_chain[:n] + over_basin + over_chain[n:]
    stages = list(zip(*orders, strict=True))
    returned = {}
    sums = {}

    def back(layer, outs, after):
        up, *others = backward(outs[6:])
        grad, whole = call(
            functools.partial(back_kernel, layer, grad_scale),
            [((rows, latent), F32), ((grad_rows, LANES), F32)],
            [outs[1], local_t, *saved[layer], *weights, *outs[2:6]],
            3 * rows * ffn + 2 * rows * rows * latent,
            scratch=[
                pltpu.VMEM((rows, latent), BF16),
                pltpu.VMEM((rows, half), BF16),
            ],
            name=f"back{layer}",
            after=after,
        )
        if layer:
            up, grad, others = lax.optimization_barrier((up, grad, others))
            others = [around(up, "feat", 1), *others]
        returned[layer] = [up, *others]
        sums[layer] = Sum(whole, stages)
        return [outs[0], grad], [grad]

    def join(layer, state, after):
        if layer:
            return call(
                functools.partial(join_kernel, layer - 1, groups),
                bwd_outs,
                [*state, spread, remote_t, totals[layer - 1]]
                + [*weights, *returned[layer], *received[layer - 1]],
                2 * far_rows * ffn,
                name=f"join{layer}",
                after=after,
            )
        return call(
            last_kernel,
            [((rows, latent), F32), ((8, LANES), F32)],
            [*state, spread, *returned[layer]],
            2 * rows * far_rows * latent,
            name="join0",
            after=after,
        )

    def write(layer, written, after, which=(0, 1)):
        ready = [(sums[layer].own, 0), sums[layer].got]
        ready = [ready[i] for i in which]
        kept = [*written, *after]
        return pl.pallas_call(
            functools.partial(
                write_kernel,
                layer,
                stages[0],
                len(kept),
                [(at, i) for (_, at), i in zip(ready, which)],
            ),
            out_shape=[
                jax.ShapeDtypeStruct((layers, latent, half), F32),
                jax.ShapeDtypeStruct((layers, half, latent), F32),
                jax.ShapeDtypeStruct((8, LANES), F32),
            ],
            in_specs=[ANY] * len(kept) + [VMEM] * len(ready),
            out_specs=[ANY] * 2 + [VMEM],
            scratch_shapes=[
                pltpu.VMEM((latent, half), F32),
                pltpu.VMEM((half, latent), F32),
                pltpu.SemaphoreType.DMA((2,)),
            ],
            input_output_aliases={i: i for i in range(len(written))},
            compiler_params=pltpu.CompilerParams(vmem_limit_bytes=LIMIT),
            cost_estimate=pl.CostEstimate(flops=1, bytes_accessed=1, transcendentals=0),
            name=f"write{layer}",
        )(*written, *after, *[x for x, _ in ready])

    count = 2 * len(stages) - 1
    at = []
    for layer in reversed(range(layers)):
        state, at = back(layer, outs, at)
        arrived = [sums[above].got[0] for above in range(layer + 2, layers)]
        if layer:
            arrived += [returned[layer][0], *returned[layer][2:]]
        at = sum_step([sums[layer]], at + arrived)
        if layer:
            for above in range(layer + 1, layers):
                at = sum_step([sums[above]], at)
            outs = join(layer, state, at)
            at = outs[1:2]
    while sums[0].done < count:
        for layer in reversed(range(layers)):
            if sums[layer].done < count:
                if layer == 0 and sums[0].done == count - 1:
                    at = at + [sums[above].got[0] for above in range(2, layers)]
                at = sum_step([sums[layer]], at)
    written = []
    for layer in reversed(range(1, layers)):
        *written, token = write(layer, written, at)
        at = [token]
        if layer == last:
            up, *others = returned[0]
            up, token, others = lax.optimization_barrier((up, token, others))
            returned[0] = [up, around(up, "feat", 1), *others]
            at = [token]
    *written, token = write(0, written, at, (0,))
    grad, token = join(0, state, [token])
    *written, token = write(0, written, [token], (1,))
    return (grad, *written)


def solution(mesh):
    placed = (
        P(("runs", "chain", "basin"), None),
        P(("runs", "chain", "basin"), None),
        P(None, None, "feat"),
        P(None, "feat", None),
        P(("chain", "basin"), None),
        P(("chain", "basin"), None, None, None),
        P(("chain", "basin"), None, None),
        P(("chain", "basin"), None),
    )
    return jax.shard_map(
        shards,
        mesh=mesh,
        in_specs=placed,
        out_specs=(
            P(("runs", "chain", "basin"), None),
            P("runs", None, "feat"),
            P("runs", "feat", None),
        ),
        check_vma=False,
    )
```

```python
import functools

import jax
import jax.numpy as jnp
from jax import lax
from jax.experimental import pallas as pl
from jax.experimental.pallas import tpu as pltpu
from jax.sharding import PartitionSpec as P

BLOCK = 128
LANES = 128
EPS = 1e-06
F32 = jnp.float32
BF16 = jnp.bfloat16
VMEM = pl.BlockSpec(memory_space=pltpu.VMEM)
SMEM = pl.BlockSpec(memory_space=pltpu.SMEM)
ANY = pl.BlockSpec(memory_space=pl.ANY)
NN = (((1,), (0,)), ((), ()))
NT = (((1,), (1,)), ((), ()))
TN = (((0,), (0,)), ((), ()))


def mm(a, b, dims=NN):
    return lax.dot_general(a, b, dims, preferred_element_type=F32)


LIMIT = 24 * 1024 * 1024


def call(body, outs, ins, flops, scratch=(), name=None, after=(), bytes_accessed=4_000_000, scalars=None):
    skipped = len(after)
    return pl.pallas_call(
        lambda *refs: body(*refs[skipped:]),
        out_shape=[jax.ShapeDtypeStruct(s, d) for s, d in outs],
        in_specs=[ANY] * skipped + [SMEM if x is scalars else VMEM for x in ins],
        out_specs=[VMEM] * len(outs),
        scratch_shapes=list(scratch),
        compiler_params=pltpu.CompilerParams(vmem_limit_bytes=LIMIT),
        cost_estimate=pl.CostEstimate(
            flops=flops, bytes_accessed=bytes_accessed, transcendentals=0
        ),
        name=name,
    )(*after, *ins)


def sigmoid(v):
    return 1.0 / (1.0 + jnp.exp(-v))


def half_message(x, w_in, w_out):
    pre = mm(x, w_in)
    return mm((pre * sigmoid(pre)).astype(BF16), w_out)


def message_of(x, halves):
    total = None
    for w_in, w_out in halves:
        part = half_message(x, w_in, w_out)
        total = part if total is None else total + part
    return total.astype(BF16)


def message_grad(x, dmsg, halves):
    total = None
    kept = None
    for w_in, w_out in halves:
        pre = mm(x, w_in)
        sig = sigmoid(pre)
        dact = mm(dmsg, w_out, NT)
        dpre = (dact * (sig * (1.0 + pre * (1.0 - sig)))).astype(BF16)
        if kept is None:
            kept = ((pre * sig).astype(BF16), dpre)
        part = mm(dpre, w_in, NT)
        total = part if total is None else total + part
    return total, kept


def normed_of(total):
    scale = lax.rsqrt(jnp.mean(total * total, axis=-1, keepdims=True) + EPS)
    return scale, scale * total


def norm_grad(grad, total):
    scale, normed = normed_of(total)
    return scale * (grad - normed * jnp.mean(grad * normed, axis=-1, keepdims=True))


def setup_kernel(groups, features, sent, *refs):
    pick, spread, pick_self, held = refs[:4]
    sends = refs[4:]
    rows = features.shape[0]
    held[...] = features[...]
    b = lax.axis_index("basin")
    for route in range(-1, groups):
        if route == 0:
            chosen = lax.broadcasted_iota(jnp.int32, (1, BLOCK), 1) + (rows - BLOCK)
        else:
            chosen = sent[pl.ds(lax.rem(b + max(route, 0), groups), 1), :]
        across = jnp.broadcast_to(chosen, (BLOCK, BLOCK))
        down = across.T
        for r in range(0, rows, BLOCK):
            at = lax.broadcasted_iota(jnp.int32, (BLOCK, BLOCK), 1) + r
            hot = (down == at).astype(F32).astype(BF16)
            if route < 0:
                pick_self[:, r : r + BLOCK] = hot
                continue
            if route > 0:
                pick[(route - 1) * BLOCK : route * BLOCK, r : r + BLOCK] = hot
            at = lax.broadcasted_iota(jnp.int32, (BLOCK, BLOCK), 0) + r
            spread[r : r + BLOCK, route * BLOCK : (route + 1) * BLOCK] = (
                (across == at).astype(F32).astype(BF16)
            )
    pick_sends(features[...], pick, sends)


def pick_sends(rows, pick, sends):
    sends[0][...] = rows[rows.shape[0] - BLOCK :, :]
    for s, send in enumerate(sends[1:]):
        send[...] = mm(pick[s * BLOCK : (s + 1) * BLOCK, :], rows).astype(BF16)


def adjacency_kernel(groups, sources, values, pick_self, _, *refs):
    local, local_t, remote, remote_t, acc = refs
    rows = local.shape[0]
    own = rows // BLOCK
    b = lax.axis_index("basin")
    acc[...] = jnp.zeros_like(acc)
    for k in range(own):
        for t in range(values.shape[1]):
            v = sources[t, k]
            route = jnp.where(v == own, 0, lax.rem(b + groups - (v - own - 1), groups))
            far = jnp.where((v > own) & (route == 0), own, own + 1 + route)
            at = jnp.where(v < own, v, far)
            here = (pl.ds(k * BLOCK, BLOCK), pl.ds(pl.multiple_of(at * BLOCK, BLOCK), BLOCK))
            acc[here] += values[k, t].astype(F32)
    mine = acc[:, rows : rows + BLOCK].astype(BF16)
    full = acc[:, :rows] + mm(mine, pick_self[...])
    local[...] = full.astype(BF16)
    local_t[...] = full.T.astype(BF16)
    far = acc[:, rows + BLOCK :]
    remote[...] = far.astype(BF16)
    remote_t[...] = far.T.astype(BF16)


def message_half(x, w_in, w_out, slope, act_t=None):
    pre = mm(x, w_in)
    sig = sigmoid(pre)
    act = (pre * sig).astype(BF16)
    slope[...] = (sig * (1.0 + pre * (1.0 - sig))).astype(BF16)
    if act_t is not None:
        act_t[...] = act.T
    return mm(act, w_out)


def local_kernel(layer, x, wi0, wi1, wo0, wo1, msg, slope0, slope1, act_t, x_t):
    for r in range(0, x.shape[0], 256):
        here = slice(r, r + 256)
        rows = x[here, :]
        x_t[:, here] = rows.T
        part = message_half(rows, wi0[layer], wo0[layer], slope0.at[here, :], act_t.at[:, here])
        part = part + message_half(rows, wi1[layer], wo1[layer], slope1.at[here, :])
        msg[here, :] = part.astype(BF16)


def half_kernel(x, w_in, w_out, part, slope1):
    for r in range(0, x.shape[0], 256):
        here = slice(r, r + 256)
        part[here, :] = message_half(x[here, :], w_in[0], w_out[0], slope1.at[here, :])


def other_half_kernel(x, w_in, w_out, part, msg, slope0, act_t, x_t):
    for r in range(0, x.shape[0], 256):
        here = slice(r, r + 256)
        rows = x[here, :]
        x_t[:, here] = rows.T
        own = message_half(rows, w_in[0], w_out[0], slope0.at[here, :], act_t.at[:, here])
        msg[here, :] = (part[here, :] + own).astype(BF16)


def remote_mixed(layer, received, columns, weights):
    wi0, wi1, wo0, wo1 = weights
    halves = [(wi0[layer], wo0[layer]), (wi1[layer], wo1[layer])]
    far = jnp.concatenate([x[...] for x in received], axis=0)
    return mm(columns, message_of(far, halves))


def part_kernel(layer, *refs):
    local, msg, remote = refs[:3]
    weights, received, mixed = refs[3:7], refs[7:-1], refs[-1]
    total = mm(local[...], msg[...])
    if received:
        total = total + remote_mixed(layer, received, remote[:, BLOCK:], weights)
    mixed[...] = total


def upstream_rows(got, swapped_got):
    return got[...] + swapped_got[...]


def mixed_total(layer, state, mixed, up, remote, weights):
    return state + mixed[...] + remote_mixed(layer, [up], remote[:, :BLOCK], weights)


def mix_kernel(layer, *refs):
    prev, mixed, remote, pick = refs[:4]
    weights, up = refs[4:8], upstream_rows(*refs[8:10])
    total, inputs = refs[10:12]
    state = prev[...].astype(F32) if layer == 0 else normed_of(prev[...])[1]
    total[...] = mixed_total(layer, state, mixed, up, remote, weights)
    new = normed_of(total[...])[1].astype(BF16)
    inputs[...] = new
    pick_sends(new, pick, refs[12:])


def start_bwd(layer, dtotal_now, weights, received, remote_t, outs):
    dtotal, dround, far_x, far_dmsg, far_act, far_dpre = outs[:6]
    backs = outs[6:]
    wi0, wi1, wo0, wo1 = weights
    halves = [(wi0[layer], wo0[layer]), (wi1[layer], wo1[layer])]
    dtotal[...] = dtotal_now
    dround[...] = dtotal_now.astype(BF16)
    far_x[:BLOCK, :] = upstream_rows(*received[:2])
    for i, block in enumerate(received[2:]):
        far_x[(i + 1) * BLOCK : (i + 2) * BLOCK, :] = block[...]
    dmsg = mm(remote_t[...], dround[...]).astype(BF16)
    back, (act, dpre) = message_grad(far_x[...], dmsg, halves)
    far_dmsg[...] = dmsg
    far_act[...] = act
    far_dpre[...] = dpre
    for i, out in enumerate(backs):
        out[...] = back[i * BLOCK : (i + 1) * BLOCK, :].astype(BF16)


def turn_kernel(layer, groups, *refs):
    prev, mixed, remote, remote_t, cot = refs[:5]
    weights, received, outs = refs[5:9], refs[9 : 10 + groups], refs[10 + groups :]
    state = normed_of(prev[...])[1]
    total = mixed_total(layer, state, mixed, upstream_rows(*received[:2]), remote, weights)
    start_bwd(layer, norm_grad(cot[...], total), weights, received, remote_t, outs)


def back_kernel(layer, grad_scale, *refs):
    dround, local_t, slope0, slope1, act_t, x_t = refs[:6]
    wi0, wi1, wo0, wo1 = refs[6:10]
    far_x, far_dmsg, far_act, far_dpre = refs[10:14]
    back, grads, dmsg, dpre = refs[14:]
    dmsg[...] = mm(local_t[...], dround[...]).astype(BF16)
    for r in range(0, dmsg.shape[0], 256):
        here = slice(r, r + 256)
        rows = dmsg[here, :]
        dpre0 = (mm(rows, wo0[layer], NT) * slope0[here, :].astype(F32)).astype(BF16)
        dpre1 = (mm(rows, wo1[layer], NT) * slope1[here, :].astype(F32)).astype(BF16)
        dpre[here, :] = dpre0
        back[here, :] = mm(dpre0, wi0[layer], NT) + mm(dpre1, wi1[layer], NT)
    latent, hidden = x_t.shape[0], act_t.shape[0]
    g_in = (mm(x_t[...], dpre[...]) + mm(far_x[...], far_dpre[...], TN)) * grad_scale
    for j in range(hidden // LANES):
        grads[j * latent : (j + 1) * latent, :] = g_in[:, j * LANES : (j + 1) * LANES]
    g_out = (mm(act_t[...], dmsg[...]) + mm(far_act[...], far_dmsg[...], TN)) * grad_scale
    for j in range(latent // LANES):
        at = hidden // LANES * latent + j * hidden
        grads[at : at + hidden, :] = g_out[:, j * LANES : (j + 1) * LANES]


def upper(stage):
    (axis0, d0), (axis1, d1) = stage
    bit0 = lax.rem(lax.axis_index(axis0) // d0, 2)
    bit1 = lax.rem(lax.axis_index(axis1) // d1, 2)
    return jnp.where(lax.axis_index("feat") == 0, bit0, bit1)


def place(stage, own, got, out):
    m = own.shape[0]
    bit = upper(stage)
    out[pl.ds(pl.multiple_of(bit * m, m), m), :] = own[...].astype(out.dtype)
    out[pl.ds(pl.multiple_of((1 - bit) * m, m), m), :] = got[...].astype(out.dtype)


def sum_kernel(steps, *refs):
    n_in = sum(1 + (kind != "split") for kind, *_ in steps)
    n_out = len(steps) + 1 + max(group for *_, group, _ in steps)
    ins, outs, accs = refs[:n_in], refs[n_in : n_in + n_out], refs[n_in + n_out :]
    sends = outs[len(steps) :]
    for (kind, stage, back, at, group, to), out in zip(steps, outs):
        own, ins = ins[0], ins[1:]
        m = own.shape[0]
        send = sends[group].at[to : to + out.shape[0]]
        if kind != "split":
            got, ins = ins[0].at[at : at + m], ins[1:]
        if kind in ("split", "add_split"):
            if kind == "add_split":
                acc, accs = accs[0], accs[1:]
                acc[...] = own[...] + got[...].astype(F32)
                own = acc
            m = m // 2
            bit = upper(stage)
            out[...] = own[pl.ds(pl.multiple_of(bit * m, m), m), :]
            send[...] = own[pl.ds(pl.multiple_of((1 - bit) * m, m), m), :].astype(BF16)
        else:
            if kind == "place":
                place(back, own, got, out)
            else:
                out[...] = (own[...] + got[...].astype(F32)).astype(out.dtype)
            send[...] = out[...].astype(BF16)


def write_kernel(layer, stage, kept, halves, *refs):
    parts, (out_in, out_out, token, slab_in, slab_out, sem) = refs[kept:-6], refs[-6:]
    token[...] = jnp.zeros_like(token)
    bit = upper(stage)
    copies = []
    for part, (at, other) in zip(parts, halves):
        m = slab_in.size // LANES
        rows = part.at[at : at + m]
        upper_half = (1 - bit) if other else bit

        @pl.when(upper_half == 0)
        def _():
            write_slab(rows, slab_in, out_in.at[layer], sem.at[0])

        @pl.when(upper_half == 1)
        def _():
            write_slab(rows, slab_out, out_out.at[layer], sem.at[1])

        copies.append(upper_half)
    for upper_half in copies:

        @pl.when(upper_half == 0)
        def _():
            pltpu.make_async_copy(slab_in, out_in.at[layer], sem.at[0]).wait()

        @pl.when(upper_half == 1)
        def _():
            pltpu.make_async_copy(slab_out, out_out.at[layer], sem.at[1]).wait()


def write_slab(rows, slab, out, sem):
    n = slab.shape[0]
    for j in range(slab.shape[1] // LANES):
        slab[:, j * LANES : (j + 1) * LANES] = rows[j * n : (j + 1) * n, :].astype(F32)
    pltpu.make_async_copy(slab, out, sem).start()


class Sum:
    def __init__(self, whole, stages):
        self.own, self.got, self.stages, self.done = whole, None, stages, 0

    def next(self):
        n, i, rows = len(self.stages), self.done, self.own.shape[0]
        if i < n - 1:
            return "add_split" if i else "split", self.stages[i], None, rows // 2, F32
        if i == n - 1:
            return "add", self.stages[i], None, rows, F32
        stage = self.stages[2 * n - 2 - i]
        if i == n:
            return "add", stage, None, rows, BF16
        return "place", stage, self.stages[2 * n - 1 - i], rows * 2, BF16


def sum_step(sums, after):
    steps, ins, outs, scratch, groups = [], [], [], [], {}
    for one in sums:
        kind, stage, back, rows, dtype = one.next()
        group = groups.setdefault(stage, [len(groups), 0])
        steps.append((kind, stage, back, one.got and one.got[1], *group))
        group[1] += rows
        ins += [one.own, one.got[0]] if one.got else [one.own]
        outs.append(((rows, LANES), dtype))
        if kind == "add_split":
            scratch.append(pltpu.VMEM(one.own.shape, F32))
    made = call(
        functools.partial(sum_kernel, steps),
        outs + [((rows, LANES), BF16) for _, rows in groups.values()],
        ins,
        1,
        bytes_accessed=1,
        scratch=scratch,
        name="sum",
        after=after,
    )
    arrived = [swapped(x, stage) for x, stage in zip(made[len(sums) :], groups)]
    for one, own, (*_, group, at) in zip(sums, made, steps):
        one.own, one.got = own, (arrived[group], at)
        one.done += 1
    return [made[0]]


def gathered_grad(dtotal, back, returned, spread):
    far = jnp.concatenate([x[...] for x in returned], axis=0)
    return dtotal[...] + back[...] + mm(spread[...], far)


def join_kernel(layer, groups, *refs):
    dtotal, back, spread, remote_t, total = refs[:5]
    weights, refs = refs[5:9], refs[9:]
    returned, refs = refs[:groups], refs[groups:]
    received, outs = refs[: groups + 1], refs[groups + 1 :]
    grad = gathered_grad(dtotal, back, returned, spread)
    start_bwd(layer, norm_grad(grad, total[...]), weights, received, remote_t, outs)


def last_kernel(*refs):
    dtotal, back, spread = refs[:3]
    refs[-2][...] = gathered_grad(dtotal, back, refs[3:-2], spread)
    refs[-1][...] = jnp.zeros_like(refs[-1])


def around(x, axis, distance):
    n = lax.axis_size(axis)
    return lax.ppermute(x, axis, [(i, (i + distance) % n) for i in range(n)])


def over_mesh(x, target):
    chain, groups, cores = (lax.axis_size(axis) for axis in ("chain", "basin", "feat"))
    perm = []
    for c in range(chain):
        for b in range(groups):
            for feat in range(cores):
                to = target(c, b, feat)
                if to is not None:
                    start, end = (c * groups + b) * cores + feat, (to[0] * groups + to[1]) * cores
                    perm.append((start, end + feat))
    return lax.ppermute(x, ("chain", "basin", "feat"), perm)


def swapped(x, stage):
    def partner(c, b, feat):
        axis, d = stage[feat]
        return (c ^ d, b) if axis == "chain" else (c, b ^ d)

    return over_mesh(x, partner)


def forward(sends):
    chain = lax.axis_size("chain")

    def downstream(c, b, feat):
        return (c + 1, b) if c % 2 == feat and c + 1 < chain else None

    up = over_mesh(sends[0], downstream)
    return [up] + [around(x, "basin", s + 1) for s, x in enumerate(sends[1:])]


def backward(grads):
    chain = lax.axis_size("chain")
    up = lax.ppermute(grads[0], "chain", [(c, c - 1) for c in range(1, chain)])
    return [up] + [around(x, "basin", -s) for s, x in enumerate(grads) if s]


def shards(features, cotangent, w_in, w_out, block_index, block_values, send_rows, send_count):
    rows, latent = features.shape
    groups = lax.axis_size("basin")
    layers, _, half = w_in.shape
    far_rows = groups * BLOCK
    own = rows // BLOCK
    grad_scale = float(rows * lax.axis_size("chain") * groups) ** (-0.5)
    last = layers - 1

    def act16(n, m=latent):
        return ((n, m), BF16)

    wi1 = around(w_in, "feat", 1)
    wo1 = around(w_out, "feat", 1)
    ffn = 4 * latent * 2 * half

    live = jnp.arange(BLOCK, dtype=jnp.int32)[None, :] < send_count[0][:, None]
    sent = jnp.where(live, send_rows[0], -1)
    sources = block_index.T
    pick, spread, pick_self, features, *sends = call(
        functools.partial(setup_kernel, groups),
        [act16(max(groups - 1, 1) * BLOCK, rows), act16(rows, far_rows), act16(BLOCK, rows)]
        + [act16(rows)]
        + [act16(BLOCK)] * groups,
        [features, sent],
        2 * rows * far_rows * latent,
        name="setup",
    )
    weights = (w_in, wi1, w_out, wo1)
    inputs = [features]
    saved = []
    totals = []
    received = []
    for layer in range(layers):
        up, *others = forward(sends)
        if layer == 0:
            part, slope1 = call(
                half_kernel,
                [((rows, latent), F32), act16(rows, half)],
                [features, wi1, wo1],
                rows * ffn // 2,
                name="half",
            )
            msg, slope0, act_t, x_t = call(
                other_half_kernel,
                [act16(rows), act16(rows, half), act16(half, rows), act16(latent, rows)],
                [features, w_in, w_out, part],
                rows * ffn // 2,
                name="local0",
            )
            local, local_t, remote, remote_t = call(
                functools.partial(adjacency_kernel, groups),
                [act16(rows, rows), act16(rows, rows), act16(rows, far_rows), act16(far_rows, rows)],
                [sources, block_values, pick_self, msg],
                2 * rows * rows * BLOCK,
                scratch=[pltpu.VMEM((rows, rows + BLOCK + far_rows), F32)],
                name="adjacency",
                scalars=sources,
            )
            up, local = lax.optimization_barrier((up, local))
        else:
            msg, slope0, slope1, act_t, x_t = call(
                functools.partial(local_kernel, layer),
                [act16(rows), act16(rows, half), act16(rows, half)]
                + [act16(half, rows), act16(latent, rows)],
                [inputs[layer], *weights],
                rows * ffn,
                name=f"local{layer}",
            )
            up, msg = lax.optimization_barrier((up, msg))
        saved.append([slope0, slope1, act_t, x_t])
        received.append([up, around(up, "feat", 1), *others])
        (mixed,) = call(
            functools.partial(part_kernel, layer),
            [((rows, latent), F32)],
            [local, msg, remote, *weights, *others],
            2 * rows * rows * latent,
            name=f"part{layer}",
        )
        prev = totals[-1] if layer else features
        if layer < last:
            total, new, *sends = call(
                functools.partial(mix_kernel, layer),
                [((rows, latent), F32), act16(rows)] + [act16(BLOCK)] * groups,
                [prev, mixed, remote, pick, *weights, *received[layer][:2]],
                far_rows * ffn + 2 * rows * far_rows * latent,
                name=f"mix{layer}",
            )
            totals.append(total)
            inputs.append(new)
    bwd_outs = (
        [((rows, latent), F32), act16(rows), act16(far_rows), act16(far_rows)]
        + [act16(far_rows, half)] * 2
        + [act16(BLOCK)] * groups
    )
    outs = call(
        functools.partial(turn_kernel, last, groups),
        bwd_outs,
        [totals[-1], mixed, remote, remote_t, cotangent, *weights, *received[last]],
        2 * far_rows * ffn,
        name="turn",
    )
    grad_rows = 2 * latent * half // LANES

    def distances(axis):
        return [(axis, 1 << i) for i in range(lax.axis_size(axis).bit_length() - 1)]

    over_basin, over_chain = distances("basin"), distances("chain")
    n = len(over_basin)
    orders = over_basin + over_chain, over_chain[:n] + over_basin + over_chain[n:]
    stages = list(zip(*orders, strict=True)), list(zip(*orders[::-1], strict=True))
    returned = {}
    sums = {}

    def back(layer, outs, after):
        returned[layer] = backward(outs[6:])
        grad, whole = call(
            functools.partial(back_kernel, layer, grad_scale),
            [((rows, latent), F32), ((grad_rows, LANES), F32)],
            [outs[1], local_t, *saved[layer], *weights, *outs[2:6]],
            3 * rows * ffn + 2 * rows * rows * latent,
            scratch=[
                pltpu.VMEM((rows, latent), BF16),
                pltpu.VMEM((rows, half), BF16),
            ],
            name=f"back{layer}",
            after=after,
        )
        sums[layer] = Sum(whole, stages[layer % 2])
        return [outs[0], grad], [grad]

    def join(layer, state, after):
        if layer:
            return call(
                functools.partial(join_kernel, layer - 1, groups),
                bwd_outs,
                [*state, spread, remote_t, totals[layer - 1]]
                + [*weights, *returned[layer], *received[layer - 1]],
                2 * far_rows * ffn,
                name=f"join{layer}",
                after=after,
            )
        return call(
            last_kernel,
            [((rows, latent), F32), ((8, LANES), F32)],
            [*state, spread, *returned[layer]],
            2 * rows * far_rows * latent,
            name="join0",
            after=after,
        )

    def write(layer, written, after, which=(0, 1)):
        ready = [(sums[layer].own, 0), sums[layer].got]
        ready = [ready[i] for i in which]
        kept = [*written, *after]
        return pl.pallas_call(
            functools.partial(
                write_kernel,
                layer,
                stages[layer % 2][0],
                len(kept),
                [(at, i) for (_, at), i in zip(ready, which)],
            ),
            out_shape=[
                jax.ShapeDtypeStruct((layers, latent, half), F32),
                jax.ShapeDtypeStruct((layers, half, latent), F32),
                jax.ShapeDtypeStruct((8, LANES), F32),
            ],
            in_specs=[ANY] * len(kept) + [VMEM] * len(ready),
            out_specs=[ANY] * 2 + [VMEM],
            scratch_shapes=[
                pltpu.VMEM((latent, half), F32),
                pltpu.VMEM((half, latent), F32),
                pltpu.SemaphoreType.DMA((2,)),
            ],
            input_output_aliases={i: i for i in range(len(written))},
            compiler_params=pltpu.CompilerParams(vmem_limit_bytes=LIMIT),
            cost_estimate=pl.CostEstimate(flops=1, bytes_accessed=1, transcendentals=0),
            name=f"write{layer}",
        )(*written, *after, *[x for x, _ in ready])

    count = 2 * len(stages[0]) - 1
    at = []
    for layer in reversed(range(layers)):
        state, at = back(layer, outs, at)
        if layer:
            at = sum_step([sums[i] for i in range(layer, layers)], at + returned[layer])
            outs = join(layer, state, at)
            at = outs[1:2]
        else:
            at = sum_step([sums[0]], at)
    while sums[0].done < count:
        for layer in reversed(range(layers)):
            if sums[layer].done < count:
                if layer == 0 and sums[0].done == count - 1:
                    at = at + [sums[above].got[0] for above in range(2, layers)]
                at = sum_step([sums[layer]], at)
    written = []
    for layer in reversed(range(1, layers)):
        *written, token = write(layer, written, at)
        at = [token]
    *written, token = write(0, written, at, (0,))
    grad, token = join(0, state, [token])
    *written, token = write(0, written, [token], (1,))
    return (grad, *written)


def solution(mesh):
    placed = (
        P(("runs", "chain", "basin"), None),
        P(("runs", "chain", "basin"), None),
        P(None, None, "feat"),
        P(None, "feat", None),
        P(("chain", "basin"), None),
        P(("chain", "basin"), None, None, None),
        P(("chain", "basin"), None, None),
        P(("chain", "basin"), None),
    )
    return jax.shard_map(
        shards,
        mesh=mesh,
        in_specs=placed,
        out_specs=(
            P(("runs", "chain", "basin"), None),
            P("runs", None, "feat"),
            P("runs", "feat", None),
        ),
        check_vma=False,
    )
```

```python
import functools

import jax
import jax.numpy as jnp
from jax import lax
from jax.experimental import pallas as pl
from jax.experimental.pallas import tpu as pltpu
from jax.sharding import PartitionSpec as P

BLOCK = 128
LANES = 128
EPS = 1e-06
F32 = jnp.float32
BF16 = jnp.bfloat16
VMEM = pl.BlockSpec(memory_space=pltpu.VMEM)
SMEM = pl.BlockSpec(memory_space=pltpu.SMEM)
ANY = pl.BlockSpec(memory_space=pl.ANY)
NN = (((1,), (0,)), ((), ()))
NT = (((1,), (1,)), ((), ()))
TN = (((0,), (0,)), ((), ()))


def mm(a, b, dims=NN):
    return lax.dot_general(a, b, dims, preferred_element_type=F32)


LIMIT = 24 * 1024 * 1024


def call(body, outs, ins, flops, scratch=(), name=None, after=(), bytes_accessed=4_000_000, scalars=None):
    skipped = len(after)
    return pl.pallas_call(
        lambda *refs: body(*refs[skipped:]),
        out_shape=[jax.ShapeDtypeStruct(s, d) for s, d in outs],
        in_specs=[ANY] * skipped + [SMEM if x is scalars else VMEM for x in ins],
        out_specs=[VMEM] * len(outs),
        scratch_shapes=list(scratch),
        compiler_params=pltpu.CompilerParams(vmem_limit_bytes=LIMIT),
        cost_estimate=pl.CostEstimate(
            flops=flops, bytes_accessed=bytes_accessed, transcendentals=0
        ),
        name=name,
    )(*after, *ins)


def sigmoid(v):
    return 1.0 / (1.0 + jnp.exp(-v))


def half_message(x, w_in, w_out):
    pre = mm(x, w_in)
    return mm((pre * sigmoid(pre)).astype(BF16), w_out)


def message_of(x, halves):
    total = None
    for w_in, w_out in halves:
        part = half_message(x, w_in, w_out)
        total = part if total is None else total + part
    return total.astype(BF16)


def message_grad(x, dmsg, halves):
    total = None
    kept = None
    for w_in, w_out in halves:
        pre = mm(x, w_in)
        sig = sigmoid(pre)
        dact = mm(dmsg, w_out, NT)
        dpre = (dact * (sig * (1.0 + pre * (1.0 - sig)))).astype(BF16)
        if kept is None:
            kept = ((pre * sig).astype(BF16), dpre)
        part = mm(dpre, w_in, NT)
        total = part if total is None else total + part
    return total, kept


def normed_of(total):
    scale = lax.rsqrt(jnp.mean(total * total, axis=-1, keepdims=True) + EPS)
    return scale, scale * total


def norm_grad(grad, total):
    scale, normed = normed_of(total)
    return scale * (grad - normed * jnp.mean(grad * normed, axis=-1, keepdims=True))


def setup_kernel(groups, features, sent, *refs):
    pick, spread, pick_self, held = refs[:4]
    sends = refs[4:]
    rows = features.shape[0]
    held[...] = features[...]
    b = lax.axis_index("basin")
    for route in range(-1, groups):
        if route == 0:
            chosen = lax.broadcasted_iota(jnp.int32, (1, BLOCK), 1) + (rows - BLOCK)
        else:
            chosen = sent[pl.ds(lax.rem(b + max(route, 0), groups), 1), :]
        across = jnp.broadcast_to(chosen, (BLOCK, BLOCK))
        down = across.T
        for r in range(0, rows, BLOCK):
            at = lax.broadcasted_iota(jnp.int32, (BLOCK, BLOCK), 1) + r
            hot = (down == at).astype(F32).astype(BF16)
            if route < 0:
                pick_self[:, r : r + BLOCK] = hot
                continue
            if route > 0:
                pick[(route - 1) * BLOCK : route * BLOCK, r : r + BLOCK] = hot
            at = lax.broadcasted_iota(jnp.int32, (BLOCK, BLOCK), 0) + r
            spread[r : r + BLOCK, route * BLOCK : (route + 1) * BLOCK] = (
                (across == at).astype(F32).astype(BF16)
            )
    pick_sends(features[...], pick, sends)


def pick_sends(rows, pick, sends):
    sends[0][...] = rows[rows.shape[0] - BLOCK :, :]
    for s, send in enumerate(sends[1:]):
        send[...] = mm(pick[s * BLOCK : (s + 1) * BLOCK, :], rows).astype(BF16)


def adjacency_kernel(groups, sources, values, pick_self, _, *refs):
    local, local_t, remote, remote_t, acc = refs
    rows = local.shape[0]
    own = rows // BLOCK
    b = lax.axis_index("basin")
    acc[...] = jnp.zeros_like(acc)
    for k in range(own):
        for t in range(values.shape[1]):
            v = sources[t, k]
            route = jnp.where(v == own, 0, lax.rem(b + groups - (v - own - 1), groups))
            far = jnp.where((v > own) & (route == 0), own, own + 1 + route)
            at = jnp.where(v < own, v, far)
            here = (pl.ds(k * BLOCK, BLOCK), pl.ds(pl.multiple_of(at * BLOCK, BLOCK), BLOCK))
            acc[here] += values[k, t].astype(F32)
    mine = acc[:, rows : rows + BLOCK].astype(BF16)
    full = acc[:, :rows] + mm(mine, pick_self[...])
    local[...] = full.astype(BF16)
    local_t[...] = full.T.astype(BF16)
    far = acc[:, rows + BLOCK :]
    remote[...] = far.astype(BF16)
    remote_t[...] = far.T.astype(BF16)


def message_half(x, w_in, w_out, slope, act_t=None):
    pre = mm(x, w_in)
    sig = sigmoid(pre)
    act = (pre * sig).astype(BF16)
    slope[...] = (sig * (1.0 + pre * (1.0 - sig))).astype(BF16)
    if act_t is not None:
        act_t[...] = act.T
    return mm(act, w_out)


def local_kernel(layer, x, wi0, wi1, wo0, wo1, msg, slope0, slope1, act_t, x_t):
    for r in range(0, x.shape[0], 256):
        here = slice(r, r + 256)
        rows = x[here, :]
        x_t[:, here] = rows.T
        part = message_half(rows, wi0[layer], wo0[layer], slope0.at[here, :], act_t.at[:, here])
        part = part + message_half(rows, wi1[layer], wo1[layer], slope1.at[here, :])
        msg[here, :] = part.astype(BF16)


def half_kernel(x, w_in, w_out, part, slope1):
    for r in range(0, x.shape[0], 256):
        here = slice(r, r + 256)
        part[here, :] = message_half(x[here, :], w_in[0], w_out[0], slope1.at[here, :])


def other_half_kernel(x, w_in, w_out, part, msg, slope0, act_t, x_t):
    for r in range(0, x.shape[0], 256):
        here = slice(r, r + 256)
        rows = x[here, :]
        x_t[:, here] = rows.T
        own = message_half(rows, w_in[0], w_out[0], slope0.at[here, :], act_t.at[:, here])
        msg[here, :] = (part[here, :] + own).astype(BF16)


def remote_mixed(layer, received, columns, weights):
    wi0, wi1, wo0, wo1 = weights
    halves = [(wi0[layer], wo0[layer]), (wi1[layer], wo1[layer])]
    far = jnp.concatenate([x[...] for x in received], axis=0)
    return mm(columns, message_of(far, halves))


def part_kernel(layer, *refs):
    local, msg, remote = refs[:3]
    weights, received, mixed = refs[3:7], refs[7:-1], refs[-1]
    total = mm(local[...], msg[...])
    if received:
        total = total + remote_mixed(layer, received, remote[:, BLOCK:], weights)
    mixed[...] = total


def upstream_rows(got, swapped_got):
    return got[...] + swapped_got[...]


def mixed_total(layer, state, mixed, up, remote, weights):
    return state + mixed[...] + remote_mixed(layer, [up], remote[:, :BLOCK], weights)


def mix_kernel(layer, *refs):
    prev, mixed, remote, pick = refs[:4]
    weights, up = refs[4:8], upstream_rows(*refs[8:10])
    total, inputs = refs[10:12]
    state = prev[...].astype(F32) if layer == 0 else normed_of(prev[...])[1]
    total[...] = mixed_total(layer, state, mixed, up, remote, weights)
    new = normed_of(total[...])[1].astype(BF16)
    inputs[...] = new
    pick_sends(new, pick, refs[12:])


def start_bwd(layer, dtotal_now, weights, received, remote_t, outs):
    dtotal, dround, far_x, far_dmsg, far_act, far_dpre = outs[:6]
    backs = outs[6:]
    wi0, wi1, wo0, wo1 = weights
    halves = [(wi0[layer], wo0[layer]), (wi1[layer], wo1[layer])]
    dtotal[...] = dtotal_now
    dround[...] = dtotal_now.astype(BF16)
    far_x[:BLOCK, :] = upstream_rows(*received[:2])
    for i, block in enumerate(received[2:]):
        far_x[(i + 1) * BLOCK : (i + 2) * BLOCK, :] = block[...]
    dmsg = mm(remote_t[...], dround[...]).astype(BF16)
    back, (act, dpre) = message_grad(far_x[...], dmsg, halves)
    far_dmsg[...] = dmsg
    far_act[...] = act
    far_dpre[...] = dpre
    for i, out in enumerate(backs):
        out[...] = back[i * BLOCK : (i + 1) * BLOCK, :].astype(BF16)


def turn_kernel(layer, groups, *refs):
    prev, mixed, remote, remote_t, cot = refs[:5]
    weights, received, outs = refs[5:9], refs[9 : 10 + groups], refs[10 + groups :]
    state = normed_of(prev[...])[1]
    total = mixed_total(layer, state, mixed, upstream_rows(*received[:2]), remote, weights)
    start_bwd(layer, norm_grad(cot[...], total), weights, received, remote_t, outs)


def back_kernel(layer, grad_scale, *refs):
    dround, local_t, slope0, slope1, act_t, x_t = refs[:6]
    wi0, wi1, wo0, wo1 = refs[6:10]
    far_x, far_dmsg, far_act, far_dpre = refs[10:14]
    back, grads, dmsg, dpre = refs[14:]
    dmsg[...] = mm(local_t[...], dround[...]).astype(BF16)
    for r in range(0, dmsg.shape[0], 256):
        here = slice(r, r + 256)
        rows = dmsg[here, :]
        dpre0 = (mm(rows, wo0[layer], NT) * slope0[here, :].astype(F32)).astype(BF16)
        dpre1 = (mm(rows, wo1[layer], NT) * slope1[here, :].astype(F32)).astype(BF16)
        dpre[here, :] = dpre0
        back[here, :] = mm(dpre0, wi0[layer], NT) + mm(dpre1, wi1[layer], NT)
    latent, hidden = x_t.shape[0], act_t.shape[0]
    g_in = (mm(x_t[...], dpre[...]) + mm(far_x[...], far_dpre[...], TN)) * grad_scale
    for j in range(hidden // LANES):
        grads[j * latent : (j + 1) * latent, :] = g_in[:, j * LANES : (j + 1) * LANES]
    g_out = (mm(act_t[...], dmsg[...]) + mm(far_act[...], far_dmsg[...], TN)) * grad_scale
    for j in range(latent // LANES):
        at = hidden // LANES * latent + j * hidden
        grads[at : at + hidden, :] = g_out[:, j * LANES : (j + 1) * LANES]


def upper(stage):
    (axis0, d0), (axis1, d1) = stage
    bit0 = lax.rem(lax.axis_index(axis0) // d0, 2)
    bit1 = lax.rem(lax.axis_index(axis1) // d1, 2)
    return jnp.where(lax.axis_index("feat") == 0, bit0, bit1)


def place(stage, own, got, out):
    m = own.shape[0]
    bit = upper(stage)
    out[pl.ds(pl.multiple_of(bit * m, m), m), :] = own[...].astype(out.dtype)
    out[pl.ds(pl.multiple_of((1 - bit) * m, m), m), :] = got[...].astype(out.dtype)


def sum_kernel(steps, *refs):
    n_in = sum(1 + (kind != "split") for kind, *_ in steps)
    n_out = len(steps) + 1 + max(group for *_, group, _ in steps)
    ins, outs, accs = refs[:n_in], refs[n_in : n_in + n_out], refs[n_in + n_out :]
    sends = outs[len(steps) :]
    for (kind, stage, back, at, group, to), out in zip(steps, outs):
        own, ins = ins[0], ins[1:]
        m = own.shape[0]
        send = sends[group].at[to : to + out.shape[0]]
        if kind != "split":
            got, ins = ins[0].at[at : at + m], ins[1:]
        if kind in ("split", "add_split"):
            if kind == "add_split":
                acc, accs = accs[0], accs[1:]
                acc[...] = own[...] + got[...].astype(F32)
                own = acc
            m = m // 2
            bit = upper(stage)
            out[...] = own[pl.ds(pl.multiple_of(bit * m, m), m), :]
            send[...] = own[pl.ds(pl.multiple_of((1 - bit) * m, m), m), :].astype(BF16)
        else:
            if kind == "place":
                place(back, own, got, out)
            else:
                out[...] = (own[...] + got[...].astype(F32)).astype(out.dtype)
            send[...] = out[...].astype(BF16)


def write_kernel(layer, stage, kept, halves, *refs):
    parts, (out_in, out_out, token, slab_in, slab_out, sem) = refs[kept:-6], refs[-6:]
    token[...] = jnp.zeros_like(token)
    bit = upper(stage)
    copies = []
    for part, (at, other) in zip(parts, halves):
        m = slab_in.size // LANES
        rows = part.at[at : at + m]
        upper_half = (1 - bit) if other else bit

        @pl.when(upper_half == 0)
        def _():
            write_slab(rows, slab_in, out_in.at[layer], sem.at[0])

        @pl.when(upper_half == 1)
        def _():
            write_slab(rows, slab_out, out_out.at[layer], sem.at[1])

        copies.append(upper_half)
    for upper_half in copies:

        @pl.when(upper_half == 0)
        def _():
            pltpu.make_async_copy(slab_in, out_in.at[layer], sem.at[0]).wait()

        @pl.when(upper_half == 1)
        def _():
            pltpu.make_async_copy(slab_out, out_out.at[layer], sem.at[1]).wait()


def write_slab(rows, slab, out, sem):
    n = slab.shape[0]
    for j in range(slab.shape[1] // LANES):
        slab[:, j * LANES : (j + 1) * LANES] = rows[j * n : (j + 1) * n, :].astype(F32)
    pltpu.make_async_copy(slab, out, sem).start()


class Sum:
    def __init__(self, whole, stages):
        self.own, self.got, self.stages, self.done = whole, None, stages, 0

    def next(self):
        n, i, rows = len(self.stages), self.done, self.own.shape[0]
        if i < n - 1:
            return "add_split" if i else "split", self.stages[i], None, rows // 2, F32
        if i == n - 1:
            return "add", self.stages[i], None, rows, F32
        stage = self.stages[2 * n - 2 - i]
        if i == n:
            return "add", stage, None, rows, BF16
        return "place", stage, self.stages[2 * n - 1 - i], rows * 2, BF16


def sum_step(sums, after):
    steps, ins, outs, scratch, groups = [], [], [], [], {}
    for one in sums:
        kind, stage, back, rows, dtype = one.next()
        group = groups.setdefault(stage, [len(groups), 0])
        steps.append((kind, stage, back, one.got and one.got[1], *group))
        group[1] += rows
        ins += [one.own, one.got[0]] if one.got else [one.own]
        outs.append(((rows, LANES), dtype))
        if kind == "add_split":
            scratch.append(pltpu.VMEM(one.own.shape, F32))
    made = call(
        functools.partial(sum_kernel, steps),
        outs + [((rows, LANES), BF16) for _, rows in groups.values()],
        ins,
        1,
        bytes_accessed=1,
        scratch=scratch,
        name="sum",
        after=after,
    )
    arrived = [swapped(x, stage) for x, stage in zip(made[len(sums) :], groups)]
    for one, own, (*_, group, at) in zip(sums, made, steps):
        one.own, one.got = own, (arrived[group], at)
        one.done += 1
    return [made[0]]


def gathered_grad(dtotal, back, returned, spread):
    far = jnp.concatenate([x[...] for x in returned], axis=0)
    return dtotal[...] + back[...] + mm(spread[...], far)


def join_kernel(layer, groups, *refs):
    dtotal, back, spread, remote_t, total = refs[:5]
    weights, refs = refs[5:9], refs[9:]
    returned, refs = refs[:groups], refs[groups:]
    received, outs = refs[: groups + 1], refs[groups + 1 :]
    grad = gathered_grad(dtotal, back, returned, spread)
    start_bwd(layer, norm_grad(grad, total[...]), weights, received, remote_t, outs)


def last_kernel(*refs):
    dtotal, back, spread = refs[:3]
    refs[-2][...] = gathered_grad(dtotal, back, refs[3:-2], spread)
    refs[-1][...] = jnp.zeros_like(refs[-1])


def around(x, axis, distance):
    n = lax.axis_size(axis)
    return lax.ppermute(x, axis, [(i, (i + distance) % n) for i in range(n)])


def over_mesh(x, target):
    chain, groups, cores = (lax.axis_size(axis) for axis in ("chain", "basin", "feat"))
    perm = []
    for c in range(chain):
        for b in range(groups):
            for feat in range(cores):
                to = target(c, b, feat)
                if to is not None:
                    start, end = (c * groups + b) * cores + feat, (to[0] * groups + to[1]) * cores
                    perm.append((start, end + feat))
    return lax.ppermute(x, ("chain", "basin", "feat"), perm)


def swapped(x, stage):
    def partner(c, b, feat):
        axis, d = stage[feat]
        return (c ^ d, b) if axis == "chain" else (c, b ^ d)

    return over_mesh(x, partner)


def forward(sends):
    chain = lax.axis_size("chain")

    def downstream(c, b, feat):
        return (c + 1, b) if c % 2 == feat and c + 1 < chain else None

    up = over_mesh(sends[0], downstream)
    return [up] + [around(x, "basin", s + 1) for s, x in enumerate(sends[1:])]


def backward(grads):
    chain = lax.axis_size("chain")
    up = lax.ppermute(grads[0], "chain", [(c, c - 1) for c in range(1, chain)])
    return [up] + [around(x, "basin", -s) for s, x in enumerate(grads) if s]


def shards(features, cotangent, w_in, w_out, block_index, block_values, send_rows, send_count):
    rows, latent = features.shape
    groups = lax.axis_size("basin")
    layers, _, half = w_in.shape
    far_rows = groups * BLOCK
    own = rows // BLOCK
    grad_scale = float(rows * lax.axis_size("chain") * groups) ** (-0.5)
    last = layers - 1

    def act16(n, m=latent):
        return ((n, m), BF16)

    wi1 = around(w_in, "feat", 1)
    wo1 = around(w_out, "feat", 1)
    ffn = 4 * latent * 2 * half

    live = jnp.arange(BLOCK, dtype=jnp.int32)[None, :] < send_count[0][:, None]
    sent = jnp.where(live, send_rows[0], -1)
    sources = block_index.T
    pick, spread, pick_self, features, *sends = call(
        functools.partial(setup_kernel, groups),
        [act16(max(groups - 1, 1) * BLOCK, rows), act16(rows, far_rows), act16(BLOCK, rows)]
        + [act16(rows)]
        + [act16(BLOCK)] * groups,
        [features, sent],
        2 * rows * far_rows * latent,
        name="setup",
    )
    weights = (w_in, wi1, w_out, wo1)
    inputs = [features]
    saved = []
    totals = []
    received = []
    for layer in range(layers):
        up, *others = forward(sends)
        if layer == 0:
            part, slope1 = call(
                half_kernel,
                [((rows, latent), F32), act16(rows, half)],
                [features, wi1, wo1],
                rows * ffn // 2,
                name="half",
            )
            msg, slope0, act_t, x_t = call(
                other_half_kernel,
                [act16(rows), act16(rows, half), act16(half, rows), act16(latent, rows)],
                [features, w_in, w_out, part],
                rows * ffn // 2,
                name="local0",
            )
            local, local_t, remote, remote_t = call(
                functools.partial(adjacency_kernel, groups),
                [act16(rows, rows), act16(rows, rows), act16(rows, far_rows), act16(far_rows, rows)],
                [sources, block_values, pick_self, msg],
                2 * rows * rows * BLOCK,
                scratch=[pltpu.VMEM((rows, rows + BLOCK + far_rows), F32)],
                name="adjacency",
                scalars=sources,
            )
            up, local = lax.optimization_barrier((up, local))
        else:
            msg, slope0, slope1, act_t, x_t = call(
                functools.partial(local_kernel, layer),
                [act16(rows), act16(rows, half), act16(rows, half)]
                + [act16(half, rows), act16(latent, rows)],
                [inputs[layer], *weights],
                rows * ffn,
                name=f"local{layer}",
            )
            up, msg = lax.optimization_barrier((up, msg))
        saved.append([slope0, slope1, act_t, x_t])
        received.append([up, around(up, "feat", 1), *others])
        (mixed,) = call(
            functools.partial(part_kernel, layer),
            [((rows, latent), F32)],
            [local, msg, remote, *weights, *others],
            2 * rows * rows * latent,
            name=f"part{layer}",
        )
        prev = totals[-1] if layer else features
        if layer < last:
            total, new, *sends = call(
                functools.partial(mix_kernel, layer),
                [((rows, latent), F32), act16(rows)] + [act16(BLOCK)] * groups,
                [prev, mixed, remote, pick, *weights, *received[layer][:2]],
                far_rows * ffn + 2 * rows * far_rows * latent,
                name=f"mix{layer}",
            )
            totals.append(total)
            inputs.append(new)
    bwd_outs = (
        [((rows, latent), F32), act16(rows), act16(far_rows), act16(far_rows)]
        + [act16(far_rows, half)] * 2
        + [act16(BLOCK)] * groups
    )
    outs = call(
        functools.partial(turn_kernel, last, groups),
        bwd_outs,
        [totals[-1], mixed, remote, remote_t, cotangent, *weights, *received[last]],
        2 * far_rows * ffn,
        name="turn",
    )
    grad_rows = 2 * latent * half // LANES

    def distances(axis):
        return [(axis, 1 << i) for i in range(lax.axis_size(axis).bit_length() - 1)]

    over_basin, over_chain = distances("basin"), distances("chain")
    n = len(over_basin)
    orders = over_basin + over_chain, over_chain[:n] + over_basin + over_chain[n:]
    stages = list(zip(*orders, strict=True))
    basin_first = list(zip(orders[0], orders[0], strict=True))
    returned = {}
    sums = {}

    def back(layer, outs, after):
        returned[layer] = backward(outs[6:])
        grad, whole = call(
            functools.partial(back_kernel, layer, grad_scale),
            [((rows, latent), F32), ((grad_rows, LANES), F32)],
            [outs[1], local_t, *saved[layer], *weights, *outs[2:6]],
            3 * rows * ffn + 2 * rows * rows * latent,
            scratch=[
                pltpu.VMEM((rows, latent), BF16),
                pltpu.VMEM((rows, half), BF16),
            ],
            name=f"back{layer}",
            after=after,
        )
        sums[layer] = Sum(whole, basin_first if layer else stages)
        return [outs[0], grad], [grad]

    def join(layer, state, after):
        if layer:
            return call(
                functools.partial(join_kernel, layer - 1, groups),
                bwd_outs,
                [*state, spread, remote_t, totals[layer - 1]]
                + [*weights, *returned[layer], *received[layer - 1]],
                2 * far_rows * ffn,
                name=f"join{layer}",
                after=after,
            )
        return call(
            last_kernel,
            [((rows, latent), F32), ((8, LANES), F32)],
            [*state, spread, *returned[layer]],
            2 * rows * far_rows * latent,
            name="join0",
            after=after,
        )

    def write(layer, written, after, which=(0, 1)):
        ready = [(sums[layer].own, 0), sums[layer].got]
        ready = [ready[i] for i in which]
        kept = [*written, *after]
        return pl.pallas_call(
            functools.partial(
                write_kernel,
                layer,
                sums[layer].stages[0],
                len(kept),
                [(at, i) for (_, at), i in zip(ready, which)],
            ),
            out_shape=[
                jax.ShapeDtypeStruct((layers, latent, half), F32),
                jax.ShapeDtypeStruct((layers, half, latent), F32),
                jax.ShapeDtypeStruct((8, LANES), F32),
            ],
            in_specs=[ANY] * len(kept) + [VMEM] * len(ready),
            out_specs=[ANY] * 2 + [VMEM],
            scratch_shapes=[
                pltpu.VMEM((latent, half), F32),
                pltpu.VMEM((half, latent), F32),
                pltpu.SemaphoreType.DMA((2,)),
            ],
            input_output_aliases={i: i for i in range(len(written))},
            compiler_params=pltpu.CompilerParams(vmem_limit_bytes=LIMIT),
            cost_estimate=pl.CostEstimate(flops=1, bytes_accessed=1, transcendentals=0),
            name=f"write{layer}",
        )(*written, *after, *[x for x, _ in ready])

    count = 2 * len(stages) - 1
    at = []
    for layer in reversed(range(layers)):
        state, at = back(layer, outs, at)
        arrived = [sums[above].got[0] for above in range(layer + 2, layers)]
        if layer:
            arrived += returned[layer]
        at = sum_step([sums[layer]], at + arrived)
        if layer:
            for above in range(layer + 1, layers):
                at = sum_step([sums[above]], at)
            outs = join(layer, state, at)
            at = outs[1:2]
    while sums[0].done < count:
        for layer in reversed(range(layers)):
            if sums[layer].done < count:
                if layer == 0 and sums[0].done == count - 1:
                    at = at + [sums[above].got[0] for above in range(2, layers)]
                at = sum_step([sums[layer]], at)
    written = []
    for layer in reversed(range(1, layers)):
        *written, token = write(layer, written, at)
        at = [token]
    *written, token = write(0, written, at, (0,))
    grad, token = join(0, state, [token])
    *written, token = write(0, written, [token], (1,))
    return (grad, *written)


def solution(mesh):
    placed = (
        P(("runs", "chain", "basin"), None),
        P(("runs", "chain", "basin"), None),
        P(None, None, "feat"),
        P(None, "feat", None),
        P(("chain", "basin"), None),
        P(("chain", "basin"), None, None, None),
        P(("chain", "basin"), None, None),
        P(("chain", "basin"), None),
    )
    return jax.shard_map(
        shards,
        mesh=mesh,
        in_specs=placed,
        out_specs=(
            P(("runs", "chain", "basin"), None),
            P("runs", None, "feat"),
            P("runs", "feat", None),
        ),
        check_vma=False,
    )
```

```python
import functools

import jax
import jax.numpy as jnp
from jax import lax
from jax.experimental import pallas as pl
from jax.experimental.pallas import tpu as pltpu
from jax.sharding import PartitionSpec as P

BLOCK = 128
LANES = 128
EPS = 1e-06
F32 = jnp.float32
BF16 = jnp.bfloat16
VMEM = pl.BlockSpec(memory_space=pltpu.VMEM)
SMEM = pl.BlockSpec(memory_space=pltpu.SMEM)
ANY = pl.BlockSpec(memory_space=pl.ANY)
NN = (((1,), (0,)), ((), ()))
NT = (((1,), (1,)), ((), ()))
TN = (((0,), (0,)), ((), ()))


def mm(a, b, dims=NN):
    return lax.dot_general(a, b, dims, preferred_element_type=F32)


LIMIT = 24 * 1024 * 1024


def call(body, outs, ins, flops, scratch=(), name=None, after=(), bytes_accessed=4_000_000, scalars=None):
    skipped = len(after)
    return pl.pallas_call(
        lambda *refs: body(*refs[skipped:]),
        out_shape=[jax.ShapeDtypeStruct(s, d) for s, d in outs],
        in_specs=[ANY] * skipped + [SMEM if x is scalars else VMEM for x in ins],
        out_specs=[VMEM] * len(outs),
        scratch_shapes=list(scratch),
        compiler_params=pltpu.CompilerParams(vmem_limit_bytes=LIMIT),
        cost_estimate=pl.CostEstimate(
            flops=flops, bytes_accessed=bytes_accessed, transcendentals=0
        ),
        name=name,
    )(*after, *ins)


def sigmoid(v):
    return 1.0 / (1.0 + jnp.exp(-v))


def half_message(x, w_in, w_out):
    pre = mm(x, w_in)
    return mm((pre * sigmoid(pre)).astype(BF16), w_out)


def message_of(x, halves):
    total = None
    for w_in, w_out in halves:
        part = half_message(x, w_in, w_out)
        total = part if total is None else total + part
    return total.astype(BF16)


def message_grad(x, dmsg, halves):
    total = None
    kept = None
    for w_in, w_out in halves:
        pre = mm(x, w_in)
        sig = sigmoid(pre)
        dact = mm(dmsg, w_out, NT)
        dpre = (dact * (sig * (1.0 + pre * (1.0 - sig)))).astype(BF16)
        if kept is None:
            kept = ((pre * sig).astype(BF16), dpre)
        part = mm(dpre, w_in, NT)
        total = part if total is None else total + part
    return total, kept


def normed_of(total):
    scale = lax.rsqrt(jnp.mean(total * total, axis=-1, keepdims=True) + EPS)
    return scale, scale * total


def norm_grad(grad, total):
    scale, normed = normed_of(total)
    return scale * (grad - normed * jnp.mean(grad * normed, axis=-1, keepdims=True))


def setup_kernel(groups, features, sent, *refs):
    pick, spread, pick_self, held = refs[:4]
    sends = refs[4:]
    rows = features.shape[0]
    held[...] = features[...]
    b = lax.axis_index("basin")
    for route in range(-1, groups):
        if route == 0:
            chosen = lax.broadcasted_iota(jnp.int32, (1, BLOCK), 1) + (rows - BLOCK)
        else:
            chosen = sent[pl.ds(lax.rem(b + max(route, 0), groups), 1), :]
        across = jnp.broadcast_to(chosen, (BLOCK, BLOCK))
        down = across.T
        for r in range(0, rows, BLOCK):
            at = lax.broadcasted_iota(jnp.int32, (BLOCK, BLOCK), 1) + r
            hot = (down == at).astype(F32).astype(BF16)
            if route < 0:
                pick_self[:, r : r + BLOCK] = hot
                continue
            if route > 0:
                pick[(route - 1) * BLOCK : route * BLOCK, r : r + BLOCK] = hot
            at = lax.broadcasted_iota(jnp.int32, (BLOCK, BLOCK), 0) + r
            spread[r : r + BLOCK, route * BLOCK : (route + 1) * BLOCK] = (
                (across == at).astype(F32).astype(BF16)
            )
    pick_sends(features[...], pick, sends)


def pick_sends(rows, pick, sends):
    sends[0][...] = rows[rows.shape[0] - BLOCK :, :]
    for s, send in enumerate(sends[1:]):
        send[...] = mm(pick[s * BLOCK : (s + 1) * BLOCK, :], rows).astype(BF16)


def adjacency_kernel(groups, sources, values, pick_self, _, *refs):
    local, local_t, remote, remote_t, acc = refs
    rows = local.shape[0]
    own = rows // BLOCK
    b = lax.axis_index("basin")
    acc[...] = jnp.zeros_like(acc)
    for k in range(own):
        for t in range(values.shape[1]):
            v = sources[t, k]
            route = jnp.where(v == own, 0, lax.rem(b + groups - (v - own - 1), groups))
            far = jnp.where((v > own) & (route == 0), own, own + 1 + route)
            at = jnp.where(v < own, v, far)
            here = (pl.ds(k * BLOCK, BLOCK), pl.ds(pl.multiple_of(at * BLOCK, BLOCK), BLOCK))
            acc[here] += values[k, t].astype(F32)
    mine = acc[:, rows : rows + BLOCK].astype(BF16)
    full = acc[:, :rows] + mm(mine, pick_self[...])
    local[...] = full.astype(BF16)
    local_t[...] = full.T.astype(BF16)
    far = acc[:, rows + BLOCK :]
    remote[...] = far.astype(BF16)
    remote_t[...] = far.T.astype(BF16)


def message_half(x, w_in, w_out, slope, act_t=None):
    pre = mm(x, w_in)
    sig = sigmoid(pre)
    act = (pre * sig).astype(BF16)
    slope[...] = (sig * (1.0 + pre * (1.0 - sig))).astype(BF16)
    if act_t is not None:
        act_t[...] = act.T
    return mm(act, w_out)


def local_kernel(layer, x, wi0, wi1, wo0, wo1, msg, slope0, slope1, act_t, x_t):
    for r in range(0, x.shape[0], 256):
        here = slice(r, r + 256)
        rows = x[here, :]
        x_t[:, here] = rows.T
        part = message_half(rows, wi0[layer], wo0[layer], slope0.at[here, :], act_t.at[:, here])
        part = part + message_half(rows, wi1[layer], wo1[layer], slope1.at[here, :])
        msg[here, :] = part.astype(BF16)


def half_kernel(x, w_in, w_out, part, slope1):
    for r in range(0, x.shape[0], 256):
        here = slice(r, r + 256)
        part[here, :] = message_half(x[here, :], w_in[0], w_out[0], slope1.at[here, :])


def other_half_kernel(x, w_in, w_out, part, msg, slope0, act_t, x_t):
    for r in range(0, x.shape[0], 256):
        here = slice(r, r + 256)
        rows = x[here, :]
        x_t[:, here] = rows.T
        own = message_half(rows, w_in[0], w_out[0], slope0.at[here, :], act_t.at[:, here])
        msg[here, :] = (part[here, :] + own).astype(BF16)


def remote_mixed(layer, received, columns, weights):
    wi0, wi1, wo0, wo1 = weights
    halves = [(wi0[layer], wo0[layer]), (wi1[layer], wo1[layer])]
    far = jnp.concatenate([x[...] for x in received], axis=0)
    return mm(columns, message_of(far, halves))


def part_kernel(layer, *refs):
    local, msg, remote = refs[:3]
    weights, received, mixed = refs[3:7], refs[7:-1], refs[-1]
    total = mm(local[...], msg[...])
    if received:
        total = total + remote_mixed(layer, received, remote[:, BLOCK:], weights)
    mixed[...] = total


def upstream_rows(got, swapped_got):
    return got[...] + swapped_got[...]


def mixed_total(layer, state, mixed, up, remote, weights):
    return state + mixed[...] + remote_mixed(layer, [up], remote[:, :BLOCK], weights)


def mix_kernel(layer, *refs):
    prev, mixed, remote, pick = refs[:4]
    weights, up = refs[4:8], upstream_rows(*refs[8:10])
    total, inputs = refs[10:12]
    state = prev[...].astype(F32) if layer == 0 else normed_of(prev[...])[1]
    total[...] = mixed_total(layer, state, mixed, up, remote, weights)
    new = normed_of(total[...])[1].astype(BF16)
    inputs[...] = new
    pick_sends(new, pick, refs[12:])


def start_bwd(layer, dtotal_now, weights, received, remote_t, outs):
    dtotal, dround, far_x, far_dmsg, far_act, far_dpre = outs[:6]
    backs = outs[6:]
    wi0, wi1, wo0, wo1 = weights
    halves = [(wi0[layer], wo0[layer]), (wi1[layer], wo1[layer])]
    dtotal[...] = dtotal_now
    dround[...] = dtotal_now.astype(BF16)
    far_x[:BLOCK, :] = upstream_rows(*received[:2])
    for i, block in enumerate(received[2:]):
        far_x[(i + 1) * BLOCK : (i + 2) * BLOCK, :] = block[...]
    dmsg = mm(remote_t[...], dround[...]).astype(BF16)
    back, (act, dpre) = message_grad(far_x[...], dmsg, halves)
    far_dmsg[...] = dmsg
    far_act[...] = act
    far_dpre[...] = dpre
    for i, out in enumerate(backs):
        out[...] = back[i * BLOCK : (i + 1) * BLOCK, :].astype(BF16)


def turn_kernel(layer, groups, *refs):
    prev, mixed, remote, remote_t, cot = refs[:5]
    weights, received, outs = refs[5:9], refs[9 : 10 + groups], refs[10 + groups :]
    state = normed_of(prev[...])[1]
    total = mixed_total(layer, state, mixed, upstream_rows(*received[:2]), remote, weights)
    start_bwd(layer, norm_grad(cot[...], total), weights, received, remote_t, outs)


def back_kernel(layer, grad_scale, *refs):
    dround, local_t, slope0, slope1, act_t, x_t = refs[:6]
    wi0, wi1, wo0, wo1 = refs[6:10]
    far_x, far_dmsg, far_act, far_dpre = refs[10:14]
    back, grads, dmsg, dpre = refs[14:]
    dmsg[...] = mm(local_t[...], dround[...]).astype(BF16)
    for r in range(0, dmsg.shape[0], 256):
        here = slice(r, r + 256)
        rows = dmsg[here, :]
        dpre0 = (mm(rows, wo0[layer], NT) * slope0[here, :].astype(F32)).astype(BF16)
        dpre1 = (mm(rows, wo1[layer], NT) * slope1[here, :].astype(F32)).astype(BF16)
        dpre[here, :] = dpre0
        back[here, :] = mm(dpre0, wi0[layer], NT) + mm(dpre1, wi1[layer], NT)
    latent, hidden = x_t.shape[0], act_t.shape[0]
    g_in = (mm(x_t[...], dpre[...]) + mm(far_x[...], far_dpre[...], TN)) * grad_scale
    for j in range(hidden // LANES):
        grads[j * latent : (j + 1) * latent, :] = g_in[:, j * LANES : (j + 1) * LANES]
    g_out = (mm(act_t[...], dmsg[...]) + mm(far_act[...], far_dmsg[...], TN)) * grad_scale
    for j in range(latent // LANES):
        at = hidden // LANES * latent + j * hidden
        grads[at : at + hidden, :] = g_out[:, j * LANES : (j + 1) * LANES]


def upper(stage):
    (axis0, d0), (axis1, d1) = stage
    bit0 = lax.rem(lax.axis_index(axis0) // d0, 2)
    bit1 = lax.rem(lax.axis_index(axis1) // d1, 2)
    return jnp.where(lax.axis_index("feat") == 0, bit0, bit1)


def place(stage, own, got, out):
    m = own.shape[0]
    bit = upper(stage)
    out[pl.ds(pl.multiple_of(bit * m, m), m), :] = own[...].astype(out.dtype)
    out[pl.ds(pl.multiple_of((1 - bit) * m, m), m), :] = got[...].astype(out.dtype)


def sum_kernel(steps, *refs):
    n_in = sum(1 + (kind != "split") for kind, *_ in steps)
    n_out = len(steps) + 1 + max(group for *_, group, _ in steps)
    ins, outs, accs = refs[:n_in], refs[n_in : n_in + n_out], refs[n_in + n_out :]
    sends = outs[len(steps) :]
    for (kind, stage, back, at, group, to), out in zip(steps, outs):
        own, ins = ins[0], ins[1:]
        m = own.shape[0]
        send = sends[group].at[to : to + out.shape[0]]
        if kind != "split":
            got, ins = ins[0].at[at : at + m], ins[1:]
        if kind in ("split", "add_split"):
            if kind == "add_split":
                acc, accs = accs[0], accs[1:]
                acc[...] = own[...] + got[...].astype(F32)
                own = acc
            m = m // 2
            bit = upper(stage)
            out[...] = own[pl.ds(pl.multiple_of(bit * m, m), m), :]
            send[...] = own[pl.ds(pl.multiple_of((1 - bit) * m, m), m), :].astype(BF16)
        else:
            if kind == "place":
                place(back, own, got, out)
            else:
                out[...] = (own[...] + got[...].astype(F32)).astype(out.dtype)
            send[...] = out[...].astype(BF16)


def write_kernel(layer, stage, kept, halves, *refs):
    parts, (out_in, out_out, token, slab_in, slab_out, sem) = refs[kept:-6], refs[-6:]
    token[...] = jnp.zeros_like(token)
    bit = upper(stage)
    copies = []
    for part, (at, other) in zip(parts, halves):
        m = slab_in.size // LANES
        rows = part.at[at : at + m]
        upper_half = (1 - bit) if other else bit

        @pl.when(upper_half == 0)
        def _():
            write_slab(rows, slab_in, out_in.at[layer], sem.at[0])

        @pl.when(upper_half == 1)
        def _():
            write_slab(rows, slab_out, out_out.at[layer], sem.at[1])

        copies.append(upper_half)
    for upper_half in copies:

        @pl.when(upper_half == 0)
        def _():
            pltpu.make_async_copy(slab_in, out_in.at[layer], sem.at[0]).wait()

        @pl.when(upper_half == 1)
        def _():
            pltpu.make_async_copy(slab_out, out_out.at[layer], sem.at[1]).wait()


def write_slab(rows, slab, out, sem):
    n = slab.shape[0]
    for j in range(slab.shape[1] // LANES):
        slab[:, j * LANES : (j + 1) * LANES] = rows[j * n : (j + 1) * n, :].astype(F32)
    pltpu.make_async_copy(slab, out, sem).start()


class Sum:
    def __init__(self, whole, stages):
        self.own, self.got, self.stages, self.done = whole, None, stages, 0

    def next(self):
        n, i, rows = len(self.stages), self.done, self.own.shape[0]
        if i < n - 1:
            return "add_split" if i else "split", self.stages[i], None, rows // 2, F32
        if i == n - 1:
            return "add", self.stages[i], None, rows, F32
        stage = self.stages[2 * n - 2 - i]
        if i == n:
            return "add", stage, None, rows, BF16
        return "place", stage, self.stages[2 * n - 1 - i], rows * 2, BF16


def sum_step(sums, after):
    steps, ins, outs, scratch, groups = [], [], [], [], {}
    for one in sums:
        kind, stage, back, rows, dtype = one.next()
        group = groups.setdefault(stage, [len(groups), 0])
        steps.append((kind, stage, back, one.got and one.got[1], *group))
        group[1] += rows
        ins += [one.own, one.got[0]] if one.got else [one.own]
        outs.append(((rows, LANES), dtype))
        if kind == "add_split":
            scratch.append(pltpu.VMEM(one.own.shape, F32))
    made = call(
        functools.partial(sum_kernel, steps),
        outs + [((rows, LANES), BF16) for _, rows in groups.values()],
        ins,
        1,
        bytes_accessed=1,
        scratch=scratch,
        name="sum",
        after=after,
    )
    arrived = [swapped(x, stage) for x, stage in zip(made[len(sums) :], groups)]
    for one, own, (*_, group, at) in zip(sums, made, steps):
        one.own, one.got = own, (arrived[group], at)
        one.done += 1
    return [made[0]]


def gathered_grad(dtotal, back, returned, spread):
    far = jnp.concatenate([x[...] for x in returned], axis=0)
    return dtotal[...] + back[...] + mm(spread[...], far)


def join_kernel(layer, groups, *refs):
    dtotal, back, spread, remote_t, total = refs[:5]
    weights, refs = refs[5:9], refs[9:]
    returned, refs = refs[:groups], refs[groups:]
    received, outs = refs[: groups + 1], refs[groups + 1 :]
    grad = gathered_grad(dtotal, back, returned, spread)
    start_bwd(layer, norm_grad(grad, total[...]), weights, received, remote_t, outs)


def last_kernel(*refs):
    dtotal, back, spread = refs[:3]
    refs[-2][...] = gathered_grad(dtotal, back, refs[3:-2], spread)
    refs[-1][...] = jnp.zeros_like(refs[-1])


def around(x, axis, distance):
    n = lax.axis_size(axis)
    return lax.ppermute(x, axis, [(i, (i + distance) % n) for i in range(n)])


def over_mesh(x, target):
    chain, groups, cores = (lax.axis_size(axis) for axis in ("chain", "basin", "feat"))
    perm = []
    for c in range(chain):
        for b in range(groups):
            for feat in range(cores):
                to = target(c, b, feat)
                if to is not None:
                    start, end = (c * groups + b) * cores + feat, (to[0] * groups + to[1]) * cores
                    perm.append((start, end + feat))
    return lax.ppermute(x, ("chain", "basin", "feat"), perm)


def swapped(x, stage):
    def partner(c, b, feat):
        axis, d = stage[feat]
        return (c ^ d, b) if axis == "chain" else (c, b ^ d)

    return over_mesh(x, partner)


def forward(sends):
    chain = lax.axis_size("chain")

    def downstream(c, b, feat):
        return (c + 1, b) if c % 2 == feat and c + 1 < chain else None

    up = over_mesh(sends[0], downstream)
    return [up] + [around(x, "basin", s + 1) for s, x in enumerate(sends[1:])]


def backward(grads):
    chain = lax.axis_size("chain")
    up = lax.ppermute(grads[0], "chain", [(c, c - 1) for c in range(1, chain)])
    return [up] + [around(x, "basin", -s) for s, x in enumerate(grads) if s]


def shards(features, cotangent, w_in, w_out, block_index, block_values, send_rows, send_count):
    rows, latent = features.shape
    groups = lax.axis_size("basin")
    layers, _, half = w_in.shape
    far_rows = groups * BLOCK
    own = rows // BLOCK
    grad_scale = float(rows * lax.axis_size("chain") * groups) ** (-0.5)
    last = layers - 1

    def act16(n, m=latent):
        return ((n, m), BF16)

    wi1 = around(w_in, "feat", 1)
    wo1 = around(w_out, "feat", 1)
    ffn = 4 * latent * 2 * half

    live = jnp.arange(BLOCK, dtype=jnp.int32)[None, :] < send_count[0][:, None]
    sent = jnp.where(live, send_rows[0], -1)
    sources = block_index.T
    pick, spread, pick_self, features, *sends = call(
        functools.partial(setup_kernel, groups),
        [act16(max(groups - 1, 1) * BLOCK, rows), act16(rows, far_rows), act16(BLOCK, rows)]
        + [act16(rows)]
        + [act16(BLOCK)] * groups,
        [features, sent],
        2 * rows * far_rows * latent,
        name="setup",
    )
    weights = (w_in, wi1, w_out, wo1)
    inputs = [features]
    saved = []
    totals = []
    received = []
    for layer in range(layers):
        up, *others = forward(sends)
        if layer == 0:
            part, slope1 = call(
                half_kernel,
                [((rows, latent), F32), act16(rows, half)],
                [features, wi1, wo1],
                rows * ffn // 2,
                name="half",
            )
            msg, slope0, act_t, x_t = call(
                other_half_kernel,
                [act16(rows), act16(rows, half), act16(half, rows), act16(latent, rows)],
                [features, w_in, w_out, part],
                rows * ffn // 2,
                name="local0",
            )
            local, local_t, remote, remote_t = call(
                functools.partial(adjacency_kernel, groups),
                [act16(rows, rows), act16(rows, rows), act16(rows, far_rows), act16(far_rows, rows)],
                [sources, block_values, pick_self, msg],
                2 * rows * rows * BLOCK,
                scratch=[pltpu.VMEM((rows, rows + BLOCK + far_rows), F32)],
                name="adjacency",
                scalars=sources,
            )
            up, local = lax.optimization_barrier((up, local))
        else:
            msg, slope0, slope1, act_t, x_t = call(
                functools.partial(local_kernel, layer),
                [act16(rows), act16(rows, half), act16(rows, half)]
                + [act16(half, rows), act16(latent, rows)],
                [inputs[layer], *weights],
                rows * ffn,
                name=f"local{layer}",
            )
            up, msg = lax.optimization_barrier((up, msg))
        saved.append([slope0, slope1, act_t, x_t])
        received.append([up, around(up, "feat", 1), *others])
        (mixed,) = call(
            functools.partial(part_kernel, layer),
            [((rows, latent), F32)],
            [local, msg, remote, *weights, *others],
            2 * rows * rows * latent,
            name=f"part{layer}",
        )
        prev = totals[-1] if layer else features
        if layer < last:
            total, new, *sends = call(
                functools.partial(mix_kernel, layer),
                [((rows, latent), F32), act16(rows)] + [act16(BLOCK)] * groups,
                [prev, mixed, remote, pick, *weights, *received[layer][:2]],
                far_rows * ffn + 2 * rows * far_rows * latent,
                name=f"mix{layer}",
            )
            totals.append(total)
            inputs.append(new)
    bwd_outs = (
        [((rows, latent), F32), act16(rows), act16(far_rows), act16(far_rows)]
        + [act16(far_rows, half)] * 2
        + [act16(BLOCK)] * groups
    )
    outs = call(
        functools.partial(turn_kernel, last, groups),
        bwd_outs,
        [totals[-1], mixed, remote, remote_t, cotangent, *weights, *received[last]],
        2 * far_rows * ffn,
        name="turn",
    )
    grad_rows = 2 * latent * half // LANES

    def distances(axis):
        return [(axis, 1 << i) for i in range(lax.axis_size(axis).bit_length() - 1)]

    over_basin, over_chain = distances("basin"), distances("chain")
    n = len(over_basin)
    orders = over_basin + over_chain, over_chain[:n] + over_basin + over_chain[n:]
    stages = list(zip(*orders, strict=True))
    basin_first = list(zip(orders[0], orders[0], strict=True))
    returned = {}
    sums = {}

    def back(layer, outs, after):
        returned[layer] = backward(outs[6:])
        grad, whole = call(
            functools.partial(back_kernel, layer, grad_scale),
            [((rows, latent), F32), ((grad_rows, LANES), F32)],
            [outs[1], local_t, *saved[layer], *weights, *outs[2:6]],
            3 * rows * ffn + 2 * rows * rows * latent,
            scratch=[
                pltpu.VMEM((rows, latent), BF16),
                pltpu.VMEM((rows, half), BF16),
            ],
            name=f"back{layer}",
            after=after,
        )
        sums[layer] = Sum(whole, basin_first if layer else stages)
        return [outs[0], grad], [grad]

    def join(layer, state, after):
        if layer:
            return call(
                functools.partial(join_kernel, layer - 1, groups),
                bwd_outs,
                [*state, spread, remote_t, totals[layer - 1]]
                + [*weights, *returned[layer], *received[layer - 1]],
                2 * far_rows * ffn,
                name=f"join{layer}",
                after=after,
            )
        return call(
            last_kernel,
            [((rows, latent), F32), ((8, LANES), F32)],
            [*state, spread, *returned[layer]],
            2 * rows * far_rows * latent,
            name="join0",
            after=after,
        )

    def write(layer, written, after, which=(0, 1)):
        ready = [(sums[layer].own, 0), sums[layer].got]
        ready = [ready[i] for i in which]
        kept = [*written, *after]
        return pl.pallas_call(
            functools.partial(
                write_kernel,
                layer,
                sums[layer].stages[0],
                len(kept),
                [(at, i) for (_, at), i in zip(ready, which)],
            ),
            out_shape=[
                jax.ShapeDtypeStruct((layers, latent, half), F32),
                jax.ShapeDtypeStruct((layers, half, latent), F32),
                jax.ShapeDtypeStruct((8, LANES), F32),
            ],
            in_specs=[ANY] * len(kept) + [VMEM] * len(ready),
            out_specs=[ANY] * 2 + [VMEM],
            scratch_shapes=[
                pltpu.VMEM((latent, half), F32),
                pltpu.VMEM((half, latent), F32),
                pltpu.SemaphoreType.DMA((2,)),
            ],
            input_output_aliases={i: i for i in range(len(written))},
            compiler_params=pltpu.CompilerParams(vmem_limit_bytes=LIMIT),
            cost_estimate=pl.CostEstimate(flops=1, bytes_accessed=1, transcendentals=0),
            name=f"write{layer}",
        )(*written, *after, *[x for x, _ in ready])

    count = 2 * len(stages) - 1
    at = []
    for layer in reversed(range(layers)):
        state, at = back(layer, outs, at)
        arrived = [sums[above].got[0] for above in range(layer + 2, layers)]
        if layer:
            arrived += returned[layer]
        at = sum_step([sums[layer]], at + arrived)
        if layer:
            for above in range(layer + 1, layers):
                at = sum_step([sums[above]], at)
            outs = join(layer, state, at)
            at = outs[1:2]
    while sums[0].done < count:
        for layer in reversed(range(layers)):
            if sums[layer].done < count:
                if layer == 0 and sums[0].done == count - 1:
                    at = at + returned[0] + [sums[above].got[0] for above in range(2, layers)]
                at = sum_step([sums[layer]], at)
    grad, token = join(0, state, at)
    at = [token]
    written = []
    for layer in reversed(range(1, layers)):
        *written, token = write(layer, written, at)
        at = [token]
    *written, token = write(0, written, at, (0,))
    *written, token = write(0, written, [token], (1,))
    return (grad, *written)


def solution(mesh):
    placed = (
        P(("runs", "chain", "basin"), None),
        P(("runs", "chain", "basin"), None),
        P(None, None, "feat"),
        P(None, "feat", None),
        P(("chain", "basin"), None),
        P(("chain", "basin"), None, None, None),
        P(("chain", "basin"), None, None),
        P(("chain", "basin"), None),
    )
    return jax.shard_map(
        shards,
        mesh=mesh,
        in_specs=placed,
        out_specs=(
            P(("runs", "chain", "basin"), None),
            P("runs", None, "feat"),
            P("runs", "feat", None),
        ),
        check_vma=False,
    )
```

```python
import functools

import jax
import jax.numpy as jnp
from jax import lax
from jax.experimental import pallas as pl
from jax.experimental.pallas import tpu as pltpu
from jax.sharding import PartitionSpec as P

BLOCK = 128
LANES = 128
EPS = 1e-06
F32 = jnp.float32
BF16 = jnp.bfloat16
VMEM = pl.BlockSpec(memory_space=pltpu.VMEM)
SMEM = pl.BlockSpec(memory_space=pltpu.SMEM)
ANY = pl.BlockSpec(memory_space=pl.ANY)
NN = (((1,), (0,)), ((), ()))
NT = (((1,), (1,)), ((), ()))
TN = (((0,), (0,)), ((), ()))


def mm(a, b, dims=NN):
    return lax.dot_general(a, b, dims, preferred_element_type=F32)


LIMIT = 24 * 1024 * 1024


def call(body, outs, ins, flops, scratch=(), name=None, after=(), bytes_accessed=4_000_000, scalars=None):
    skipped = len(after)
    return pl.pallas_call(
        lambda *refs: body(*refs[skipped:]),
        out_shape=[jax.ShapeDtypeStruct(s, d) for s, d in outs],
        in_specs=[ANY] * skipped + [SMEM if x is scalars else VMEM for x in ins],
        out_specs=[VMEM] * len(outs),
        scratch_shapes=list(scratch),
        compiler_params=pltpu.CompilerParams(vmem_limit_bytes=LIMIT),
        cost_estimate=pl.CostEstimate(
            flops=flops, bytes_accessed=bytes_accessed, transcendentals=0
        ),
        name=name,
    )(*after, *ins)


def sigmoid(v):
    return 1.0 / (1.0 + jnp.exp(-v))


def half_message(x, w_in, w_out):
    pre = mm(x, w_in)
    return mm((pre * sigmoid(pre)).astype(BF16), w_out)


def message_of(x, halves):
    total = None
    for w_in, w_out in halves:
        part = half_message(x, w_in, w_out)
        total = part if total is None else total + part
    return total.astype(BF16)


def message_grad(x, dmsg, halves):
    total = None
    kept = None
    for w_in, w_out in halves:
        pre = mm(x, w_in)
        sig = sigmoid(pre)
        dact = mm(dmsg, w_out, NT)
        dpre = (dact * (sig * (1.0 + pre * (1.0 - sig)))).astype(BF16)
        if kept is None:
            kept = ((pre * sig).astype(BF16), dpre)
        part = mm(dpre, w_in, NT)
        total = part if total is None else total + part
    return total, kept


def normed_of(total):
    scale = lax.rsqrt(jnp.mean(total * total, axis=-1, keepdims=True) + EPS)
    return scale, scale * total


def norm_grad(grad, total):
    scale, normed = normed_of(total)
    return scale * (grad - normed * jnp.mean(grad * normed, axis=-1, keepdims=True))


def setup_kernel(groups, features, sent, *refs):
    pick, spread, pick_self, held = refs[:4]
    sends = refs[4:]
    rows = features.shape[0]
    held[...] = features[...]
    b = lax.axis_index("basin")
    for route in range(-1, groups):
        if route == 0:
            chosen = lax.broadcasted_iota(jnp.int32, (1, BLOCK), 1) + (rows - BLOCK)
        else:
            chosen = sent[pl.ds(lax.rem(b + max(route, 0), groups), 1), :]
        across = jnp.broadcast_to(chosen, (BLOCK, BLOCK))
        down = across.T
        for r in range(0, rows, BLOCK):
            at = lax.broadcasted_iota(jnp.int32, (BLOCK, BLOCK), 1) + r
            hot = (down == at).astype(F32).astype(BF16)
            if route < 0:
                pick_self[:, r : r + BLOCK] = hot
                continue
            if route > 0:
                pick[(route - 1) * BLOCK : route * BLOCK, r : r + BLOCK] = hot
            at = lax.broadcasted_iota(jnp.int32, (BLOCK, BLOCK), 0) + r
            spread[r : r + BLOCK, route * BLOCK : (route + 1) * BLOCK] = (
                (across == at).astype(F32).astype(BF16)
            )
    pick_sends(features[...], pick, sends)


def pick_sends(rows, pick, sends):
    sends[0][...] = rows[rows.shape[0] - BLOCK :, :]
    for s, send in enumerate(sends[1:]):
        send[...] = mm(pick[s * BLOCK : (s + 1) * BLOCK, :], rows).astype(BF16)


def adjacency_kernel(groups, sources, values, pick_self, _, *refs):
    local, local_t, remote, remote_t, acc = refs
    rows = local.shape[0]
    own = rows // BLOCK
    b = lax.axis_index("basin")
    acc[...] = jnp.zeros_like(acc)
    for k in range(own):
        for t in range(values.shape[1]):
            v = sources[t, k]
            route = jnp.where(v == own, 0, lax.rem(b + groups - (v - own - 1), groups))
            far = jnp.where((v > own) & (route == 0), own, own + 1 + route)
            at = jnp.where(v < own, v, far)
            here = (pl.ds(k * BLOCK, BLOCK), pl.ds(pl.multiple_of(at * BLOCK, BLOCK), BLOCK))
            acc[here] += values[k, t].astype(F32)
    mine = acc[:, rows : rows + BLOCK].astype(BF16)
    full = acc[:, :rows] + mm(mine, pick_self[...])
    local[...] = full.astype(BF16)
    local_t[...] = full.T.astype(BF16)
    far = acc[:, rows + BLOCK :]
    remote[...] = far.astype(BF16)
    remote_t[...] = far.T.astype(BF16)


def message_half(x, w_in, w_out, slope, act_t=None):
    pre = mm(x, w_in)
    sig = sigmoid(pre)
    act = (pre * sig).astype(BF16)
    slope[...] = (sig * (1.0 + pre * (1.0 - sig))).astype(BF16)
    if act_t is not None:
        act_t[...] = act.T
    return mm(act, w_out)


def local_kernel(layer, x, wi0, wi1, wo0, wo1, msg, slope0, slope1, act_t, x_t):
    for r in range(0, x.shape[0], 256):
        here = slice(r, r + 256)
        rows = x[here, :]
        x_t[:, here] = rows.T
        part = message_half(rows, wi0[layer], wo0[layer], slope0.at[here, :], act_t.at[:, here])
        part = part + message_half(rows, wi1[layer], wo1[layer], slope1.at[here, :])
        msg[here, :] = part.astype(BF16)


def half_kernel(x, w_in, w_out, part, slope1):
    for r in range(0, x.shape[0], 256):
        here = slice(r, r + 256)
        part[here, :] = message_half(x[here, :], w_in[0], w_out[0], slope1.at[here, :])


def other_half_kernel(x, w_in, w_out, part, msg, slope0, act_t, x_t):
    for r in range(0, x.shape[0], 256):
        here = slice(r, r + 256)
        rows = x[here, :]
        x_t[:, here] = rows.T
        own = message_half(rows, w_in[0], w_out[0], slope0.at[here, :], act_t.at[:, here])
        msg[here, :] = (part[here, :] + own).astype(BF16)


def remote_mixed(layer, received, columns, weights):
    wi0, wi1, wo0, wo1 = weights
    halves = [(wi0[layer], wo0[layer]), (wi1[layer], wo1[layer])]
    far = jnp.concatenate([x[...] for x in received], axis=0)
    return mm(columns, message_of(far, halves))


def part_kernel(layer, *refs):
    local, msg, remote = refs[:3]
    weights, received, mixed = refs[3:7], refs[7:-1], refs[-1]
    total = mm(local[...], msg[...])
    if received:
        total = total + remote_mixed(layer, received, remote[:, BLOCK:], weights)
    mixed[...] = total


def upstream_rows(got, swapped_got):
    return got[...] + swapped_got[...]


def mixed_total(layer, state, mixed, up, remote, weights):
    return state + mixed[...] + remote_mixed(layer, [up], remote[:, :BLOCK], weights)


def mix_kernel(layer, *refs):
    prev, mixed, remote, pick = refs[:4]
    weights, up = refs[4:8], upstream_rows(*refs[8:10])
    total, inputs = refs[10:12]
    state = prev[...].astype(F32) if layer == 0 else normed_of(prev[...])[1]
    total[...] = mixed_total(layer, state, mixed, up, remote, weights)
    new = normed_of(total[...])[1].astype(BF16)
    inputs[...] = new
    pick_sends(new, pick, refs[12:])


def start_bwd(layer, dtotal_now, weights, received, remote_t, outs):
    dtotal, dround, far_x, far_dmsg, far_act, far_dpre = outs[:6]
    backs = outs[6:]
    wi0, wi1, wo0, wo1 = weights
    halves = [(wi0[layer], wo0[layer]), (wi1[layer], wo1[layer])]
    dtotal[...] = dtotal_now
    dround[...] = dtotal_now.astype(BF16)
    far_x[:BLOCK, :] = upstream_rows(*received[:2])
    for i, block in enumerate(received[2:]):
        far_x[(i + 1) * BLOCK : (i + 2) * BLOCK, :] = block[...]
    dmsg = mm(remote_t[...], dround[...]).astype(BF16)
    back, (act, dpre) = message_grad(far_x[...], dmsg, halves)
    far_dmsg[...] = dmsg
    far_act[...] = act
    far_dpre[...] = dpre
    for i, out in enumerate(backs):
        out[...] = back[i * BLOCK : (i + 1) * BLOCK, :].astype(BF16)


def turn_kernel(layer, groups, *refs):
    prev, mixed, remote, remote_t, cot = refs[:5]
    weights, received, outs = refs[5:9], refs[9 : 10 + groups], refs[10 + groups :]
    state = normed_of(prev[...])[1]
    total = mixed_total(layer, state, mixed, upstream_rows(*received[:2]), remote, weights)
    start_bwd(layer, norm_grad(cot[...], total), weights, received, remote_t, outs)


def back_kernel(layer, grad_scale, *refs):
    dround, local_t, slope0, slope1, act_t, x_t = refs[:6]
    wi0, wi1, wo0, wo1 = refs[6:10]
    far_x, far_dmsg, far_act, far_dpre = refs[10:14]
    back, grads, dmsg, dpre = refs[14:]
    dmsg[...] = mm(local_t[...], dround[...]).astype(BF16)
    for r in range(0, dmsg.shape[0], 256):
        here = slice(r, r + 256)
        rows = dmsg[here, :]
        dpre0 = (mm(rows, wo0[layer], NT) * slope0[here, :].astype(F32)).astype(BF16)
        dpre1 = (mm(rows, wo1[layer], NT) * slope1[here, :].astype(F32)).astype(BF16)
        dpre[here, :] = dpre0
        back[here, :] = mm(dpre0, wi0[layer], NT) + mm(dpre1, wi1[layer], NT)
    latent, hidden = x_t.shape[0], act_t.shape[0]
    g_in = (mm(x_t[...], dpre[...]) + mm(far_x[...], far_dpre[...], TN)) * grad_scale
    for j in range(hidden // LANES):
        grads[j * latent : (j + 1) * latent, :] = g_in[:, j * LANES : (j + 1) * LANES]
    g_out = (mm(act_t[...], dmsg[...]) + mm(far_act[...], far_dmsg[...], TN)) * grad_scale
    for j in range(latent // LANES):
        at = hidden // LANES * latent + j * hidden
        grads[at : at + hidden, :] = g_out[:, j * LANES : (j + 1) * LANES]


def upper(stage):
    (axis0, d0), (axis1, d1) = stage
    bit0 = lax.rem(lax.axis_index(axis0) // d0, 2)
    bit1 = lax.rem(lax.axis_index(axis1) // d1, 2)
    return jnp.where(lax.axis_index("feat") == 0, bit0, bit1)


def place(stage, own, got, out):
    m = own.shape[0]
    bit = upper(stage)
    out[pl.ds(pl.multiple_of(bit * m, m), m), :] = own[...].astype(out.dtype)
    out[pl.ds(pl.multiple_of((1 - bit) * m, m), m), :] = got[...].astype(out.dtype)


def sum_kernel(steps, *refs):
    n_in = sum(1 + (kind != "split") for kind, *_ in steps)
    n_out = len(steps) + 1 + max(group for *_, group, _ in steps)
    ins, outs, accs = refs[:n_in], refs[n_in : n_in + n_out], refs[n_in + n_out :]
    sends = outs[len(steps) :]
    for (kind, stage, back, at, group, to), out in zip(steps, outs):
        own, ins = ins[0], ins[1:]
        m = own.shape[0]
        send = sends[group].at[to : to + out.shape[0]]
        if kind != "split":
            got, ins = ins[0].at[at : at + m], ins[1:]
        if kind in ("split", "add_split"):
            if kind == "add_split":
                acc, accs = accs[0], accs[1:]
                acc[...] = own[...] + got[...].astype(F32)
                own = acc
            m = m // 2
            bit = upper(stage)
            out[...] = own[pl.ds(pl.multiple_of(bit * m, m), m), :]
            send[...] = own[pl.ds(pl.multiple_of((1 - bit) * m, m), m), :].astype(BF16)
        else:
            if kind == "place":
                place(back, own, got, out)
            else:
                out[...] = (own[...] + got[...].astype(F32)).astype(out.dtype)
            send[...] = out[...].astype(BF16)


def write_kernel(layer, stage, kept, halves, *refs):
    parts, (out_in, out_out, token, slab_in, slab_out, sem) = refs[kept:-6], refs[-6:]
    token[...] = jnp.zeros_like(token)
    bit = upper(stage)
    copies = []
    for part, (at, other) in zip(parts, halves):
        m = slab_in.size // LANES
        rows = part.at[at : at + m]
        upper_half = (1 - bit) if other else bit

        @pl.when(upper_half == 0)
        def _():
            write_slab(rows, slab_in, out_in.at[layer], sem.at[0])

        @pl.when(upper_half == 1)
        def _():
            write_slab(rows, slab_out, out_out.at[layer], sem.at[1])

        copies.append(upper_half)
    for upper_half in copies:

        @pl.when(upper_half == 0)
        def _():
            pltpu.make_async_copy(slab_in, out_in.at[layer], sem.at[0]).wait()

        @pl.when(upper_half == 1)
        def _():
            pltpu.make_async_copy(slab_out, out_out.at[layer], sem.at[1]).wait()


def write_slab(rows, slab, out, sem):
    n = slab.shape[0]
    for j in range(slab.shape[1] // LANES):
        slab[:, j * LANES : (j + 1) * LANES] = rows[j * n : (j + 1) * n, :].astype(F32)
    pltpu.make_async_copy(slab, out, sem).start()


class Sum:
    def __init__(self, whole, stages):
        self.own, self.got, self.stages, self.done = whole, None, stages, 0

    def next(self):
        n, i, rows = len(self.stages), self.done, self.own.shape[0]
        if i < n - 1:
            return "add_split" if i else "split", self.stages[i], None, rows // 2, F32
        if i == n - 1:
            return "add", self.stages[i], None, rows, F32
        stage = self.stages[2 * n - 2 - i]
        if i == n:
            return "add", stage, None, rows, BF16
        return "place", stage, self.stages[2 * n - 1 - i], rows * 2, BF16


def sum_step(sums, after):
    steps, ins, outs, scratch, groups = [], [], [], [], {}
    for one in sums:
        kind, stage, back, rows, dtype = one.next()
        group = groups.setdefault(stage, [len(groups), 0])
        steps.append((kind, stage, back, one.got and one.got[1], *group))
        group[1] += rows
        ins += [one.own, one.got[0]] if one.got else [one.own]
        outs.append(((rows, LANES), dtype))
        if kind == "add_split":
            scratch.append(pltpu.VMEM(one.own.shape, F32))
    made = call(
        functools.partial(sum_kernel, steps),
        outs + [((rows, LANES), BF16) for _, rows in groups.values()],
        ins,
        1,
        bytes_accessed=1,
        scratch=scratch,
        name="sum",
        after=after,
    )
    arrived = [swapped(x, stage) for x, stage in zip(made[len(sums) :], groups)]
    for one, own, (*_, group, at) in zip(sums, made, steps):
        one.own, one.got = own, (arrived[group], at)
        one.done += 1
    return [made[0]]


def gathered_grad(dtotal, back, returned, spread):
    far = jnp.concatenate([x[...] for x in returned], axis=0)
    return dtotal[...] + back[...] + mm(spread[...], far)


def join_kernel(layer, groups, *refs):
    dtotal, back, spread, remote_t, total = refs[:5]
    weights, refs = refs[5:9], refs[9:]
    returned, refs = refs[:groups], refs[groups:]
    received, outs = refs[: groups + 1], refs[groups + 1 :]
    grad = gathered_grad(dtotal, back, returned, spread)
    start_bwd(layer, norm_grad(grad, total[...]), weights, received, remote_t, outs)


def last_kernel(parts, *refs):
    dtotal, back, spread = refs[:3]
    returned, outs, token = refs[3 : -1 - parts], refs[-1 - parts : -1], refs[-1]
    token[...] = jnp.zeros_like(token)

    @pl.when(lax.axis_index("feat") > 0)
    def _():
        grad = gathered_grad(dtotal, back, returned, spread)
        m = grad.shape[0] // parts
        for i, out in enumerate(outs):
            out[...] = grad[i * m : (i + 1) * m, :]


def choose_kernel(parts, *refs):
    out, sems = refs[-2:]
    feat = lax.axis_index("feat")
    m = out.shape[0] // parts
    for i in range(parts):
        own, got, to = refs[i], refs[parts + i], out.at[i * m : (i + 1) * m]

        @pl.when(feat > 0)
        def _():
            pltpu.make_async_copy(own, to, sems.at[i]).start()

        @pl.when(feat == 0)
        def _():
            pltpu.make_async_copy(got, to, sems.at[i]).start()

    for i in range(parts):
        to = out.at[i * m : (i + 1) * m]
        pltpu.make_async_copy(refs[i], to, sems.at[i]).wait()


def around(x, axis, distance):
    n = lax.axis_size(axis)
    return lax.ppermute(x, axis, [(i, (i + distance) % n) for i in range(n)])


def over_mesh(x, target):
    chain, groups, cores = (lax.axis_size(axis) for axis in ("chain", "basin", "feat"))
    perm = []
    for c in range(chain):
        for b in range(groups):
            for feat in range(cores):
                to = target(c, b, feat)
                if to is not None:
                    start, end = (c * groups + b) * cores + feat, (to[0] * groups + to[1]) * cores
                    perm.append((start, end + feat))
    return lax.ppermute(x, ("chain", "basin", "feat"), perm)


def swapped(x, stage):
    def partner(c, b, feat):
        axis, d = stage[feat]
        return (c ^ d, b) if axis == "chain" else (c, b ^ d)

    return over_mesh(x, partner)


def forward(sends):
    chain = lax.axis_size("chain")

    def downstream(c, b, feat):
        return (c + 1, b) if c % 2 == feat and c + 1 < chain else None

    up = over_mesh(sends[0], downstream)
    return [up] + [around(x, "basin", s + 1) for s, x in enumerate(sends[1:])]


def backward(grads):
    chain = lax.axis_size("chain")
    up = lax.ppermute(grads[0], "chain", [(c, c - 1) for c in range(1, chain)])
    return [up] + [around(x, "basin", -s) for s, x in enumerate(grads) if s]


def backward_on_one(grads):
    groups = lax.axis_size("basin")

    def target(s, c, b, feat):
        if feat == 0 or (s == 0 and c == 0):
            return None
        return (c, (b - s) % groups) if s else (c - 1, b)

    return [over_mesh(x, functools.partial(target, s)) for s, x in enumerate(grads)]


def shards(features, cotangent, w_in, w_out, block_index, block_values, send_rows, send_count):
    rows, latent = features.shape
    groups = lax.axis_size("basin")
    layers, _, half = w_in.shape
    far_rows = groups * BLOCK
    own = rows // BLOCK
    grad_scale = float(rows * lax.axis_size("chain") * groups) ** (-0.5)
    last = layers - 1

    def act16(n, m=latent):
        return ((n, m), BF16)

    wi1 = around(w_in, "feat", 1)
    wo1 = around(w_out, "feat", 1)
    ffn = 4 * latent * 2 * half

    live = jnp.arange(BLOCK, dtype=jnp.int32)[None, :] < send_count[0][:, None]
    sent = jnp.where(live, send_rows[0], -1)
    sources = block_index.T
    pick, spread, pick_self, features, *sends = call(
        functools.partial(setup_kernel, groups),
        [act16(max(groups - 1, 1) * BLOCK, rows), act16(rows, far_rows), act16(BLOCK, rows)]
        + [act16(rows)]
        + [act16(BLOCK)] * groups,
        [features, sent],
        2 * rows * far_rows * latent,
        name="setup",
    )
    weights = (w_in, wi1, w_out, wo1)
    inputs = [features]
    saved = []
    totals = []
    received = []
    for layer in range(layers):
        up, *others = forward(sends)
        if layer == 0:
            part, slope1 = call(
                half_kernel,
                [((rows, latent), F32), act16(rows, half)],
                [features, wi1, wo1],
                rows * ffn // 2,
                name="half",
            )
            msg, slope0, act_t, x_t = call(
                other_half_kernel,
                [act16(rows), act16(rows, half), act16(half, rows), act16(latent, rows)],
                [features, w_in, w_out, part],
                rows * ffn // 2,
                name="local0",
            )
            local, local_t, remote, remote_t = call(
                functools.partial(adjacency_kernel, groups),
                [act16(rows, rows), act16(rows, rows), act16(rows, far_rows), act16(far_rows, rows)],
                [sources, block_values, pick_self, msg],
                2 * rows * rows * BLOCK,
                scratch=[pltpu.VMEM((rows, rows + BLOCK + far_rows), F32)],
                name="adjacency",
                scalars=sources,
            )
            up, local = lax.optimization_barrier((up, local))
        else:
            msg, slope0, slope1, act_t, x_t = call(
                functools.partial(local_kernel, layer),
                [act16(rows), act16(rows, half), act16(rows, half)]
                + [act16(half, rows), act16(latent, rows)],
                [inputs[layer], *weights],
                rows * ffn,
                name=f"local{layer}",
            )
            up, msg = lax.optimization_barrier((up, msg))
        saved.append([slope0, slope1, act_t, x_t])
        received.append([up, around(up, "feat", 1), *others])
        (mixed,) = call(
            functools.partial(part_kernel, layer),
            [((rows, latent), F32)],
            [local, msg, remote, *weights, *others],
            2 * rows * rows * latent,
            name=f"part{layer}",
        )
        prev = totals[-1] if layer else features
        if layer < last:
            total, new, *sends = call(
                functools.partial(mix_kernel, layer),
                [((rows, latent), F32), act16(rows)] + [act16(BLOCK)] * groups,
                [prev, mixed, remote, pick, *weights, *received[layer][:2]],
                far_rows * ffn + 2 * rows * far_rows * latent,
                name=f"mix{layer}",
            )
            totals.append(total)
            inputs.append(new)
    bwd_outs = (
        [((rows, latent), F32), act16(rows), act16(far_rows), act16(far_rows)]
        + [act16(far_rows, half)] * 2
        + [act16(BLOCK)] * groups
    )
    outs = call(
        functools.partial(turn_kernel, last, groups),
        bwd_outs,
        [totals[-1], mixed, remote, remote_t, cotangent, *weights, *received[last]],
        2 * far_rows * ffn,
        name="turn",
    )
    grad_rows = 2 * latent * half // LANES

    def distances(axis):
        return [(axis, 1 << i) for i in range(lax.axis_size(axis).bit_length() - 1)]

    over_basin, over_chain = distances("basin"), distances("chain")
    n = len(over_basin)
    orders = over_basin + over_chain, over_chain[:n] + over_basin + over_chain[n:]
    stages = list(zip(*orders, strict=True))
    basin_first = list(zip(orders[0], orders[0], strict=True))
    returned = {}
    sums = {}
    parts = rows // 256

    def back(layer, outs, after):
        returned[layer] = backward(outs[6:]) if layer else backward_on_one(outs[6:])
        grad, whole = call(
            functools.partial(back_kernel, layer, grad_scale),
            [((rows, latent), F32), ((grad_rows, LANES), F32)],
            [outs[1], local_t, *saved[layer], *weights, *outs[2:6]],
            3 * rows * ffn + 2 * rows * rows * latent,
            scratch=[
                pltpu.VMEM((rows, latent), BF16),
                pltpu.VMEM((rows, half), BF16),
            ],
            name=f"back{layer}",
            after=after,
        )
        sums[layer] = Sum(whole, basin_first if layer else stages)
        return [outs[0], grad], [grad]

    def join(layer, state, after):
        if layer:
            return call(
                functools.partial(join_kernel, layer - 1, groups),
                bwd_outs,
                [*state, spread, remote_t, totals[layer - 1]]
                + [*weights, *returned[layer], *received[layer - 1]],
                2 * far_rows * ffn,
                name=f"join{layer}",
                after=after,
            )
        return call(
            functools.partial(last_kernel, parts),
            [((rows // parts, latent), F32)] * parts + [((8, LANES), F32)],
            [*state, spread, *returned[layer]],
            2 * rows * far_rows * latent,
            name="join0",
            after=after,
        )

    def write(layer, written, after, which=(0, 1)):
        ready = [(sums[layer].own, 0), sums[layer].got]
        ready = [ready[i] for i in which]
        kept = [*written, *after]
        return pl.pallas_call(
            functools.partial(
                write_kernel,
                layer,
                sums[layer].stages[0],
                len(kept),
                [(at, i) for (_, at), i in zip(ready, which)],
            ),
            out_shape=[
                jax.ShapeDtypeStruct((layers, latent, half), F32),
                jax.ShapeDtypeStruct((layers, half, latent), F32),
                jax.ShapeDtypeStruct((8, LANES), F32),
            ],
            in_specs=[ANY] * len(kept) + [VMEM] * len(ready),
            out_specs=[ANY] * 2 + [VMEM],
            scratch_shapes=[
                pltpu.VMEM((latent, half), F32),
                pltpu.VMEM((half, latent), F32),
                pltpu.SemaphoreType.DMA((2,)),
            ],
            input_output_aliases={i: i for i in range(len(written))},
            compiler_params=pltpu.CompilerParams(vmem_limit_bytes=LIMIT),
            cost_estimate=pl.CostEstimate(flops=1, bytes_accessed=1, transcendentals=0),
            name=f"write{layer}",
        )(*written, *after, *[x for x, _ in ready])

    count = 2 * len(stages) - 1
    at = []
    for layer in reversed(range(layers)):
        state, at = back(layer, outs, at)
        arrived = [sums[above].got[0] for above in range(layer + 2, layers)]
        if layer:
            arrived += returned[layer]
        at = sum_step([sums[layer]], at + arrived)
        if layer:
            for above in range(layer + 1, layers):
                at = sum_step([sums[above]], at)
            outs = join(layer, state, at)
            at = outs[1:2]
    while sums[0].done < count:
        for layer in reversed(range(layers)):
            if sums[layer].done < count:
                if layer == 0 and sums[0].done == count - 1:
                    at = at + returned[0] + [sums[above].got[0] for above in range(2, layers)]
                at = sum_step([sums[layer]], at)
    *mine, token = join(0, state, at)
    got = [lax.ppermute(x, "feat", [(1, 0)]) for x in mine]
    at = [token]
    written = []
    for layer in reversed(range(1, layers)):
        *written, token = write(layer, written, at)
        at = [token]
    *written, token = write(0, written, at, (0,))
    grad = pl.pallas_call(
        functools.partial(choose_kernel, parts),
        out_shape=jax.ShapeDtypeStruct((rows, latent), F32),
        in_specs=[ANY] * (2 * parts),
        out_specs=ANY,
        scratch_shapes=[pltpu.SemaphoreType.DMA((parts,))],
        cost_estimate=pl.CostEstimate(flops=1, bytes_accessed=1, transcendentals=0),
        name="choose",
    )(*mine, *got)
    grad, token = lax.optimization_barrier((grad, token))
    *written, token = write(0, written, [token], (1,))
    return (grad, *written)


def solution(mesh):
    placed = (
        P(("runs", "chain", "basin"), None),
        P(("runs", "chain", "basin"), None),
        P(None, None, "feat"),
        P(None, "feat", None),
        P(("chain", "basin"), None),
        P(("chain", "basin"), None, None, None),
        P(("chain", "basin"), None, None),
        P(("chain", "basin"), None),
    )
    return jax.shard_map(
        shards,
        mesh=mesh,
        in_specs=placed,
        out_specs=(
            P(("runs", "chain", "basin"), None),
            P("runs", None, "feat"),
            P("runs", "feat", None),
        ),
        check_vma=False,
    )
```

```python
import functools

import jax
import jax.numpy as jnp
from jax import lax
from jax.experimental import pallas as pl
from jax.experimental.pallas import tpu as pltpu
from jax.sharding import PartitionSpec as P

BLOCK = 128
LANES = 128
EPS = 1e-06
F32 = jnp.float32
BF16 = jnp.bfloat16
VMEM = pl.BlockSpec(memory_space=pltpu.VMEM)
SMEM = pl.BlockSpec(memory_space=pltpu.SMEM)
ANY = pl.BlockSpec(memory_space=pl.ANY)
NN = (((1,), (0,)), ((), ()))
NT = (((1,), (1,)), ((), ()))
TN = (((0,), (0,)), ((), ()))


def mm(a, b, dims=NN):
    return lax.dot_general(a, b, dims, preferred_element_type=F32)


LIMIT = 24 * 1024 * 1024


def call(body, outs, ins, flops, scratch=(), name=None, after=(), bytes_accessed=4_000_000, scalars=None):
    skipped = len(after)
    return pl.pallas_call(
        lambda *refs: body(*refs[skipped:]),
        out_shape=[jax.ShapeDtypeStruct(s, d) for s, d in outs],
        in_specs=[ANY] * skipped + [SMEM if x is scalars else VMEM for x in ins],
        out_specs=[VMEM] * len(outs),
        scratch_shapes=list(scratch),
        compiler_params=pltpu.CompilerParams(vmem_limit_bytes=LIMIT),
        cost_estimate=pl.CostEstimate(
            flops=flops, bytes_accessed=bytes_accessed, transcendentals=0
        ),
        name=name,
    )(*after, *ins)


def sigmoid(v):
    return 1.0 / (1.0 + jnp.exp(-v))


def half_message(x, w_in, w_out):
    pre = mm(x, w_in)
    return mm((pre * sigmoid(pre)).astype(BF16), w_out)


def message_of(x, halves):
    total = None
    for w_in, w_out in halves:
        part = half_message(x, w_in, w_out)
        total = part if total is None else total + part
    return total.astype(BF16)


def message_grad(x, dmsg, halves):
    total = None
    kept = None
    for w_in, w_out in halves:
        pre = mm(x, w_in)
        sig = sigmoid(pre)
        dact = mm(dmsg, w_out, NT)
        dpre = (dact * (sig * (1.0 + pre * (1.0 - sig)))).astype(BF16)
        if kept is None:
            kept = ((pre * sig).astype(BF16), dpre)
        part = mm(dpre, w_in, NT)
        total = part if total is None else total + part
    return total, kept


def normed_of(total):
    scale = lax.rsqrt(jnp.mean(total * total, axis=-1, keepdims=True) + EPS)
    return scale, scale * total


def norm_grad(grad, total):
    scale, normed = normed_of(total)
    return scale * (grad - normed * jnp.mean(grad * normed, axis=-1, keepdims=True))


def setup_kernel(groups, features, sent, *refs):
    pick, spread, pick_self, held = refs[:4]
    sends = refs[4:]
    rows = features.shape[0]
    held[...] = features[...]
    b = lax.axis_index("basin")
    for route in range(-1, groups):
        if route == 0:
            chosen = lax.broadcasted_iota(jnp.int32, (1, BLOCK), 1) + (rows - BLOCK)
        else:
            chosen = sent[pl.ds(lax.rem(b + max(route, 0), groups), 1), :]
        across = jnp.broadcast_to(chosen, (BLOCK, BLOCK))
        down = across.T
        for r in range(0, rows, BLOCK):
            at = lax.broadcasted_iota(jnp.int32, (BLOCK, BLOCK), 1) + r
            hot = (down == at).astype(F32).astype(BF16)
            if route < 0:
                pick_self[:, r : r + BLOCK] = hot
                continue
            if route > 0:
                pick[(route - 1) * BLOCK : route * BLOCK, r : r + BLOCK] = hot
            at = lax.broadcasted_iota(jnp.int32, (BLOCK, BLOCK), 0) + r
            spread[r : r + BLOCK, route * BLOCK : (route + 1) * BLOCK] = (
                (across == at).astype(F32).astype(BF16)
            )
    pick_sends(features[...], pick, sends)


def pick_sends(rows, pick, sends):
    sends[0][...] = rows[rows.shape[0] - BLOCK :, :]
    for s, send in enumerate(sends[1:]):
        send[...] = mm(pick[s * BLOCK : (s + 1) * BLOCK, :], rows).astype(BF16)


def adjacency_kernel(groups, sources, values, pick_self, _, *refs):
    local, local_t, remote, remote_t, acc = refs
    rows = local.shape[0]
    own = rows // BLOCK
    b = lax.axis_index("basin")
    acc[...] = jnp.zeros_like(acc)
    for k in range(own):
        for t in range(values.shape[1]):
            v = sources[t, k]
            route = jnp.where(v == own, 0, lax.rem(b + groups - (v - own - 1), groups))
            far = jnp.where((v > own) & (route == 0), own, own + 1 + route)
            at = jnp.where(v < own, v, far)
            here = (pl.ds(k * BLOCK, BLOCK), pl.ds(pl.multiple_of(at * BLOCK, BLOCK), BLOCK))
            acc[here] += values[k, t].astype(F32)
    mine = acc[:, rows : rows + BLOCK].astype(BF16)
    full = acc[:, :rows] + mm(mine, pick_self[...])
    local[...] = full.astype(BF16)
    local_t[...] = full.T.astype(BF16)
    far = acc[:, rows + BLOCK :]
    remote[...] = far.astype(BF16)
    remote_t[...] = far.T.astype(BF16)


def message_half(x, w_in, w_out, slope, act_t=None):
    pre = mm(x, w_in)
    sig = sigmoid(pre)
    act = (pre * sig).astype(BF16)
    slope[...] = (sig * (1.0 + pre * (1.0 - sig))).astype(BF16)
    if act_t is not None:
        act_t[...] = act.T
    return mm(act, w_out)


def local_kernel(layer, x, wi0, wi1, wo0, wo1, msg, slope0, slope1, act_t, x_t):
    for r in range(0, x.shape[0], 256):
        here = slice(r, r + 256)
        rows = x[here, :]
        x_t[:, here] = rows.T
        part = message_half(rows, wi0[layer], wo0[layer], slope0.at[here, :], act_t.at[:, here])
        part = part + message_half(rows, wi1[layer], wo1[layer], slope1.at[here, :])
        msg[here, :] = part.astype(BF16)


def half_kernel(x, w_in, w_out, part, slope1):
    for r in range(0, x.shape[0], 256):
        here = slice(r, r + 256)
        part[here, :] = message_half(x[here, :], w_in[0], w_out[0], slope1.at[here, :])


def other_half_kernel(x, w_in, w_out, part, msg, slope0, act_t, x_t):
    for r in range(0, x.shape[0], 256):
        here = slice(r, r + 256)
        rows = x[here, :]
        x_t[:, here] = rows.T
        own = message_half(rows, w_in[0], w_out[0], slope0.at[here, :], act_t.at[:, here])
        msg[here, :] = (part[here, :] + own).astype(BF16)


def remote_mixed(layer, received, columns, weights):
    wi0, wi1, wo0, wo1 = weights
    halves = [(wi0[layer], wo0[layer]), (wi1[layer], wo1[layer])]
    far = jnp.concatenate([x[...] for x in received], axis=0)
    return mm(columns, message_of(far, halves))


def part_kernel(layer, *refs):
    local, msg, remote = refs[:3]
    weights, received, mixed = refs[3:7], refs[7:-1], refs[-1]
    total = mm(local[...], msg[...])
    if received:
        total = total + remote_mixed(layer, received, remote[:, BLOCK:], weights)
    mixed[...] = total


def upstream_rows(got, swapped_got):
    return got[...] + swapped_got[...]


def mixed_total(layer, state, mixed, up, remote, weights):
    return state + mixed[...] + remote_mixed(layer, [up], remote[:, :BLOCK], weights)


def mix_kernel(layer, *refs):
    prev, mixed, remote, pick = refs[:4]
    weights, up = refs[4:8], upstream_rows(*refs[8:10])
    total, inputs = refs[10:12]
    state = prev[...].astype(F32) if layer == 0 else normed_of(prev[...])[1]
    total[...] = mixed_total(layer, state, mixed, up, remote, weights)
    new = normed_of(total[...])[1].astype(BF16)
    inputs[...] = new
    pick_sends(new, pick, refs[12:])


def start_bwd(layer, dtotal_now, weights, received, remote_t, outs):
    dtotal, dround, far_x, far_dmsg, far_act, far_dpre = outs[:6]
    backs = outs[6:]
    wi0, wi1, wo0, wo1 = weights
    halves = [(wi0[layer], wo0[layer]), (wi1[layer], wo1[layer])]
    dtotal[...] = dtotal_now
    dround[...] = dtotal_now.astype(BF16)
    far_x[:BLOCK, :] = upstream_rows(*received[:2])
    for i, block in enumerate(received[2:]):
        far_x[(i + 1) * BLOCK : (i + 2) * BLOCK, :] = block[...]
    dmsg = mm(remote_t[...], dround[...]).astype(BF16)
    back, (act, dpre) = message_grad(far_x[...], dmsg, halves)
    far_dmsg[...] = dmsg
    far_act[...] = act
    far_dpre[...] = dpre
    for i, out in enumerate(backs):
        out[...] = back[i * BLOCK : (i + 1) * BLOCK, :].astype(BF16)


def turn_kernel(layer, groups, *refs):
    prev, mixed, remote, remote_t, cot = refs[:5]
    weights, received, outs = refs[5:9], refs[9 : 10 + groups], refs[10 + groups :]
    state = normed_of(prev[...])[1]
    total = mixed_total(layer, state, mixed, upstream_rows(*received[:2]), remote, weights)
    start_bwd(layer, norm_grad(cot[...], total), weights, received, remote_t, outs)


def back_kernel(layer, grad_scale, *refs):
    dround, local_t, slope0, slope1, act_t, x_t = refs[:6]
    wi0, wi1, wo0, wo1 = refs[6:10]
    far_x, far_dmsg, far_act, far_dpre = refs[10:14]
    back, grads, dmsg, dpre = refs[14:]
    dmsg[...] = mm(local_t[...], dround[...]).astype(BF16)
    for r in range(0, dmsg.shape[0], 256):
        here = slice(r, r + 256)
        rows = dmsg[here, :]
        dpre0 = (mm(rows, wo0[layer], NT) * slope0[here, :].astype(F32)).astype(BF16)
        dpre1 = (mm(rows, wo1[layer], NT) * slope1[here, :].astype(F32)).astype(BF16)
        dpre[here, :] = dpre0
        back[here, :] = mm(dpre0, wi0[layer], NT) + mm(dpre1, wi1[layer], NT)
    latent, hidden = x_t.shape[0], act_t.shape[0]
    g_in = (mm(x_t[...], dpre[...]) + mm(far_x[...], far_dpre[...], TN)) * grad_scale
    for j in range(hidden // LANES):
        grads[j * latent : (j + 1) * latent, :] = g_in[:, j * LANES : (j + 1) * LANES]
    g_out = (mm(act_t[...], dmsg[...]) + mm(far_act[...], far_dmsg[...], TN)) * grad_scale
    for j in range(latent // LANES):
        at = hidden // LANES * latent + j * hidden
        grads[at : at + hidden, :] = g_out[:, j * LANES : (j + 1) * LANES]


def upper(stage):
    (axis0, d0), (axis1, d1) = stage
    bit0 = lax.rem(lax.axis_index(axis0) // d0, 2)
    bit1 = lax.rem(lax.axis_index(axis1) // d1, 2)
    return jnp.where(lax.axis_index("feat") == 0, bit0, bit1)


def place(stage, own, got, out):
    m = own.shape[0]
    bit = upper(stage)
    out[pl.ds(pl.multiple_of(bit * m, m), m), :] = own[...].astype(out.dtype)
    out[pl.ds(pl.multiple_of((1 - bit) * m, m), m), :] = got[...].astype(out.dtype)


def sum_kernel(steps, *refs):
    n_in = sum(1 + (kind != "split") for kind, *_ in steps)
    n_out = len(steps) + 1 + max(group for *_, group, _ in steps)
    ins, outs, accs = refs[:n_in], refs[n_in : n_in + n_out], refs[n_in + n_out :]
    sends = outs[len(steps) :]
    for (kind, stage, back, at, group, to), out in zip(steps, outs):
        own, ins = ins[0], ins[1:]
        m = own.shape[0]
        send = sends[group].at[to : to + out.shape[0]]
        if kind != "split":
            got, ins = ins[0].at[at : at + m], ins[1:]
        if kind in ("split", "add_split"):
            if kind == "add_split":
                acc, accs = accs[0], accs[1:]
                acc[...] = own[...] + got[...].astype(F32)
                own = acc
            m = m // 2
            bit = upper(stage)
            out[...] = own[pl.ds(pl.multiple_of(bit * m, m), m), :]
            send[...] = own[pl.ds(pl.multiple_of((1 - bit) * m, m), m), :].astype(BF16)
        else:
            if kind == "place":
                place(back, own, got, out)
            else:
                out[...] = (own[...] + got[...].astype(F32)).astype(out.dtype)
            send[...] = out[...].astype(BF16)


def write_kernel(layer, stage, kept, halves, *refs):
    parts, (out_in, out_out, token, slab_in, slab_out, sem) = refs[kept:-6], refs[-6:]
    token[...] = jnp.zeros_like(token)
    bit = upper(stage)
    copies = []
    for part, (at, other) in zip(parts, halves):
        m = slab_in.size // LANES
        rows = part.at[at : at + m]
        upper_half = (1 - bit) if other else bit

        @pl.when(upper_half == 0)
        def _():
            write_slab(rows, slab_in, out_in.at[layer], sem.at[0])

        @pl.when(upper_half == 1)
        def _():
            write_slab(rows, slab_out, out_out.at[layer], sem.at[1])

        copies.append(upper_half)
    for upper_half in copies:

        @pl.when(upper_half == 0)
        def _():
            pltpu.make_async_copy(slab_in, out_in.at[layer], sem.at[0]).wait()

        @pl.when(upper_half == 1)
        def _():
            pltpu.make_async_copy(slab_out, out_out.at[layer], sem.at[1]).wait()


def write_slab(rows, slab, out, sem):
    n = slab.shape[0]
    for j in range(slab.shape[1] // LANES):
        slab[:, j * LANES : (j + 1) * LANES] = rows[j * n : (j + 1) * n, :].astype(F32)
    pltpu.make_async_copy(slab, out, sem).start()


class Sum:
    def __init__(self, whole, stages):
        self.own, self.got, self.stages, self.done = whole, None, stages, 0

    def next(self):
        n, i, rows = len(self.stages), self.done, self.own.shape[0]
        if i < n - 1:
            return "add_split" if i else "split", self.stages[i], None, rows // 2, F32
        if i == n - 1:
            return "add", self.stages[i], None, rows, F32
        stage = self.stages[2 * n - 2 - i]
        if i == n:
            return "add", stage, None, rows, BF16
        return "place", stage, self.stages[2 * n - 1 - i], rows * 2, BF16


def sum_step(sums, after):
    steps, ins, outs, scratch, groups = [], [], [], [], {}
    for one in sums:
        kind, stage, back, rows, dtype = one.next()
        group = groups.setdefault(stage, [len(groups), 0])
        steps.append((kind, stage, back, one.got and one.got[1], *group))
        group[1] += rows
        ins += [one.own, one.got[0]] if one.got else [one.own]
        outs.append(((rows, LANES), dtype))
        if kind == "add_split":
            scratch.append(pltpu.VMEM(one.own.shape, F32))
    made = call(
        functools.partial(sum_kernel, steps),
        outs + [((rows, LANES), BF16) for _, rows in groups.values()],
        ins,
        1,
        bytes_accessed=1,
        scratch=scratch,
        name="sum",
        after=after,
    )
    arrived = [swapped(x, stage) for x, stage in zip(made[len(sums) :], groups)]
    for one, own, (*_, group, at) in zip(sums, made, steps):
        one.own, one.got = own, (arrived[group], at)
        one.done += 1
    return [made[0]]


def gathered_grad(dtotal, back, returned, spread):
    far = jnp.concatenate([x[...] for x in returned], axis=0)
    return dtotal[...] + back[...] + mm(spread[...], far)


def join_kernel(layer, groups, *refs):
    dtotal, back, spread, remote_t, total = refs[:5]
    weights, refs = refs[5:9], refs[9:]
    returned, refs = refs[:groups], refs[groups:]
    received, outs = refs[: groups + 1], refs[groups + 1 :]
    grad = gathered_grad(dtotal, back, returned, spread)
    start_bwd(layer, norm_grad(grad, total[...]), weights, received, remote_t, outs)


def last_kernel(*refs):
    dtotal, back, spread = refs[:3]
    refs[-2][...] = gathered_grad(dtotal, back, refs[3:-2], spread)
    refs[-1][...] = jnp.zeros_like(refs[-1])


def around(x, axis, distance):
    n = lax.axis_size(axis)
    return lax.ppermute(x, axis, [(i, (i + distance) % n) for i in range(n)])


def over_mesh(x, target):
    chain, groups, cores = (lax.axis_size(axis) for axis in ("chain", "basin", "feat"))
    perm = []
    for c in range(chain):
        for b in range(groups):
            for feat in range(cores):
                to = target(c, b, feat)
                if to is not None:
                    start, end = (c * groups + b) * cores + feat, (to[0] * groups + to[1]) * cores
                    perm.append((start, end + feat))
    return lax.ppermute(x, ("chain", "basin", "feat"), perm)


def swapped(x, stage):
    def partner(c, b, feat):
        axis, d = stage[feat]
        return (c ^ d, b) if axis == "chain" else (c, b ^ d)

    return over_mesh(x, partner)


def forward(sends):
    chain = lax.axis_size("chain")

    def downstream(c, b, feat):
        return (c + 1, b) if c % 2 == feat and c + 1 < chain else None

    up = over_mesh(sends[0], downstream)
    return [up] + [around(x, "basin", s + 1) for s, x in enumerate(sends[1:])]


def backward(grads):
    chain = lax.axis_size("chain")
    up = lax.ppermute(grads[0], "chain", [(c, c - 1) for c in range(1, chain)])
    return [up] + [around(x, "basin", -s) for s, x in enumerate(grads) if s]


def shards(features, cotangent, w_in, w_out, block_index, block_values, send_rows, send_count):
    rows, latent = features.shape
    groups = lax.axis_size("basin")
    layers, _, half = w_in.shape
    far_rows = groups * BLOCK
    own = rows // BLOCK
    grad_scale = float(rows * lax.axis_size("chain") * groups) ** (-0.5)
    last = layers - 1

    def act16(n, m=latent):
        return ((n, m), BF16)

    wi1 = around(w_in, "feat", 1)
    wo1 = around(w_out, "feat", 1)
    ffn = 4 * latent * 2 * half

    live = jnp.arange(BLOCK, dtype=jnp.int32)[None, :] < send_count[0][:, None]
    sent = jnp.where(live, send_rows[0], -1)
    sources = block_index.T
    pick, spread, pick_self, features, *sends = call(
        functools.partial(setup_kernel, groups),
        [act16(max(groups - 1, 1) * BLOCK, rows), act16(rows, far_rows), act16(BLOCK, rows)]
        + [act16(rows)]
        + [act16(BLOCK)] * groups,
        [features, sent],
        2 * rows * far_rows * latent,
        name="setup",
    )
    weights = (w_in, wi1, w_out, wo1)
    inputs = [features]
    saved = []
    totals = []
    received = []
    for layer in range(layers):
        up, *others = forward(sends)
        if layer == 0:
            part, slope1 = call(
                half_kernel,
                [((rows, latent), F32), act16(rows, half)],
                [features, wi1, wo1],
                rows * ffn // 2,
                name="half",
            )
            msg, slope0, act_t, x_t = call(
                other_half_kernel,
                [act16(rows), act16(rows, half), act16(half, rows), act16(latent, rows)],
                [features, w_in, w_out, part],
                rows * ffn // 2,
                name="local0",
            )
            local, local_t, remote, remote_t = call(
                functools.partial(adjacency_kernel, groups),
                [act16(rows, rows), act16(rows, rows), act16(rows, far_rows), act16(far_rows, rows)],
                [sources, block_values, pick_self, msg],
                2 * rows * rows * BLOCK,
                scratch=[pltpu.VMEM((rows, rows + BLOCK + far_rows), F32)],
                name="adjacency",
                scalars=sources,
            )
            up, local = lax.optimization_barrier((up, local))
        else:
            msg, slope0, slope1, act_t, x_t = call(
                functools.partial(local_kernel, layer),
                [act16(rows), act16(rows, half), act16(rows, half)]
                + [act16(half, rows), act16(latent, rows)],
                [inputs[layer], *weights],
                rows * ffn,
                name=f"local{layer}",
            )
            up, msg = lax.optimization_barrier((up, msg))
        saved.append([slope0, slope1, act_t, x_t])
        received.append([up, around(up, "feat", 1), *others])
        (mixed,) = call(
            functools.partial(part_kernel, layer),
            [((rows, latent), F32)],
            [local, msg, remote, *weights, *others],
            2 * rows * rows * latent,
            name=f"part{layer}",
        )
        prev = totals[-1] if layer else features
        if layer < last:
            total, new, *sends = call(
                functools.partial(mix_kernel, layer),
                [((rows, latent), F32), act16(rows)] + [act16(BLOCK)] * groups,
                [prev, mixed, remote, pick, *weights, *received[layer][:2]],
                far_rows * ffn + 2 * rows * far_rows * latent,
                name=f"mix{layer}",
            )
            totals.append(total)
            inputs.append(new)
    bwd_outs = (
        [((rows, latent), F32), act16(rows), act16(far_rows), act16(far_rows)]
        + [act16(far_rows, half)] * 2
        + [act16(BLOCK)] * groups
    )
    outs = call(
        functools.partial(turn_kernel, last, groups),
        bwd_outs,
        [totals[-1], mixed, remote, remote_t, cotangent, *weights, *received[last]],
        2 * far_rows * ffn,
        name="turn",
    )
    grad_rows = 2 * latent * half // LANES

    def distances(axis):
        return [(axis, 1 << i) for i in range(lax.axis_size(axis).bit_length() - 1)]

    over_basin, over_chain = distances("basin"), distances("chain")
    n = len(over_basin)
    orders = over_basin + over_chain, over_chain[:n] + over_basin + over_chain[n:]
    stages = list(zip(*orders, strict=True))
    basin_first = list(zip(orders[0], orders[0], strict=True))
    returned = {}
    sums = {}

    def back(layer, outs, after):
        returned[layer] = backward(outs[6:])
        grad, whole = call(
            functools.partial(back_kernel, layer, grad_scale),
            [((rows, latent), F32), ((grad_rows, LANES), F32)],
            [outs[1], local_t, *saved[layer], *weights, *outs[2:6]],
            3 * rows * ffn + 2 * rows * rows * latent,
            scratch=[
                pltpu.VMEM((rows, latent), BF16),
                pltpu.VMEM((rows, half), BF16),
            ],
            name=f"back{layer}",
            after=after,
        )
        sums[layer] = Sum(whole, basin_first if layer else stages)
        return [outs[0], grad], [grad]

    def join(layer, state, after):
        if layer:
            return call(
                functools.partial(join_kernel, layer - 1, groups),
                bwd_outs,
                [*state, spread, remote_t, totals[layer - 1]]
                + [*weights, *returned[layer], *received[layer - 1]],
                2 * far_rows * ffn,
                name=f"join{layer}",
                after=after,
            )
        return call(
            last_kernel,
            [((rows, latent), F32), ((8, LANES), F32)],
            [*state, spread, *returned[layer]],
            2 * rows * far_rows * latent,
            name="join0",
            after=after,
        )

    def write(layer, written, after, which=(0, 1)):
        ready = [(sums[layer].own, 0), sums[layer].got]
        ready = [ready[i] for i in which]
        kept = [*written, *after]
        return pl.pallas_call(
            functools.partial(
                write_kernel,
                layer,
                sums[layer].stages[0],
                len(kept),
                [(at, i) for (_, at), i in zip(ready, which)],
            ),
            out_shape=[
                jax.ShapeDtypeStruct((layers, latent, half), F32),
                jax.ShapeDtypeStruct((layers, half, latent), F32),
                jax.ShapeDtypeStruct((8, LANES), F32),
            ],
            in_specs=[ANY] * len(kept) + [VMEM] * len(ready),
            out_specs=[ANY] * 2 + [VMEM],
            scratch_shapes=[
                pltpu.VMEM((latent, half), F32),
                pltpu.VMEM((half, latent), F32),
                pltpu.SemaphoreType.DMA((2,)),
            ],
            input_output_aliases={i: i for i in range(len(written))},
            compiler_params=pltpu.CompilerParams(vmem_limit_bytes=LIMIT),
            cost_estimate=pl.CostEstimate(flops=1, bytes_accessed=1, transcendentals=0),
            name=f"write{layer}",
        )(*written, *after, *[x for x, _ in ready])

    count = 2 * len(stages) - 1
    at = []
    for layer in reversed(range(layers)):
        state, at = back(layer, outs, at)
        arrived = [sums[above].got[0] for above in range(layer + 2, layers)]
        at = sum_step([sums[layer]], at + arrived + returned[layer])
        if layer:
            for above in range(layer + 1, layers):
                at = sum_step([sums[above]], at)
            outs = join(layer, state, at)
            at = outs[1:2]
    while sums[0].done < count:
        for layer in reversed(range(layers)):
            if sums[layer].done < count:
                if layer == 0 and sums[0].done == count - 1:
                    at = at + [sums[above].got[0] for above in range(2, layers)]
                at = sum_step([sums[layer]], at)
    grad, token = join(0, state, at)
    at = [token]
    written = []
    for layer in reversed(range(1, layers)):
        *written, token = write(layer, written, at)
        at = [token]
    *written, token = write(0, written, at, (0,))
    *written, token = write(0, written, [token], (1,))
    return (grad, *written)


def solution(mesh):
    placed = (
        P(("runs", "chain", "basin"), None),
        P(("runs", "chain", "basin"), None),
        P(None, None, "feat"),
        P(None, "feat", None),
        P(("chain", "basin"), None),
        P(("chain", "basin"), None, None, None),
        P(("chain", "basin"), None, None),
        P(("chain", "basin"), None),
    )
    return jax.shard_map(
        shards,
        mesh=mesh,
        in_specs=placed,
        out_specs=(
            P(("runs", "chain", "basin"), None),
            P("runs", None, "feat"),
            P("runs", "feat", None),
        ),
        check_vma=False,
    )
```

```python
import functools

import jax
import jax.numpy as jnp
from jax import lax
from jax.experimental import pallas as pl
from jax.experimental.pallas import tpu as pltpu
from jax.sharding import PartitionSpec as P

BLOCK = 128
LANES = 128
EPS = 1e-06
F32 = jnp.float32
BF16 = jnp.bfloat16
VMEM = pl.BlockSpec(memory_space=pltpu.VMEM)
SMEM = pl.BlockSpec(memory_space=pltpu.SMEM)
ANY = pl.BlockSpec(memory_space=pl.ANY)
NN = (((1,), (0,)), ((), ()))
NT = (((1,), (1,)), ((), ()))
TN = (((0,), (0,)), ((), ()))


def mm(a, b, dims=NN):
    return lax.dot_general(a, b, dims, preferred_element_type=F32)


LIMIT = 24 * 1024 * 1024


def call(body, outs, ins, flops, scratch=(), name=None, after=(), bytes_accessed=4_000_000, scalars=None):
    skipped = len(after)
    return pl.pallas_call(
        lambda *refs: body(*refs[skipped:]),
        out_shape=[jax.ShapeDtypeStruct(s, d) for s, d in outs],
        in_specs=[ANY] * skipped + [SMEM if x is scalars else VMEM for x in ins],
        out_specs=[VMEM] * len(outs),
        scratch_shapes=list(scratch),
        compiler_params=pltpu.CompilerParams(vmem_limit_bytes=LIMIT),
        cost_estimate=pl.CostEstimate(
            flops=flops, bytes_accessed=bytes_accessed, transcendentals=0
        ),
        name=name,
    )(*after, *ins)


def sigmoid(v):
    return 1.0 / (1.0 + jnp.exp(-v))


def half_message(x, w_in, w_out):
    pre = mm(x, w_in)
    return mm((pre * sigmoid(pre)).astype(BF16), w_out)


def message_of(x, halves):
    total = None
    for w_in, w_out in halves:
        part = half_message(x, w_in, w_out)
        total = part if total is None else total + part
    return total.astype(BF16)


def message_grad(x, dmsg, halves):
    total = None
    kept = None
    for w_in, w_out in halves:
        pre = mm(x, w_in)
        sig = sigmoid(pre)
        dact = mm(dmsg, w_out, NT)
        dpre = (dact * (sig * (1.0 + pre * (1.0 - sig)))).astype(BF16)
        if kept is None:
            kept = ((pre * sig).astype(BF16), dpre)
        part = mm(dpre, w_in, NT)
        total = part if total is None else total + part
    return total, kept


def normed_of(total):
    scale = lax.rsqrt(jnp.mean(total * total, axis=-1, keepdims=True) + EPS)
    return scale, scale * total


def norm_grad(grad, total):
    scale, normed = normed_of(total)
    return scale * (grad - normed * jnp.mean(grad * normed, axis=-1, keepdims=True))


def setup_kernel(groups, pairs, features, sent, *refs):
    pick, spread, pick_self, held = refs[:4]
    sends = refs[4:]
    rows = features.shape[0]
    held[...] = features[...]
    b, feat = lax.axis_index("basin"), lax.axis_index("feat")
    for route in range(-1, 2 * pairs):
        if route == 0:
            chosen = lax.broadcasted_iota(jnp.int32, (1, BLOCK), 1) + (rows - BLOCK)
        elif route >= groups:
            chosen = jnp.full((1, BLOCK), -1, jnp.int32)
        else:
            chosen = sent[pl.ds(lax.rem(b + max(route, 0), groups), 1), :]
        across = jnp.broadcast_to(chosen, (BLOCK, BLOCK))
        down = across.T
        for r in range(0, rows, BLOCK):
            at = lax.broadcasted_iota(jnp.int32, (BLOCK, BLOCK), 1) + r
            hot = (down == at).astype(F32).astype(BF16)
            if route < 0:
                pick_self[:, r : r + BLOCK] = hot
                continue

            @pl.when(route % 2 == feat)
            def _():
                pick[route // 2 * BLOCK : (route // 2 + 1) * BLOCK, r : r + BLOCK] = hot

            at = lax.broadcasted_iota(jnp.int32, (BLOCK, BLOCK), 0) + r
            if route < groups:
                spread[r : r + BLOCK, route * BLOCK : (route + 1) * BLOCK] = (
                    (across == at).astype(F32).astype(BF16)
                )
    for i, send in enumerate(sends):
        send[...] = mm(pick[i * BLOCK : (i + 1) * BLOCK, :], features[...]).astype(BF16)


def adjacency_kernel(groups, sources, values, pick_self, _, *refs):
    local, local_t, remote, remote_t, acc = refs
    rows = local.shape[0]
    own = rows // BLOCK
    b = lax.axis_index("basin")
    acc[...] = jnp.zeros_like(acc)
    for k in range(own):
        for t in range(values.shape[1]):
            v = sources[t, k]
            route = jnp.where(v == own, 0, lax.rem(b + groups - (v - own - 1), groups))
            far = jnp.where((v > own) & (route == 0), own, own + 1 + route)
            at = jnp.where(v < own, v, far)
            here = (pl.ds(k * BLOCK, BLOCK), pl.ds(pl.multiple_of(at * BLOCK, BLOCK), BLOCK))
            acc[here] += values[k, t].astype(F32)
    mine = acc[:, rows : rows + BLOCK].astype(BF16)
    full = acc[:, :rows] + mm(mine, pick_self[...])
    local[...] = full.astype(BF16)
    local_t[...] = full.T.astype(BF16)
    far = acc[:, rows + BLOCK :]
    remote[...] = far.astype(BF16)
    remote_t[...] = far.T.astype(BF16)


def message_half(x, w_in, w_out, slope, act_t=None):
    pre = mm(x, w_in)
    sig = sigmoid(pre)
    act = (pre * sig).astype(BF16)
    slope[...] = (sig * (1.0 + pre * (1.0 - sig))).astype(BF16)
    if act_t is not None:
        act_t[...] = act.T
    return mm(act, w_out)


def local_kernel(layer, x, wi0, wi1, wo0, wo1, msg, slope0, slope1, act_t, x_t):
    for r in range(0, x.shape[0], 256):
        here = slice(r, r + 256)
        rows = x[here, :]
        x_t[:, here] = rows.T
        part = message_half(rows, wi0[layer], wo0[layer], slope0.at[here, :], act_t.at[:, here])
        part = part + message_half(rows, wi1[layer], wo1[layer], slope1.at[here, :])
        msg[here, :] = part.astype(BF16)


def half_kernel(x, w_in, w_out, part, slope1):
    for r in range(0, x.shape[0], 256):
        here = slice(r, r + 256)
        part[here, :] = message_half(x[here, :], w_in[0], w_out[0], slope1.at[here, :])


def other_half_kernel(x, w_in, w_out, part, msg, slope0, act_t, x_t):
    for r in range(0, x.shape[0], 256):
        here = slice(r, r + 256)
        rows = x[here, :]
        x_t[:, here] = rows.T
        own = message_half(rows, w_in[0], w_out[0], slope0.at[here, :], act_t.at[:, here])
        msg[here, :] = (part[here, :] + own).astype(BF16)


def remote_mixed(layer, received, remote, feat, weights):
    wi0, wi1, wo0, wo1 = weights
    halves = [(wi0[layer], wo0[layer]), (wi1[layer], wo1[layer])]
    total = None
    for i, block in enumerate(received):
        route = jnp.minimum(2 * i + feat, remote.shape[1] // BLOCK - 1)
        columns = remote[:, pl.ds(pl.multiple_of(route * BLOCK, BLOCK), BLOCK)]
        part = mm(columns, message_of(block[...], halves))
        total = part if total is None else total + part
    return total


def part_kernel(layer, pairs, *refs):
    local, msg, remote = refs[:3]
    weights, received, mixed = refs[3:7], refs[7 : 7 + pairs], refs[-1]
    mixed[...] = mm(local[...], msg[...]) + remote_mixed(
        layer, received, remote, lax.axis_index("feat"), weights
    )


def mixed_total(layer, state, mixed, received, remote, weights):
    return state + mixed[...] + remote_mixed(
        layer, received, remote, 1 - lax.axis_index("feat"), weights
    )


def mix_kernel(layer, pairs, *refs):
    prev, mixed, remote, pick = refs[:4]
    weights = refs[4:8]
    received = refs[8 : 8 + pairs]
    total, inputs = refs[8 + pairs : 10 + pairs]
    sends = refs[10 + pairs :]
    state = prev[...].astype(F32) if layer == 0 else normed_of(prev[...])[1]
    total[...] = mixed_total(layer, state, mixed, received, remote, weights)
    new = normed_of(total[...])[1].astype(BF16)
    inputs[...] = new
    for i, send in enumerate(sends):
        send[...] = mm(pick[i * BLOCK : (i + 1) * BLOCK, :], new).astype(BF16)


def start_bwd(layer, groups, dtotal_now, weights, mine, others, remote_t, outs):
    dtotal, dround, far_x, far_dmsg, far_act, far_dpre = outs[:6]
    backs = outs[6:]
    wi0, wi1, wo0, wo1 = weights
    halves = [(wi0[layer], wo0[layer]), (wi1[layer], wo1[layer])]
    dtotal[...] = dtotal_now
    dround[...] = dtotal_now.astype(BF16)
    for first in range(2):

        @pl.when(lax.axis_index("feat") == first)
        def _():
            for route in range(groups):
                block = (mine, others)[(route + first) % 2][route // 2]
                far_x[route * BLOCK : (route + 1) * BLOCK, :] = block[...]

    dmsg = mm(remote_t[...], dround[...]).astype(BF16)
    back, (act, dpre) = message_grad(far_x[...], dmsg, halves)
    far_dmsg[...] = dmsg
    far_act[...] = act
    far_dpre[...] = dpre
    for i, out in enumerate(backs):
        out[...] = back[i * BLOCK : (i + 1) * BLOCK, :].astype(BF16)


def turn_kernel(layer, groups, pairs, *refs):
    prev, mixed, remote, remote_t, cot = refs[:5]
    weights = refs[5:9]
    mine, others = refs[9 : 9 + pairs], refs[9 + pairs : 9 + 2 * pairs]
    outs = refs[9 + 2 * pairs :]
    state = normed_of(prev[...])[1]
    total = mixed_total(layer, state, mixed, others, remote, weights)
    dtotal = norm_grad(cot[...], total)
    start_bwd(layer, groups, dtotal, weights, mine, others, remote_t, outs)


def back_kernel(layer, grad_scale, *refs):
    dround, local_t, slope0, slope1, act_t, x_t = refs[:6]
    wi0, wi1, wo0, wo1 = refs[6:10]
    far_x, far_dmsg, far_act, far_dpre = refs[10:14]
    back, grads, dmsg, dpre = refs[14:]
    dmsg[...] = mm(local_t[...], dround[...]).astype(BF16)
    for r in range(0, dmsg.shape[0], 256):
        here = slice(r, r + 256)
        rows = dmsg[here, :]
        dpre0 = (mm(rows, wo0[layer], NT) * slope0[here, :].astype(F32)).astype(BF16)
        dpre1 = (mm(rows, wo1[layer], NT) * slope1[here, :].astype(F32)).astype(BF16)
        dpre[here, :] = dpre0
        back[here, :] = mm(dpre0, wi0[layer], NT) + mm(dpre1, wi1[layer], NT)
    latent, hidden = x_t.shape[0], act_t.shape[0]
    g_in = (mm(x_t[...], dpre[...]) + mm(far_x[...], far_dpre[...], TN)) * grad_scale
    for j in range(hidden // LANES):
        grads[j * latent : (j + 1) * latent, :] = g_in[:, j * LANES : (j + 1) * LANES]
    g_out = (mm(act_t[...], dmsg[...]) + mm(far_act[...], far_dmsg[...], TN)) * grad_scale
    for j in range(latent // LANES):
        at = hidden // LANES * latent + j * hidden
        grads[at : at + hidden, :] = g_out[:, j * LANES : (j + 1) * LANES]


def upper(stage):
    (axis0, d0), (axis1, d1) = stage
    bit0 = lax.rem(lax.axis_index(axis0) // d0, 2)
    bit1 = lax.rem(lax.axis_index(axis1) // d1, 2)
    return jnp.where(lax.axis_index("feat") == 0, bit0, bit1)


def place(stage, own, got, out):
    m = own.shape[0]
    bit = upper(stage)
    out[pl.ds(pl.multiple_of(bit * m, m), m), :] = own[...].astype(out.dtype)
    out[pl.ds(pl.multiple_of((1 - bit) * m, m), m), :] = got[...].astype(out.dtype)


def sum_kernel(steps, *refs):
    n_in = sum(1 + (kind != "split") for kind, *_ in steps)
    n_out = len(steps) + 1 + max(group for *_, group, _ in steps)
    ins, outs, accs = refs[:n_in], refs[n_in : n_in + n_out], refs[n_in + n_out :]
    sends = outs[len(steps) :]
    for (kind, stage, back, at, group, to), out in zip(steps, outs):
        own, ins = ins[0], ins[1:]
        m = own.shape[0]
        send = sends[group].at[to : to + out.shape[0]]
        if kind != "split":
            got, ins = ins[0].at[at : at + m], ins[1:]
        if kind in ("split", "add_split"):
            if kind == "add_split":
                acc, accs = accs[0], accs[1:]
                acc[...] = own[...] + got[...].astype(F32)
                own = acc
            m = m // 2
            bit = upper(stage)
            out[...] = own[pl.ds(pl.multiple_of(bit * m, m), m), :]
            send[...] = own[pl.ds(pl.multiple_of((1 - bit) * m, m), m), :].astype(BF16)
        else:
            if kind == "place":
                place(back, own, got, out)
            else:
                out[...] = (own[...] + got[...].astype(F32)).astype(out.dtype)
            send[...] = out[...].astype(BF16)


def write_kernel(layer, stage, kept, halves, *refs):
    parts, (out_in, out_out, token, slab_in, slab_out, sem) = refs[kept:-6], refs[-6:]
    token[...] = jnp.zeros_like(token)
    bit = upper(stage)
    copies = []
    for part, (at, other) in zip(parts, halves):
        m = slab_in.size // LANES
        rows = part.at[at : at + m]
        upper_half = (1 - bit) if other else bit

        @pl.when(upper_half == 0)
        def _():
            write_slab(rows, slab_in, out_in.at[layer], sem.at[0])

        @pl.when(upper_half == 1)
        def _():
            write_slab(rows, slab_out, out_out.at[layer], sem.at[1])

        copies.append(upper_half)
    for upper_half in copies:

        @pl.when(upper_half == 0)
        def _():
            pltpu.make_async_copy(slab_in, out_in.at[layer], sem.at[0]).wait()

        @pl.when(upper_half == 1)
        def _():
            pltpu.make_async_copy(slab_out, out_out.at[layer], sem.at[1]).wait()


def write_slab(rows, slab, out, sem):
    n = slab.shape[0]
    for j in range(slab.shape[1] // LANES):
        slab[:, j * LANES : (j + 1) * LANES] = rows[j * n : (j + 1) * n, :].astype(F32)
    pltpu.make_async_copy(slab, out, sem).start()


class Sum:
    def __init__(self, whole, stages):
        self.own, self.got, self.stages, self.done = whole, None, stages, 0

    def next(self):
        n, i, rows = len(self.stages), self.done, self.own.shape[0]
        if i < n - 1:
            return "add_split" if i else "split", self.stages[i], None, rows // 2, F32
        if i == n - 1:
            return "add", self.stages[i], None, rows, F32
        stage = self.stages[2 * n - 2 - i]
        if i == n:
            return "add", stage, None, rows, BF16
        return "place", stage, self.stages[2 * n - 1 - i], rows * 2, BF16


def sum_step(sums, after):
    steps, ins, outs, scratch, groups = [], [], [], [], {}
    for one in sums:
        kind, stage, back, rows, dtype = one.next()
        group = groups.setdefault(stage, [len(groups), 0])
        steps.append((kind, stage, back, one.got and one.got[1], *group))
        group[1] += rows
        ins += [one.own, one.got[0]] if one.got else [one.own]
        outs.append(((rows, LANES), dtype))
        if kind == "add_split":
            scratch.append(pltpu.VMEM(one.own.shape, F32))
    made = call(
        functools.partial(sum_kernel, steps),
        outs + [((rows, LANES), BF16) for _, rows in groups.values()],
        ins,
        1,
        bytes_accessed=1,
        scratch=scratch,
        name="sum",
        after=after,
    )
    arrived = [swapped(x, stage) for x, stage in zip(made[len(sums) :], groups)]
    for one, own, (*_, group, at) in zip(sums, made, steps):
        one.own, one.got = own, (arrived[group], at)
        one.done += 1
    return [made[0]]


def gathered_grad(dtotal, back, returned, spread):
    far = jnp.concatenate([x[...] for x in returned], axis=0)
    return dtotal[...] + back[...] + mm(spread[...], far)


def join_kernel(layer, groups, pairs, *refs):
    dtotal, back, spread, remote_t, total = refs[:5]
    weights, refs = refs[5:9], refs[9:]
    returned, refs = refs[:groups], refs[groups:]
    mine, others, outs = refs[:pairs], refs[pairs : 2 * pairs], refs[2 * pairs :]
    grad = gathered_grad(dtotal, back, returned, spread)
    dtotal = norm_grad(grad, total[...])
    start_bwd(layer, groups, dtotal, weights, mine, others, remote_t, outs)


def last_kernel(*refs):
    dtotal, back, spread = refs[:3]
    refs[-2][...] = gathered_grad(dtotal, back, refs[3:-2], spread)
    refs[-1][...] = jnp.zeros_like(refs[-1])


def around(x, axis, distance):
    n = lax.axis_size(axis)
    return lax.ppermute(x, axis, [(i, (i + distance) % n) for i in range(n)])


def over_mesh(x, target):
    chain, groups, cores = (lax.axis_size(axis) for axis in ("chain", "basin", "feat"))
    perm = []
    for c in range(chain):
        for b in range(groups):
            for feat in range(cores):
                to = target(c, b, feat)
                if to is not None:
                    start, end = (c * groups + b) * cores + feat, (to[0] * groups + to[1]) * cores
                    perm.append((start, end + feat))
    return lax.ppermute(x, ("chain", "basin", "feat"), perm)


def swapped(x, stage):
    def partner(c, b, feat):
        axis, d = stage[feat]
        return (c ^ d, b) if axis == "chain" else (c, b ^ d)

    return over_mesh(x, partner)


def forward(sends):
    def target(i, c, b, feat):
        route = 2 * i + feat
        if route == 0:
            return (c + 1, b) if c + 1 < lax.axis_size("chain") else None
        groups = lax.axis_size("basin")
        return (c, (b + route) % groups) if route < groups else None

    return [over_mesh(x, functools.partial(target, i)) for i, x in enumerate(sends)]


def other_core(got):
    return [around(x, "feat", 1) for x in got]


def backward(grads):
    chain = lax.axis_size("chain")
    up = lax.ppermute(grads[0], "chain", [(c, c - 1) for c in range(1, chain)])
    return [up] + [around(x, "basin", -s) for s, x in enumerate(grads) if s]


def shards(features, cotangent, w_in, w_out, block_index, block_values, send_rows, send_count):
    rows, latent = features.shape
    groups = lax.axis_size("basin")
    pairs = (groups + 1) // 2
    layers, _, half = w_in.shape
    far_rows = groups * BLOCK
    own = rows // BLOCK
    grad_scale = float(rows * lax.axis_size("chain") * groups) ** (-0.5)
    last = layers - 1

    def act16(n, m=latent):
        return ((n, m), BF16)

    wi1 = around(w_in, "feat", 1)
    wo1 = around(w_out, "feat", 1)
    ffn = 4 * latent * 2 * half

    live = jnp.arange(BLOCK, dtype=jnp.int32)[None, :] < send_count[0][:, None]
    sent = jnp.where(live, send_rows[0], -1)
    sources = block_index.T
    pick, spread, pick_self, features, *sends = call(
        functools.partial(setup_kernel, groups, pairs),
        [act16(pairs * BLOCK, rows), act16(rows, far_rows), act16(BLOCK, rows), act16(rows)]
        + [act16(BLOCK)] * pairs,
        [features, sent],
        2 * rows * far_rows * latent,
        name="setup",
    )
    weights = (w_in, wi1, w_out, wo1)
    inputs = [features]
    saved = []
    totals = []
    mine = []
    others = []
    for layer in range(layers):
        mine.append(forward(sends))
        if layer == 0:
            part, slope1 = call(
                half_kernel,
                [((rows, latent), F32), act16(rows, half)],
                [features, wi1, wo1],
                rows * ffn // 2,
                name="half",
            )
            msg, slope0, act_t, x_t = call(
                other_half_kernel,
                [act16(rows), act16(rows, half), act16(half, rows), act16(latent, rows)],
                [features, w_in, w_out, part],
                rows * ffn // 2,
                name="local0",
            )
            local, local_t, remote, remote_t = call(
                functools.partial(adjacency_kernel, groups),
                [act16(rows, rows), act16(rows, rows), act16(rows, far_rows), act16(far_rows, rows)],
                [sources, block_values, pick_self, msg],
                2 * rows * rows * BLOCK,
                scratch=[pltpu.VMEM((rows, rows + BLOCK + far_rows), F32)],
                name="adjacency",
                scalars=sources,
            )
            mine[0], local = lax.optimization_barrier((mine[0], local))
        else:
            msg, slope0, slope1, act_t, x_t = call(
                functools.partial(local_kernel, layer),
                [act16(rows), act16(rows, half), act16(rows, half)]
                + [act16(half, rows), act16(latent, rows)],
                [inputs[layer], *weights],
                rows * ffn,
                name=f"local{layer}",
            )
            mine[layer], msg = lax.optimization_barrier((mine[layer], msg))
        saved.append([slope0, slope1, act_t, x_t])
        others.append(other_core(mine[layer]))
        (mixed,) = call(
            functools.partial(part_kernel, layer, pairs),
            [((rows, latent), F32)],
            [local, msg, remote, *weights, *mine[layer]],
            2 * rows * rows * latent,
            name=f"part{layer}",
        )
        prev = totals[-1] if layer else features
        if layer < last:
            total, new, *sends = call(
                functools.partial(mix_kernel, layer, pairs),
                [((rows, latent), F32), act16(rows)] + [act16(BLOCK)] * pairs,
                [prev, mixed, remote, pick, *weights, *others[layer]],
                far_rows * ffn + 2 * rows * far_rows * latent,
                name=f"mix{layer}",
            )
            totals.append(total)
            inputs.append(new)
    bwd_outs = (
        [((rows, latent), F32), act16(rows), act16(far_rows), act16(far_rows)]
        + [act16(far_rows, half)] * 2
        + [act16(BLOCK)] * groups
    )
    outs = call(
        functools.partial(turn_kernel, last, groups, pairs),
        bwd_outs,
        [totals[-1], mixed, remote, remote_t, cotangent, *weights, *mine[last], *others[last]],
        2 * far_rows * ffn,
        name="turn",
    )
    grad_rows = 2 * latent * half // LANES

    def distances(axis):
        return [(axis, 1 << i) for i in range(lax.axis_size(axis).bit_length() - 1)]

    over_basin, over_chain = distances("basin"), distances("chain")
    n = len(over_basin)
    orders = over_basin + over_chain, over_chain[:n] + over_basin + over_chain[n:]
    stages = list(zip(*orders, strict=True))
    basin_first = list(zip(orders[0], orders[0], strict=True))
    returned = {}
    sums = {}

    def back(layer, outs, after):
        returned[layer] = backward(outs[6:])
        grad, whole = call(
            functools.partial(back_kernel, layer, grad_scale),
            [((rows, latent), F32), ((grad_rows, LANES), F32)],
            [outs[1], local_t, *saved[layer], *weights, *outs[2:6]],
            3 * rows * ffn + 2 * rows * rows * latent,
            scratch=[
                pltpu.VMEM((rows, latent), BF16),
                pltpu.VMEM((rows, half), BF16),
            ],
            name=f"back{layer}",
            after=after,
        )
        sums[layer] = Sum(whole, basin_first if layer else stages)
        return [outs[0], grad], [grad]

    def join(layer, state, after):
        if layer:
            return call(
                functools.partial(join_kernel, layer - 1, groups, pairs),
                bwd_outs,
                [*state, spread, remote_t, totals[layer - 1]]
                + [*weights, *returned[layer], *mine[layer - 1], *others[layer - 1]],
                2 * far_rows * ffn,
                name=f"join{layer}",
                after=after,
            )
        return call(
            last_kernel,
            [((rows, latent), F32), ((8, LANES), F32)],
            [*state, spread, *returned[layer]],
            2 * rows * far_rows * latent,
            name="join0",
            after=after,
        )

    def write(layer, written, after, which=(0, 1)):
        ready = [(sums[layer].own, 0), sums[layer].got]
        ready = [ready[i] for i in which]
        kept = [*written, *after]
        return pl.pallas_call(
            functools.partial(
                write_kernel,
                layer,
                sums[layer].stages[0],
                len(kept),
                [(at, i) for (_, at), i in zip(ready, which)],
            ),
            out_shape=[
                jax.ShapeDtypeStruct((layers, latent, half), F32),
                jax.ShapeDtypeStruct((layers, half, latent), F32),
                jax.ShapeDtypeStruct((8, LANES), F32),
            ],
            in_specs=[ANY] * len(kept) + [VMEM] * len(ready),
            out_specs=[ANY] * 2 + [VMEM],
            scratch_shapes=[
                pltpu.VMEM((latent, half), F32),
                pltpu.VMEM((half, latent), F32),
                pltpu.SemaphoreType.DMA((2,)),
            ],
            input_output_aliases={i: i for i in range(len(written))},
            compiler_params=pltpu.CompilerParams(vmem_limit_bytes=LIMIT),
            cost_estimate=pl.CostEstimate(flops=1, bytes_accessed=1, transcendentals=0),
            name=f"write{layer}",
        )(*written, *after, *[x for x, _ in ready])

    count = 2 * len(stages) - 1
    at = []
    for layer in reversed(range(layers)):
        state, at = back(layer, outs, at)
        arrived = [sums[above].got[0] for above in range(layer + 2, layers)]
        if layer:
            arrived += returned[layer]
        at = sum_step([sums[layer]], at + arrived)
        if layer:
            for above in range(layer + 1, layers):
                at = sum_step([sums[above]], at)
            outs = join(layer, state, at)
            at = outs[1:2]
    while sums[0].done < count:
        for layer in reversed(range(layers)):
            if sums[layer].done < count:
                if layer == 0 and sums[0].done == count - 1:
                    at = at + returned[0] + [sums[above].got[0] for above in range(2, layers)]
                at = sum_step([sums[layer]], at)
    grad, token = join(0, state, at)
    at = [token]
    written = []
    for layer in reversed(range(1, layers)):
        *written, token = write(layer, written, at)
        at = [token]
    *written, token = write(0, written, at, (0,))
    *written, token = write(0, written, [token], (1,))
    return (grad, *written)


def solution(mesh):
    placed = (
        P(("runs", "chain", "basin"), None),
        P(("runs", "chain", "basin"), None),
        P(None, None, "feat"),
        P(None, "feat", None),
        P(("chain", "basin"), None),
        P(("chain", "basin"), None, None, None),
        P(("chain", "basin"), None, None),
        P(("chain", "basin"), None),
    )
    return jax.shard_map(
        shards,
        mesh=mesh,
        in_specs=placed,
        out_specs=(
            P(("runs", "chain", "basin"), None),
            P("runs", None, "feat"),
            P("runs", "feat", None),
        ),
        check_vma=False,
    )
```

```python
import functools

import jax
import jax.numpy as jnp
from jax import lax
from jax.experimental import pallas as pl
from jax.experimental.pallas import tpu as pltpu
from jax.sharding import PartitionSpec as P

BLOCK = 128
LANES = 128
EPS = 1e-06
F32 = jnp.float32
BF16 = jnp.bfloat16
VMEM = pl.BlockSpec(memory_space=pltpu.VMEM)
SMEM = pl.BlockSpec(memory_space=pltpu.SMEM)
ANY = pl.BlockSpec(memory_space=pl.ANY)
NN = (((1,), (0,)), ((), ()))
NT = (((1,), (1,)), ((), ()))
TN = (((0,), (0,)), ((), ()))


def mm(a, b, dims=NN):
    return lax.dot_general(a, b, dims, preferred_element_type=F32)


LIMIT = 24 * 1024 * 1024


def call(body, outs, ins, flops, scratch=(), name=None, after=(), bytes_accessed=4_000_000, scalars=None):
    skipped = len(after)
    return pl.pallas_call(
        lambda *refs: body(*refs[skipped:]),
        out_shape=[jax.ShapeDtypeStruct(s, d) for s, d in outs],
        in_specs=[ANY] * skipped + [SMEM if x is scalars else VMEM for x in ins],
        out_specs=[VMEM] * len(outs),
        scratch_shapes=list(scratch),
        compiler_params=pltpu.CompilerParams(vmem_limit_bytes=LIMIT),
        cost_estimate=pl.CostEstimate(
            flops=flops, bytes_accessed=bytes_accessed, transcendentals=0
        ),
        name=name,
    )(*after, *ins)


def sigmoid(v):
    return 1.0 / (1.0 + jnp.exp(-v))


def half_message(x, w_in, w_out):
    pre = mm(x, w_in)
    return mm((pre * sigmoid(pre)).astype(BF16), w_out)


def message_of(x, halves):
    total = None
    for w_in, w_out in halves:
        part = half_message(x, w_in, w_out)
        total = part if total is None else total + part
    return total.astype(BF16)


def message_grad(x, dmsg, halves):
    total = None
    kept = None
    for w_in, w_out in halves:
        pre = mm(x, w_in)
        sig = sigmoid(pre)
        dact = mm(dmsg, w_out, NT)
        dpre = (dact * (sig * (1.0 + pre * (1.0 - sig)))).astype(BF16)
        if kept is None:
            kept = ((pre * sig).astype(BF16), dpre)
        part = mm(dpre, w_in, NT)
        total = part if total is None else total + part
    return total, kept


def normed_of(total):
    scale = lax.rsqrt(jnp.mean(total * total, axis=-1, keepdims=True) + EPS)
    return scale, scale * total


def norm_grad(grad, total):
    scale, normed = normed_of(total)
    return scale * (grad - normed * jnp.mean(grad * normed, axis=-1, keepdims=True))


def setup_kernel(groups, pairs, features, sent, *refs):
    pick, spread, pick_self, held = refs[:4]
    sends = refs[4:]
    rows = features.shape[0]
    held[...] = features[...]
    b, feat = lax.axis_index("basin"), lax.axis_index("feat")
    for route in range(-1, 2 * pairs):
        if route == 0:
            chosen = lax.broadcasted_iota(jnp.int32, (1, BLOCK), 1) + (rows - BLOCK)
        elif route >= groups:
            chosen = jnp.full((1, BLOCK), -1, jnp.int32)
        else:
            chosen = sent[pl.ds(lax.rem(b + max(route, 0), groups), 1), :]
        across = jnp.broadcast_to(chosen, (BLOCK, BLOCK))
        down = across.T
        for r in range(0, rows, BLOCK):
            at = lax.broadcasted_iota(jnp.int32, (BLOCK, BLOCK), 1) + r
            hot = (down == at).astype(F32).astype(BF16)
            if route < 0:
                pick_self[:, r : r + BLOCK] = hot
                continue

            @pl.when(route % 2 == feat)
            def _():
                pick[route // 2 * BLOCK : (route // 2 + 1) * BLOCK, r : r + BLOCK] = hot

            at = lax.broadcasted_iota(jnp.int32, (BLOCK, BLOCK), 0) + r
            if route < groups:
                spread[r : r + BLOCK, route * BLOCK : (route + 1) * BLOCK] = (
                    (across == at).astype(F32).astype(BF16)
                )
    for i, send in enumerate(sends):
        send[...] = mm(pick[i * BLOCK : (i + 1) * BLOCK, :], features[...]).astype(BF16)


def adjacency_kernel(groups, sources, values, pick_self, _, *refs):
    local, local_t, remote, remote_t, acc = refs
    rows = local.shape[0]
    own = rows // BLOCK
    b = lax.axis_index("basin")
    acc[...] = jnp.zeros_like(acc)
    for k in range(own):
        for t in range(values.shape[1]):
            v = sources[t, k]
            route = jnp.where(v == own, 0, lax.rem(b + groups - (v - own - 1), groups))
            far = jnp.where((v > own) & (route == 0), own, own + 1 + route)
            at = jnp.where(v < own, v, far)
            here = (pl.ds(k * BLOCK, BLOCK), pl.ds(pl.multiple_of(at * BLOCK, BLOCK), BLOCK))
            acc[here] += values[k, t].astype(F32)
    mine = acc[:, rows : rows + BLOCK].astype(BF16)
    full = acc[:, :rows] + mm(mine, pick_self[...])
    local[...] = full.astype(BF16)
    local_t[...] = full.T.astype(BF16)
    far = acc[:, rows + BLOCK :]
    remote[...] = far.astype(BF16)
    remote_t[...] = far.T.astype(BF16)


def message_half(x, w_in, w_out, slope, act_t=None):
    pre = mm(x, w_in)
    sig = sigmoid(pre)
    act = (pre * sig).astype(BF16)
    slope[...] = (sig * (1.0 + pre * (1.0 - sig))).astype(BF16)
    if act_t is not None:
        act_t[...] = act.T
    return mm(act, w_out)


def local_kernel(layer, x, wi0, wi1, wo0, wo1, msg, slope0, slope1, act_t, x_t):
    for r in range(0, x.shape[0], 256):
        here = slice(r, r + 256)
        rows = x[here, :]
        x_t[:, here] = rows.T
        part = message_half(rows, wi0[layer], wo0[layer], slope0.at[here, :], act_t.at[:, here])
        part = part + message_half(rows, wi1[layer], wo1[layer], slope1.at[here, :])
        msg[here, :] = part.astype(BF16)


def half_kernel(x, w_in, w_out, part, slope1):
    for r in range(0, x.shape[0], 256):
        here = slice(r, r + 256)
        part[here, :] = message_half(x[here, :], w_in[0], w_out[0], slope1.at[here, :])


def other_half_kernel(x, w_in, w_out, part, msg, slope0, act_t, x_t):
    for r in range(0, x.shape[0], 256):
        here = slice(r, r + 256)
        rows = x[here, :]
        x_t[:, here] = rows.T
        own = message_half(rows, w_in[0], w_out[0], slope0.at[here, :], act_t.at[:, here])
        msg[here, :] = (part[here, :] + own).astype(BF16)


def remote_mixed(layer, received, remote, feat, weights):
    wi0, wi1, wo0, wo1 = weights
    halves = [(wi0[layer], wo0[layer]), (wi1[layer], wo1[layer])]
    total = None
    for i, block in enumerate(received):
        route = jnp.minimum(2 * i + feat, remote.shape[1] // BLOCK - 1)
        columns = remote[:, pl.ds(pl.multiple_of(route * BLOCK, BLOCK), BLOCK)]
        part = mm(columns, message_of(block[...], halves))
        total = part if total is None else total + part
    return total


def part_kernel(layer, pairs, *refs):
    local, msg, remote = refs[:3]
    weights, received, mixed = refs[3:7], refs[7 : 7 + pairs], refs[-1]
    mixed[...] = mm(local[...], msg[...]) + remote_mixed(
        layer, received, remote, lax.axis_index("feat"), weights
    )


def mixed_total(layer, state, mixed, received, remote, weights):
    return state + mixed[...] + remote_mixed(
        layer, received, remote, 1 - lax.axis_index("feat"), weights
    )


def mix_kernel(layer, pairs, *refs):
    prev, mixed, remote, pick = refs[:4]
    weights = refs[4:8]
    received = refs[8 : 8 + pairs]
    total, inputs = refs[8 + pairs : 10 + pairs]
    sends = refs[10 + pairs :]
    state = prev[...].astype(F32) if layer == 0 else normed_of(prev[...])[1]
    total[...] = mixed_total(layer, state, mixed, received, remote, weights)
    new = normed_of(total[...])[1].astype(BF16)
    inputs[...] = new
    for i, send in enumerate(sends):
        send[...] = mm(pick[i * BLOCK : (i + 1) * BLOCK, :], new).astype(BF16)


def start_bwd(layer, groups, dtotal_now, weights, mine, others, remote_t, outs):
    dtotal, dround, far_x, far_dmsg, far_act, far_dpre = outs[:6]
    backs = outs[6:]
    wi0, wi1, wo0, wo1 = weights
    halves = [(wi0[layer], wo0[layer]), (wi1[layer], wo1[layer])]
    dtotal[...] = dtotal_now
    dround[...] = dtotal_now.astype(BF16)
    for first in range(2):

        @pl.when(lax.axis_index("feat") == first)
        def _():
            for route in range(groups):
                block = (mine, others)[(route + first) % 2][route // 2]
                far_x[route * BLOCK : (route + 1) * BLOCK, :] = block[...]

    dmsg = mm(remote_t[...], dround[...]).astype(BF16)
    back, (act, dpre) = message_grad(far_x[...], dmsg, halves)
    far_dmsg[...] = dmsg
    far_act[...] = act
    far_dpre[...] = dpre
    for i, out in enumerate(backs):
        out[...] = back[i * BLOCK : (i + 1) * BLOCK, :].astype(BF16)


def turn_kernel(layer, groups, pairs, *refs):
    prev, mixed, remote, remote_t, cot = refs[:5]
    weights = refs[5:9]
    mine, others = refs[9 : 9 + pairs], refs[9 + pairs : 9 + 2 * pairs]
    outs = refs[9 + 2 * pairs :]
    state = normed_of(prev[...])[1]
    total = mixed_total(layer, state, mixed, others, remote, weights)
    dtotal = norm_grad(cot[...], total)
    start_bwd(layer, groups, dtotal, weights, mine, others, remote_t, outs)


def back_kernel(layer, grad_scale, *refs):
    dround, local_t, slope0, slope1, act_t, x_t = refs[:6]
    wi0, wi1, wo0, wo1 = refs[6:10]
    far_x, far_dmsg, far_act, far_dpre = refs[10:14]
    back, grads, dmsg, dpre = refs[14:]
    dmsg[...] = mm(local_t[...], dround[...]).astype(BF16)
    for r in range(0, dmsg.shape[0], 256):
        here = slice(r, r + 256)
        rows = dmsg[here, :]
        dpre0 = (mm(rows, wo0[layer], NT) * slope0[here, :].astype(F32)).astype(BF16)
        dpre1 = (mm(rows, wo1[layer], NT) * slope1[here, :].astype(F32)).astype(BF16)
        dpre[here, :] = dpre0
        back[here, :] = mm(dpre0, wi0[layer], NT) + mm(dpre1, wi1[layer], NT)
    latent, hidden = x_t.shape[0], act_t.shape[0]
    g_in = (mm(x_t[...], dpre[...]) + mm(far_x[...], far_dpre[...], TN)) * grad_scale
    for j in range(hidden // LANES):
        grads[j * latent : (j + 1) * latent, :] = g_in[:, j * LANES : (j + 1) * LANES]
    g_out = (mm(act_t[...], dmsg[...]) + mm(far_act[...], far_dmsg[...], TN)) * grad_scale
    for j in range(latent // LANES):
        at = hidden // LANES * latent + j * hidden
        grads[at : at + hidden, :] = g_out[:, j * LANES : (j + 1) * LANES]


def upper(stage):
    (axis0, d0), (axis1, d1) = stage
    bit0 = lax.rem(lax.axis_index(axis0) // d0, 2)
    bit1 = lax.rem(lax.axis_index(axis1) // d1, 2)
    return jnp.where(lax.axis_index("feat") == 0, bit0, bit1)


def place(stage, own, got, out):
    m = own.shape[0]
    bit = upper(stage)
    out[pl.ds(pl.multiple_of(bit * m, m), m), :] = own[...].astype(out.dtype)
    out[pl.ds(pl.multiple_of((1 - bit) * m, m), m), :] = got[...].astype(out.dtype)


def sum_kernel(steps, *refs):
    n_in = sum(1 + (kind != "split") for kind, *_ in steps)
    n_out = len(steps) + 1 + max(group for *_, group, _ in steps)
    ins, outs, accs = refs[:n_in], refs[n_in : n_in + n_out], refs[n_in + n_out :]
    sends = outs[len(steps) :]
    for (kind, stage, back, at, group, to), out in zip(steps, outs):
        own, ins = ins[0], ins[1:]
        m = own.shape[0]
        send = sends[group].at[to : to + out.shape[0]]
        if kind != "split":
            got, ins = ins[0].at[at : at + m], ins[1:]
        if kind in ("split", "add_split"):
            if kind == "add_split":
                acc, accs = accs[0], accs[1:]
                acc[...] = own[...] + got[...].astype(F32)
                own = acc
            m = m // 2
            bit = upper(stage)
            out[...] = own[pl.ds(pl.multiple_of(bit * m, m), m), :]
            send[...] = own[pl.ds(pl.multiple_of((1 - bit) * m, m), m), :].astype(BF16)
        else:
            if kind == "place":
                place(back, own, got, out)
            else:
                out[...] = (own[...] + got[...].astype(F32)).astype(out.dtype)
            send[...] = out[...].astype(BF16)


def write_kernel(layer, stage, kept, halves, *refs):
    parts, (out_in, out_out, token, slab_in, slab_out, sem) = refs[kept:-6], refs[-6:]
    token[...] = jnp.zeros_like(token)
    bit = upper(stage)
    copies = []
    for part, (at, other) in zip(parts, halves):
        m = slab_in.size // LANES
        rows = part.at[at : at + m]
        upper_half = (1 - bit) if other else bit

        @pl.when(upper_half == 0)
        def _():
            write_slab(rows, slab_in, out_in.at[layer], sem.at[0])

        @pl.when(upper_half == 1)
        def _():
            write_slab(rows, slab_out, out_out.at[layer], sem.at[1])

        copies.append(upper_half)
    for upper_half in copies:

        @pl.when(upper_half == 0)
        def _():
            pltpu.make_async_copy(slab_in, out_in.at[layer], sem.at[0]).wait()

        @pl.when(upper_half == 1)
        def _():
            pltpu.make_async_copy(slab_out, out_out.at[layer], sem.at[1]).wait()


def write_slab(rows, slab, out, sem):
    n = slab.shape[0]
    for j in range(slab.shape[1] // LANES):
        slab[:, j * LANES : (j + 1) * LANES] = rows[j * n : (j + 1) * n, :].astype(F32)
    pltpu.make_async_copy(slab, out, sem).start()


class Sum:
    def __init__(self, whole, stages):
        self.own, self.got, self.stages, self.done = whole, None, stages, 0

    def next(self):
        n, i, rows = len(self.stages), self.done, self.own.shape[0]
        if i < n - 1:
            return "add_split" if i else "split", self.stages[i], None, rows // 2, F32
        if i == n - 1:
            return "add", self.stages[i], None, rows, F32
        stage = self.stages[2 * n - 2 - i]
        if i == n:
            return "add", stage, None, rows, BF16
        return "place", stage, self.stages[2 * n - 1 - i], rows * 2, BF16


def sum_step(sums, after):
    steps, ins, outs, scratch, groups = [], [], [], [], {}
    for one in sums:
        kind, stage, back, rows, dtype = one.next()
        group = groups.setdefault(stage, [len(groups), 0])
        steps.append((kind, stage, back, one.got and one.got[1], *group))
        group[1] += rows
        ins += [one.own, one.got[0]] if one.got else [one.own]
        outs.append(((rows, LANES), dtype))
        if kind == "add_split":
            scratch.append(pltpu.VMEM(one.own.shape, F32))
    made = call(
        functools.partial(sum_kernel, steps),
        outs + [((rows, LANES), BF16) for _, rows in groups.values()],
        ins,
        1,
        bytes_accessed=1,
        scratch=scratch,
        name="sum",
        after=after,
    )
    arrived = [swapped(x, stage) for x, stage in zip(made[len(sums) :], groups)]
    for one, own, (*_, group, at) in zip(sums, made, steps):
        one.own, one.got = own, (arrived[group], at)
        one.done += 1
    return [made[0]]


def gathered_grad(dtotal, back, returned, spread):
    far = jnp.concatenate([x[...] for x in returned], axis=0)
    return dtotal[...] + back[...] + mm(spread[...], far)


def join_kernel(layer, groups, pairs, *refs):
    dtotal, back, spread, remote_t, total = refs[:5]
    weights, refs = refs[5:9], refs[9:]
    returned, refs = refs[:groups], refs[groups:]
    mine, others, outs = refs[:pairs], refs[pairs : 2 * pairs], refs[2 * pairs :]
    grad = gathered_grad(dtotal, back, returned, spread)
    dtotal = norm_grad(grad, total[...])
    start_bwd(layer, groups, dtotal, weights, mine, others, remote_t, outs)


def last_kernel(*refs):
    dtotal, back, spread = refs[:3]
    refs[-2][...] = gathered_grad(dtotal, back, refs[3:-2], spread)
    refs[-1][...] = jnp.zeros_like(refs[-1])


def around(x, axis, distance):
    n = lax.axis_size(axis)
    return lax.ppermute(x, axis, [(i, (i + distance) % n) for i in range(n)])


def over_mesh(x, target):
    chain, groups, cores = (lax.axis_size(axis) for axis in ("chain", "basin", "feat"))
    perm = []
    for c in range(chain):
        for b in range(groups):
            for feat in range(cores):
                to = target(c, b, feat)
                if to is not None:
                    start, end = (c * groups + b) * cores + feat, (to[0] * groups + to[1]) * cores
                    perm.append((start, end + feat))
    return lax.ppermute(x, ("chain", "basin", "feat"), perm)


def swapped(x, stage):
    def partner(c, b, feat):
        axis, d = stage[feat]
        return (c ^ d, b) if axis == "chain" else (c, b ^ d)

    return over_mesh(x, partner)


def forward(sends):
    def target(i, c, b, feat):
        route = 2 * i + feat
        if route == 0:
            return (c + 1, b) if c + 1 < lax.axis_size("chain") else None
        groups = lax.axis_size("basin")
        return (c, (b + route) % groups) if route < groups else None

    return [over_mesh(x, functools.partial(target, i)) for i, x in enumerate(sends)]


def other_core(got):
    return [around(x, "feat", 1) for x in got]


def backward(grads):
    chain = lax.axis_size("chain")
    up = lax.ppermute(grads[0], "chain", [(c, c - 1) for c in range(1, chain)])
    return [up] + [around(x, "basin", -s) for s, x in enumerate(grads) if s]


def shards(features, cotangent, w_in, w_out, block_index, block_values, send_rows, send_count):
    rows, latent = features.shape
    groups = lax.axis_size("basin")
    pairs = (groups + 1) // 2
    layers, _, half = w_in.shape
    far_rows = groups * BLOCK
    own = rows // BLOCK
    grad_scale = float(rows * lax.axis_size("chain") * groups) ** (-0.5)
    last = layers - 1

    def act16(n, m=latent):
        return ((n, m), BF16)

    wi1 = around(w_in, "feat", 1)
    wo1 = around(w_out, "feat", 1)
    ffn = 4 * latent * 2 * half

    live = jnp.arange(BLOCK, dtype=jnp.int32)[None, :] < send_count[0][:, None]
    sent = jnp.where(live, send_rows[0], -1)
    sources = block_index.T
    pick, spread, pick_self, features, *sends = call(
        functools.partial(setup_kernel, groups, pairs),
        [act16(pairs * BLOCK, rows), act16(rows, far_rows), act16(BLOCK, rows), act16(rows)]
        + [act16(BLOCK)] * pairs,
        [features, sent],
        2 * rows * far_rows * latent,
        name="setup",
    )
    weights = (w_in, wi1, w_out, wo1)
    inputs = [features]
    saved = []
    totals = []
    mine = []
    others = []
    for layer in range(layers):
        mine.append(forward(sends))
        if layer == 0:
            part, slope1 = call(
                half_kernel,
                [((rows, latent), F32), act16(rows, half)],
                [features, wi1, wo1],
                rows * ffn // 2,
                name="half",
            )
            msg, slope0, act_t, x_t = call(
                other_half_kernel,
                [act16(rows), act16(rows, half), act16(half, rows), act16(latent, rows)],
                [features, w_in, w_out, part],
                rows * ffn // 2,
                name="local0",
            )
            local, local_t, remote, remote_t = call(
                functools.partial(adjacency_kernel, groups),
                [act16(rows, rows), act16(rows, rows), act16(rows, far_rows), act16(far_rows, rows)],
                [sources, block_values, pick_self, msg],
                2 * rows * rows * BLOCK,
                scratch=[pltpu.VMEM((rows, rows + BLOCK + far_rows), F32)],
                name="adjacency",
                scalars=sources,
            )
            mine[0], local = lax.optimization_barrier((mine[0], local))
        else:
            msg, slope0, slope1, act_t, x_t = call(
                functools.partial(local_kernel, layer),
                [act16(rows), act16(rows, half), act16(rows, half)]
                + [act16(half, rows), act16(latent, rows)],
                [inputs[layer], *weights],
                rows * ffn,
                name=f"local{layer}",
            )
            mine[layer], msg = lax.optimization_barrier((mine[layer], msg))
        saved.append([slope0, slope1, act_t, x_t])
        others.append(other_core(mine[layer]))
        (mixed,) = call(
            functools.partial(part_kernel, layer, pairs),
            [((rows, latent), F32)],
            [local, msg, remote, *weights, *mine[layer]],
            2 * rows * rows * latent,
            name=f"part{layer}",
        )
        prev = totals[-1] if layer else features
        if layer < last:
            total, new, *sends = call(
                functools.partial(mix_kernel, layer, pairs),
                [((rows, latent), F32), act16(rows)] + [act16(BLOCK)] * pairs,
                [prev, mixed, remote, pick, *weights, *others[layer]],
                far_rows * ffn + 2 * rows * far_rows * latent,
                name=f"mix{layer}",
            )
            totals.append(total)
            inputs.append(new)
    bwd_outs = (
        [((rows, latent), F32), act16(rows), act16(far_rows), act16(far_rows)]
        + [act16(far_rows, half)] * 2
        + [act16(BLOCK)] * groups
    )
    outs = call(
        functools.partial(turn_kernel, last, groups, pairs),
        bwd_outs,
        [totals[-1], mixed, remote, remote_t, cotangent, *weights, *mine[last], *others[last]],
        2 * far_rows * ffn,
        name="turn",
    )
    grad_rows = 2 * latent * half // LANES

    def distances(axis):
        return [(axis, 1 << i) for i in range(lax.axis_size(axis).bit_length() - 1)]

    over_basin, over_chain = distances("basin"), distances("chain")
    n = len(over_basin)
    orders = over_basin + over_chain, over_chain[:n] + over_basin + over_chain[n:]
    stages = list(zip(*orders, strict=True))
    basin_first = list(zip(orders[0], orders[0], strict=True))
    returned = {}
    sums = {}

    def back(layer, outs, after):
        returned[layer] = backward(outs[6:])
        grad, whole = call(
            functools.partial(back_kernel, layer, grad_scale),
            [((rows, latent), F32), ((grad_rows, LANES), F32)],
            [outs[1], local_t, *saved[layer], *weights, *outs[2:6]],
            3 * rows * ffn + 2 * rows * rows * latent,
            scratch=[
                pltpu.VMEM((rows, latent), BF16),
                pltpu.VMEM((rows, half), BF16),
            ],
            name=f"back{layer}",
            after=after,
        )
        sums[layer] = Sum(whole, basin_first if layer > 1 else stages)
        return [outs[0], grad], [grad]

    def join(layer, state, after):
        if layer:
            return call(
                functools.partial(join_kernel, layer - 1, groups, pairs),
                bwd_outs,
                [*state, spread, remote_t, totals[layer - 1]]
                + [*weights, *returned[layer], *mine[layer - 1], *others[layer - 1]],
                2 * far_rows * ffn,
                name=f"join{layer}",
                after=after,
            )
        return call(
            last_kernel,
            [((rows, latent), F32), ((8, LANES), F32)],
            [*state, spread, *returned[layer]],
            2 * rows * far_rows * latent,
            name="join0",
            after=after,
        )

    def write(layer, written, after, which=(0, 1)):
        ready = [(sums[layer].own, 0), sums[layer].got]
        ready = [ready[i] for i in which]
        kept = [*written, *after]
        return pl.pallas_call(
            functools.partial(
                write_kernel,
                layer,
                sums[layer].stages[0],
                len(kept),
                [(at, i) for (_, at), i in zip(ready, which)],
            ),
            out_shape=[
                jax.ShapeDtypeStruct((layers, latent, half), F32),
                jax.ShapeDtypeStruct((layers, half, latent), F32),
                jax.ShapeDtypeStruct((8, LANES), F32),
            ],
            in_specs=[ANY] * len(kept) + [VMEM] * len(ready),
            out_specs=[ANY] * 2 + [VMEM],
            scratch_shapes=[
                pltpu.VMEM((latent, half), F32),
                pltpu.VMEM((half, latent), F32),
                pltpu.SemaphoreType.DMA((2,)),
            ],
            input_output_aliases={i: i for i in range(len(written))},
            compiler_params=pltpu.CompilerParams(vmem_limit_bytes=LIMIT),
            cost_estimate=pl.CostEstimate(flops=1, bytes_accessed=1, transcendentals=0),
            name=f"write{layer}",
        )(*written, *after, *[x for x, _ in ready])

    count = 2 * len(stages) - 1
    at = []
    for layer in reversed(range(layers)):
        state, at = back(layer, outs, at)
        arrived = [sums[above].got[0] for above in range(layer + 2, layers)]
        if layer:
            arrived += returned[layer]
        at = sum_step([sums[layer]], at + arrived)
        if layer:
            for above in range(layer + 1, layers):
                at = sum_step([sums[above]], at)
            outs = join(layer, state, at)
            at = outs[1:2]
    while sums[0].done < count:
        for layer in reversed(range(layers)):
            if sums[layer].done < count:
                if layer == 0 and sums[0].done == count - 1:
                    at = at + returned[0] + [sums[above].got[0] for above in range(2, layers)]
                at = sum_step([sums[layer]], at)
    grad, token = join(0, state, at)
    at = [token]
    written = []
    for layer in reversed(range(1, layers)):
        *written, token = write(layer, written, at)
        at = [token]
    *written, token = write(0, written, at, (0,))
    *written, token = write(0, written, [token], (1,))
    return (grad, *written)


def solution(mesh):
    placed = (
        P(("runs", "chain", "basin"), None),
        P(("runs", "chain", "basin"), None),
        P(None, None, "feat"),
        P(None, "feat", None),
        P(("chain", "basin"), None),
        P(("chain", "basin"), None, None, None),
        P(("chain", "basin"), None, None),
        P(("chain", "basin"), None),
    )
    return jax.shard_map(
        shards,
        mesh=mesh,
        in_specs=placed,
        out_specs=(
            P(("runs", "chain", "basin"), None),
            P("runs", None, "feat"),
            P("runs", "feat", None),
        ),
        check_vma=False,
    )
```

```python
import functools

import jax
import jax.numpy as jnp
from jax import lax
from jax.experimental import pallas as pl
from jax.experimental.pallas import tpu as pltpu
from jax.sharding import PartitionSpec as P

BLOCK = 128
LANES = 128
EPS = 1e-06
F32 = jnp.float32
BF16 = jnp.bfloat16
VMEM = pl.BlockSpec(memory_space=pltpu.VMEM)
SMEM = pl.BlockSpec(memory_space=pltpu.SMEM)
ANY = pl.BlockSpec(memory_space=pl.ANY)
NN = (((1,), (0,)), ((), ()))
NT = (((1,), (1,)), ((), ()))
TN = (((0,), (0,)), ((), ()))


def mm(a, b, dims=NN):
    return lax.dot_general(a, b, dims, preferred_element_type=F32)


LIMIT = 24 * 1024 * 1024


def call(body, outs, ins, flops, scratch=(), name=None, after=(), bytes_accessed=4_000_000, scalars=None):
    skipped = len(after)
    return pl.pallas_call(
        lambda *refs: body(*refs[skipped:]),
        out_shape=[jax.ShapeDtypeStruct(s, d) for s, d in outs],
        in_specs=[ANY] * skipped + [SMEM if x is scalars else VMEM for x in ins],
        out_specs=[VMEM] * len(outs),
        scratch_shapes=list(scratch),
        compiler_params=pltpu.CompilerParams(vmem_limit_bytes=LIMIT),
        cost_estimate=pl.CostEstimate(
            flops=flops, bytes_accessed=bytes_accessed, transcendentals=0
        ),
        name=name,
    )(*after, *ins)


def sigmoid(v):
    return 1.0 / (1.0 + jnp.exp(-v))


def half_message(x, w_in, w_out):
    pre = mm(x, w_in)
    return mm((pre * sigmoid(pre)).astype(BF16), w_out)


def message_of(x, halves):
    total = None
    for w_in, w_out in halves:
        part = half_message(x, w_in, w_out)
        total = part if total is None else total + part
    return total.astype(BF16)


def message_grad(x, dmsg, halves):
    total = None
    kept = None
    for w_in, w_out in halves:
        pre = mm(x, w_in)
        sig = sigmoid(pre)
        dact = mm(dmsg, w_out, NT)
        dpre = (dact * (sig * (1.0 + pre * (1.0 - sig)))).astype(BF16)
        if kept is None:
            kept = ((pre * sig).astype(BF16), dpre)
        part = mm(dpre, w_in, NT)
        total = part if total is None else total + part
    return total, kept


def normed_of(total):
    scale = lax.rsqrt(jnp.mean(total * total, axis=-1, keepdims=True) + EPS)
    return scale, scale * total


def norm_grad(grad, total):
    scale, normed = normed_of(total)
    return scale * (grad - normed * jnp.mean(grad * normed, axis=-1, keepdims=True))


def setup_kernel(groups, pairs, features, sent, *refs):
    pick, spread, pick_self, held = refs[:4]
    sends = refs[4:]
    rows = features.shape[0]
    held[...] = features[...]
    b, feat = lax.axis_index("basin"), lax.axis_index("feat")
    for route in range(-1, 2 * pairs):
        if route == 0:
            chosen = lax.broadcasted_iota(jnp.int32, (1, BLOCK), 1) + (rows - BLOCK)
        elif route >= groups:
            chosen = jnp.full((1, BLOCK), -1, jnp.int32)
        else:
            chosen = sent[pl.ds(lax.rem(b + max(route, 0), groups), 1), :]
        across = jnp.broadcast_to(chosen, (BLOCK, BLOCK))
        down = across.T
        for r in range(0, rows, BLOCK):
            at = lax.broadcasted_iota(jnp.int32, (BLOCK, BLOCK), 1) + r
            hot = (down == at).astype(F32).astype(BF16)
            if route < 0:
                pick_self[:, r : r + BLOCK] = hot
                continue

            @pl.when(route % 2 == feat)
            def _():
                pick[route // 2 * BLOCK : (route // 2 + 1) * BLOCK, r : r + BLOCK] = hot

            at = lax.broadcasted_iota(jnp.int32, (BLOCK, BLOCK), 0) + r
            if route < groups:
                spread[r : r + BLOCK, route * BLOCK : (route + 1) * BLOCK] = (
                    (across == at).astype(F32).astype(BF16)
                )
    for i, send in enumerate(sends):
        send[...] = mm(pick[i * BLOCK : (i + 1) * BLOCK, :], features[...]).astype(BF16)


def adjacency_kernel(groups, sources, values, pick_self, _, *refs):
    local, local_t, remote, remote_t, acc = refs
    rows = local.shape[0]
    own = rows // BLOCK
    b = lax.axis_index("basin")
    acc[...] = jnp.zeros_like(acc)
    for k in range(own):
        for t in range(values.shape[1]):
            v = sources[t, k]
            route = jnp.where(v == own, 0, lax.rem(b + groups - (v - own - 1), groups))
            far = jnp.where((v > own) & (route == 0), own, own + 1 + route)
            at = jnp.where(v < own, v, far)
            here = (pl.ds(k * BLOCK, BLOCK), pl.ds(pl.multiple_of(at * BLOCK, BLOCK), BLOCK))
            acc[here] += values[k, t].astype(F32)
    mine = acc[:, rows : rows + BLOCK].astype(BF16)
    full = acc[:, :rows] + mm(mine, pick_self[...])
    local[...] = full.astype(BF16)
    local_t[...] = full.T.astype(BF16)
    far = acc[:, rows + BLOCK :]
    remote[...] = far.astype(BF16)
    remote_t[...] = far.T.astype(BF16)


def message_half(x, w_in, w_out, slope, act_t=None):
    pre = mm(x, w_in)
    sig = sigmoid(pre)
    act = (pre * sig).astype(BF16)
    slope[...] = (sig * (1.0 + pre * (1.0 - sig))).astype(BF16)
    if act_t is not None:
        act_t[...] = act.T
    return mm(act, w_out)


def local_kernel(layer, x, wi0, wi1, wo0, wo1, msg, slope0, slope1, act_t, x_t):
    for r in range(0, x.shape[0], 256):
        here = slice(r, r + 256)
        rows = x[here, :]
        x_t[:, here] = rows.T
        part = message_half(rows, wi0[layer], wo0[layer], slope0.at[here, :], act_t.at[:, here])
        part = part + message_half(rows, wi1[layer], wo1[layer], slope1.at[here, :])
        msg[here, :] = part.astype(BF16)


def half_kernel(x, w_in, w_out, part, slope1):
    for r in range(0, x.shape[0], 256):
        here = slice(r, r + 256)
        part[here, :] = message_half(x[here, :], w_in[0], w_out[0], slope1.at[here, :])


def other_half_kernel(x, w_in, w_out, part, msg, slope0, act_t, x_t):
    for r in range(0, x.shape[0], 256):
        here = slice(r, r + 256)
        rows = x[here, :]
        x_t[:, here] = rows.T
        own = message_half(rows, w_in[0], w_out[0], slope0.at[here, :], act_t.at[:, here])
        msg[here, :] = (part[here, :] + own).astype(BF16)


def remote_mixed(layer, received, remote, feat, weights):
    wi0, wi1, wo0, wo1 = weights
    halves = [(wi0[layer], wo0[layer]), (wi1[layer], wo1[layer])]
    total = None
    for i, block in enumerate(received):
        route = jnp.minimum(2 * i + feat, remote.shape[1] // BLOCK - 1)
        columns = remote[:, pl.ds(pl.multiple_of(route * BLOCK, BLOCK), BLOCK)]
        part = mm(columns, message_of(block[...], halves))
        total = part if total is None else total + part
    return total


def part_kernel(layer, pairs, *refs):
    local, msg, remote = refs[:3]
    weights, received, mixed = refs[3:7], refs[7 : 7 + pairs], refs[-1]
    mixed[...] = mm(local[...], msg[...]) + remote_mixed(
        layer, received, remote, lax.axis_index("feat"), weights
    )


def mixed_total(layer, state, mixed, received, remote, weights):
    return state + mixed[...] + remote_mixed(
        layer, received, remote, 1 - lax.axis_index("feat"), weights
    )


def mix_kernel(layer, pairs, *refs):
    prev, mixed, remote, pick = refs[:4]
    weights = refs[4:8]
    received = refs[8 : 8 + pairs]
    total, inputs = refs[8 + pairs : 10 + pairs]
    sends = refs[10 + pairs :]
    state = prev[...].astype(F32) if layer == 0 else normed_of(prev[...])[1]
    total[...] = mixed_total(layer, state, mixed, received, remote, weights)
    new = normed_of(total[...])[1].astype(BF16)
    inputs[...] = new
    for i, send in enumerate(sends):
        send[...] = mm(pick[i * BLOCK : (i + 1) * BLOCK, :], new).astype(BF16)


def start_bwd(layer, groups, dtotal_now, weights, mine, others, remote_t, outs):
    dtotal, dround, far_x, far_dmsg, far_act, far_dpre = outs[:6]
    backs = outs[6:]
    wi0, wi1, wo0, wo1 = weights
    halves = [(wi0[layer], wo0[layer]), (wi1[layer], wo1[layer])]
    dtotal[...] = dtotal_now
    dround[...] = dtotal_now.astype(BF16)
    for first in range(2):

        @pl.when(lax.axis_index("feat") == first)
        def _():
            for route in range(groups):
                block = (mine, others)[(route + first) % 2][route // 2]
                far_x[route * BLOCK : (route + 1) * BLOCK, :] = block[...]

    dmsg = mm(remote_t[...], dround[...]).astype(BF16)
    back, (act, dpre) = message_grad(far_x[...], dmsg, halves)
    far_dmsg[...] = dmsg
    far_act[...] = act
    far_dpre[...] = dpre
    for i, out in enumerate(backs):
        out[...] = back[i * BLOCK : (i + 1) * BLOCK, :].astype(BF16)


def turn_kernel(layer, groups, pairs, *refs):
    prev, mixed, remote, remote_t, cot = refs[:5]
    weights = refs[5:9]
    mine, others = refs[9 : 9 + pairs], refs[9 + pairs : 9 + 2 * pairs]
    outs = refs[9 + 2 * pairs :]
    state = normed_of(prev[...])[1]
    total = mixed_total(layer, state, mixed, others, remote, weights)
    dtotal = norm_grad(cot[...], total)
    start_bwd(layer, groups, dtotal, weights, mine, others, remote_t, outs)


def back_kernel(layer, grad_scale, *refs):
    dround, local_t, slope0, slope1, act_t, x_t = refs[:6]
    wi0, wi1, wo0, wo1 = refs[6:10]
    far_x, far_dmsg, far_act, far_dpre = refs[10:14]
    back, grads, dmsg, dpre = refs[14:]
    dmsg[...] = mm(local_t[...], dround[...]).astype(BF16)
    for r in range(0, dmsg.shape[0], 256):
        here = slice(r, r + 256)
        rows = dmsg[here, :]
        dpre0 = (mm(rows, wo0[layer], NT) * slope0[here, :].astype(F32)).astype(BF16)
        dpre1 = (mm(rows, wo1[layer], NT) * slope1[here, :].astype(F32)).astype(BF16)
        dpre[here, :] = dpre0
        back[here, :] = mm(dpre0, wi0[layer], NT) + mm(dpre1, wi1[layer], NT)
    latent, hidden = x_t.shape[0], act_t.shape[0]
    g_in = (mm(x_t[...], dpre[...]) + mm(far_x[...], far_dpre[...], TN)) * grad_scale
    for j in range(hidden // LANES):
        grads[j * latent : (j + 1) * latent, :] = g_in[:, j * LANES : (j + 1) * LANES]
    g_out = (mm(act_t[...], dmsg[...]) + mm(far_act[...], far_dmsg[...], TN)) * grad_scale
    for j in range(latent // LANES):
        at = hidden // LANES * latent + j * hidden
        grads[at : at + hidden, :] = g_out[:, j * LANES : (j + 1) * LANES]


def upper(stage):
    (axis0, d0), (axis1, d1) = stage
    bit0 = lax.rem(lax.axis_index(axis0) // d0, 2)
    bit1 = lax.rem(lax.axis_index(axis1) // d1, 2)
    return jnp.where(lax.axis_index("feat") == 0, bit0, bit1)


def place(stage, own, got, out):
    m = own.shape[0]
    bit = upper(stage)
    out[pl.ds(pl.multiple_of(bit * m, m), m), :] = own[...].astype(out.dtype)
    out[pl.ds(pl.multiple_of((1 - bit) * m, m), m), :] = got[...].astype(out.dtype)


def sum_kernel(steps, *refs):
    n_in = sum(1 + (kind != "split") for kind, *_ in steps)
    n_out = len(steps) + 1 + max(group for *_, group, _ in steps)
    ins, outs, accs = refs[:n_in], refs[n_in : n_in + n_out], refs[n_in + n_out :]
    sends = outs[len(steps) :]
    for (kind, stage, back, at, group, to), out in zip(steps, outs):
        own, ins = ins[0], ins[1:]
        m = own.shape[0]
        send = sends[group].at[to : to + out.shape[0]]
        if kind != "split":
            got, ins = ins[0].at[at : at + m], ins[1:]
        if kind in ("split", "add_split"):
            if kind == "add_split":
                acc, accs = accs[0], accs[1:]
                acc[...] = own[...] + got[...].astype(F32)
                own = acc
            m = m // 2
            bit = upper(stage)
            out[...] = own[pl.ds(pl.multiple_of(bit * m, m), m), :]
            send[...] = own[pl.ds(pl.multiple_of((1 - bit) * m, m), m), :].astype(BF16)
        else:
            if kind == "place":
                place(back, own, got, out)
            else:
                out[...] = (own[...] + got[...].astype(F32)).astype(out.dtype)
            send[...] = out[...].astype(BF16)


def write_kernel(layer, stage, kept, halves, *refs):
    parts, (out_in, out_out, token, slab_in, slab_out, sem) = refs[kept:-6], refs[-6:]
    token[...] = jnp.zeros_like(token)
    bit = upper(stage)
    copies = []
    for part, (at, other) in zip(parts, halves):
        m = slab_in.size // LANES
        rows = part.at[at : at + m]
        upper_half = (1 - bit) if other else bit

        @pl.when(upper_half == 0)
        def _():
            write_slab(rows, slab_in, out_in.at[layer], sem.at[0])

        @pl.when(upper_half == 1)
        def _():
            write_slab(rows, slab_out, out_out.at[layer], sem.at[1])

        copies.append(upper_half)
    for upper_half in copies:

        @pl.when(upper_half == 0)
        def _():
            pltpu.make_async_copy(slab_in, out_in.at[layer], sem.at[0]).wait()

        @pl.when(upper_half == 1)
        def _():
            pltpu.make_async_copy(slab_out, out_out.at[layer], sem.at[1]).wait()


def write_slab(rows, slab, out, sem):
    n = slab.shape[0]
    for j in range(slab.shape[1] // LANES):
        slab[:, j * LANES : (j + 1) * LANES] = rows[j * n : (j + 1) * n, :].astype(F32)
    pltpu.make_async_copy(slab, out, sem).start()


class Sum:
    def __init__(self, whole, stages):
        self.own, self.got, self.stages, self.done = whole, None, stages, 0

    def next(self):
        n, i, rows = len(self.stages), self.done, self.own.shape[0]
        if i < n - 1:
            return "add_split" if i else "split", self.stages[i], None, rows // 2, F32
        if i == n - 1:
            return "add", self.stages[i], None, rows, F32
        stage = self.stages[2 * n - 2 - i]
        if i == n:
            return "add", stage, None, rows, BF16
        return "place", stage, self.stages[2 * n - 1 - i], rows * 2, BF16


def sum_step(sums, after):
    steps, ins, outs, scratch, groups = [], [], [], [], {}
    for one in sums:
        kind, stage, back, rows, dtype = one.next()
        group = groups.setdefault(stage, [len(groups), 0])
        steps.append((kind, stage, back, one.got and one.got[1], *group))
        group[1] += rows
        ins += [one.own, one.got[0]] if one.got else [one.own]
        outs.append(((rows, LANES), dtype))
        if kind == "add_split":
            scratch.append(pltpu.VMEM(one.own.shape, F32))
    made = call(
        functools.partial(sum_kernel, steps),
        outs + [((rows, LANES), BF16) for _, rows in groups.values()],
        ins,
        1,
        bytes_accessed=1,
        scratch=scratch,
        name="sum",
        after=after,
    )
    arrived = [swapped(x, stage) for x, stage in zip(made[len(sums) :], groups)]
    for one, own, (*_, group, at) in zip(sums, made, steps):
        one.own, one.got = own, (arrived[group], at)
        one.done += 1
    return [made[0]]


def gathered_grad(dtotal, back, returned, spread):
    far = jnp.concatenate([x[...] for x in returned], axis=0)
    return dtotal[...] + back[...] + mm(spread[...], far)


def join_kernel(layer, groups, pairs, *refs):
    dtotal, back, spread, remote_t, total = refs[:5]
    weights, refs = refs[5:9], refs[9:]
    returned, refs = refs[:groups], refs[groups:]
    mine, others, outs = refs[:pairs], refs[pairs : 2 * pairs], refs[2 * pairs :]
    grad = gathered_grad(dtotal, back, returned, spread)
    dtotal = norm_grad(grad, total[...])
    start_bwd(layer, groups, dtotal, weights, mine, others, remote_t, outs)


def last_kernel(*refs):
    dtotal, back, spread = refs[:3]
    refs[-2][...] = gathered_grad(dtotal, back, refs[3:-2], spread)
    refs[-1][...] = jnp.zeros_like(refs[-1])


def around(x, axis, distance):
    n = lax.axis_size(axis)
    return lax.ppermute(x, axis, [(i, (i + distance) % n) for i in range(n)])


def over_mesh(x, target):
    chain, groups, cores = (lax.axis_size(axis) for axis in ("chain", "basin", "feat"))
    perm = []
    for c in range(chain):
        for b in range(groups):
            for feat in range(cores):
                to = target(c, b, feat)
                if to is not None:
                    start, end = (c * groups + b) * cores + feat, (to[0] * groups + to[1]) * cores
                    perm.append((start, end + feat))
    return lax.ppermute(x, ("chain", "basin", "feat"), perm)


def swapped(x, stage):
    def partner(c, b, feat):
        axis, d = stage[feat]
        return (c ^ d, b) if axis == "chain" else (c, b ^ d)

    return over_mesh(x, partner)


def forward(sends):
    def target(i, c, b, feat):
        route = 2 * i + feat
        if route == 0:
            return (c + 1, b) if c + 1 < lax.axis_size("chain") else None
        groups = lax.axis_size("basin")
        return (c, (b + route) % groups) if route < groups else None

    return [over_mesh(x, functools.partial(target, i)) for i, x in enumerate(sends)]


def other_core(got):
    return [around(x, "feat", 1) for x in got]


def backward(grads):
    chain = lax.axis_size("chain")
    up = lax.ppermute(grads[0], "chain", [(c, c - 1) for c in range(1, chain)])
    return [up] + [around(x, "basin", -s) for s, x in enumerate(grads) if s]


def shards(features, cotangent, w_in, w_out, block_index, block_values, send_rows, send_count):
    rows, latent = features.shape
    groups = lax.axis_size("basin")
    pairs = (groups + 1) // 2
    layers, _, half = w_in.shape
    far_rows = groups * BLOCK
    own = rows // BLOCK
    grad_scale = float(rows * lax.axis_size("chain") * groups) ** (-0.5)
    last = layers - 1

    def act16(n, m=latent):
        return ((n, m), BF16)

    wi1 = around(w_in, "feat", 1)
    wo1 = around(w_out, "feat", 1)
    ffn = 4 * latent * 2 * half

    live = jnp.arange(BLOCK, dtype=jnp.int32)[None, :] < send_count[0][:, None]
    sent = jnp.where(live, send_rows[0], -1)
    sources = block_index.T
    pick, spread, pick_self, features, *sends = call(
        functools.partial(setup_kernel, groups, pairs),
        [act16(pairs * BLOCK, rows), act16(rows, far_rows), act16(BLOCK, rows), act16(rows)]
        + [act16(BLOCK)] * pairs,
        [features, sent],
        2 * rows * far_rows * latent,
        name="setup",
    )
    weights = (w_in, wi1, w_out, wo1)
    inputs = [features]
    saved = []
    totals = []
    mine = []
    others = []
    for layer in range(layers):
        mine.append(forward(sends))
        if layer == 0:
            part, slope1 = call(
                half_kernel,
                [((rows, latent), F32), act16(rows, half)],
                [features, wi1, wo1],
                rows * ffn // 2,
                name="half",
            )
            msg, slope0, act_t, x_t = call(
                other_half_kernel,
                [act16(rows), act16(rows, half), act16(half, rows), act16(latent, rows)],
                [features, w_in, w_out, part],
                rows * ffn // 2,
                name="local0",
            )
            local, local_t, remote, remote_t = call(
                functools.partial(adjacency_kernel, groups),
                [act16(rows, rows), act16(rows, rows), act16(rows, far_rows), act16(far_rows, rows)],
                [sources, block_values, pick_self, msg],
                2 * rows * rows * BLOCK,
                scratch=[pltpu.VMEM((rows, rows + BLOCK + far_rows), F32)],
                name="adjacency",
                scalars=sources,
            )
            mine[0], local = lax.optimization_barrier((mine[0], local))
        else:
            msg, slope0, slope1, act_t, x_t = call(
                functools.partial(local_kernel, layer),
                [act16(rows), act16(rows, half), act16(rows, half)]
                + [act16(half, rows), act16(latent, rows)],
                [inputs[layer], *weights],
                rows * ffn,
                name=f"local{layer}",
            )
            mine[layer], msg = lax.optimization_barrier((mine[layer], msg))
        saved.append([slope0, slope1, act_t, x_t])
        others.append(other_core(mine[layer]))
        (mixed,) = call(
            functools.partial(part_kernel, layer, pairs),
            [((rows, latent), F32)],
            [local, msg, remote, *weights, *mine[layer]],
            2 * rows * rows * latent,
            name=f"part{layer}",
        )
        prev = totals[-1] if layer else features
        if layer < last:
            total, new, *sends = call(
                functools.partial(mix_kernel, layer, pairs),
                [((rows, latent), F32), act16(rows)] + [act16(BLOCK)] * pairs,
                [prev, mixed, remote, pick, *weights, *others[layer]],
                far_rows * ffn + 2 * rows * far_rows * latent,
                name=f"mix{layer}",
            )
            totals.append(total)
            inputs.append(new)
    bwd_outs = (
        [((rows, latent), F32), act16(rows), act16(far_rows), act16(far_rows)]
        + [act16(far_rows, half)] * 2
        + [act16(BLOCK)] * groups
    )
    outs = call(
        functools.partial(turn_kernel, last, groups, pairs),
        bwd_outs,
        [totals[-1], mixed, remote, remote_t, cotangent, *weights, *mine[last], *others[last]],
        2 * far_rows * ffn,
        name="turn",
    )
    grad_rows = 2 * latent * half // LANES

    def distances(axis):
        return [(axis, 1 << i) for i in range(lax.axis_size(axis).bit_length() - 1)]

    over_basin, over_chain = distances("basin"), distances("chain")
    n = len(over_basin)
    orders = over_basin + over_chain, over_chain[:n] + over_basin + over_chain[n:]
    stages = list(zip(*orders, strict=True))
    basin_first = list(zip(orders[0], orders[0], strict=True))
    returned = {}
    sums = {}

    def back(layer, outs, after):
        returned[layer] = backward(outs[6:])
        grad, whole = call(
            functools.partial(back_kernel, layer, grad_scale),
            [((rows, latent), F32), ((grad_rows, LANES), F32)],
            [outs[1], local_t, *saved[layer], *weights, *outs[2:6]],
            3 * rows * ffn + 2 * rows * rows * latent,
            scratch=[
                pltpu.VMEM((rows, latent), BF16),
                pltpu.VMEM((rows, half), BF16),
            ],
            name=f"back{layer}",
            after=after,
        )
        sums[layer] = Sum(whole, basin_first)
        return [outs[0], grad], [grad]

    def join(layer, state, after):
        if layer:
            return call(
                functools.partial(join_kernel, layer - 1, groups, pairs),
                bwd_outs,
                [*state, spread, remote_t, totals[layer - 1]]
                + [*weights, *returned[layer], *mine[layer - 1], *others[layer - 1]],
                2 * far_rows * ffn,
                name=f"join{layer}",
                after=after,
            )
        return call(
            last_kernel,
            [((rows, latent), F32), ((8, LANES), F32)],
            [*state, spread, *returned[layer]],
            2 * rows * far_rows * latent,
            name="join0",
            after=after,
        )

    def write(layer, written, after, which=(0, 1)):
        ready = [(sums[layer].own, 0), sums[layer].got]
        ready = [ready[i] for i in which]
        kept = [*written, *after]
        return pl.pallas_call(
            functools.partial(
                write_kernel,
                layer,
                sums[layer].stages[0],
                len(kept),
                [(at, i) for (_, at), i in zip(ready, which)],
            ),
            out_shape=[
                jax.ShapeDtypeStruct((layers, latent, half), F32),
                jax.ShapeDtypeStruct((layers, half, latent), F32),
                jax.ShapeDtypeStruct((8, LANES), F32),
            ],
            in_specs=[ANY] * len(kept) + [VMEM] * len(ready),
            out_specs=[ANY] * 2 + [VMEM],
            scratch_shapes=[
                pltpu.VMEM((latent, half), F32),
                pltpu.VMEM((half, latent), F32),
                pltpu.SemaphoreType.DMA((2,)),
            ],
            input_output_aliases={i: i for i in range(len(written))},
            compiler_params=pltpu.CompilerParams(vmem_limit_bytes=LIMIT),
            cost_estimate=pl.CostEstimate(flops=1, bytes_accessed=1, transcendentals=0),
            name=f"write{layer}",
        )(*written, *after, *[x for x, _ in ready])

    count = 2 * len(stages) - 1
    at = []
    for layer in reversed(range(layers)):
        state, at = back(layer, outs, at)
        arrived = [sums[above].got[0] for above in range(layer + 2, layers)]
        if layer:
            arrived += returned[layer]
        at = sum_step([sums[layer]], at + arrived)
        if layer:
            for above in range(layer + 1, layers):
                at = sum_step([sums[above]], at)
            outs = join(layer, state, at)
            at = outs[1:2]
    while sums[0].done < count:
        for layer in reversed(range(layers)):
            if sums[layer].done < count:
                if layer == 0 and sums[0].done == count - 1:
                    at = at + returned[0] + [sums[above].got[0] for above in range(2, layers)]
                at = sum_step([sums[layer]], at)
    grad, token = join(0, state, at)
    at = [token]
    written = []
    for layer in reversed(range(1, layers)):
        *written, token = write(layer, written, at)
        at = [token]
    *written, token = write(0, written, at, (0,))
    *written, token = write(0, written, [token], (1,))
    return (grad, *written)


def solution(mesh):
    placed = (
        P(("runs", "chain", "basin"), None),
        P(("runs", "chain", "basin"), None),
        P(None, None, "feat"),
        P(None, "feat", None),
        P(("chain", "basin"), None),
        P(("chain", "basin"), None, None, None),
        P(("chain", "basin"), None, None),
        P(("chain", "basin"), None),
    )
    return jax.shard_map(
        shards,
        mesh=mesh,
        in_specs=placed,
        out_specs=(
            P(("runs", "chain", "basin"), None),
            P("runs", None, "feat"),
            P("runs", "feat", None),
        ),
        check_vma=False,
    )
```

```python
import functools

import jax
import jax.numpy as jnp
from jax import lax
from jax.experimental import pallas as pl
from jax.experimental.pallas import tpu as pltpu
from jax.sharding import PartitionSpec as P

BLOCK = 128
LANES = 128
EPS = 1e-06
F32 = jnp.float32
BF16 = jnp.bfloat16
VMEM = pl.BlockSpec(memory_space=pltpu.VMEM)
SMEM = pl.BlockSpec(memory_space=pltpu.SMEM)
ANY = pl.BlockSpec(memory_space=pl.ANY)
NN = (((1,), (0,)), ((), ()))
NT = (((1,), (1,)), ((), ()))
TN = (((0,), (0,)), ((), ()))


def mm(a, b, dims=NN):
    return lax.dot_general(a, b, dims, preferred_element_type=F32)


LIMIT = 24 * 1024 * 1024


def call(body, outs, ins, flops, scratch=(), name=None, after=(), bytes_accessed=4_000_000, scalars=None):
    skipped = len(after)
    return pl.pallas_call(
        lambda *refs: body(*refs[skipped:]),
        out_shape=[jax.ShapeDtypeStruct(s, d) for s, d in outs],
        in_specs=[ANY] * skipped + [SMEM if x is scalars else VMEM for x in ins],
        out_specs=[VMEM] * len(outs),
        scratch_shapes=list(scratch),
        compiler_params=pltpu.CompilerParams(vmem_limit_bytes=LIMIT),
        cost_estimate=pl.CostEstimate(
            flops=flops, bytes_accessed=bytes_accessed, transcendentals=0
        ),
        name=name,
    )(*after, *ins)


def sigmoid(v):
    return 1.0 / (1.0 + jnp.exp(-v))


def half_message(x, w_in, w_out):
    pre = mm(x, w_in)
    return mm((pre * sigmoid(pre)).astype(BF16), w_out)


def message_of(x, halves):
    total = None
    for w_in, w_out in halves:
        part = half_message(x, w_in, w_out)
        total = part if total is None else total + part
    return total.astype(BF16)


def message_grad(x, dmsg, halves):
    total = None
    kept = None
    for w_in, w_out in halves:
        pre = mm(x, w_in)
        sig = sigmoid(pre)
        dact = mm(dmsg, w_out, NT)
        dpre = (dact * (sig * (1.0 + pre * (1.0 - sig)))).astype(BF16)
        if kept is None:
            kept = ((pre * sig).astype(BF16), dpre)
        part = mm(dpre, w_in, NT)
        total = part if total is None else total + part
    return total, kept


def normed_of(total):
    scale = lax.rsqrt(jnp.mean(total * total, axis=-1, keepdims=True) + EPS)
    return scale, scale * total


def norm_grad(grad, total):
    scale, normed = normed_of(total)
    return scale * (grad - normed * jnp.mean(grad * normed, axis=-1, keepdims=True))


def setup_kernel(groups, pairs, features, sent, *refs):
    pick, spread, pick_self, held = refs[:4]
    sends = refs[4:]
    rows = features.shape[0]
    held[...] = features[...]
    b, feat = lax.axis_index("basin"), lax.axis_index("feat")
    for route in range(-1, 2 * pairs):
        if route == 0:
            chosen = lax.broadcasted_iota(jnp.int32, (1, BLOCK), 1) + (rows - BLOCK)
        elif route >= groups:
            chosen = jnp.full((1, BLOCK), -1, jnp.int32)
        else:
            chosen = sent[pl.ds(lax.rem(b + max(route, 0), groups), 1), :]
        across = jnp.broadcast_to(chosen, (BLOCK, BLOCK))
        down = across.T
        for r in range(0, rows, BLOCK):
            at = lax.broadcasted_iota(jnp.int32, (BLOCK, BLOCK), 1) + r
            hot = (down == at).astype(F32).astype(BF16)
            if route < 0:
                pick_self[:, r : r + BLOCK] = hot
                continue

            @pl.when(route % 2 == feat)
            def _():
                pick[route // 2 * BLOCK : (route // 2 + 1) * BLOCK, r : r + BLOCK] = hot

            at = lax.broadcasted_iota(jnp.int32, (BLOCK, BLOCK), 0) + r
            if route < groups:
                spread[r : r + BLOCK, route * BLOCK : (route + 1) * BLOCK] = (
                    (across == at).astype(F32).astype(BF16)
                )
    for i, send in enumerate(sends):
        send[...] = mm(pick[i * BLOCK : (i + 1) * BLOCK, :], features[...]).astype(BF16)


def adjacency_kernel(groups, sources, values, pick_self, _, *refs):
    local, local_t, remote, remote_t, acc = refs
    rows = local.shape[0]
    own = rows // BLOCK
    b = lax.axis_index("basin")
    acc[...] = jnp.zeros_like(acc)
    for k in range(own):
        for t in range(values.shape[1]):
            v = sources[t, k]
            route = jnp.where(v == own, 0, lax.rem(b + groups - (v - own - 1), groups))
            far = jnp.where((v > own) & (route == 0), own, own + 1 + route)
            at = jnp.where(v < own, v, far)
            here = (pl.ds(k * BLOCK, BLOCK), pl.ds(pl.multiple_of(at * BLOCK, BLOCK), BLOCK))
            acc[here] += values[k, t].astype(F32)
    mine = acc[:, rows : rows + BLOCK].astype(BF16)
    full = acc[:, :rows] + mm(mine, pick_self[...])
    local[...] = full.astype(BF16)
    local_t[...] = full.T.astype(BF16)
    far = acc[:, rows + BLOCK :]
    remote[...] = far.astype(BF16)
    remote_t[...] = far.T.astype(BF16)


def message_half(x, w_in, w_out, slope, act_t=None):
    pre = mm(x, w_in)
    sig = sigmoid(pre)
    act = (pre * sig).astype(BF16)
    slope[...] = (sig * (1.0 + pre * (1.0 - sig))).astype(BF16)
    if act_t is not None:
        act_t[...] = act.T
    return mm(act, w_out)


def local_kernel(layer, x, wi0, wi1, wo0, wo1, msg, slope0, slope1, act_t, x_t):
    for r in range(0, x.shape[0], 256):
        here = slice(r, r + 256)
        rows = x[here, :]
        x_t[:, here] = rows.T
        part = message_half(rows, wi0[layer], wo0[layer], slope0.at[here, :], act_t.at[:, here])
        part = part + message_half(rows, wi1[layer], wo1[layer], slope1.at[here, :])
        msg[here, :] = part.astype(BF16)


def half_kernel(x, w_in, w_out, part, slope1):
    for r in range(0, x.shape[0], 256):
        here = slice(r, r + 256)
        part[here, :] = message_half(x[here, :], w_in[0], w_out[0], slope1.at[here, :])


def other_half_kernel(x, w_in, w_out, part, msg, slope0, act_t, x_t):
    for r in range(0, x.shape[0], 256):
        here = slice(r, r + 256)
        rows = x[here, :]
        x_t[:, here] = rows.T
        own = message_half(rows, w_in[0], w_out[0], slope0.at[here, :], act_t.at[:, here])
        msg[here, :] = (part[here, :] + own).astype(BF16)


def remote_mixed(layer, received, remote, feat, weights):
    wi0, wi1, wo0, wo1 = weights
    halves = [(wi0[layer], wo0[layer]), (wi1[layer], wo1[layer])]
    total = None
    for i, block in enumerate(received):
        route = jnp.minimum(2 * i + feat, remote.shape[1] // BLOCK - 1)
        columns = remote[:, pl.ds(pl.multiple_of(route * BLOCK, BLOCK), BLOCK)]
        part = mm(columns, message_of(block[...], halves))
        total = part if total is None else total + part
    return total


def part_kernel(layer, pairs, *refs):
    local, msg, remote = refs[:3]
    weights, received, mixed = refs[3:7], refs[7 : 7 + pairs], refs[-1]
    mixed[...] = mm(local[...], msg[...]) + remote_mixed(
        layer, received, remote, lax.axis_index("feat"), weights
    )


def mixed_total(layer, state, mixed, received, remote, weights):
    return state + mixed[...] + remote_mixed(
        layer, received, remote, 1 - lax.axis_index("feat"), weights
    )


def mix_kernel(layer, pairs, *refs):
    prev, mixed, remote, pick = refs[:4]
    weights = refs[4:8]
    received = refs[8 : 8 + pairs]
    total, inputs = refs[8 + pairs : 10 + pairs]
    sends = refs[10 + pairs :]
    state = prev[...].astype(F32) if layer == 0 else normed_of(prev[...])[1]
    total[...] = mixed_total(layer, state, mixed, received, remote, weights)
    new = normed_of(total[...])[1].astype(BF16)
    inputs[...] = new
    for i, send in enumerate(sends):
        send[...] = mm(pick[i * BLOCK : (i + 1) * BLOCK, :], new).astype(BF16)


def start_bwd(layer, groups, dtotal_now, weights, mine, others, remote_t, outs):
    dtotal, dround, far_x, far_dmsg, far_act, far_dpre = outs[:6]
    backs = outs[6:]
    wi0, wi1, wo0, wo1 = weights
    halves = [(wi0[layer], wo0[layer]), (wi1[layer], wo1[layer])]
    dtotal[...] = dtotal_now
    dround[...] = dtotal_now.astype(BF16)
    for first in range(2):

        @pl.when(lax.axis_index("feat") == first)
        def _():
            for route in range(groups):
                block = (mine, others)[(route + first) % 2][route // 2]
                far_x[route * BLOCK : (route + 1) * BLOCK, :] = block[...]

    dmsg = mm(remote_t[...], dround[...]).astype(BF16)
    back, (act, dpre) = message_grad(far_x[...], dmsg, halves)
    far_dmsg[...] = dmsg
    far_act[...] = act
    far_dpre[...] = dpre
    for i, out in enumerate(backs):
        out[...] = back[i * BLOCK : (i + 1) * BLOCK, :].astype(BF16)


def turn_kernel(layer, groups, pairs, *refs):
    prev, mixed, remote, remote_t, cot = refs[:5]
    weights = refs[5:9]
    mine, others = refs[9 : 9 + pairs], refs[9 + pairs : 9 + 2 * pairs]
    outs = refs[9 + 2 * pairs :]
    state = normed_of(prev[...])[1]
    total = mixed_total(layer, state, mixed, others, remote, weights)
    dtotal = norm_grad(cot[...], total)
    start_bwd(layer, groups, dtotal, weights, mine, others, remote_t, outs)


def back_kernel(layer, grad_scale, *refs):
    dround, local_t, slope0, slope1, act_t, x_t = refs[:6]
    wi0, wi1, wo0, wo1 = refs[6:10]
    far_x, far_dmsg, far_act, far_dpre = refs[10:14]
    back, grads, dmsg, dpre = refs[14:]
    dmsg[...] = mm(local_t[...], dround[...]).astype(BF16)
    for r in range(0, dmsg.shape[0], 256):
        here = slice(r, r + 256)
        rows = dmsg[here, :]
        dpre0 = (mm(rows, wo0[layer], NT) * slope0[here, :].astype(F32)).astype(BF16)
        dpre1 = (mm(rows, wo1[layer], NT) * slope1[here, :].astype(F32)).astype(BF16)
        dpre[here, :] = dpre0
        back[here, :] = mm(dpre0, wi0[layer], NT) + mm(dpre1, wi1[layer], NT)
    latent, hidden = x_t.shape[0], act_t.shape[0]
    g_in = (mm(x_t[...], dpre[...]) + mm(far_x[...], far_dpre[...], TN)) * grad_scale
    for j in range(hidden // LANES):
        grads[j * latent : (j + 1) * latent, :] = g_in[:, j * LANES : (j + 1) * LANES]
    g_out = (mm(act_t[...], dmsg[...]) + mm(far_act[...], far_dmsg[...], TN)) * grad_scale
    for j in range(latent // LANES):
        at = hidden // LANES * latent + j * hidden
        grads[at : at + hidden, :] = g_out[:, j * LANES : (j + 1) * LANES]


def upper(stage):
    (axis0, d0), (axis1, d1) = stage
    bit0 = lax.rem(lax.axis_index(axis0) // d0, 2)
    bit1 = lax.rem(lax.axis_index(axis1) // d1, 2)
    return jnp.where(lax.axis_index("feat") == 0, bit0, bit1)


def place(stage, own, got, out):
    m = own.shape[0]
    bit = upper(stage)
    out[pl.ds(pl.multiple_of(bit * m, m), m), :] = own[...].astype(out.dtype)
    out[pl.ds(pl.multiple_of((1 - bit) * m, m), m), :] = got[...].astype(out.dtype)


def sum_kernel(steps, *refs):
    n_in = sum(1 + (kind != "split") for kind, *_ in steps)
    n_out = len(steps) + 1 + max(group for *_, group, _ in steps)
    ins, outs, accs = refs[:n_in], refs[n_in : n_in + n_out], refs[n_in + n_out :]
    sends = outs[len(steps) :]
    for (kind, stage, back, at, group, to), out in zip(steps, outs):
        own, ins = ins[0], ins[1:]
        m = own.shape[0]
        send = sends[group].at[to : to + out.shape[0]]
        if kind != "split":
            got, ins = ins[0].at[at : at + m], ins[1:]
        if kind in ("split", "add_split"):
            if kind == "add_split":
                acc, accs = accs[0], accs[1:]
                acc[...] = own[...] + got[...].astype(F32)
                own = acc
            m = m // 2
            bit = upper(stage)
            out[...] = own[pl.ds(pl.multiple_of(bit * m, m), m), :]
            send[...] = own[pl.ds(pl.multiple_of((1 - bit) * m, m), m), :].astype(BF16)
        else:
            if kind == "place":
                place(back, own, got, out)
            else:
                out[...] = (own[...] + got[...].astype(F32)).astype(out.dtype)
            send[...] = out[...].astype(BF16)


def write_kernel(layer, stage, kept, halves, *refs):
    parts, (out_in, out_out, token, slab_in, slab_out, sem) = refs[kept:-6], refs[-6:]
    token[...] = jnp.zeros_like(token)
    bit = upper(stage)
    copies = []
    for part, (at, other) in zip(parts, halves):
        m = slab_in.size // LANES
        rows = part.at[at : at + m]
        upper_half = (1 - bit) if other else bit

        @pl.when(upper_half == 0)
        def _():
            write_slab(rows, slab_in, out_in.at[layer], sem.at[0])

        @pl.when(upper_half == 1)
        def _():
            write_slab(rows, slab_out, out_out.at[layer], sem.at[1])

        copies.append(upper_half)
    for upper_half in copies:

        @pl.when(upper_half == 0)
        def _():
            pltpu.make_async_copy(slab_in, out_in.at[layer], sem.at[0]).wait()

        @pl.when(upper_half == 1)
        def _():
            pltpu.make_async_copy(slab_out, out_out.at[layer], sem.at[1]).wait()


def write_slab(rows, slab, out, sem):
    n = slab.shape[0]
    for j in range(slab.shape[1] // LANES):
        slab[:, j * LANES : (j + 1) * LANES] = rows[j * n : (j + 1) * n, :].astype(F32)
    pltpu.make_async_copy(slab, out, sem).start()


class Sum:
    def __init__(self, whole, stages):
        self.own, self.got, self.stages, self.done = whole, None, stages, 0

    def next(self):
        n, i, rows = len(self.stages), self.done, self.own.shape[0]
        if i < n - 1:
            return "add_split" if i else "split", self.stages[i], None, rows // 2, F32
        if i == n - 1:
            return "add", self.stages[i], None, rows, F32
        stage = self.stages[2 * n - 2 - i]
        if i == n:
            return "add", stage, None, rows, BF16
        return "place", stage, self.stages[2 * n - 1 - i], rows * 2, BF16


def sum_step(sums, after):
    steps, ins, outs, scratch, groups = [], [], [], [], {}
    for one in sums:
        kind, stage, back, rows, dtype = one.next()
        group = groups.setdefault(stage, [len(groups), 0])
        steps.append((kind, stage, back, one.got and one.got[1], *group))
        group[1] += rows
        ins += [one.own, one.got[0]] if one.got else [one.own]
        outs.append(((rows, LANES), dtype))
        if kind == "add_split":
            scratch.append(pltpu.VMEM(one.own.shape, F32))
    made = call(
        functools.partial(sum_kernel, steps),
        outs + [((rows, LANES), BF16) for _, rows in groups.values()],
        ins,
        1,
        bytes_accessed=1,
        scratch=scratch,
        name="sum",
        after=after,
    )
    arrived = [swapped(x, stage) for x, stage in zip(made[len(sums) :], groups)]
    for one, own, (*_, group, at) in zip(sums, made, steps):
        one.own, one.got = own, (arrived[group], at)
        one.done += 1
    return [made[0]]


def gathered_grad(dtotal, back, returned, spread):
    far = jnp.concatenate([x[...] for x in returned], axis=0)
    return dtotal[...] + back[...] + mm(spread[...], far)


def join_kernel(layer, groups, pairs, *refs):
    dtotal, back, spread, remote_t, total = refs[:5]
    weights, refs = refs[5:9], refs[9:]
    returned, refs = refs[:groups], refs[groups:]
    mine, others, outs = refs[:pairs], refs[pairs : 2 * pairs], refs[2 * pairs :]
    grad = gathered_grad(dtotal, back, returned, spread)
    dtotal = norm_grad(grad, total[...])
    start_bwd(layer, groups, dtotal, weights, mine, others, remote_t, outs)


def last_kernel(*refs):
    dtotal, back, spread = refs[:3]
    refs[-2][...] = gathered_grad(dtotal, back, refs[3:-2], spread)
    refs[-1][...] = jnp.zeros_like(refs[-1])


def around(x, axis, distance):
    n = lax.axis_size(axis)
    return lax.ppermute(x, axis, [(i, (i + distance) % n) for i in range(n)])


def over_mesh(x, target):
    chain, groups, cores = (lax.axis_size(axis) for axis in ("chain", "basin", "feat"))
    perm = []
    for c in range(chain):
        for b in range(groups):
            for feat in range(cores):
                to = target(c, b, feat)
                if to is not None:
                    start, end = (c * groups + b) * cores + feat, (to[0] * groups + to[1]) * cores
                    perm.append((start, end + feat))
    return lax.ppermute(x, ("chain", "basin", "feat"), perm)


def swapped(x, stage):
    def partner(c, b, feat):
        axis, d = stage[feat]
        return (c ^ d, b) if axis == "chain" else (c, b ^ d)

    return over_mesh(x, partner)


def forward(sends):
    def target(i, c, b, feat):
        route = 2 * i + feat
        if route == 0:
            return (c + 1, b) if c + 1 < lax.axis_size("chain") else None
        groups = lax.axis_size("basin")
        return (c, (b + route) % groups) if route < groups else None

    return [over_mesh(x, functools.partial(target, i)) for i, x in enumerate(sends)]


def other_core(got):
    return [around(x, "feat", 1) for x in got]


def backward(grads):
    chain = lax.axis_size("chain")
    up = lax.ppermute(grads[0], "chain", [(c, c - 1) for c in range(1, chain)])
    return [up] + [around(x, "basin", -s) for s, x in enumerate(grads) if s]


def shards(features, cotangent, w_in, w_out, block_index, block_values, send_rows, send_count):
    rows, latent = features.shape
    groups = lax.axis_size("basin")
    pairs = (groups + 1) // 2
    layers, _, half = w_in.shape
    far_rows = groups * BLOCK
    own = rows // BLOCK
    grad_scale = float(rows * lax.axis_size("chain") * groups) ** (-0.5)
    last = layers - 1

    def act16(n, m=latent):
        return ((n, m), BF16)

    wi1 = around(w_in, "feat", 1)
    wo1 = around(w_out, "feat", 1)
    ffn = 4 * latent * 2 * half

    live = jnp.arange(BLOCK, dtype=jnp.int32)[None, :] < send_count[0][:, None]
    sent = jnp.where(live, send_rows[0], -1)
    sources = block_index.T
    pick, spread, pick_self, features, *sends = call(
        functools.partial(setup_kernel, groups, pairs),
        [act16(pairs * BLOCK, rows), act16(rows, far_rows), act16(BLOCK, rows), act16(rows)]
        + [act16(BLOCK)] * pairs,
        [features, sent],
        2 * rows * far_rows * latent,
        name="setup",
    )
    weights = (w_in, wi1, w_out, wo1)
    inputs = [features]
    saved = []
    totals = []
    mine = []
    others = []
    for layer in range(layers):
        mine.append(forward(sends))
        if layer == 0:
            part, slope1 = call(
                half_kernel,
                [((rows, latent), F32), act16(rows, half)],
                [features, wi1, wo1],
                rows * ffn // 2,
                name="half",
            )
            msg, slope0, act_t, x_t = call(
                other_half_kernel,
                [act16(rows), act16(rows, half), act16(half, rows), act16(latent, rows)],
                [features, w_in, w_out, part],
                rows * ffn // 2,
                name="local0",
            )
            local, local_t, remote, remote_t = call(
                functools.partial(adjacency_kernel, groups),
                [act16(rows, rows), act16(rows, rows), act16(rows, far_rows), act16(far_rows, rows)],
                [sources, block_values, pick_self, msg],
                2 * rows * rows * BLOCK,
                scratch=[pltpu.VMEM((rows, rows + BLOCK + far_rows), F32)],
                name="adjacency",
                scalars=sources,
            )
            mine[0], local = lax.optimization_barrier((mine[0], local))
        else:
            msg, slope0, slope1, act_t, x_t = call(
                functools.partial(local_kernel, layer),
                [act16(rows), act16(rows, half), act16(rows, half)]
                + [act16(half, rows), act16(latent, rows)],
                [inputs[layer], *weights],
                rows * ffn,
                name=f"local{layer}",
            )
            mine[layer], msg = lax.optimization_barrier((mine[layer], msg))
        saved.append([slope0, slope1, act_t, x_t])
        others.append(other_core(mine[layer]))
        (mixed,) = call(
            functools.partial(part_kernel, layer, pairs),
            [((rows, latent), F32)],
            [local, msg, remote, *weights, *mine[layer]],
            2 * rows * rows * latent,
            name=f"part{layer}",
        )
        prev = totals[-1] if layer else features
        if layer < last:
            total, new, *sends = call(
                functools.partial(mix_kernel, layer, pairs),
                [((rows, latent), F32), act16(rows)] + [act16(BLOCK)] * pairs,
                [prev, mixed, remote, pick, *weights, *others[layer]],
                far_rows * ffn + 2 * rows * far_rows * latent,
                name=f"mix{layer}",
            )
            totals.append(total)
            inputs.append(new)
    bwd_outs = (
        [((rows, latent), F32), act16(rows), act16(far_rows), act16(far_rows)]
        + [act16(far_rows, half)] * 2
        + [act16(BLOCK)] * groups
    )
    outs = call(
        functools.partial(turn_kernel, last, groups, pairs),
        bwd_outs,
        [totals[-1], mixed, remote, remote_t, cotangent, *weights, *mine[last], *others[last]],
        2 * far_rows * ffn,
        name="turn",
    )
    grad_rows = 2 * latent * half // LANES

    def distances(axis):
        return [(axis, 1 << i) for i in range(lax.axis_size(axis).bit_length() - 1)]

    over_basin, over_chain = distances("basin"), distances("chain")
    n = len(over_basin)
    orders = over_basin + over_chain, over_chain[:n] + over_basin + over_chain[n:]
    stages = list(zip(*orders, strict=True))
    basin_first = list(zip(orders[0], orders[0], strict=True))
    returned = {}
    sums = {}

    def back(layer, outs, after):
        returned[layer] = backward(outs[6:])
        grad, whole = call(
            functools.partial(back_kernel, layer, grad_scale),
            [((rows, latent), F32), ((grad_rows, LANES), F32)],
            [outs[1], local_t, *saved[layer], *weights, *outs[2:6]],
            3 * rows * ffn + 2 * rows * rows * latent,
            scratch=[
                pltpu.VMEM((rows, latent), BF16),
                pltpu.VMEM((rows, half), BF16),
            ],
            name=f"back{layer}",
            after=after,
        )
        sums[layer] = Sum(whole, basin_first if layer else stages)
        return [outs[0], grad], [grad]

    def join(layer, state, after):
        if layer:
            return call(
                functools.partial(join_kernel, layer - 1, groups, pairs),
                bwd_outs,
                [*state, spread, remote_t, totals[layer - 1]]
                + [*weights, *returned[layer], *mine[layer - 1], *others[layer - 1]],
                2 * far_rows * ffn,
                name=f"join{layer}",
                after=after,
            )
        return call(
            last_kernel,
            [((rows, latent), F32), ((8, LANES), F32)],
            [*state, spread, *returned[layer]],
            2 * rows * far_rows * latent,
            name="join0",
            after=after,
        )

    def write(layer, written, after, which=(0, 1)):
        ready = [(sums[layer].own, 0), sums[layer].got]
        ready = [ready[i] for i in which]
        kept = [*written, *after]
        return pl.pallas_call(
            functools.partial(
                write_kernel,
                layer,
                sums[layer].stages[0],
                len(kept),
                [(at, i) for (_, at), i in zip(ready, which)],
            ),
            out_shape=[
                jax.ShapeDtypeStruct((layers, latent, half), F32),
                jax.ShapeDtypeStruct((layers, half, latent), F32),
                jax.ShapeDtypeStruct((8, LANES), F32),
            ],
            in_specs=[ANY] * len(kept) + [VMEM] * len(ready),
            out_specs=[ANY] * 2 + [VMEM],
            scratch_shapes=[
                pltpu.VMEM((latent, half), F32),
                pltpu.VMEM((half, latent), F32),
                pltpu.SemaphoreType.DMA((2,)),
            ],
            input_output_aliases={i: i for i in range(len(written))},
            compiler_params=pltpu.CompilerParams(vmem_limit_bytes=LIMIT),
            cost_estimate=pl.CostEstimate(flops=1, bytes_accessed=1, transcendentals=0),
            name=f"write{layer}",
        )(*written, *after, *[x for x, _ in ready])

    count = 2 * len(stages) - 1
    at = []
    for layer in reversed(range(layers)):
        state, at = back(layer, outs, at)
        arrived = [sums[above].got[0] for above in range(layer + 2, layers)]
        if layer:
            arrived += returned[layer]
        at = sum_step([sums[layer]], at + arrived)
        if layer:
            for above in range(layer + 1, layers):
                at = sum_step([sums[above]], at)
            outs = join(layer, state, at)
            at = outs[1:2]
    while sums[0].done < count:
        turn = list(reversed(range(layers)))
        if sums[0].done == 1 and layers > 2:
            turn = [*turn[1:-1], turn[0], 0]
        for layer in turn:
            if sums[layer].done < count:
                if layer == 0 and sums[0].done == count - 1:
                    at = at + returned[0] + [sums[above].got[0] for above in range(2, layers)]
                at = sum_step([sums[layer]], at)
    grad, token = join(0, state, at)
    at = [token]
    written = []
    for layer in reversed(range(1, layers)):
        *written, token = write(layer, written, at)
        at = [token]
    *written, token = write(0, written, at, (0,))
    *written, token = write(0, written, [token], (1,))
    return (grad, *written)


def solution(mesh):
    placed = (
        P(("runs", "chain", "basin"), None),
        P(("runs", "chain", "basin"), None),
        P(None, None, "feat"),
        P(None, "feat", None),
        P(("chain", "basin"), None),
        P(("chain", "basin"), None, None, None),
        P(("chain", "basin"), None, None),
        P(("chain", "basin"), None),
    )
    return jax.shard_map(
        shards,
        mesh=mesh,
        in_specs=placed,
        out_specs=(
            P(("runs", "chain", "basin"), None),
            P("runs", None, "feat"),
            P("runs", "feat", None),
        ),
        check_vma=False,
    )
```
